256 devices in a mesh: gx: 8 (over x, core), gy: 8 (over z), gz: 4 (over y).
Axes of the slice: x: 4, y: 4, z: 8, core: 2. Of those that a mesh axis runs over, the one named last changes fastest.
Arguments:
- coarse_state: float32 [5, 128, 128, 256], P(None, 'gx', 'gy', 'gz'), may hold values from -1 to 5.75, as said below
- fine_state: float32 [2048, 5, 4096], P(('gx', 'gy', 'gz')), may hold values from -1 to 5.75, as said below
- slot_parent: int32 [2048], replicated, may hold values from -1 to 255, as said below
- slot_corner: int32 [2048, 3], replicated, may hold values from 0 to 55, as said below
Outputs:
- coarse_next: float32 [5, 128, 128, 256], P(None, 'gx', 'gy', 'gz')
- fine_next: float32 [2048, 5, 4096], P(('gx', 'gy', 'gz'))
The draws below stay inside these ranges and needn't reach their ends.
Inputs may be any that keep to these rules, and one draw needn't show every extreme that they name: `coarse_state`: each cell is a gas state with density and pressure in [0.5, 2] and velocity components in [-0.5, 0.5]. `fine_state`: each cell is a gas state with density and pressure in [0.5, 2] and velocity components in [-0.5, 0.5]. `slot_parent`: slots d * 8 to d * 8 + 7 belong to device d (gx slowest, gz fastest); a device's filled slots come first. A parent has the same gx index as the owner. Every device is the parent of exactly 4 boxes, owned by 4 different devices. In every draw some device fills all 8 slots. `slot_corner`: for a filled slot, the footprint and the cycle of coarse cells around it lie inside the parent's block of 16 x 16 x 64 cells, and footprints and cycles of different boxes are disjoint. Empty slots hold 0, 0, 0.
All inputs are finite; a program needn't handle non-finite values.
Results may differ from the reference program's by a relative error of at most 0.0003.
Values sent between devices are 32-bit elements; how exact they have to be, the bound alone decides.
A program may use at most 128 MiB of HBM per device.

```python
import math
import jax
import jax.numpy as jnp
from jax import lax

FX = 16
FY = 16
FZ = 16
REGIONS = 4
BOXMAX = 8
CX = 16
CY = 16
CZ = 64
NX = 128
NY = 128
NZ = 256
SLOTS = 2048
FCELLS = 4096
N_GX = 8
N_GY = 8
N_GZ = 4


ADIABATIC = 1.4


def conserved(density, velocity_x, velocity_y, velocity_z, pressure, stack_axis):
    energy = pressure / (ADIABATIC - 1.0) + 0.5 * density * (velocity_x * velocity_x + velocity_y * velocity_y + velocity_z * velocity_z)
    return jnp.stack([density, density * velocity_x, density * velocity_y, density * velocity_z, energy], axis=stack_axis)


def layout(key):
    members = N_GY * N_GZ
    pairs = members // 2
    subkeys = jax.random.split(key, 8)
    order = jax.vmap(lambda subkey: jax.random.permutation(subkey, members))(jax.random.split(subkeys[0], N_GX))
    shifts = jax.random.randint(subkeys[1], (N_GX, pairs), 0, REGIONS + 1)
    picked = jax.random.randint(subkeys[2], (N_GX, 1), 0, pairs)
    shifts = jnp.where(jnp.arange(pairs, dtype=jnp.int32)[None, :] == picked, REGIONS, shifts)
    rows_index = jnp.arange(N_GX, dtype=jnp.int32)[:, None]
    loads = jnp.zeros((N_GX, members), jnp.int32)
    loads = loads.at[rows_index, order[:, 0::2]].set(REGIONS + shifts)
    loads = loads.at[rows_index, order[:, 1::2]].set(REGIONS - shifts)
    starts = jnp.cumsum(loads, axis=1) - loads
    parent_order = jax.vmap(lambda subkey: jax.random.permutation(subkey, members))(jax.random.split(subkeys[3], N_GX))
    slot_ids = jnp.arange(BOXMAX, dtype=jnp.int32)
    filled = slot_ids[None, None, :] < loads[:, :, None]
    tokens = jnp.where(filled, starts[:, :, None] + slot_ids[None, None, :], 0)
    region = tokens // members
    within = jnp.take_along_axis(parent_order, (tokens % members).reshape(N_GX, -1), axis=1).reshape(N_GX, members, BOXMAX)
    parent = jnp.where(filled, rows_index[:, :, None] * members + within, -1)
    extent = (N_GX, members, BOXMAX)
    offset_x = jax.random.randint(subkeys[4], extent, 1, FX // 2)
    offset_y = jax.random.randint(subkeys[5], extent, 1, FY // 2)
    offset_z = jax.random.randint(subkeys[6], extent, 1, FZ // 2)
    offset_z = jnp.where(tokens == (REGIONS - 1) * members, FZ // 2 - 1, offset_z)
    corner_x = offset_x
    corner_y = offset_y
    corner_z = region * FZ + offset_z
    corner = jnp.stack([corner_x, corner_y, corner_z], axis=-1)
    corner = jnp.where(filled[..., None], corner, 0)
    return (parent.reshape(-1).astype(jnp.int32), corner.reshape(-1, 3).astype(jnp.int32))


def draw_slot_parent(key, part):
    parent, corner = layout(key)
    return parent


def draw_slot_corner(key, part):
    parent, corner = layout(key)
    return corner


def draw_coarse_state(key, part):
    key = jax.random.fold_in(key, 11)
    subkeys = jax.random.split(key, 5)
    extent = (NX, NY, NZ)
    density = jnp.exp(jax.random.uniform(subkeys[0], extent, jnp.float32, math.log(0.5), math.log(2.0)))
    velocity_x = jax.random.uniform(subkeys[1], extent, jnp.float32, -0.5, 0.5)
    velocity_y = jax.random.uniform(subkeys[2], extent, jnp.float32, -0.5, 0.5)
    velocity_z = jax.random.uniform(subkeys[3], extent, jnp.float32, -0.5, 0.5)
    pressure = jnp.exp(jax.random.uniform(subkeys[4], extent, jnp.float32, math.log(0.5), math.log(2.0)))
    return conserved(density, velocity_x, velocity_y, velocity_z, pressure, 0)


def draw_fine_state(key, part):
    key = jax.random.fold_in(key, 13)
    subkeys = jax.random.split(key, 5)
    extent = (SLOTS, FCELLS)
    density = jnp.exp(jax.random.uniform(subkeys[0], extent, jnp.float32, math.log(0.5), math.log(2.0)))
    velocity_x = jax.random.uniform(subkeys[1], extent, jnp.float32, -0.5, 0.5)
    velocity_y = jax.random.uniform(subkeys[2], extent, jnp.float32, -0.5, 0.5)
    velocity_z = jax.random.uniform(subkeys[3], extent, jnp.float32, -0.5, 0.5)
    pressure = jnp.exp(jax.random.uniform(subkeys[4], extent, jnp.float32, math.log(0.5), math.log(2.0)))
    return conserved(density, velocity_x, velocity_y, velocity_z, pressure, 1)


def setup_inputs(seed: int = 0) -> dict:
    key_of = jax.random.split(jax.random.key(seed), 5)
    coarse_state = draw_coarse_state(jax.random.fold_in(key_of[4], 71), 0)
    fine_state = draw_fine_state(jax.random.fold_in(key_of[4], 71), 0)
    slot_parent = draw_slot_parent(jax.random.fold_in(key_of[4], 71), 0)
    slot_corner = draw_slot_corner(jax.random.fold_in(key_of[4], 71), 0)
    return {"coarse_state": coarse_state, "fine_state": fine_state, "slot_parent": slot_parent, "slot_corner": slot_corner}


ADIABATIC = 1.4
COURANT = 0.04

def face_flux(padded, direction):
    window = [slice(1, -1)] * 3
    window[direction] = slice(None)
    window = tuple(window)
    values = padded[(slice(None),) + window]
    inverse = 1.0 / values[0]
    kinetic = 0.5 * (values[1] * values[1] + values[2] * values[2] + values[3] * values[3]) * inverse
    pressure = (ADIABATIC - 1.0) * (values[4] - kinetic)
    sound_speed = jnp.sqrt(ADIABATIC * pressure * inverse)
    velocity = values[1 + direction] * inverse
    signal = jnp.abs(velocity) + sound_speed
    pieces = [values[0] * velocity, values[1] * velocity, values[2] * velocity, values[3] * velocity, (values[4] + pressure) * velocity]
    pieces[1 + direction] = pieces[1 + direction] + pressure
    physical = jnp.stack(pieces)
    lower_face = [slice(None)] * 3
    upper_face = [slice(None)] * 3
    lower_face[direction] = slice(0, -1)
    upper_face[direction] = slice(1, None)
    lower_face = tuple(lower_face)
    upper_face = tuple(upper_face)
    whole_lower = (slice(None),) + lower_face
    whole_upper = (slice(None),) + upper_face
    return 0.5 * (physical[whole_lower] + physical[whole_upper]) - 0.5 * jnp.maximum(signal[lower_face], signal[upper_face]) * (values[whole_upper] - values[whole_lower])

def advance(padded):
    fluxes = (face_flux(padded, 0), face_flux(padded, 1), face_flux(padded, 2))
    change = fluxes[0][:, 1:] - fluxes[0][:, :-1] + (fluxes[1][:, :, 1:] - fluxes[1][:, :, :-1]) + (fluxes[2][:, :, :, 1:] - fluxes[2][:, :, :, :-1])
    return (padded[:, 1:-1, 1:-1, 1:-1] - COURANT * change, fluxes)

def widen_face(face_plane):
    fields, height, across = face_plane.shape
    return jnp.broadcast_to(face_plane[:, :, None, :, None], (fields, height, 2, across, 2)).reshape(fields, 2 * height, 2 * across)

def coarsen(face_plane):
    fields, height, across = face_plane.shape
    return face_plane.reshape(fields, height // 2, 2, across // 2, 2).sum(axis=(2, 4))

def pack_faces(side_list, end_list):
    side_cells = jnp.stack(side_list, axis=1)
    end_cells = jnp.stack(end_list, axis=1)
    return (side_cells.reshape(side_cells.shape[0], -1), end_cells.reshape(end_cells.shape[0], -1))

def boundary_faces(fluxes):
    along_x, along_y, along_z = fluxes
    return ([along_x[:, 0], along_x[:, -1], along_y[:, :, 0], along_y[:, :, -1]], [along_z[:, :, :, 0], along_z[:, :, :, -1]])

def patch_rims(patch):
    return pack_faces([patch[:, 0, 1:-1, 1:-1], patch[:, -1, 1:-1, 1:-1], patch[:, 1:-1, 0, 1:-1], patch[:, 1:-1, -1, 1:-1]], [patch[:, 1:-1, 1:-1, 0], patch[:, 1:-1, 1:-1, -1]])

def ghost_box(fine_box, side_rims, end_rims):
    fields, span_x, span_y, span_z = fine_box.shape
    coarse_x = span_x // 2
    coarse_z = span_z // 2
    side_cells = side_rims.reshape(fields, 4, coarse_x, coarse_z)
    end_cells = end_rims.reshape(fields, 2, coarse_x, coarse_x)
    padded = jnp.pad(fine_box, ((0, 0), (1, 1), (1, 1), (1, 1)), mode='edge')
    padded = padded.at[:, 0, 1:-1, 1:-1].set(widen_face(side_cells[:, 0]))
    padded = padded.at[:, -1, 1:-1, 1:-1].set(widen_face(side_cells[:, 1]))
    padded = padded.at[:, 1:-1, 0, 1:-1].set(widen_face(side_cells[:, 2]))
    padded = padded.at[:, 1:-1, -1, 1:-1].set(widen_face(side_cells[:, 3]))
    padded = padded.at[:, 1:-1, 1:-1, 0].set(widen_face(end_cells[:, 0]))
    padded = padded.at[:, 1:-1, 1:-1, -1].set(widen_face(end_cells[:, 1]))
    return padded

def fine_registers(fluxes):
    side_list, end_list = boundary_faces(fluxes)
    return pack_faces([coarsen(member) for member in side_list], [coarsen(member) for member in end_list])

def fine_first(fine_box, old_sides, old_ends):
    halfway, fluxes = advance(ghost_box(fine_box, old_sides, old_ends))
    side_sum, end_sum = fine_registers(fluxes)
    return (halfway, side_sum, end_sum)

def fine_second(halfway, old_sides, old_ends, new_sides, new_ends, side_sum, end_sum):
    second, fluxes = advance(ghost_box(halfway, 0.5 * (old_sides + new_sides), 0.5 * (old_ends + new_ends)))
    side_more, end_more = fine_registers(fluxes)
    fields, span_x, span_y, span_z = second.shape
    average = 0.125 * second.reshape(fields, span_x // 2, 2, span_y // 2, 2, span_z // 2, 2).sum(axis=(2, 4, 6))
    return (second, average.reshape(fields, -1), 0.125 * (side_sum + side_more), 0.125 * (end_sum + end_more))

def settle(patch, average, side_reg, end_reg, coarse_sides, coarse_ends):
    fields = patch.shape[0]
    inner_x = patch.shape[1] - 2
    inner_z = patch.shape[3] - 2
    side_fix = (COURANT * (side_reg - coarse_sides)).reshape(fields, 4, inner_x, inner_z)
    end_fix = (COURANT * (end_reg - coarse_ends)).reshape(fields, 2, inner_x, inner_x)
    patch = patch.at[:, 1:-1, 1:-1, 1:-1].set(average.reshape(fields, inner_x, inner_x, inner_z))
    patch = patch.at[:, 0, 1:-1, 1:-1].add(-side_fix[:, 0])
    patch = patch.at[:, -1, 1:-1, 1:-1].add(side_fix[:, 1])
    patch = patch.at[:, 1:-1, 0, 1:-1].add(-side_fix[:, 2])
    patch = patch.at[:, 1:-1, -1, 1:-1].add(side_fix[:, 3])
    patch = patch.at[:, 1:-1, 1:-1, 0].add(-end_fix[:, 0])
    patch = patch.at[:, 1:-1, 1:-1, -1].add(end_fix[:, 1])
    return patch

def coarse_advance(coarse_state):
    fields, extent_x, extent_y, extent_z = coarse_state.shape
    slab_count = extent_x // CX
    wrapped = jnp.pad(coarse_state, ((0, 0), (0, 0), (1, 1), (1, 1)), mode='wrap')

    def one_slab(slab_index):
        planes_x = (slab_index * CX - 1 + jnp.arange(CX + 2, dtype=jnp.int32)) % extent_x
        padded = jnp.take(wrapped, planes_x, axis=1)
        return advance(padded)[0]
    stacked = lax.map(one_slab, jnp.arange(slab_count, dtype=jnp.int32))
    return jnp.moveaxis(stacked, 0, 1).reshape(fields, extent_x, extent_y, extent_z)

def reference(coarse_state, fine_state, slot_parent, slot_corner):
    coarse_new = coarse_advance(coarse_state)
    members = N_GY * N_GZ
    fields = 5
    coarse_x = FX // 2
    coarse_z = FZ // 2
    extent = (fields, coarse_x + 2, coarse_x + 2, coarse_z + 2)

    def visit_slot(slot_index, carried):
        parent = slot_parent[slot_index]

        def refine_slot(holding):
            coarse_out, fine_out = holding
            plane_index = parent // members
            within = parent % members
            corner = slot_corner[slot_index]
            starts = (jnp.int32(0), (plane_index * CX + corner[0] - 1).astype(jnp.int32), (within // N_GZ * CY + corner[1] - 1).astype(jnp.int32), (within % N_GZ * CZ + corner[2] - 1).astype(jnp.int32))
            old_patch = lax.dynamic_slice(coarse_state, starts, extent)
            new_patch = lax.dynamic_slice(coarse_new, starts, extent)
            old_sides, old_ends = patch_rims(old_patch)
            new_sides, new_ends = patch_rims(new_patch)
            fine_box = fine_out[slot_index].reshape(fields, FX, FY, FZ)
            halfway, side_sum, end_sum = fine_first(fine_box, old_sides, old_ends)
            second, average, side_reg, end_reg = fine_second(halfway, old_sides, old_ends, new_sides, new_ends, side_sum, end_sum)
            coarse_sides, coarse_ends = pack_faces(*boundary_faces(advance(old_patch)[1]))
            current = lax.dynamic_slice(coarse_out, starts, extent)
            settled = settle(current, average, side_reg, end_reg, coarse_sides, coarse_ends)
            coarse_out = lax.dynamic_update_slice(coarse_out, settled, starts)
            fine_out = lax.dynamic_update_slice(fine_out, second.reshape(1, fields, FCELLS), (slot_index.astype(jnp.int32), jnp.int32(0), jnp.int32(0)))
            return (coarse_out, fine_out)
        return lax.cond(parent >= 0, refine_slot, lambda holding: holding, carried)
    coarse_next, fine_next = lax.fori_loop(jnp.int32(0), jnp.int32(SLOTS), visit_slot, (coarse_new, fine_state))
    return (coarse_next, fine_next)
```

```python
import functools

import jax
import jax.numpy as jnp
from jax import lax
from jax.experimental import pallas as pl
from jax.experimental.pallas import tpu as pltpu
from jax.sharding import PartitionSpec as P

GAMMA = 1.4
COURANT = 0.04
FIELDS = 5
REGIONS = 4
BOXMAX = 8
MESH = pl.DeviceIdType.MESH
F32 = jnp.float32
I32 = jnp.int32


def iota(shape, dim):
    return lax.broadcasted_iota(I32, shape, dim)


def pick(values, lanes):
    numbers = lax.GatherDimensionNumbers(
        offset_dims=(),
        collapsed_slice_dims=(1,),
        start_index_map=(1,),
        operand_batching_dims=(0,),
        start_indices_batching_dims=(0,),
    )
    return lax.gather(
        values,
        lanes[..., None],
        numbers,
        (1, 1),
        mode=lax.GatherScatterMode.PROMISE_IN_BOUNDS,
    )


def prims(q):
    inverse = 1.0 / q[0]
    kinetic = 0.5 * (q[1] * q[1] + q[2] * q[2] + q[3] * q[3]) * inverse
    pressure = (GAMMA - 1.0) * (q[4] - kinetic)
    sound = jnp.sqrt(GAMMA * pressure * inverse)
    return inverse, pressure, sound, q[4] + pressure


def along(q, prim, axis):
    inverse, pressure, sound, total = prim
    velocity = q[1 + axis] * inverse
    flux = [q[1 + axis], q[1] * velocity, q[2] * velocity, q[3] * velocity, total * velocity]
    flux[1 + axis] = flux[1 + axis] + pressure
    return flux, jnp.abs(velocity) + sound


def face(low, low_terms, high, high_terms):
    signal = jnp.maximum(low_terms[1], high_terms[1])
    return [
        (low_terms[0][f] + high_terms[0][f]) - signal * (high[f] - low[f]) for f in range(FIELDS)
    ]


def moved(q, terms, move):
    return [move(v) for v in q], [move(v) for v in terms[0]], move(terms[1])


def fine_step(box, rim, reg, put, second):
    lane = iota((BOXMAX, 128), 1)
    first_row = lane < 16
    last_row = lane >= 112
    k_first = lane % 16 == 0
    k_last = lane % 16 == 15
    half_k = (lane % 16) // 2
    quarter = lane // 32
    squeeze = ((lane % 32) // 8) * 32 + (lane % 8) * 2
    part = (lane % 64) // 8

    def halves(f, plane):
        return [box[f, plane, :, 128 * h : 128 * h + 128] for h in range(2)]

    for f in range(FIELDS):
        for h in range(2):
            spread = (h * 4 + quarter) * 8 + half_k
            box[f, 0, :, 128 * h : 128 * h + 128] = pick(rim[3 * f], spread)
            box[f, 17, :, 128 * h : 128 * h + 128] = pick(rim[3 * f], spread + 64)

    def load(plane):
        both = [halves(f, plane) for f in range(FIELDS)]
        return [[both[f][h] for f in range(FIELDS)] for h in range(2)]

    def x_faces(low, low_prim, high, high_prim):
        return [
            face(low[h], along(low[h], low_prim[h], 0), high[h], along(high[h], high_prim[h], 0))
            for h in range(2)
        ]

    def roll(v, by):
        return pltpu.roll(v, by % 128, 1)

    ghost = load(0)
    here = load(1)
    here_prim = [prims(here[h]) for h in range(2)]
    x_low = x_faces(ghost, [prims(ghost[h]) for h in range(2)], here, here_prim)

    def x_register(faces, side):
        for f in range(FIELDS):
            out = []
            for h in range(2):
                v = faces[h][f]
                v = v + roll(v, -1)
                v = v + roll(v, -16)
                out.append(pick(v, squeeze))
            both = jnp.where((lane % 64) < 32, out[0], out[1])
            mine = (lane < 64) if side == 0 else (lane >= 64)
            reg[7 * f] = reg[7 * f] + jnp.where(mine, both, 0.0)

    x_register(x_low, 0)

    def pair(big, carried):
        here, here_prim, x_low = carried
        y_lanes = big * 8 + half_k + jnp.where(lane >= 64, 64, 0)
        y_ghost = [pick(rim[3 * f + 1], y_lanes) for f in range(FIELDS)]
        y_ghost_terms = along(y_ghost, prims(y_ghost), 1)
        z_ghost = []
        z_ghost_terms = []
        for h in range(2):
            z_lanes = big * 8 + h * 4 + quarter + jnp.where(lane % 16 >= 8, 64, 0)
            ghost = [pick(rim[3 * f + 2], z_lanes) for f in range(FIELDS)]
            z_ghost.append(ghost)
            z_ghost_terms.append(along(ghost, prims(ghost), 2))
        y_sum = [None] * FIELDS
        z_sum = [[None] * FIELDS for _ in range(2)]
        new_sum = [[None] * FIELDS for _ in range(2)]

        def accumulate(total, v):
            return v if total is None else total + v

        for sub in range(2):
            plane = 2 * big + sub
            after = load(plane + 2)
            after_prim = [prims(after[h]) for h in range(2)]
            x_high = x_faces(here, here_prim, after, after_prim)

            y_terms = [along(here[h], here_prim[h], 1) for h in range(2)]
            rolled = [moved(here[h], y_terms[h], lambda v: roll(v, 16)) for h in range(2)]

            def y_select(h, low, high):
                return jnp.where(first_row, low, high)

            low0 = [jnp.where(first_row, y_ghost[f], rolled[0][0][f]) for f in range(FIELDS)]
            low0_terms = (
                [jnp.where(first_row, y_ghost_terms[0][f], rolled[0][1][f]) for f in range(FIELDS)],
                jnp.where(first_row, y_ghost_terms[1], rolled[0][2]),
            )
            low1 = [jnp.where(first_row, rolled[0][0][f], rolled[1][0][f]) for f in range(FIELDS)]
            low1_terms = (
                [jnp.where(first_row, rolled[0][1][f], rolled[1][1][f]) for f in range(FIELDS)],
                jnp.where(first_row, rolled[0][2], rolled[1][2]),
            )
            y0 = face(low0, low0_terms, here[0], y_terms[0])
            y1 = face(low1, low1_terms, here[1], y_terms[1])
            y_end = face(here[1], y_terms[1], y_ghost, y_ghost_terms)
            y_diff = [[], []]
            for f in range(FIELDS):
                up0 = roll(y0[f], -16)
                up1 = roll(y1[f], -16)
                y_diff[0].append(jnp.where(last_row, up1, up0) - y0[f])
                y_diff[1].append(jnp.where(last_row, y_end[f], up1) - y1[f])
                y_sum[f] = accumulate(y_sum[f], jnp.where(lane < 64, y0[f], y_end[f]))

            z_diff = [[], []]
            for h in range(2):
                terms = along(here[h], here_prim[h], 2)
                shifted = moved(here[h], terms, lambda v: roll(v, 1))
                low = [jnp.where(k_first, z_ghost[h][f], shifted[0][f]) for f in range(FIELDS)]
                low_terms = (
                    [
                        jnp.where(k_first, z_ghost_terms[h][0][f], shifted[1][f])
                        for f in range(FIELDS)
                    ],
                    jnp.where(k_first, z_ghost_terms[h][1], shifted[2]),
                )
                z = face(low, low_terms, here[h], terms)
                z_end = face(here[h], terms, z_ghost[h], z_ghost_terms[h])
                for f in range(FIELDS):
                    z_diff[h].append(jnp.where(k_last, z_end[f], roll(z[f], -1)) - z[f])
                    z_sum[h][f] = accumulate(z_sum[h][f], jnp.where(k_last, z_end[f], z[f]))

            for h in range(2):
                for f in range(FIELDS):
                    change = (x_high[h][f] - x_low[h][f]) + y_diff[h][f] + z_diff[h][f]
                    new = here[h][f] - (0.5 * COURANT) * change
                    put(f, plane, h, new)
                    if second:
                        new_sum[h][f] = accumulate(new_sum[h][f], new)
            here, here_prim, x_low = after, after_prim, x_high

        mine = part == big
        y_from = (lane % 8) * 2 + jnp.where(lane >= 64, 112, 0)
        z_from = (lane % 4) * 32 + jnp.where(lane >= 64, 15, 0)
        for f in range(FIELDS):
            v = y_sum[f] + roll(y_sum[f], -1)
            reg[7 * f + 1] = reg[7 * f + 1] + jnp.where(mine, pick(v, y_from), 0.0)
            out = []
            for h in range(2):
                v = z_sum[h][f] + roll(z_sum[h][f], -16)
                out.append(pick(v, z_from))
            v = jnp.where(lane % 8 < 4, out[0], out[1])
            reg[7 * f + 2] = reg[7 * f + 2] + jnp.where(mine, v, 0.0)
            if second:
                out = []
                for h in range(2):
                    v = new_sum[h][f]
                    v = v + roll(v, -1)
                    v = v + roll(v, -16)
                    out.append(pick(v, squeeze))
                v = jnp.where((lane % 64) < 32, out[0], out[1])
                where = 7 * f + 3 + big // 2
                reg[where] = jnp.where(lane // 64 == big % 2, v, reg[where])
        return here, here_prim, x_low

    last = lax.fori_loop(0, 8, pair, (here, here_prim, x_low))
    x_register(last[2], 1)


def coarse_step(block, y_rim, z_rim, new, x_face, y_low, y_high, z_low, z_high):
    lane = iota((16, 128), 1)
    row = iota((16, 128), 0)
    tip = iota((8, 128), 0)

    def load(plane):
        return [block[f, plane] for f in range(FIELDS)]

    ghost = load(0)
    here = load(1)
    here_prim = prims(here)
    low = face(ghost, along(ghost, prims(ghost), 0), here, along(here, here_prim, 0))
    for f in range(FIELDS):
        x_face[f, 0] = low[f]

    def one(x, carried):
        here, here_prim, x_low = carried
        after = load(x + 2)
        after_prim = prims(after)
        x_high = face(here, along(here, here_prim, 0), after, along(after, after_prim, 0))

        tips = []
        wide = []
        column = (x % 8) * 16 + row
        for f in range(FIELDS):
            above = y_rim[1, f, pl.ds(x, 1), :]
            below = y_rim[0, f, pl.ds(x, 1), :]
            tips.append(
                jnp.where(
                    tip == 0,
                    jnp.broadcast_to(above, (8, 128)),
                    jnp.broadcast_to(below, (8, 128)),
                )
            )
            below = jnp.broadcast_to(z_rim[0, x // 8, f : f + 1, :], (16, 128))
            above = jnp.broadcast_to(z_rim[1, x // 8, f : f + 1, :], (16, 128))
            side = jnp.where(lane == 64, pick(above, column), pick(below, column))
            wide.append(jnp.where(lane < 64, here[f], side))

        tall = [jnp.concatenate([here[f], tips[f]], axis=0) for f in range(FIELDS)]
        terms = along(tall, prims(tall), 1)
        shifted = moved(tall, terms, lambda v: pltpu.roll(v, 1, 0))
        y = face(shifted[0], (shifted[1], shifted[2]), tall, terms)

        terms = along(wide, prims(wide), 2)
        shifted = moved(wide, terms, lambda v: pltpu.roll(v, 1, 1))
        z = face(shifted[0], (shifted[1], shifted[2]), wide, terms)
        for f in range(FIELDS):
            up = pltpu.roll(y[f], 23, 0)[:16]
            down = y[f][:16]
            right = pltpu.roll(z[f], 127, 1)
            x_face[f, x + 1] = x_high[f]
            y_low[f, x] = down
            y_high[f, x] = up
            z_low[f, x] = z[f]
            z_high[f, x] = right
            change = (x_high[f] - x_low[f]) + (up - down) + (right - z[f])
            new[f, x] = here[f] - (0.5 * COURANT) * change
        return after, after_prim, x_high

    lax.fori_loop(0, 16, one, (here, here_prim, low))


def cut_rims(source, corner, put):
    cx, cy, cz = corner
    lane = iota((16, 128), 1)
    row = iota((16, 128), 0)
    part = (lane % 64) // 8
    along_z = cz + lane % 8
    rows_x = row - cy == part
    rows_y = row == jnp.where(lane < 64, cy - 1, cy + 8)
    rows_z = row - cy == lane % 8
    ends = jnp.where(lane < 64, cz - 1, cz + 8)
    for f in range(FIELDS):
        low = pick(source(f, cx - 1), along_z)
        high = pick(source(f, cx + 8), along_z)
        v = jnp.where(rows_x, jnp.where(lane < 64, low, high), 0.0)
        put(f, 0, jnp.sum(v, axis=0, keepdims=True))
        y_total = jnp.zeros((16, 128), F32)
        z_total = jnp.zeros((16, 128), F32)
        for big in range(8):
            plane = source(f, cx + big)
            y_total = jnp.where(part == big, pick(plane, along_z), y_total)
            z_total = jnp.where(part == big, pick(plane, ends), z_total)
        put(f, 1, jnp.sum(jnp.where(rows_y, y_total, 0.0), axis=0, keepdims=True))
        put(f, 2, jnp.sum(jnp.where(rows_z, z_total, 0.0), axis=0, keepdims=True))


def settle(corners, answers, new, x_face, y_low, y_high, z_low, z_high, out):
    lane = iota((16, 128), 1)
    row = iota((16, 128), 0)

    def one(x, _):
        values = [jnp.zeros((16, 128), F32) for _ in range(FIELDS)]
        kind = jnp.zeros((16, 128), I32)
        for c in range(REGIONS):
            cx, cy, cz = corners[c]
            step = x - cx
            inside = jnp.logical_and(step >= 0, step < 8)
            big = jnp.clip(step, 0, 7)
            dy = row - cy
            dz = lane - cz
            in_y = jnp.logical_and(dy >= 0, dy < 8)
            in_z = jnp.logical_and(dz >= 0, dz < 8)
            near = jnp.where(dy == -1, 4, jnp.where(dy == 8, 5, 0))
            side = jnp.where(dz == -1, 6, jnp.where(dz == 8, 7, 0))
            plain = jnp.where(
                inside, 1, jnp.where(step == -1, 2, jnp.where(step == 8, 3, 0))
            )
            kind_main = jnp.where(
                jnp.logical_and(in_y, in_z),
                plain,
                jnp.where(
                    inside,
                    jnp.where(in_z, near, jnp.where(in_y, side, 0)),
                    0,
                ),
            )
            ys = jnp.clip(dy, 0, 7)
            zs = jnp.clip(dz, 0, 7)
            main_base = jnp.where(
                inside, (big % 2) * 64, jnp.where(step == 8, 64, 0)
            )
            main_row = jnp.where(inside, 3 + big // 2, 0)
            y_rows = near > 0
            first = jnp.where(
                y_rows,
                jnp.where(near == 5, 64, 0) + big * 8 + zs,
                main_base + ys * 8 + zs,
            )
            ends = jnp.where(side == 7, 64, 0) + big * 8 + ys
            use_end = kind_main >= 6
            used = kind_main > 0
            kind = jnp.where(used, kind_main, kind)
            for f in range(FIELDS):
                main = jnp.broadcast_to(answers[c, pl.ds(7 * f + main_row, 1), :], (16, 128))
                y_face = jnp.broadcast_to(answers[c, 7 * f + 1 : 7 * f + 2, :], (16, 128))
                z_face = jnp.broadcast_to(answers[c, 7 * f + 2 : 7 * f + 3, :], (16, 128))
                v = pick(jnp.where(y_rows, y_face, main), first)
                v = jnp.where(use_end, pick(z_face, ends), v)
                values[f] = jnp.where(used, v, values[f])
        factor = jnp.where(kind < 2, 0.0, jnp.where(kind % 2 == 0, -COURANT, COURANT))
        for f in range(FIELDS):
            flux = jnp.where(
                kind < 4,
                jnp.where(kind == 2, x_face[f, x + 1], x_face[f, x]),
                jnp.where(
                    kind < 6,
                    jnp.where(kind == 4, y_high[f, x], y_low[f, x]),
                    jnp.where(kind == 6, z_high[f, x], z_low[f, x]),
                ),
            )
            plain = new[f, x]
            ring = plain + factor * (0.0625 * values[f] - 0.5 * flux)
            v = jnp.where(kind == 0, plain, jnp.where(kind == 1, 0.125 * values[f], ring))
            out[f, x] = v[:, :64]
        return 0

    lax.fori_loop(0, 16, one, 0)


def whole(
    sizes,
    parent_ref,
    corner_ref,
    coarse_ref,
    fine_ref,
    coarse_out,
    fine_out,
    block,
    new,
    x_face,
    y_low,
    y_high,
    z_low,
    z_high,
    y_stage,
    z_stage,
    x_rim,
    y_rim,
    z_rim,
    cut,
    rim_out,
    rim_in_old,
    rim_in_mid,
    rim,
    box,
    half,
    reg,
    row_stage,
    answer_out,
    answer_in,
    answers,
    table,
    halo_send,
    halo_recv,
    many_send,
    many_recv,
):
    n_gx, n_gy, n_gz = sizes
    members = n_gy * n_gz
    rim_in = (rim_in_old, rim_in_mid)
    gx = lax.axis_index("gx")
    gy = lax.axis_index("gy")
    gz = lax.axis_index("gz")
    within = gy * n_gz + gz
    myself = gx * members + within
    start = gx * (members * BOXMAX)

    def peer(distance):
        other = lax.rem(within + distance, members)
        return other, (gx, other // n_gz, lax.rem(other, n_gz))

    barrier = pltpu.get_barrier_semaphore()

    def greet(distance, _):
        pl.semaphore_signal(barrier, inc=1, device_id=peer(distance)[1], device_id_type=MESH)
        return 0

    lax.fori_loop(1, members, greet, 0)
    x_next = (lax.rem(gx + 1, n_gx), gy, gz)
    x_prev = (lax.rem(gx + n_gx - 1, n_gx), gy, gz)
    y_next = (gx, lax.rem(gy + 1, n_gy), gz)
    y_prev = (gx, lax.rem(gy + n_gy - 1, n_gy), gz)
    z_next = (gx, gy, lax.rem(gz + 1, n_gz))
    z_prev = (gx, gy, lax.rem(gz + n_gz - 1, n_gz))
    pl.semaphore_signal(barrier, inc=1, device_id=x_next, device_id_type=MESH)
    pl.semaphore_signal(barrier, inc=1, device_id=x_prev, device_id_type=MESH)

    def scan(entry, found):
        c0, c1, c2, c3 = found
        hit = parent_ref[start + entry] == myself
        return (
            jnp.where(hit, entry, c0),
            jnp.where(hit, c0, c1),
            jnp.where(hit, c1, c2),
            jnp.where(hit, c2, c3),
        )

    zero = jnp.int32(0)
    children = lax.fori_loop(0, members * BOXMAX, scan, (zero, zero, zero, zero), unroll=8)
    for c in range(REGIONS):
        for k in range(3):
            table[4 * c + k] = jnp.clip(corner_ref[k, start + children[c]], 1, 55 if k == 2 else 7)
    child_peer = [child // BOXMAX for child in children]

    lane16 = iota((16, 128), 1)
    row16 = iota((16, 128), 0)
    for f in range(FIELDS):
        block[f, 1:17, :, 0:64] = coarse_ref[f]
    for f in range(FIELDS):
        y_stage[0, f] = block[f, 1:17, 0, :]
        y_stage[1, f] = block[f, 1:17, 15, :]
        for h in range(2):
            low = jnp.zeros((16, 128), F32)
            high = jnp.zeros((16, 128), F32)
            for x in range(8):
                plane = block[f, 1 + 8 * h + x]
                here = lane16 // 16 == x
                low = jnp.where(here, jnp.broadcast_to(plane[:, 0:1], (16, 128)), low)
                high = jnp.where(here, jnp.broadcast_to(plane[:, 63:64], (16, 128)), high)
            match = row16 == lane16 % 16
            z_stage[0, h, f : f + 1, :] = jnp.sum(
                jnp.where(match, low, 0.0), axis=0, keepdims=True
            )
            z_stage[1, h, f : f + 1, :] = jnp.sum(
                jnp.where(match, high, 0.0), axis=0, keepdims=True
            )

    def cut_all(when, source):
        def one(c, _):
            corner = (table[4 * c], table[4 * c + 1], table[4 * c + 2])

            def put(f, v, line):
                cut[when, c, 3 * f + v : 3 * f + v + 1, :] = line

            cut_rims(source, corner, put)
            return 0

        lax.fori_loop(0, REGIONS, one, 0)

    def copies(outgoing, incoming, index):
        def send(distance, _):
            other, device = peer(distance)
            pltpu.make_async_remote_copy(
                src_ref=outgoing.at[distance - 1],
                dst_ref=incoming.at[distance - 1],
                send_sem=many_send.at[index],
                recv_sem=many_recv.at[index],
                device_id=device,
                device_id_type=MESH,
            ).start()
            return 0

        return send

    def slot_of(other):
        return lax.rem(within - other + 2 * members - 1, members)

    def rank_of(other):
        rank = jnp.where(child_peer[1] == other, 1, 0)
        rank = jnp.where(child_peer[2] == other, 2, rank)
        return jnp.where(child_peer[3] == other, 3, rank)

    def fill_rims(when):
        def fill(distance, _):
            other = lax.rem(within + distance, members)
            rim_out[when, distance - 1] = cut[when, rank_of(other)]
            return 0

        lax.fori_loop(1, members, fill, 0)
        rim_in[when][members - 1] = cut[when, rank_of(within)]

    def wait_many(outgoing, index, semaphores):
        every = outgoing.at[pl.ds(0, members - 1)]
        pltpu.make_async_copy(every, every, semaphores.at[index]).wait()

    cut_all(0, lambda f, x: block[f, x + 1])
    fill_rims(0)

    pl.semaphore_wait(barrier, members + 1)

    def halo(src, dst, index, device):
        copy = pltpu.make_async_remote_copy(
            src_ref=src,
            dst_ref=dst,
            send_sem=halo_send.at[index],
            recv_sem=halo_recv.at[index],
            device_id=device,
            device_id_type=MESH,
        )
        copy.start()
        return copy

    halos = [
        halo(block.at[:, 16], x_rim.at[0], 0, x_next),
        halo(block.at[:, 1], x_rim.at[1], 1, x_prev),
        halo(y_stage.at[1], y_rim.at[0], 2, y_next),
        halo(y_stage.at[0], y_rim.at[1], 3, y_prev),
        halo(z_stage.at[1], z_rim.at[0], 4, z_next),
        halo(z_stage.at[0], z_rim.at[1], 5, z_prev),
    ]
    lax.fori_loop(1, members, copies(rim_out.at[0], rim_in[0], 0), 0)

    for i in range(16):
        for f in range(FIELDS):
            box[f, 1 + i] = fine_ref[f, :, 256 * i : 256 * i + 256]
    for v in range(7 * FIELDS):
        reg[v] = jnp.zeros((BOXMAX, 128), F32)

    for copy in halos:
        copy.wait()
    for f in range(FIELDS):
        block[f, 0] = x_rim[0, f]
        block[f, 17] = x_rim[1, f]
    coarse_step(block, y_rim, z_rim, new, x_face, y_low, y_high, z_low, z_high)
    cut_all(1, lambda f, x: 0.5 * (block[f, x + 1] + new[f, x]))
    fill_rims(1)
    lax.fori_loop(1, members, copies(rim_out.at[1], rim_in[1], 1), 0)

    own = [parent_ref[start + within * BOXMAX + s] for s in range(BOXMAX)]
    own_peer = [lax.rem(jnp.maximum(own[s], 0), members) for s in range(BOXMAX)]
    sub = iota((BOXMAX, 128), 0)
    owner = jnp.zeros((BOXMAX, 128), I32)
    for s in range(BOXMAX):
        owner = jnp.where(sub == s, own[s], owner)
    filled = owner >= 0

    def take_rims(when):
        wait_many(rim_in[when], when, many_recv)
        for s in range(BOXMAX):
            rows = rim_in[when][slot_of(own_peer[s])]
            for v in range(3 * FIELDS):
                rim[v, s : s + 1, :] = rows[v : v + 1, :]

    take_rims(0)

    def put_half(f, plane, h, value):
        half[f, plane + 1, :, 128 * h : 128 * h + 128] = value

    fine_step(box, rim, reg, put_half, False)
    take_rims(1)

    def put_last(f, plane, h, value):
        old = box[f, plane + 1, :, 128 * h : 128 * h + 128]
        where = pl.multiple_of(plane * 256 + h * 128, 128)
        fine_out[f, :, pl.ds(where, 128)] = jnp.where(filled, value, old)

    fine_step(half, rim, reg, put_last, True)

    for s in range(BOXMAX):
        row_stage[s] = reg[:, s, :]

    def pick_row(other):
        found = zero
        for s in range(BOXMAX):
            found = jnp.where(jnp.logical_and(own[s] >= 0, own_peer[s] == other), s, found)
        return found

    def fill_answer(distance, _):
        other = lax.rem(within + distance, members)
        answer_out[distance - 1] = row_stage[pick_row(other)]
        return copies(answer_out, answer_in, 2)(distance, 0)

    lax.fori_loop(1, members, fill_answer, 0)
    answer_in[members - 1] = row_stage[pick_row(within)]
    wait_many(answer_in, 2, many_recv)
    for c in range(REGIONS):
        answers[c] = answer_in[slot_of(child_peer[c])]
    corners = [(table[4 * c], table[4 * c + 1], table[4 * c + 2]) for c in range(REGIONS)]
    settle(corners, answers, new, x_face, y_low, y_high, z_low, z_high, coarse_out)
    wait_many(rim_out.at[0], 0, many_send)
    wait_many(rim_out.at[1], 1, many_send)
    wait_many(answer_out, 2, many_send)


def on_device(sizes, coarse_state, fine_state, slot_parent, slot_corner):
    members = sizes[1] * sizes[2]
    vmem = pl.BlockSpec(memory_space=pltpu.VMEM)
    smem = pl.BlockSpec(memory_space=pltpu.SMEM)
    fine = jnp.transpose(fine_state, (1, 0, 2))
    corner = jnp.transpose(slot_corner, (1, 0))
    field_block = (FIELDS, 16, 16, 128)
    rows = 7 * FIELDS
    coarse_next, fine_next = pl.pallas_call(
        functools.partial(whole, sizes),
        out_shape=(
            jax.ShapeDtypeStruct(coarse_state.shape, F32),
            jax.ShapeDtypeStruct(fine.shape, F32),
        ),
        in_specs=[smem, smem, vmem, vmem],
        out_specs=(vmem, vmem),
        scratch_shapes=[
            pltpu.VMEM((FIELDS, 18, 16, 128), F32),
            pltpu.VMEM(field_block, F32),
            pltpu.VMEM((FIELDS, 17, 16, 128), F32),
            pltpu.VMEM(field_block, F32),
            pltpu.VMEM(field_block, F32),
            pltpu.VMEM(field_block, F32),
            pltpu.VMEM(field_block, F32),
            pltpu.VMEM((2, FIELDS, 16, 128), F32),
            pltpu.VMEM((2, 2, FIELDS, 128), F32),
            pltpu.VMEM((2, FIELDS, 16, 128), F32),
            pltpu.VMEM((2, FIELDS, 16, 128), F32),
            pltpu.VMEM((2, 2, FIELDS, 128), F32),
            pltpu.VMEM((2, REGIONS, 3 * FIELDS, 128), F32),
            pltpu.VMEM((2, members, 3 * FIELDS, 128), F32),
            pltpu.VMEM((members, 3 * FIELDS, 128), F32),
            pltpu.VMEM((members, 3 * FIELDS, 128), F32),
            pltpu.VMEM((3 * FIELDS, BOXMAX, 128), F32),
            pltpu.VMEM((FIELDS, 18, BOXMAX, 256), F32),
            pltpu.VMEM((FIELDS, 18, BOXMAX, 256), F32),
            pltpu.VMEM((rows, BOXMAX, 128), F32),
            pltpu.VMEM((BOXMAX, rows, 128), F32),
            pltpu.VMEM((members, rows, 128), F32),
            pltpu.VMEM((members, rows, 128), F32),
            pltpu.VMEM((REGIONS, rows, 128), F32),
            pltpu.SMEM((4 * REGIONS,), I32),
            pltpu.SemaphoreType.DMA((6,)),
            pltpu.SemaphoreType.DMA((6,)),
            pltpu.SemaphoreType.DMA((3,)),
            pltpu.SemaphoreType.DMA((3,)),
        ],
        compiler_params=pltpu.CompilerParams(
            collective_id=0, has_side_effects=True, vmem_limit_bytes=48 * 1024 * 1024
        ),
    )(slot_parent, corner, coarse_state, fine)
    return coarse_next, jnp.transpose(fine_next, (1, 0, 2))


def solution(mesh):
    sizes = tuple(mesh.shape[name] for name in ("gx", "gy", "gz"))
    return jax.shard_map(
        functools.partial(on_device, sizes),
        mesh=mesh,
        in_specs=(P(None, "gx", "gy", "gz"), P(("gx", "gy", "gz"), None, None), P(), P()),
        out_specs=(P(None, "gx", "gy", "gz"), P(("gx", "gy", "gz"), None, None)),
        check_vma=False,
    )
```

```python
import functools

import jax
import jax.numpy as jnp
from jax import lax
from jax.experimental import pallas as pl
from jax.experimental.pallas import tpu as pltpu
from jax.sharding import PartitionSpec as P

GAMMA = 1.4
COURANT = 0.04
FIELDS = 5
REGIONS = 4
BOXMAX = 8
MESH = pl.DeviceIdType.MESH
F32 = jnp.float32
I32 = jnp.int32


def iota(shape, dim):
    return lax.broadcasted_iota(I32, shape, dim)


def pick(values, lanes):
    numbers = lax.GatherDimensionNumbers(
        offset_dims=(),
        collapsed_slice_dims=(1,),
        start_index_map=(1,),
        operand_batching_dims=(0,),
        start_indices_batching_dims=(0,),
    )
    return lax.gather(
        values,
        lanes[..., None],
        numbers,
        (1, 1),
        mode=lax.GatherScatterMode.PROMISE_IN_BOUNDS,
    )


def prims(q):
    inverse = pl.reciprocal(q[0], approx=True)
    inverse = inverse * (2.0 - q[0] * inverse)
    kinetic = 0.5 * (q[1] * q[1] + q[2] * q[2] + q[3] * q[3]) * inverse
    pressure = (GAMMA - 1.0) * (q[4] - kinetic)
    square = GAMMA * pressure * inverse
    sound = square * lax.rsqrt(jnp.maximum(square, 1e-30))
    return inverse, pressure, sound, q[4] + pressure


def along(q, prim, axis):
    inverse, pressure, sound, total = prim
    velocity = q[1 + axis] * inverse
    flux = [q[1 + axis], q[1] * velocity, q[2] * velocity, q[3] * velocity, total * velocity]
    flux[1 + axis] = flux[1 + axis] + pressure
    return flux, jnp.abs(velocity) + sound


def face(low, low_terms, high, high_terms):
    signal = jnp.maximum(low_terms[1], high_terms[1])
    return [
        (low_terms[0][f] + high_terms[0][f]) - signal * (high[f] - low[f]) for f in range(FIELDS)
    ]


def moved(q, terms, move):
    return [move(v) for v in q], [move(v) for v in terms[0]], move(terms[1])


def fine_step(box, rim, reg, filled, put, second, done=None):
    lane = iota((BOXMAX, 128), 1)
    first_row = lane < 16
    last_row = lane >= 112
    k_first = lane % 16 == 0
    k_last = lane % 16 == 15
    half_k = (lane % 16) // 2
    quarter = lane // 32
    squeeze = ((lane % 32) // 8) * 32 + (lane % 8) * 2
    part = (lane % 64) // 8

    def halves(f, plane):
        return [box[f, plane, :, 128 * h : 128 * h + 128] for h in range(2)]

    for f in range(FIELDS):
        for h in range(2):
            spread = (h * 4 + quarter) * 8 + half_k
            box[f, 0, :, 128 * h : 128 * h + 128] = pick(rim[3 * f], spread)
            box[f, 17, :, 128 * h : 128 * h + 128] = pick(rim[3 * f], spread + 64)

    def load(plane):
        both = [halves(f, plane) for f in range(FIELDS)]
        return [[both[f][h] for f in range(FIELDS)] for h in range(2)]

    def x_faces(low, low_prim, high, high_prim):
        return [
            face(low[h], along(low[h], low_prim[h], 0), high[h], along(high[h], high_prim[h], 0))
            for h in range(2)
        ]

    def roll(v, by):
        return pltpu.roll(v, by % 128, 1)

    ghost = load(0)
    here = load(1)
    here_prim = [prims(here[h]) for h in range(2)]
    x_low = x_faces(ghost, [prims(ghost[h]) for h in range(2)], here, here_prim)

    def x_register(faces, side):
        for f in range(FIELDS):
            out = []
            for h in range(2):
                v = faces[h][f]
                v = v + roll(v, -1)
                v = v + roll(v, -16)
                out.append(pick(v, squeeze))
            both = jnp.where((lane % 64) < 32, out[0], out[1])
            mine = jnp.logical_and(filled, (lane < 64) if side == 0 else (lane >= 64))
            reg[7 * f] = reg[7 * f] + jnp.where(mine, both, 0.0)

    x_register(x_low, 0)

    def pair(big, carried):
        here, here_prim, x_low = carried
        y_lanes = big * 8 + half_k + jnp.where(lane >= 64, 64, 0)
        y_ghost = [pick(rim[3 * f + 1], y_lanes) for f in range(FIELDS)]
        y_ghost_terms = along(y_ghost, prims(y_ghost), 1)
        z_ghost = []
        z_ghost_terms = []
        for h in range(2):
            z_lanes = big * 8 + h * 4 + quarter + jnp.where(lane % 16 >= 8, 64, 0)
            ghost = [pick(rim[3 * f + 2], z_lanes) for f in range(FIELDS)]
            z_ghost.append(ghost)
            z_ghost_terms.append(along(ghost, prims(ghost), 2))
        y_sum = [None] * FIELDS
        z_sum = [[None] * FIELDS for _ in range(2)]
        new_sum = [[None] * FIELDS for _ in range(2)]

        def accumulate(total, v):
            return v if total is None else total + v

        for sub in range(2):
            plane = 2 * big + sub
            after = load(plane + 2)
            after_prim = [prims(after[h]) for h in range(2)]
            x_high = x_faces(here, here_prim, after, after_prim)

            y_terms = [along(here[h], here_prim[h], 1) for h in range(2)]
            rolled = [moved(here[h], y_terms[h], lambda v: roll(v, 16)) for h in range(2)]

            def y_select(h, low, high):
                return jnp.where(first_row, low, high)

            low0 = [jnp.where(first_row, y_ghost[f], rolled[0][0][f]) for f in range(FIELDS)]
            low0_terms = (
                [jnp.where(first_row, y_ghost_terms[0][f], rolled[0][1][f]) for f in range(FIELDS)],
                jnp.where(first_row, y_ghost_terms[1], rolled[0][2]),
            )
            low1 = [jnp.where(first_row, rolled[0][0][f], rolled[1][0][f]) for f in range(FIELDS)]
            low1_terms = (
                [jnp.where(first_row, rolled[0][1][f], rolled[1][1][f]) for f in range(FIELDS)],
                jnp.where(first_row, rolled[0][2], rolled[1][2]),
            )
            y0 = face(low0, low0_terms, here[0], y_terms[0])
            y1 = face(low1, low1_terms, here[1], y_terms[1])
            y_end = face(here[1], y_terms[1], y_ghost, y_ghost_terms)
            y_diff = [[], []]
            for f in range(FIELDS):
                up0 = roll(y0[f], -16)
                up1 = roll(y1[f], -16)
                y_diff[0].append(jnp.where(last_row, up1, up0) - y0[f])
                y_diff[1].append(jnp.where(last_row, y_end[f], up1) - y1[f])
                y_sum[f] = accumulate(y_sum[f], jnp.where(lane < 64, y0[f], y_end[f]))

            z_diff = [[], []]
            for h in range(2):
                terms = along(here[h], here_prim[h], 2)
                shifted = moved(here[h], terms, lambda v: roll(v, 1))
                low = [jnp.where(k_first, z_ghost[h][f], shifted[0][f]) for f in range(FIELDS)]
                low_terms = (
                    [
                        jnp.where(k_first, z_ghost_terms[h][0][f], shifted[1][f])
                        for f in range(FIELDS)
                    ],
                    jnp.where(k_first, z_ghost_terms[h][1], shifted[2]),
                )
                z = face(low, low_terms, here[h], terms)
                z_end = face(here[h], terms, z_ghost[h], z_ghost_terms[h])
                for f in range(FIELDS):
                    z_diff[h].append(jnp.where(k_last, z_end[f], roll(z[f], -1)) - z[f])
                    z_sum[h][f] = accumulate(z_sum[h][f], jnp.where(k_last, z_end[f], z[f]))

            for h in range(2):
                for f in range(FIELDS):
                    change = (x_high[h][f] - x_low[h][f]) + y_diff[h][f] + z_diff[h][f]
                    new = here[h][f] - (0.5 * COURANT) * change
                    put(f, plane, h, new)
                    if second:
                        new_sum[h][f] = accumulate(new_sum[h][f], new)
            here, here_prim, x_low = after, after_prim, x_high

        mine = jnp.logical_and(filled, part == big)
        y_from = (lane % 8) * 2 + jnp.where(lane >= 64, 112, 0)
        z_from = (lane % 4) * 32 + jnp.where(lane >= 64, 15, 0)
        for f in range(FIELDS):
            v = y_sum[f] + roll(y_sum[f], -1)
            reg[7 * f + 1] = reg[7 * f + 1] + jnp.where(mine, pick(v, y_from), 0.0)
            out = []
            for h in range(2):
                v = z_sum[h][f] + roll(z_sum[h][f], -16)
                out.append(pick(v, z_from))
            v = jnp.where(lane % 8 < 4, out[0], out[1])
            reg[7 * f + 2] = reg[7 * f + 2] + jnp.where(mine, v, 0.0)
            if second:
                out = []
                for h in range(2):
                    v = new_sum[h][f]
                    v = v + roll(v, -1)
                    v = v + roll(v, -16)
                    out.append(pick(v, squeeze))
                v = jnp.where((lane % 64) < 32, out[0], out[1])
                v = jnp.where(filled, v, 0.0)
                where = 7 * f + 3 + big // 2
                reg[where] = jnp.where(lane // 64 == big % 2, v, reg[where])
        if second:
            done(big)
        return here, here_prim, x_low

    last = lax.fori_loop(0, 8, pair, (here, here_prim, x_low))
    x_register(last[2], 1)


def coarse_step(block, y_rim, z_rim, new, x_face, y_low, y_high, z_low, z_high):
    lane = iota((16, 128), 1)
    row = iota((16, 128), 0)
    tip = iota((8, 128), 0)

    def load(plane):
        x = jnp.clip(plane - 1, 0, 15)
        column = (x % 8) * 16 + row
        cells = []
        for f in range(FIELDS):
            below = jnp.broadcast_to(z_rim[0, x // 8, f : f + 1, :], (16, 128))
            above = jnp.broadcast_to(z_rim[1, x // 8, f : f + 1, :], (16, 128))
            side = jnp.where(lane == 64, pick(above, column), pick(below, column))
            cells.append(jnp.where(lane < 64, block[f, plane], side))
        return cells

    ghost = load(0)
    here = load(1)
    here_prim = prims(here)
    low = face(ghost, along(ghost, prims(ghost), 0), here, along(here, here_prim, 0))
    for f in range(FIELDS):
        x_face[f, 0] = low[f]

    def one(x, carried):
        here, here_prim, x_low = carried
        after = load(x + 2)
        after_prim = prims(after)
        x_high = face(here, along(here, here_prim, 0), after, along(after, after_prim, 0))

        tips = []
        for f in range(FIELDS):
            above = y_rim[1, f, pl.ds(x, 1), :]
            below = y_rim[0, f, pl.ds(x, 1), :]
            tips.append(
                jnp.where(
                    tip == 0,
                    jnp.broadcast_to(above, (8, 128)),
                    jnp.broadcast_to(below, (8, 128)),
                )
            )
        tip_terms = along(tips, prims(tips), 1)
        terms = along(here, here_prim, 1)

        def tall(low, high):
            return jnp.concatenate([low, high], axis=0)

        cells = [tall(here[f], tips[f]) for f in range(FIELDS)]
        terms = ([tall(terms[0][f], tip_terms[0][f]) for f in range(FIELDS)], tall(terms[1], tip_terms[1]))
        shifted = moved(cells, terms, lambda v: pltpu.roll(v, 1, 0))
        y = face(shifted[0], (shifted[1], shifted[2]), cells, terms)

        terms = along(here, here_prim, 2)
        shifted = moved(here, terms, lambda v: pltpu.roll(v, 1, 1))
        z = face(shifted[0], (shifted[1], shifted[2]), here, terms)
        for f in range(FIELDS):
            up = pltpu.roll(y[f], 23, 0)[:16]
            down = y[f][:16]
            right = pltpu.roll(z[f], 127, 1)
            x_face[f, x + 1] = x_high[f]
            y_low[f, x] = down
            y_high[f, x] = up
            z_low[f, x] = z[f]
            z_high[f, x] = right
            change = (x_high[f] - x_low[f]) + (up - down) + (right - z[f])
            new[f, x] = here[f] - (0.5 * COURANT) * change
        return after, after_prim, x_high

    lax.fori_loop(0, 16, one, (here, here_prim, low))


def cut_rims(source, corner, put):
    cx, cy, cz = corner
    lane = iota((16, 128), 1)
    row = iota((16, 128), 0)
    part = (lane % 64) // 8
    along_z = cz + lane % 8
    rows_x = row - cy == part
    rows_y = row == jnp.where(lane < 64, cy - 1, cy + 8)
    rows_z = row - cy == lane % 8
    ends = jnp.where(lane < 64, cz - 1, cz + 8)
    for f in range(FIELDS):
        low = pick(source(f, cx - 1), along_z)
        high = pick(source(f, cx + 8), along_z)
        v = jnp.where(rows_x, jnp.where(lane < 64, low, high), 0.0)
        put(f, 0, jnp.sum(v, axis=0, keepdims=True))
        y_total = jnp.zeros((16, 128), F32)
        z_total = jnp.zeros((16, 128), F32)
        for big in range(8):
            plane = source(f, cx + big)
            y_total = jnp.where(part == big, pick(plane, along_z), y_total)
            z_total = jnp.where(part == big, pick(plane, ends), z_total)
        put(f, 1, jnp.sum(jnp.where(rows_y, y_total, 0.0), axis=0, keepdims=True))
        put(f, 2, jnp.sum(jnp.where(rows_z, z_total, 0.0), axis=0, keepdims=True))


def plan_settle(corners, new, x_face, y_low, y_high, z_low, z_high, weight, index):
    lane = iota((16, 128), 1)
    row = iota((16, 128), 0)

    def one(x, _):
        kind = jnp.zeros((16, 128), I32)
        for c in range(REGIONS):
            cx, cy, cz = corners[c]
            step = x - cx
            inside = jnp.logical_and(step >= 0, step < 8)
            big = jnp.clip(step, 0, 7)
            dy = row - cy
            dz = lane - cz
            in_y = jnp.logical_and(dy >= 0, dy < 8)
            in_z = jnp.logical_and(dz >= 0, dz < 8)
            near = jnp.where(dy == -1, 4, jnp.where(dy == 8, 5, 0))
            side = jnp.where(dz == -1, 6, jnp.where(dz == 8, 7, 0))
            plain = jnp.where(inside, 1, jnp.where(step == -1, 2, jnp.where(step == 8, 3, 0)))
            mine = jnp.where(
                jnp.logical_and(in_y, in_z),
                plain,
                jnp.where(inside, jnp.where(in_z, near, jnp.where(in_y, side, 0)), 0),
            )
            ys = jnp.clip(dy, 0, 7)
            zs = jnp.clip(dz, 0, 7)
            base = jnp.where(inside, (big % 2) * 64, jnp.where(step == 8, 64, 0))
            first = jnp.where(
                near > 0,
                jnp.where(near == 5, 64, 0) + big * 8 + zs,
                base + ys * 8 + zs,
            )
            ends = jnp.where(side == 7, 64, 0) + big * 8 + ys
            used = mine > 0
            kind = jnp.where(used, mine, kind)
            index[x, c, 0] = first + jnp.where(used, 128, 0)
            index[x, c, 1] = ends + jnp.where(mine >= 6, 128, 0)
        factor = jnp.where(kind < 2, 0.0, jnp.where(kind % 2 == 0, -COURANT, COURANT))
        weight[x] = jnp.where(kind == 1, 0.125, 0.0625 * factor)
        for f in range(FIELDS):
            flux = jnp.where(
                kind < 4,
                jnp.where(kind == 2, x_face[f, x + 1], x_face[f, x]),
                jnp.where(
                    kind < 6,
                    jnp.where(kind == 4, y_high[f, x], y_low[f, x]),
                    jnp.where(kind == 6, z_high[f, x], z_low[f, x]),
                ),
            )
            plain = new[f, x]
            ring = jnp.where(kind >= 2, plain - 0.5 * factor * flux, plain)
            new[f, x] = jnp.where(kind == 1, 0.0, ring)
        return 0

    lax.fori_loop(0, 16, one, 0)


def settle(corners, answers, new, weight, index, out):
    row = iota((16, 128), 0)
    y_rows = [
        jnp.logical_or(row == corners[c][1] - 1, row == corners[c][1] + 8) for c in range(REGIONS)
    ]

    def one(x, _):
        values = [jnp.zeros((16, 128), F32) for _ in range(FIELDS)]
        for c in range(REGIONS):
            step = x - corners[c][0]
            inside = jnp.logical_and(step >= 0, step < 8)
            main_row = jnp.where(inside, 3 + jnp.clip(step, 0, 7) // 2, 0)
            first = index[x, c, 0]
            ends = index[x, c, 1]
            used = first >= 128
            use_end = ends >= 128
            first = first & 127
            ends = ends & 127
            for f in range(FIELDS):
                main = jnp.broadcast_to(answers[7 * f + main_row, c : c + 1, :], (16, 128))
                y_face = jnp.broadcast_to(answers[7 * f + 1, c : c + 1, :], (16, 128))
                z_face = jnp.broadcast_to(answers[7 * f + 2, c : c + 1, :], (16, 128))
                v = pick(jnp.where(y_rows[c], y_face, main), first)
                v = jnp.where(use_end, pick(z_face, ends), v)
                values[f] = jnp.where(used, v, values[f])
        for f in range(FIELDS):
            v = new[f, x] + weight[x] * values[f]
            out[f, x] = v[:, :64]
        return 0

    lax.fori_loop(0, 16, one, 0)


def whole(
    sizes,
    parent_hbm,
    plane_hbm,
    corner_hbm,
    coarse_hbm,
    fine_hbm,
    coarse_out,
    fine_out,
    parent_ref,
    corner_ref,
    plane_ref,
    coarse_ref,
    block,
    new,
    x_face,
    y_low,
    y_high,
    z_low,
    z_high,
    weight,
    index,
    y_stage,
    z_stage,
    x_rim,
    y_rim,
    z_rim,
    cut,
    rim_out,
    rim_in_old,
    rim_in_mid,
    rim,
    fine_ref,
    box,
    half,
    reg,
    route,
    relay_in,
    relay_out,
    row_stage,
    direct_out,
    direct_in,
    answer_in,
    answers,
    table,
    load_sems,
    halo_send,
    halo_recv,
    many_send,
    many_recv,
):
    n_gx, n_gy, n_gz = sizes
    members = n_gy * n_gz
    relayed = min(members, 7 * FIELDS)
    direct = 7 * FIELDS - relayed
    rim_in = (rim_in_old, rim_in_mid)
    gx = lax.axis_index("gx")
    gy = lax.axis_index("gy")
    gz = lax.axis_index("gz")
    within = gy * n_gz + gz
    myself = gx * members + within
    start = gx * (members * BOXMAX)

    def peer(distance):
        other = lax.rem(within + distance, members)
        return other, (gx, other // n_gz, lax.rem(other, n_gz))

    barrier = pltpu.get_barrier_semaphore()

    def greet(distance, _):
        pl.semaphore_signal(barrier, inc=1, device_id=peer(distance)[1], device_id_type=MESH)
        return 0

    x_next = (lax.rem(gx + 1, n_gx), gy, gz)
    x_prev = (lax.rem(gx + n_gx - 1, n_gx), gy, gz)
    y_next = (gx, lax.rem(gy + 1, n_gy), gz)
    y_prev = (gx, lax.rem(gy + n_gy - 1, n_gy), gz)
    z_next = (gx, gy, lax.rem(gz + 1, n_gz))
    z_prev = (gx, gy, lax.rem(gz + n_gz - 1, n_gz))
    pl.semaphore_signal(barrier, inc=1, device_id=x_next, device_id_type=MESH)
    pl.semaphore_signal(barrier, inc=1, device_id=x_prev, device_id_type=MESH)
    lax.fori_loop(1, members, greet, 0)

    def fetch(src, dst, index):
        copy = pltpu.make_async_copy(src, dst, load_sems.at[index])
        copy.start()
        return copy

    coarse_load = fetch(coarse_hbm, coarse_ref, 0)
    parent_load = fetch(parent_hbm, parent_ref, 1)
    corner_load = fetch(corner_hbm, corner_ref, 2)
    plane_load = fetch(plane_hbm, plane_ref, 3)
    fine_load = fetch(fine_hbm, fine_ref, 4)

    lane16 = iota((16, 128), 1)
    row16 = iota((16, 128), 0)
    coarse_load.wait()
    for f in range(FIELDS):
        block[f, 1:17, :, 0:64] = coarse_ref[f]
    for f in range(FIELDS):
        y_stage[0, f] = block[f, 1:17, 0, :]
        y_stage[1, f] = block[f, 1:17, 15, :]
        for h in range(2):
            low = jnp.zeros((16, 128), F32)
            high = jnp.zeros((16, 128), F32)
            for x in range(8):
                plane = block[f, 1 + 8 * h + x]
                here = lane16 // 16 == x
                low = jnp.where(here, jnp.broadcast_to(plane[:, 0:1], (16, 128)), low)
                high = jnp.where(here, jnp.broadcast_to(plane[:, 63:64], (16, 128)), high)
            match = row16 == lane16 % 16
            z_stage[0, h, f : f + 1, :] = jnp.sum(
                jnp.where(match, low, 0.0), axis=0, keepdims=True
            )
            z_stage[1, h, f : f + 1, :] = jnp.sum(
                jnp.where(match, high, 0.0), axis=0, keepdims=True
            )

    pl.semaphore_wait(barrier, members + 1)

    def halo(src, dst, index, device):
        copy = pltpu.make_async_remote_copy(
            src_ref=src,
            dst_ref=dst,
            send_sem=halo_send.at[index],
            recv_sem=halo_recv.at[index],
            device_id=device,
            device_id_type=MESH,
        )
        copy.start()
        return copy

    halos = [
        halo(block.at[:, 16], x_rim.at[0], 0, x_next),
        halo(block.at[:, 1], x_rim.at[1], 1, x_prev),
        halo(y_stage.at[1], y_rim.at[0], 2, y_next),
        halo(y_stage.at[0], y_rim.at[1], 3, y_prev),
        halo(z_stage.at[1], z_rim.at[0], 4, z_next),
        halo(z_stage.at[0], z_rim.at[1], 5, z_prev),
    ]

    parent_load.wait()
    corner_load.wait()

    def scan(entry, found):
        c0, c1, c2, c3 = found
        hit = parent_ref[start + entry] == myself
        return (
            jnp.where(hit, c1, c0),
            jnp.where(hit, c2, c1),
            jnp.where(hit, c3, c2),
            jnp.where(hit, entry, c3),
        )

    zero = jnp.int32(0)
    children = lax.fori_loop(0, members * BOXMAX, scan, (zero, zero, zero, zero), unroll=8)
    for c in range(REGIONS):
        for k in range(3):
            table[4 * c + k] = jnp.clip(corner_ref[k, start + children[c]], 1, 55 if k == 2 else 7)
    child_peer = [child // BOXMAX for child in children]
    own = [parent_ref[start + within * BOXMAX + s] for s in range(BOXMAX)]
    own_peer = [lax.rem(jnp.maximum(own[s], 0), members) for s in range(BOXMAX)]

    def look_up(distance, _):
        other = lax.rem(within + distance, members)
        rank = zero
        for c in range(1, REGIONS):
            rank = jnp.where(child_peer[c] == other, c, rank)
        found = zero
        for s in range(BOXMAX):
            found = jnp.where(jnp.logical_and(own[s] >= 0, own_peer[s] == other), s, found)
        table[32 + distance] = rank
        table[32 + members + distance] = found
        return 0

    lax.fori_loop(0, members, look_up, 0)

    def cut_all(when, source):
        def one(c, _):
            corner = (table[4 * c], table[4 * c + 1], table[4 * c + 2])

            def put(f, v, line):
                cut[when, c, 3 * f + v : 3 * f + v + 1, :] = line

            cut_rims(source, corner, put)
            return 0

        lax.fori_loop(0, REGIONS, one, 0)

    def ship(src, dst, index, device):
        pltpu.make_async_remote_copy(
            src_ref=src,
            dst_ref=dst,
            send_sem=many_send.at[index],
            recv_sem=many_recv.at[index],
            device_id=device,
            device_id_type=MESH,
        ).start()

    def slot_of(other):
        return lax.rem(within - other + 2 * members - 1, members)

    def wait_many(every, index, semaphores):
        pltpu.make_async_copy(every, every, semaphores.at[index]).wait()

    others = pl.ds(0, members - 1)

    def send_rims(when):
        def one(distance, _):
            rim_out[when, distance - 1] = cut[when, table[32 + distance]]
            ship(
                rim_out.at[when, distance - 1],
                rim_in[when].at[distance - 1],
                when,
                peer(distance)[1],
            )
            return 0

        lax.fori_loop(1, members, one, 0)
        rim_in[when][members - 1] = cut[when, table[32]]

    cut_all(0, lambda f, x: block[f, x + 1])
    send_rims(0)

    plane_load.wait()
    n_rows = REGIONS * members
    columns = members * BOXMAX
    row = iota((n_rows, columns), 0)
    column = iota((n_rows, columns), 1)
    slots = plane_ref[pl.ds(gx * (columns // 128), columns // 128), :] if columns >= 128 else None
    if columns >= 128:
        slots = jnp.concatenate(
            [
                jnp.broadcast_to(slots[h : h + 1, :], (n_rows, 128))
                for h in range(columns // 128)
            ],
            axis=1,
        )
    else:
        slots = jnp.broadcast_to(plane_ref[0:1, 0:columns], (n_rows, columns))
    number = column.astype(F32)
    far = 65536.0
    candidate = jnp.where(slots == row // REGIONS + gx * members, number, far)
    chosen = jnp.full((n_rows, 1), far)
    for r in range(REGIONS):
        least = jnp.min(candidate, axis=1, keepdims=True)
        chosen = jnp.where(row[:, 0:1] % REGIONS == r, least, chosen)
        candidate = jnp.where(candidate == least, far, candidate)
    arrival = lax.rem(within - column // BOXMAX - 1 + members, members) * BOXMAX + column % BOXMAX
    route[...] = jnp.where(arrival.astype(F32) == chosen, 1.0, 0.0)

    fine_load.wait()
    for i in range(16):
        for f in range(FIELDS):
            box[f, 1 + i] = fine_ref[f, :, 256 * i : 256 * i + 256]
    for v in range(7 * FIELDS):
        reg[v] = jnp.zeros((BOXMAX, 128), F32)

    for copy in halos:
        copy.wait()
    for f in range(FIELDS):
        block[f, 0] = x_rim[0, f]
        block[f, 17] = x_rim[1, f]
    coarse_step(block, y_rim, z_rim, new, x_face, y_low, y_high, z_low, z_high)
    cut_all(1, lambda f, x: 0.5 * (block[f, x + 1] + new[f, x]))
    send_rims(1)

    sub = iota((BOXMAX, 128), 0)
    owner = jnp.zeros((BOXMAX, 128), I32)
    for s in range(BOXMAX):
        owner = jnp.where(sub == s, own[s], owner)
    filled = owner >= 0

    def take_rims(when):
        wait_many(rim_in[when].at[others], when, many_recv)
        for s in range(BOXMAX):
            rows = rim_in[when][slot_of(own_peer[s])]
            for v in range(3 * FIELDS):
                rim[v, s : s + 1, :] = rows[v : v + 1, :]

    take_rims(0)

    def put_half(f, plane, h, value):
        half[f, plane + 1, :, 128 * h : 128 * h + 128] = value

    fine_step(box, rim, reg, filled, put_half, False)
    take_rims(1)

    def put_last(f, plane, h, value):
        old = box[f, plane + 1, :, 128 * h : 128 * h + 128]
        where = pl.multiple_of(plane * 256 + h * 128, 128)
        fine_out[f, :, pl.ds(where, 128)] = jnp.where(filled, value, old)

    def relay(tile):
        @pl.when(jnp.logical_and(tile != within, tile < relayed))
        def _():
            distance = lax.rem(tile - within + members, members)
            device = (gx, tile // n_gz, lax.rem(tile, n_gz))
            ship(reg.at[tile], relay_in.at[distance - 1], 2, device)

    def relay_ready(big):
        @pl.when(big % 2 == 1)
        def _():
            for f in range(FIELDS):
                relay(7 * f + 3 + big // 2)

    fine_step(half, rim, reg, filled, put_last, True, relay_ready)
    for f in range(FIELDS):
        for v in range(3):
            relay(7 * f + v)
    relay_in[members - 1] = reg[within]

    if direct:
        for s in range(BOXMAX):
            row_stage[s] = reg[relayed:, s, :]

        def direct_one(distance, _):
            direct_out[distance - 1] = row_stage[table[32 + members + distance]]
            ship(direct_out.at[distance - 1], direct_in.at[distance - 1], 3, peer(distance)[1])
            return 0

        lax.fori_loop(1, members, direct_one, 0)
        direct_in[members - 1] = row_stage[table[32 + members]]

    wait_many(relay_in.at[others], 2, many_recv)
    sorted_rows = jnp.dot(
        route[...],
        relay_in[...].reshape(columns, 128),
        precision=lax.Precision.HIGHEST,
        preferred_element_type=F32,
    )
    for p in range(members):
        relay_out[p] = sorted_rows[REGIONS * p : REGIONS * p + REGIONS]

    def answer_one(distance, _):
        other, device = peer(distance)
        ship(relay_out.at[other], answer_in.at[distance - 1], 4, device)
        return 0

    lax.fori_loop(1, members, answer_one, 0)
    answer_in[members - 1] = relay_out[within]

    corners = [(table[4 * c], table[4 * c + 1], table[4 * c + 2]) for c in range(REGIONS)]
    plan_settle(corners, new, x_face, y_low, y_high, z_low, z_high, weight, index)

    if direct:
        wait_many(direct_in.at[others], 3, many_recv)
        for c in range(REGIONS):
            rows = direct_in[slot_of(child_peer[c])]
            for v in range(direct):
                answers[relayed + v, c : c + 1, :] = rows[v : v + 1, :]
    wait_many(answer_in.at[others], 4, many_recv)
    for v in range(relayed):
        answers[v] = answer_in[lax.rem(within - v + 2 * members - 1, members)]
    settle(corners, answers, new, weight, index, coarse_out)
    wait_many(rim_out.at[0, others], 0, many_send)
    wait_many(rim_out.at[1, others], 1, many_send)
    wait_many(relay_in.at[others], 2, many_send)
    if direct:
        wait_many(direct_out.at[others], 3, many_send)
    wait_many(relay_out.at[others], 4, many_send)


def on_device(sizes, coarse_state, fine_state, slot_parent, slot_corner):
    members = sizes[1] * sizes[2]
    relayed = min(members, 7 * FIELDS)
    vmem = pl.BlockSpec(memory_space=pltpu.VMEM)
    hbm = pl.BlockSpec(memory_space=pltpu.HBM)
    fine = jnp.transpose(fine_state, (1, 0, 2))
    corner = jnp.transpose(slot_corner, (1, 0))
    plane = slot_parent.reshape(-1, min(128, slot_parent.shape[0]))
    field_block = (FIELDS, 16, 16, 128)
    rows = 7 * FIELDS
    direct = max(rows - relayed, 1)
    coarse_next, fine_next = pl.pallas_call(
        functools.partial(whole, sizes),
        out_shape=(
            jax.ShapeDtypeStruct(coarse_state.shape, F32),
            jax.ShapeDtypeStruct(fine.shape, F32),
        ),
        in_specs=[hbm] * 5,
        out_specs=(vmem, vmem),
        scratch_shapes=[
            pltpu.SMEM(slot_parent.shape, I32),
            pltpu.SMEM(corner.shape, I32),
            pltpu.VMEM(plane.shape, I32),
            pltpu.VMEM(coarse_state.shape, F32),
            pltpu.VMEM((FIELDS, 18, 16, 128), F32),
            pltpu.VMEM(field_block, F32),
            pltpu.VMEM((FIELDS, 17, 16, 128), F32),
            pltpu.VMEM(field_block, F32),
            pltpu.VMEM(field_block, F32),
            pltpu.VMEM(field_block, F32),
            pltpu.VMEM(field_block, F32),
            pltpu.VMEM((16, 16, 128), F32),
            pltpu.VMEM((16, REGIONS, 2, 16, 128), I32),
            pltpu.VMEM((2, FIELDS, 16, 128), F32),
            pltpu.VMEM((2, 2, FIELDS, 128), F32),
            pltpu.VMEM((2, FIELDS, 16, 128), F32),
            pltpu.VMEM((2, FIELDS, 16, 128), F32),
            pltpu.VMEM((2, 2, FIELDS, 128), F32),
            pltpu.VMEM((2, REGIONS, 3 * FIELDS, 128), F32),
            pltpu.VMEM((2, members, 3 * FIELDS, 128), F32),
            pltpu.VMEM((members, 3 * FIELDS, 128), F32),
            pltpu.VMEM((members, 3 * FIELDS, 128), F32),
            pltpu.VMEM((3 * FIELDS, BOXMAX, 128), F32),
            pltpu.VMEM(fine.shape, F32),
            pltpu.VMEM((FIELDS, 18, BOXMAX, 256), F32),
            pltpu.VMEM((FIELDS, 18, BOXMAX, 256), F32),
            pltpu.VMEM((rows, BOXMAX, 128), F32),
            pltpu.VMEM((REGIONS * members, BOXMAX * members), F32),
            pltpu.VMEM((members, BOXMAX, 128), F32),
            pltpu.VMEM((members, REGIONS, 128), F32),
            pltpu.VMEM((BOXMAX, direct, 128), F32),
            pltpu.VMEM((members, direct, 128), F32),
            pltpu.VMEM((members, direct, 128), F32),
            pltpu.VMEM((members, REGIONS, 128), F32),
            pltpu.VMEM((rows, REGIONS, 128), F32),
            pltpu.SMEM((32 + 2 * members,), I32),
            pltpu.SemaphoreType.DMA((5,)),
            pltpu.SemaphoreType.DMA((6,)),
            pltpu.SemaphoreType.DMA((6,)),
            pltpu.SemaphoreType.DMA((5,)),
            pltpu.SemaphoreType.DMA((5,)),
        ],
        compiler_params=pltpu.CompilerParams(
            collective_id=0, has_side_effects=True, vmem_limit_bytes=48 * 1024 * 1024
        ),
    )(slot_parent, plane, corner, coarse_state, fine)
    return coarse_next, jnp.transpose(fine_next, (1, 0, 2))


def solution(mesh):
    sizes = tuple(mesh.shape[name] for name in ("gx", "gy", "gz"))
    return jax.shard_map(
        functools.partial(on_device, sizes),
        mesh=mesh,
        in_specs=(P(None, "gx", "gy", "gz"), P(("gx", "gy", "gz"), None, None), P(), P()),
        out_specs=(P(None, "gx", "gy", "gz"), P(("gx", "gy", "gz"), None, None)),
        check_vma=False,
    )
```

```python
import functools

import jax
import jax.numpy as jnp
from jax import lax
from jax.experimental import pallas as pl
from jax.experimental.pallas import tpu as pltpu
from jax.sharding import PartitionSpec as P

GAMMA = 1.4
COURANT = 0.04
FINE_UNROLL = 1
COARSE_UNROLL = 4
CUT_UNROLL = 4
SETTLE_UNROLL = 4
FIELDS = 5
REGIONS = 4
BOXMAX = 8
MESH = pl.DeviceIdType.MESH
F32 = jnp.float32
I32 = jnp.int32


def iota(shape, dim):
    return lax.broadcasted_iota(I32, shape, dim)


def pick(values, lanes):
    numbers = lax.GatherDimensionNumbers(
        offset_dims=(),
        collapsed_slice_dims=(1,),
        start_index_map=(1,),
        operand_batching_dims=(0,),
        start_indices_batching_dims=(0,),
    )
    return lax.gather(
        values,
        lanes[..., None],
        numbers,
        (1, 1),
        mode=lax.GatherScatterMode.PROMISE_IN_BOUNDS,
    )


def prims(q):
    inverse = pl.reciprocal(q[0], approx=True)
    inverse = inverse * (2.0 - q[0] * inverse)
    kinetic = 0.5 * (q[1] * q[1] + q[2] * q[2] + q[3] * q[3]) * inverse
    pressure = (GAMMA - 1.0) * (q[4] - kinetic)
    square = GAMMA * pressure * inverse
    sound = square * lax.rsqrt(jnp.maximum(square, 1e-30))
    return inverse, pressure, sound, q[4] + pressure


def along(q, prim, axis):
    inverse, pressure, sound, total = prim
    velocity = q[1 + axis] * inverse
    flux = [q[1 + axis], q[1] * velocity, q[2] * velocity, q[3] * velocity, total * velocity]
    flux[1 + axis] = flux[1 + axis] + pressure
    return flux, jnp.abs(velocity) + sound


def face(low, low_terms, high, high_terms):
    signal = jnp.maximum(low_terms[1], high_terms[1])
    return [
        (low_terms[0][f] + high_terms[0][f]) - signal * (high[f] - low[f]) for f in range(FIELDS)
    ]


def moved(q, terms, move):
    return [move(v) for v in q], [move(v) for v in terms[0]], move(terms[1])


def fine_step(box, rim, reg, filled, put, second, done=None):
    lane = iota((BOXMAX, 128), 1)
    first_row = lane < 16
    last_row = lane >= 112
    k_first = lane % 16 == 0
    k_last = lane % 16 == 15
    half_k = (lane % 16) // 2
    quarter = lane // 32
    squeeze = ((lane % 32) // 8) * 32 + (lane % 8) * 2
    part = (lane % 64) // 8

    def halves(f, plane):
        return [box[f, plane, :, 128 * h : 128 * h + 128] for h in range(2)]

    for f in range(FIELDS):
        for h in range(2):
            spread = (h * 4 + quarter) * 8 + half_k
            box[f, 0, :, 128 * h : 128 * h + 128] = pick(rim[3 * f], spread)
            box[f, 17, :, 128 * h : 128 * h + 128] = pick(rim[3 * f], spread + 64)

    def load(plane):
        both = [halves(f, plane) for f in range(FIELDS)]
        return [[both[f][h] for f in range(FIELDS)] for h in range(2)]

    def x_faces(low, low_prim, high, high_prim):
        return [
            face(low[h], along(low[h], low_prim[h], 0), high[h], along(high[h], high_prim[h], 0))
            for h in range(2)
        ]

    def roll(v, by):
        return pltpu.roll(v, by % 128, 1)

    ghost = load(0)
    here = load(1)
    here_prim = [prims(here[h]) for h in range(2)]
    x_low = x_faces(ghost, [prims(ghost[h]) for h in range(2)], here, here_prim)

    def x_register(faces, side):
        for f in range(FIELDS):
            out = []
            for h in range(2):
                v = faces[h][f]
                v = v + roll(v, -1)
                v = v + roll(v, -16)
                out.append(pick(v, squeeze))
            both = jnp.where((lane % 64) < 32, out[0], out[1])
            mine = jnp.logical_and(filled, (lane < 64) if side == 0 else (lane >= 64))
            reg[7 * f] = reg[7 * f] + jnp.where(mine, both, 0.0)

    x_register(x_low, 0)

    def pair(big, carried):
        here, here_prim, x_low = carried
        y_lanes = big * 8 + half_k + jnp.where(lane >= 64, 64, 0)
        y_ghost = [pick(rim[3 * f + 1], y_lanes) for f in range(FIELDS)]
        y_ghost_terms = along(y_ghost, prims(y_ghost), 1)
        z_ghost = []
        z_ghost_terms = []
        for h in range(2):
            z_lanes = big * 8 + h * 4 + quarter + jnp.where(lane % 16 >= 8, 64, 0)
            ghost = [pick(rim[3 * f + 2], z_lanes) for f in range(FIELDS)]
            z_ghost.append(ghost)
            z_ghost_terms.append(along(ghost, prims(ghost), 2))
        y_sum = [None] * FIELDS
        z_sum = [[None] * FIELDS for _ in range(2)]
        new_sum = [[None] * FIELDS for _ in range(2)]

        def accumulate(total, v):
            return v if total is None else total + v

        for sub in range(2):
            plane = 2 * big + sub
            after = load(plane + 2)
            after_prim = [prims(after[h]) for h in range(2)]
            x_high = x_faces(here, here_prim, after, after_prim)

            y_terms = [along(here[h], here_prim[h], 1) for h in range(2)]
            rolled = [moved(here[h], y_terms[h], lambda v: roll(v, 16)) for h in range(2)]

            def y_select(h, low, high):
                return jnp.where(first_row, low, high)

            low0 = [jnp.where(first_row, y_ghost[f], rolled[0][0][f]) for f in range(FIELDS)]
            low0_terms = (
                [jnp.where(first_row, y_ghost_terms[0][f], rolled[0][1][f]) for f in range(FIELDS)],
                jnp.where(first_row, y_ghost_terms[1], rolled[0][2]),
            )
            low1 = [jnp.where(first_row, rolled[0][0][f], rolled[1][0][f]) for f in range(FIELDS)]
            low1_terms = (
                [jnp.where(first_row, rolled[0][1][f], rolled[1][1][f]) for f in range(FIELDS)],
                jnp.where(first_row, rolled[0][2], rolled[1][2]),
            )
            y0 = face(low0, low0_terms, here[0], y_terms[0])
            y1 = face(low1, low1_terms, here[1], y_terms[1])
            y_end = face(here[1], y_terms[1], y_ghost, y_ghost_terms)
            y_diff = [[], []]
            for f in range(FIELDS):
                up0 = roll(y0[f], -16)
                up1 = roll(y1[f], -16)
                y_diff[0].append(jnp.where(last_row, up1, up0) - y0[f])
                y_diff[1].append(jnp.where(last_row, y_end[f], up1) - y1[f])
                y_sum[f] = accumulate(y_sum[f], jnp.where(lane < 64, y0[f], y_end[f]))

            z_diff = [[], []]
            for h in range(2):
                terms = along(here[h], here_prim[h], 2)
                shifted = moved(here[h], terms, lambda v: roll(v, 1))
                low = [jnp.where(k_first, z_ghost[h][f], shifted[0][f]) for f in range(FIELDS)]
                low_terms = (
                    [
                        jnp.where(k_first, z_ghost_terms[h][0][f], shifted[1][f])
                        for f in range(FIELDS)
                    ],
                    jnp.where(k_first, z_ghost_terms[h][1], shifted[2]),
                )
                z = face(low, low_terms, here[h], terms)
                z_end = face(here[h], terms, z_ghost[h], z_ghost_terms[h])
                for f in range(FIELDS):
                    z_diff[h].append(jnp.where(k_last, z_end[f], roll(z[f], -1)) - z[f])
                    z_sum[h][f] = accumulate(z_sum[h][f], jnp.where(k_last, z_end[f], z[f]))

            for h in range(2):
                for f in range(FIELDS):
                    change = (x_high[h][f] - x_low[h][f]) + y_diff[h][f] + z_diff[h][f]
                    new = here[h][f] - (0.5 * COURANT) * change
                    put(f, plane, h, new)
                    if second:
                        new_sum[h][f] = accumulate(new_sum[h][f], new)
            here, here_prim, x_low = after, after_prim, x_high

        mine = jnp.logical_and(filled, part == big)
        y_from = (lane % 8) * 2 + jnp.where(lane >= 64, 112, 0)
        z_from = (lane % 4) * 32 + jnp.where(lane >= 64, 15, 0)
        for f in range(FIELDS):
            v = y_sum[f] + roll(y_sum[f], -1)
            reg[7 * f + 1] = reg[7 * f + 1] + jnp.where(mine, pick(v, y_from), 0.0)
            out = []
            for h in range(2):
                v = z_sum[h][f] + roll(z_sum[h][f], -16)
                out.append(pick(v, z_from))
            v = jnp.where(lane % 8 < 4, out[0], out[1])
            reg[7 * f + 2] = reg[7 * f + 2] + jnp.where(mine, v, 0.0)
            if second:
                out = []
                for h in range(2):
                    v = new_sum[h][f]
                    v = v + roll(v, -1)
                    v = v + roll(v, -16)
                    out.append(pick(v, squeeze))
                v = jnp.where((lane % 64) < 32, out[0], out[1])
                v = jnp.where(filled, v, 0.0)
                where = 7 * f + 3 + big // 2
                reg[where] = jnp.where(lane // 64 == big % 2, v, reg[where])
        if second:
            done(big)
        return here, here_prim, x_low

    last = lax.fori_loop(0, 8, pair, (here, here_prim, x_low), unroll=FINE_UNROLL)
    x_register(last[2], 1)


def coarse_step(block, y_rim, z_rim, new, x_face, y_low, y_high, z_low, z_high):
    lane = iota((16, 128), 1)
    row = iota((16, 128), 0)
    tip = iota((8, 128), 0)

    def load(plane):
        return [block[f, plane] for f in range(FIELDS)]

    def widen(x, _):
        column = (x % 8) * 16 + row
        for f in range(FIELDS):
            below = jnp.broadcast_to(z_rim[0, x // 8, f : f + 1, :], (16, 128))
            above = jnp.broadcast_to(z_rim[1, x // 8, f : f + 1, :], (16, 128))
            side = jnp.where(lane == 64, pick(above, column), pick(below, column))
            block[f, x + 1] = jnp.where(lane < 64, block[f, x + 1], side)
        return 0

    lax.fori_loop(0, 16, widen, 0, unroll=4)

    ghost = load(0)
    here = load(1)
    here_prim = prims(here)
    low = face(ghost, along(ghost, prims(ghost), 0), here, along(here, here_prim, 0))
    for f in range(FIELDS):
        x_face[f, 0] = low[f]

    def one(x, carried):
        here, here_prim, x_low = carried
        after = load(x + 2)
        after_prim = prims(after)
        x_high = face(here, along(here, here_prim, 0), after, along(after, after_prim, 0))

        tips = []
        for f in range(FIELDS):
            above = y_rim[1, f, pl.ds(x, 1), :]
            below = y_rim[0, f, pl.ds(x, 1), :]
            tips.append(
                jnp.where(
                    tip == 0,
                    jnp.broadcast_to(above, (8, 128)),
                    jnp.broadcast_to(below, (8, 128)),
                )
            )
        tip_terms = along(tips, prims(tips), 1)
        terms = along(here, here_prim, 1)

        def tall(low, high):
            return jnp.concatenate([low, high], axis=0)

        cells = [tall(here[f], tips[f]) for f in range(FIELDS)]
        terms = ([tall(terms[0][f], tip_terms[0][f]) for f in range(FIELDS)], tall(terms[1], tip_terms[1]))
        shifted = moved(cells, terms, lambda v: pltpu.roll(v, 1, 0))
        y = face(shifted[0], (shifted[1], shifted[2]), cells, terms)

        terms = along(here, here_prim, 2)
        shifted = moved(here, terms, lambda v: pltpu.roll(v, 1, 1))
        z = face(shifted[0], (shifted[1], shifted[2]), here, terms)
        for f in range(FIELDS):
            up = pltpu.roll(y[f], 23, 0)[:16]
            down = y[f][:16]
            right = pltpu.roll(z[f], 127, 1)
            x_face[f, x + 1] = x_high[f]
            y_low[f, x] = down
            y_high[f, x] = up
            z_low[f, x] = z[f]
            z_high[f, x] = right
            change = (x_high[f] - x_low[f]) + (up - down) + (right - z[f])
            new[f, x] = here[f] - (0.5 * COURANT) * change
        return after, after_prim, x_high

    lax.fori_loop(0, 16, one, (here, here_prim, low), unroll=COARSE_UNROLL)


def cut_rims(source, corner, put):
    cx, cy, cz = corner
    lane = iota((8, 128), 1)
    row = iota((8, 128), 0)
    low_half = lane < 64
    part = (lane % 64) // 8
    along_z = cz + lane % 8
    ends = jnp.where(low_half, cz - 1, cz + 8)
    rows_x = row == part
    rows_z = row == lane % 8
    for f in range(FIELDS):
        low = pick(source(f, cx - 1, cy, 8), along_z)
        high = pick(source(f, cx + 8, cy, 8), along_z)
        v = jnp.where(rows_x, jnp.where(low_half, low, high), 0.0)
        put(f, 0, jnp.sum(v, axis=0, keepdims=True))
        low = jnp.zeros((8, 128), F32)
        high = jnp.zeros((8, 128), F32)
        total = jnp.zeros((8, 128), F32)
        for big in range(8):
            here = row == big
            low = jnp.where(here, jnp.broadcast_to(source(f, cx + big, cy - 1, 1), (8, 128)), low)
            high = jnp.where(here, jnp.broadcast_to(source(f, cx + big, cy + 8, 1), (8, 128)), high)
            total = jnp.where(part == big, pick(source(f, cx + big, cy, 8), ends), total)
        v = jnp.where(low_half, pick(low, along_z), pick(high, along_z))
        put(f, 1, jnp.sum(jnp.where(rows_x, v, 0.0), axis=0, keepdims=True))
        put(f, 2, jnp.sum(jnp.where(rows_z, total, 0.0), axis=0, keepdims=True))


def plan_settle(corners, new, x_face, y_low, y_high, z_low, z_high, weight, index):
    lane = iota((16, 128), 1)
    row = iota((16, 128), 0)

    def one(x, _):
        kind = jnp.zeros((16, 128), I32)
        for c in range(REGIONS):
            cx, cy, cz = corners[c]
            step = x - cx
            inside = jnp.logical_and(step >= 0, step < 8)
            dy = row - cy
            dz = lane - cz
            in_y = jnp.logical_and(dy >= 0, dy < 8)
            in_z = jnp.logical_and(dz >= 0, dz < 8)
            near = jnp.where(dy == -1, 4, jnp.where(dy == 8, 5, 0))
            side = jnp.where(dz == -1, 6, jnp.where(dz == 8, 7, 0))
            plain = jnp.where(inside, 1, jnp.where(step == -1, 2, jnp.where(step == 8, 3, 0)))
            mine = jnp.where(
                jnp.logical_and(in_y, in_z),
                plain,
                jnp.where(inside, jnp.where(in_z, near, jnp.where(in_y, side, 0)), 0),
            )
            ys = jnp.clip(dy, 0, 7)
            zs = jnp.clip(dz, 0, 7)
            lanes = jnp.where(mine < 4, ys * 8 + zs, 32 + 8 * mine + jnp.where(mine < 6, zs, ys))
            used = mine > 0
            kind = jnp.where(used, mine, kind)
            index[x, c] = jnp.where(used, lanes + 128, 0)
        factor = jnp.where(kind < 2, 0.0, jnp.where(kind % 2 == 0, -COURANT, COURANT))
        weight[x] = jnp.where(kind == 1, 0.125, 0.0625 * factor)
        for f in range(FIELDS):
            flux = jnp.where(
                kind < 4,
                jnp.where(kind == 2, x_face[f, x + 1], x_face[f, x]),
                jnp.where(
                    kind < 6,
                    jnp.where(kind == 4, y_high[f, x], y_low[f, x]),
                    jnp.where(kind == 6, z_high[f, x], z_low[f, x]),
                ),
            )
            plain = new[f, x]
            ring = jnp.where(kind >= 2, plain - 0.5 * factor * flux, plain)
            new[f, x] = jnp.where(kind == 1, 0.0, ring)
        return 0

    lax.fori_loop(0, 16, one, 0)


def settle_rows(answers, rows):
    lane = iota((REGIONS, 128), 1)
    spot = ((lane % 16) // 8) * 64 + lane % 8
    for f in range(FIELDS):
        ends = answers[7 * f]
        rows[f, 0] = ends
        rows[f, 9] = pltpu.roll(ends, 64, 1)
        y_face = answers[7 * f + 1]
        z_face = answers[7 * f + 2]
        for big in range(8):
            cells = answers[7 * f + 3 + big // 2]
            if big % 2:
                cells = pltpu.roll(cells, 64, 1)
            around = jnp.where(
                lane < 80, pick(y_face, spot + 8 * big), pick(z_face, spot + 8 * big)
            )
            rows[f, 1 + big] = jnp.where(lane < 64, cells, around)


def settle(corners, rows, new, weight, index, out):
    def one(x, _):
        values = [jnp.zeros((16, 128), F32) for _ in range(FIELDS)]
        for c in range(REGIONS):
            which = jnp.clip(x - corners[c][0] + 1, 0, 9)
            lanes = index[x, c]
            used = lanes >= 128
            lanes = lanes & 127
            for f in range(FIELDS):
                line = jnp.broadcast_to(rows[f, which, c : c + 1, :], (16, 128))
                values[f] = jnp.where(used, pick(line, lanes), values[f])
        for f in range(FIELDS):
            v = new[f, x] + weight[x] * values[f]
            out[f, x] = v[:, :64]
        return 0

    lax.fori_loop(0, 16, one, 0, unroll=SETTLE_UNROLL)


def whole(
    sizes,
    parent_hbm,
    plane_hbm,
    corner_hbm,
    coarse_hbm,
    fine_hbm,
    coarse_out,
    fine_out,
    parent_ref,
    corner_ref,
    plane_ref,
    coarse_ref,
    block,
    new,
    x_face,
    y_low,
    y_high,
    z_low,
    z_high,
    weight,
    index,
    y_stage,
    z_stage,
    x_rim,
    y_rim,
    z_rim,
    cut,
    rim_out,
    rim_in_old,
    rim_in_mid,
    rim,
    fine_ref,
    box,
    half,
    reg,
    route,
    relay_in,
    relay_out,
    row_stage,
    direct_out,
    direct_in,
    answer_in,
    answers,
    answer_rows,
    table,
    load_sems,
    halo_send,
    halo_recv,
    many_send,
    many_recv,
):
    n_gx, n_gy, n_gz = sizes
    members = n_gy * n_gz
    relayed = min(members, 7 * FIELDS)
    direct = 7 * FIELDS - relayed
    rim_in = (rim_in_old, rim_in_mid)
    gx = lax.axis_index("gx")
    gy = lax.axis_index("gy")
    gz = lax.axis_index("gz")
    within = gy * n_gz + gz
    myself = gx * members + within
    start = gx * (members * BOXMAX)

    def peer(distance):
        other = lax.rem(within + distance, members)
        return other, (gx, other // n_gz, lax.rem(other, n_gz))

    barrier = pltpu.get_barrier_semaphore()

    def greet(distance, _):
        pl.semaphore_signal(barrier, inc=1, device_id=peer(distance)[1], device_id_type=MESH)
        return 0

    x_next = (lax.rem(gx + 1, n_gx), gy, gz)
    x_prev = (lax.rem(gx + n_gx - 1, n_gx), gy, gz)
    y_next = (gx, lax.rem(gy + 1, n_gy), gz)
    y_prev = (gx, lax.rem(gy + n_gy - 1, n_gy), gz)
    z_next = (gx, gy, lax.rem(gz + 1, n_gz))
    z_prev = (gx, gy, lax.rem(gz + n_gz - 1, n_gz))
    pl.semaphore_signal(barrier, inc=1, device_id=x_next, device_id_type=MESH)
    pl.semaphore_signal(barrier, inc=1, device_id=x_prev, device_id_type=MESH)
    lax.fori_loop(1, members, greet, 0)

    def fetch(src, dst, index):
        copy = pltpu.make_async_copy(src, dst, load_sems.at[index])
        copy.start()
        return copy

    coarse_load = fetch(coarse_hbm, coarse_ref, 0)
    parent_load = fetch(parent_hbm, parent_ref, 1)
    corner_load = fetch(corner_hbm, corner_ref, 2)
    plane_load = fetch(plane_hbm, plane_ref, 3)
    fine_load = fetch(fine_hbm, fine_ref, 4)

    lane16 = iota((16, 128), 1)
    row16 = iota((16, 128), 0)
    coarse_load.wait()
    for f in range(FIELDS):
        block[f, 1:17, :, 0:64] = coarse_ref[f]
    for f in range(FIELDS):
        y_stage[0, f] = block[f, 1:17, 0, :]
        y_stage[1, f] = block[f, 1:17, 15, :]
        for h in range(2):
            low = jnp.zeros((16, 128), F32)
            high = jnp.zeros((16, 128), F32)
            for x in range(8):
                plane = block[f, 1 + 8 * h + x]
                here = lane16 // 16 == x
                low = jnp.where(here, jnp.broadcast_to(plane[:, 0:1], (16, 128)), low)
                high = jnp.where(here, jnp.broadcast_to(plane[:, 63:64], (16, 128)), high)
            match = row16 == lane16 % 16
            z_stage[0, h, f : f + 1, :] = jnp.sum(
                jnp.where(match, low, 0.0), axis=0, keepdims=True
            )
            z_stage[1, h, f : f + 1, :] = jnp.sum(
                jnp.where(match, high, 0.0), axis=0, keepdims=True
            )

    pl.semaphore_wait(barrier, members + 1)

    def halo(src, dst, index, device):
        copy = pltpu.make_async_remote_copy(
            src_ref=src,
            dst_ref=dst,
            send_sem=halo_send.at[index],
            recv_sem=halo_recv.at[index],
            device_id=device,
            device_id_type=MESH,
        )
        copy.start()
        return copy

    halos = [
        halo(block.at[:, 16], x_rim.at[0], 0, x_next),
        halo(block.at[:, 1], x_rim.at[1], 1, x_prev),
        halo(y_stage.at[1], y_rim.at[0], 2, y_next),
        halo(y_stage.at[0], y_rim.at[1], 3, y_prev),
        halo(z_stage.at[1], z_rim.at[0], 4, z_next),
        halo(z_stage.at[0], z_rim.at[1], 5, z_prev),
    ]

    parent_load.wait()
    corner_load.wait()

    def scan(entry, found):
        c0, c1, c2, c3 = found
        hit = parent_ref[start + entry] == myself
        return (
            jnp.where(hit, c1, c0),
            jnp.where(hit, c2, c1),
            jnp.where(hit, c3, c2),
            jnp.where(hit, entry, c3),
        )

    zero = jnp.int32(0)
    children = lax.fori_loop(0, members * BOXMAX, scan, (zero, zero, zero, zero), unroll=8)
    for c in range(REGIONS):
        for k in range(3):
            table[4 * c + k] = jnp.clip(corner_ref[k, start + children[c]], 1, 55 if k == 2 else 7)
    child_peer = [child // BOXMAX for child in children]
    own = [parent_ref[start + within * BOXMAX + s] for s in range(BOXMAX)]
    own_peer = [lax.rem(jnp.maximum(own[s], 0), members) for s in range(BOXMAX)]

    def look_up(distance, _):
        other = lax.rem(within + distance, members)
        rank = zero
        for c in range(1, REGIONS):
            rank = jnp.where(child_peer[c] == other, c, rank)
        found = zero
        for s in range(BOXMAX):
            found = jnp.where(jnp.logical_and(own[s] >= 0, own_peer[s] == other), s, found)
        table[32 + distance] = rank
        table[32 + members + distance] = found
        return 0

    lax.fori_loop(0, members, look_up, 0)

    def cut_all(when, source):
        def one(c, _):
            corner = (table[4 * c], table[4 * c + 1], table[4 * c + 2])

            def put(f, v, line):
                cut[when, c, 3 * f + v : 3 * f + v + 1, :] = line

            cut_rims(source, corner, put)
            return 0

        lax.fori_loop(0, REGIONS, one, 0, unroll=CUT_UNROLL)

    def ship(src, dst, index, device):
        pltpu.make_async_remote_copy(
            src_ref=src,
            dst_ref=dst,
            send_sem=many_send.at[index],
            recv_sem=many_recv.at[index],
            device_id=device,
            device_id_type=MESH,
        ).start()

    def slot_of(other):
        return lax.rem(within - other + 2 * members - 1, members)

    def wait_many(every, index, semaphores):
        pltpu.make_async_copy(every, every, semaphores.at[index]).wait()

    others = pl.ds(0, members - 1)

    def send_rims(when):
        def one(distance, _):
            rim_out[when, distance - 1] = cut[when, table[32 + distance]]
            ship(
                rim_out.at[when, distance - 1],
                rim_in[when].at[distance - 1],
                when,
                peer(distance)[1],
            )
            return 0

        lax.fori_loop(1, members, one, 0)
        rim_in[when][members - 1] = cut[when, table[32]]

    cut_all(0, lambda f, x, y, n: block[f, x + 1, pl.ds(y, n), :])
    send_rims(0)

    plane_load.wait()
    n_rows = REGIONS * members
    columns = members * BOXMAX
    row = iota((n_rows, columns), 0)
    column = iota((n_rows, columns), 1)
    slots = plane_ref[pl.ds(gx * (columns // 128), columns // 128), :] if columns >= 128 else None
    if columns >= 128:
        slots = jnp.concatenate(
            [
                jnp.broadcast_to(slots[h : h + 1, :], (n_rows, 128))
                for h in range(columns // 128)
            ],
            axis=1,
        )
    else:
        slots = jnp.broadcast_to(plane_ref[0:1, 0:columns], (n_rows, columns))
    number = column.astype(F32)
    far = 65536.0
    candidate = jnp.where(slots == row // REGIONS + gx * members, number, far)
    chosen = jnp.full((n_rows, 1), far)
    for r in range(REGIONS):
        least = jnp.min(candidate, axis=1, keepdims=True)
        chosen = jnp.where(row[:, 0:1] % REGIONS == r, least, chosen)
        candidate = jnp.where(candidate == least, far, candidate)
    arrival = lax.rem(within - column // BOXMAX - 1 + members, members) * BOXMAX + column % BOXMAX
    route[...] = jnp.where(arrival.astype(F32) == chosen, 1.0, 0.0)

    fine_load.wait()
    for i in range(16):
        for f in range(FIELDS):
            box[f, 1 + i] = fine_ref[f, :, 256 * i : 256 * i + 256]
    for v in range(7 * FIELDS):
        reg[v] = jnp.zeros((BOXMAX, 128), F32)

    for copy in halos:
        copy.wait()
    for f in range(FIELDS):
        block[f, 0] = x_rim[0, f]
        block[f, 17] = x_rim[1, f]
    coarse_step(block, y_rim, z_rim, new, x_face, y_low, y_high, z_low, z_high)
    cut_all(
        1,
        lambda f, x, y, n: 0.5 * (block[f, x + 1, pl.ds(y, n), :] + new[f, x, pl.ds(y, n), :]),
    )
    send_rims(1)

    sub = iota((BOXMAX, 128), 0)
    owner = jnp.zeros((BOXMAX, 128), I32)
    for s in range(BOXMAX):
        owner = jnp.where(sub == s, own[s], owner)
    filled = owner >= 0

    def take_rims(when):
        wait_many(rim_in[when].at[others], when, many_recv)
        for s in range(BOXMAX):
            rows = rim_in[when][slot_of(own_peer[s])]
            for v in range(3 * FIELDS):
                rim[v, s : s + 1, :] = rows[v : v + 1, :]

    take_rims(0)

    def put_half(f, plane, h, value):
        half[f, plane + 1, :, 128 * h : 128 * h + 128] = value

    fine_step(box, rim, reg, filled, put_half, False)
    take_rims(1)

    def put_last(f, plane, h, value):
        old = box[f, plane + 1, :, 128 * h : 128 * h + 128]
        where = pl.multiple_of(plane * 256 + h * 128, 128)
        fine_out[f, :, pl.ds(where, 128)] = jnp.where(filled, value, old)

    def relay(tile):
        @pl.when(jnp.logical_and(tile != within, tile < relayed))
        def _():
            distance = lax.rem(tile - within + members, members)
            device = (gx, tile // n_gz, lax.rem(tile, n_gz))
            ship(reg.at[tile], relay_in.at[distance - 1], 2, device)

    def relay_ready(big):
        @pl.when(big % 2 == 1)
        def _():
            for f in range(FIELDS):
                relay(7 * f + 3 + big // 2)

    fine_step(half, rim, reg, filled, put_last, True, relay_ready)
    for f in range(FIELDS):
        for v in range(3):
            relay(7 * f + v)
    relay_in[members - 1] = reg[within]

    if direct:
        for s in range(BOXMAX):
            row_stage[s] = reg[relayed:, s, :]

        def direct_one(distance, _):
            direct_out[distance - 1] = row_stage[table[32 + members + distance]]
            ship(direct_out.at[distance - 1], direct_in.at[distance - 1], 3, peer(distance)[1])
            return 0

        lax.fori_loop(1, members, direct_one, 0)
        direct_in[members - 1] = row_stage[table[32 + members]]

    wait_many(relay_in.at[others], 2, many_recv)
    sorted_rows = jnp.dot(
        route[...],
        relay_in[...].reshape(columns, 128),
        precision=lax.Precision.HIGHEST,
        preferred_element_type=F32,
    )
    for p in range(members):
        relay_out[p] = sorted_rows[REGIONS * p : REGIONS * p + REGIONS]

    def answer_one(distance, _):
        other, device = peer(distance)
        ship(relay_out.at[other], answer_in.at[distance - 1], 4, device)
        return 0

    lax.fori_loop(1, members, answer_one, 0)
    answer_in[members - 1] = relay_out[within]

    corners = [(table[4 * c], table[4 * c + 1], table[4 * c + 2]) for c in range(REGIONS)]
    plan_settle(corners, new, x_face, y_low, y_high, z_low, z_high, weight, index)

    if direct:
        wait_many(direct_in.at[others], 3, many_recv)
        for c in range(REGIONS):
            rows = direct_in[slot_of(child_peer[c])]
            for v in range(direct):
                answers[relayed + v, c : c + 1, :] = rows[v : v + 1, :]
    wait_many(answer_in.at[others], 4, many_recv)
    for v in range(relayed):
        answers[v] = answer_in[lax.rem(within - v + 2 * members - 1, members)]
    settle_rows(answers, answer_rows)
    settle(corners, answer_rows, new, weight, index, coarse_out)
    wait_many(rim_out.at[0, others], 0, many_send)
    wait_many(rim_out.at[1, others], 1, many_send)
    wait_many(relay_in.at[others], 2, many_send)
    if direct:
        wait_many(direct_out.at[others], 3, many_send)
    wait_many(relay_out.at[others], 4, many_send)


def on_device(sizes, coarse_state, fine_state, slot_parent, slot_corner):
    members = sizes[1] * sizes[2]
    relayed = min(members, 7 * FIELDS)
    vmem = pl.BlockSpec(memory_space=pltpu.VMEM)
    hbm = pl.BlockSpec(memory_space=pltpu.HBM)
    fine = jnp.transpose(fine_state, (1, 0, 2))
    corner = jnp.transpose(slot_corner, (1, 0))
    plane = slot_parent.reshape(-1, min(128, slot_parent.shape[0]))
    field_block = (FIELDS, 16, 16, 128)
    rows = 7 * FIELDS
    direct = max(rows - relayed, 1)
    coarse_next, fine_next = pl.pallas_call(
        functools.partial(whole, sizes),
        out_shape=(
            jax.ShapeDtypeStruct(coarse_state.shape, F32),
            jax.ShapeDtypeStruct(fine.shape, F32),
        ),
        in_specs=[hbm] * 5,
        out_specs=(vmem, vmem),
        scratch_shapes=[
            pltpu.SMEM(slot_parent.shape, I32),
            pltpu.SMEM(corner.shape, I32),
            pltpu.VMEM(plane.shape, I32),
            pltpu.VMEM(coarse_state.shape, F32),
            pltpu.VMEM((FIELDS, 18, 16, 128), F32),
            pltpu.VMEM(field_block, F32),
            pltpu.VMEM((FIELDS, 17, 16, 128), F32),
            pltpu.VMEM(field_block, F32),
            pltpu.VMEM(field_block, F32),
            pltpu.VMEM(field_block, F32),
            pltpu.VMEM(field_block, F32),
            pltpu.VMEM((16, 16, 128), F32),
            pltpu.VMEM((16, REGIONS, 16, 128), I32),
            pltpu.VMEM((2, FIELDS, 16, 128), F32),
            pltpu.VMEM((2, 2, FIELDS, 128), F32),
            pltpu.VMEM((2, FIELDS, 16, 128), F32),
            pltpu.VMEM((2, FIELDS, 16, 128), F32),
            pltpu.VMEM((2, 2, FIELDS, 128), F32),
            pltpu.VMEM((2, REGIONS, 3 * FIELDS, 128), F32),
            pltpu.VMEM((2, members, 3 * FIELDS, 128), F32),
            pltpu.VMEM((members, 3 * FIELDS, 128), F32),
            pltpu.VMEM((members, 3 * FIELDS, 128), F32),
            pltpu.VMEM((3 * FIELDS, BOXMAX, 128), F32),
            pltpu.VMEM(fine.shape, F32),
            pltpu.VMEM((FIELDS, 18, BOXMAX, 256), F32),
            pltpu.VMEM((FIELDS, 18, BOXMAX, 256), F32),
            pltpu.VMEM((rows, BOXMAX, 128), F32),
            pltpu.VMEM((REGIONS * members, BOXMAX * members), F32),
            pltpu.VMEM((members, BOXMAX, 128), F32),
            pltpu.VMEM((members, REGIONS, 128), F32),
            pltpu.VMEM((BOXMAX, direct, 128), F32),
            pltpu.VMEM((members, direct, 128), F32),
            pltpu.VMEM((members, direct, 128), F32),
            pltpu.VMEM((members, REGIONS, 128), F32),
            pltpu.VMEM((rows, REGIONS, 128), F32),
            pltpu.VMEM((FIELDS, 10, REGIONS, 128), F32),
            pltpu.SMEM((32 + 2 * members,), I32),
            pltpu.SemaphoreType.DMA((5,)),
            pltpu.SemaphoreType.DMA((6,)),
            pltpu.SemaphoreType.DMA((6,)),
            pltpu.SemaphoreType.DMA((5,)),
            pltpu.SemaphoreType.DMA((5,)),
        ],
        compiler_params=pltpu.CompilerParams(
            collective_id=0, has_side_effects=True, vmem_limit_bytes=62 * 1024 * 1024
        ),
    )(slot_parent, plane, corner, coarse_state, fine)
    return coarse_next, jnp.transpose(fine_next, (1, 0, 2))


def solution(mesh):
    sizes = tuple(mesh.shape[name] for name in ("gx", "gy", "gz"))
    return jax.shard_map(
        functools.partial(on_device, sizes),
        mesh=mesh,
        in_specs=(P(None, "gx", "gy", "gz"), P(("gx", "gy", "gz"), None, None), P(), P()),
        out_specs=(P(None, "gx", "gy", "gz"), P(("gx", "gy", "gz"), None, None)),
        check_vma=False,
    )
```

```python
import functools

import jax
import jax.numpy as jnp
from jax import lax
from jax.experimental import pallas as pl
from jax.experimental.pallas import tpu as pltpu
from jax.sharding import PartitionSpec as P

GAMMA = 1.4
COURANT = 0.04
PRIM_UNROLL = 2
X_UNROLL = 5
YZ_UNROLL = 4
OUTER_UNROLL = 4
COARSE_UNROLL = 4
CUT_UNROLL = 4
SETTLE_UNROLL = 4
FIELDS = 5
REGIONS = 4
BOXMAX = 8
MESH = pl.DeviceIdType.MESH
F32 = jnp.float32
I32 = jnp.int32


def iota(shape, dim):
    return lax.broadcasted_iota(I32, shape, dim)


def pick(values, lanes):
    numbers = lax.GatherDimensionNumbers(
        offset_dims=(),
        collapsed_slice_dims=(1,),
        start_index_map=(1,),
        operand_batching_dims=(0,),
        start_indices_batching_dims=(0,),
    )
    return lax.gather(
        values,
        lanes[..., None],
        numbers,
        (1, 1),
        mode=lax.GatherScatterMode.PROMISE_IN_BOUNDS,
    )


def prims(q):
    inverse = pl.reciprocal(q[0], approx=True)
    inverse = inverse * (2.0 - q[0] * inverse)
    kinetic = 0.5 * (q[1] * q[1] + q[2] * q[2] + q[3] * q[3]) * inverse
    pressure = (GAMMA - 1.0) * (q[4] - kinetic)
    square = GAMMA * pressure * inverse
    sound = square * lax.rsqrt(jnp.maximum(square, 1e-30))
    return inverse, pressure, sound, q[4] + pressure


def along(q, prim, axis):
    inverse, pressure, sound, total = prim
    velocity = q[1 + axis] * inverse
    flux = [q[1 + axis], q[1] * velocity, q[2] * velocity, q[3] * velocity, total * velocity]
    flux[1 + axis] = flux[1 + axis] + pressure
    return flux, jnp.abs(velocity) + sound


def face(low, low_terms, high, high_terms):
    signal = jnp.maximum(low_terms[1], high_terms[1])
    return [
        (low_terms[0][f] + high_terms[0][f]) - signal * (high[f] - low[f]) for f in range(FIELDS)
    ]


def moved(q, terms, move):
    return [move(v) for v in q], [move(v) for v in terms[0]], move(terms[1])


def span(plane, h):
    return pl.ds(pl.multiple_of(plane * 256 + h * 128, 128), 128)


def roll(v, by):
    return pltpu.roll(v, by % 128, 1)


def fine_prims(cells, prim):
    def one(plane, _):
        for h in range(2):
            where = span(plane, h)
            inverse, pressure, sound, _ = prims([cells[f, :, where] for f in range(FIELDS)])
            prim[0, :, where] = inverse
            prim[1, :, where] = pressure
            prim[2, :, where] = sound
        return 0

    lax.fori_loop(0, 16, one, 0, unroll=PRIM_UNROLL)


def fine_inner(cells, prim, out):
    lane = iota((BOXMAX, 128), 1)
    first_row = lane < 16
    last_row = lane >= 112
    k_first = lane % 16 == 0

    def load(plane, h):
        where = span(plane, h)
        q = [cells[f, :, where] for f in range(FIELDS)]
        pressure = prim[1, :, where]
        return q, (prim[0, :, where], pressure, prim[2, :, where], q[4] + pressure)

    def x_one(plane, low):
        high = []
        for h in range(2):
            q, q_prim = load(plane, h)
            up, up_prim = load(plane + 1, h)
            flux = face(q, along(q, q_prim, 0), up, along(up, up_prim, 0))
            for f in range(FIELDS):
                out[f, :, span(plane, h)] = q[f] - (0.5 * COURANT) * (flux[f] - low[h][f])
            high.append(flux)
        return high

    none = [[jnp.zeros((BOXMAX, 128), F32)] * FIELDS] * 2
    high = lax.fori_loop(0, 15, x_one, none, unroll=X_UNROLL)
    for h in range(2):
        for f in range(FIELDS):
            out[f, :, span(15, h)] = cells[f, :, span(15, h)] + (0.5 * COURANT) * high[h][f]

    def yz_one(plane, _):
        for h in range(2):
            q, q_prim = load(plane, h)
            terms = along(q, q_prim, 2)
            shifted = moved(q, terms, lambda v: roll(v, 1))
            z = face(shifted[0], (shifted[1], shifted[2]), q, terms)
            for f in range(FIELDS):
                low = jnp.where(k_first, 0.0, z[f])
                where = span(plane, h)
                out[f, :, where] = out[f, :, where] - (0.5 * COURANT) * (roll(low, -1) - low)
        q0, prim0 = load(plane, 0)
        q1, prim1 = load(plane, 1)
        terms0 = along(q0, prim0, 1)
        terms1 = along(q1, prim1, 1)
        shifted0 = moved(q0, terms0, lambda v: roll(v, 16))
        shifted1 = moved(q1, terms1, lambda v: roll(v, 16))

        def seam(low, high):
            return jnp.where(first_row, low, high)

        low1 = (
            [seam(shifted0[0][f], shifted1[0][f]) for f in range(FIELDS)],
            ([seam(shifted0[1][f], shifted1[1][f]) for f in range(FIELDS)], seam(shifted0[2], shifted1[2])),
        )
        y0 = face(shifted0[0], (shifted0[1], shifted0[2]), q0, terms0)
        y1 = face(low1[0], low1[1], q1, terms1)
        for f in range(FIELDS):
            low = jnp.where(first_row, 0.0, y0[f])
            up0 = roll(low, -16)
            up1 = roll(y1[f], -16)
            for h, up, down in ((0, jnp.where(last_row, up1, up0), low), (1, jnp.where(last_row, up0, up1), y1[f])):
                where = span(plane, h)
                out[f, :, where] = out[f, :, where] - (0.5 * COURANT) * (up - down)
        return 0

    lax.fori_loop(0, 16, yz_one, 0, unroll=YZ_UNROLL)


def fine_outer(cells, prim, rim, reg, filled, out, old):
    second = old is not None
    lane = iota((BOXMAX, 128), 1)
    k = lane % 16
    half_k = k // 2
    quarter = lane // 32
    squeeze = ((lane % 32) // 8) * 32 + (lane % 8) * 2
    part = (lane % 64) // 8
    low_half = lane < 64
    step = 0.5 * COURANT
    y_sign = jnp.where(low_half, 1.0, -1.0)
    z_sign = jnp.where(k < 8, 1.0, -1.0)
    y_weight = (jnp.where(lane < 16, step, 0.0), jnp.where(lane >= 112, -step, 0.0))
    z_weight = jnp.where(k == 0, step, jnp.where(k == 15, -step, 0.0))

    def load(plane, h):
        where = span(plane, h)
        q = [cells[f, :, where] for f in range(FIELDS)]
        pressure = prim[1, :, where]
        return q, (prim[0, :, where], pressure, prim[2, :, where], q[4] + pressure)

    def edge(ghost, ghost_terms, q, terms, sign):
        signal = jnp.maximum(ghost_terms[1], terms[1]) * sign
        return [
            (ghost_terms[0][f] + terms[0][f]) - signal * (q[f] - ghost[f]) for f in range(FIELDS)
        ]

    for plane, side, sign in ((0, 0, 1.0), (15, 64, -1.0)):
        flux = []
        for h in range(2):
            spread = (h * 4 + quarter) * 8 + half_k + side
            ghost = [pick(rim[3 * f], spread) for f in range(FIELDS)]
            q, q_prim = load(plane, h)
            flux.append(edge(ghost, along(ghost, prims(ghost), 0), q, along(q, q_prim, 0), sign))
            for f in range(FIELDS):
                where = span(plane, h)
                out[f, :, where] = out[f, :, where] + (sign * step) * flux[h][f]
        mine = jnp.logical_and(filled, low_half if side == 0 else lane >= 64)
        for f in range(FIELDS):
            found = []
            for h in range(2):
                v = flux[h][f]
                v = v + roll(v, -1)
                v = v + roll(v, -16)
                found.append(pick(v, squeeze))
            both = jnp.where((lane % 64) < 32, found[0], found[1])
            reg[7 * f] = reg[7 * f] + jnp.where(mine, both, 0.0)

    def pair(big, _):
        y_lanes = big * 8 + half_k + jnp.where(low_half, 0, 64)
        y_ghost = [pick(rim[3 * f + 1], y_lanes) for f in range(FIELDS)]
        y_ghost_terms = along(y_ghost, prims(y_ghost), 1)
        z_ghost = []
        z_ghost_terms = []
        for h in range(2):
            z_lanes = big * 8 + h * 4 + quarter + jnp.where(k >= 8, 64, 0)
            ghost = [pick(rim[3 * f + 2], z_lanes) for f in range(FIELDS)]
            z_ghost.append(ghost)
            z_ghost_terms.append(along(ghost, prims(ghost), 2))
        y_sum = [None] * FIELDS
        z_sum = [[None] * FIELDS for _ in range(2)]
        new_sum = [[None] * FIELDS for _ in range(2)]

        def accumulate(total, v):
            return v if total is None else total + v

        for sub in range(2):
            plane = 2 * big + sub
            q, q_prim = zip(*[load(plane, h) for h in range(2)])
            near = [jnp.where(low_half, q[0][f], q[1][f]) for f in range(FIELDS)]
            near_prim = [jnp.where(low_half, q_prim[0][i], q_prim[1][i]) for i in range(4)]
            y = edge(y_ghost, y_ghost_terms, near, along(near, near_prim, 1), y_sign)
            for f in range(FIELDS):
                y_sum[f] = accumulate(y_sum[f], y[f])
            for h in range(2):
                z = edge(z_ghost[h], z_ghost_terms[h], q[h], along(q[h], q_prim[h], 2), z_sign)
                for f in range(FIELDS):
                    z_sum[h][f] = accumulate(z_sum[h][f], z[f])
                    where = span(plane, h)
                    new = out[f, :, where] + y_weight[h] * y[f] + z_weight * z[f]
                    if second:
                        new_sum[h][f] = accumulate(new_sum[h][f], new)
                        new = jnp.where(filled, new, old[f, :, where])
                    out[f, :, where] = new

        mine = jnp.logical_and(filled, part == big)
        y_from = (lane % 8) * 2 + jnp.where(low_half, 0, 112)
        z_from = (lane % 4) * 32 + jnp.where(low_half, 0, 15)
        for f in range(FIELDS):
            v = y_sum[f] + roll(y_sum[f], -1)
            reg[7 * f + 1] = reg[7 * f + 1] + jnp.where(mine, pick(v, y_from), 0.0)
            found = []
            for h in range(2):
                v = z_sum[h][f] + roll(z_sum[h][f], -16)
                found.append(pick(v, z_from))
            v = jnp.where(lane % 8 < 4, found[0], found[1])
            reg[7 * f + 2] = reg[7 * f + 2] + jnp.where(mine, v, 0.0)
            if second:
                found = []
                for h in range(2):
                    v = new_sum[h][f]
                    v = v + roll(v, -1)
                    v = v + roll(v, -16)
                    found.append(pick(v, squeeze))
                v = jnp.where((lane % 64) < 32, found[0], found[1])
                v = jnp.where(filled, v, 0.0)
                where = 7 * f + 3 + big // 2
                reg[where] = jnp.where(lane // 64 == big % 2, v, reg[where])
        return 0

    lax.fori_loop(0, 8, pair, 0, unroll=OUTER_UNROLL)


def coarse_step(block, y_rim, z_rim, new, x_face, y_low, y_high, z_low, z_high):
    lane = iota((16, 128), 1)
    row = iota((16, 128), 0)
    tip = iota((8, 128), 0)

    def load(plane):
        return [block[f, plane] for f in range(FIELDS)]

    def widen(x, _):
        column = (x % 8) * 16 + row
        for f in range(FIELDS):
            below = jnp.broadcast_to(z_rim[0, x // 8, f : f + 1, :], (16, 128))
            above = jnp.broadcast_to(z_rim[1, x // 8, f : f + 1, :], (16, 128))
            side = jnp.where(lane == 64, pick(above, column), pick(below, column))
            block[f, x + 1] = jnp.where(lane < 64, block[f, x + 1], side)
        return 0

    lax.fori_loop(0, 16, widen, 0, unroll=4)

    ghost = load(0)
    here = load(1)
    here_prim = prims(here)
    low = face(ghost, along(ghost, prims(ghost), 0), here, along(here, here_prim, 0))
    for f in range(FIELDS):
        x_face[f, 0] = low[f]

    def one(x, carried):
        here, here_prim, x_low = carried
        after = load(x + 2)
        after_prim = prims(after)
        x_high = face(here, along(here, here_prim, 0), after, along(after, after_prim, 0))

        tips = []
        for f in range(FIELDS):
            above = y_rim[1, f, pl.ds(x, 1), :]
            below = y_rim[0, f, pl.ds(x, 1), :]
            tips.append(
                jnp.where(
                    tip == 0,
                    jnp.broadcast_to(above, (8, 128)),
                    jnp.broadcast_to(below, (8, 128)),
                )
            )
        tip_terms = along(tips, prims(tips), 1)
        terms = along(here, here_prim, 1)

        def tall(low, high):
            return jnp.concatenate([low, high], axis=0)

        cells = [tall(here[f], tips[f]) for f in range(FIELDS)]
        terms = ([tall(terms[0][f], tip_terms[0][f]) for f in range(FIELDS)], tall(terms[1], tip_terms[1]))
        shifted = moved(cells, terms, lambda v: pltpu.roll(v, 1, 0))
        y = face(shifted[0], (shifted[1], shifted[2]), cells, terms)

        terms = along(here, here_prim, 2)
        shifted = moved(here, terms, lambda v: pltpu.roll(v, 1, 1))
        z = face(shifted[0], (shifted[1], shifted[2]), here, terms)
        for f in range(FIELDS):
            up = pltpu.roll(y[f], 23, 0)[:16]
            down = y[f][:16]
            right = pltpu.roll(z[f], 127, 1)
            x_face[f, x + 1] = x_high[f]
            y_low[f, x] = down
            y_high[f, x] = up
            z_low[f, x] = z[f]
            z_high[f, x] = right
            change = (x_high[f] - x_low[f]) + (up - down) + (right - z[f])
            new[f, x] = here[f] - (0.5 * COURANT) * change
        return after, after_prim, x_high

    lax.fori_loop(0, 16, one, (here, here_prim, low), unroll=COARSE_UNROLL)


def cut_rims(source, corner, put):
    cx, cy, cz = corner
    lane = iota((8, 128), 1)
    row = iota((8, 128), 0)
    low_half = lane < 64
    part = (lane % 64) // 8
    along_z = cz + lane % 8
    ends = jnp.where(low_half, cz - 1, cz + 8)
    rows_x = row == part
    rows_z = row == lane % 8
    for f in range(FIELDS):
        low = pick(source(f, cx - 1, cy, 8), along_z)
        high = pick(source(f, cx + 8, cy, 8), along_z)
        v = jnp.where(rows_x, jnp.where(low_half, low, high), 0.0)
        put(f, 0, jnp.sum(v, axis=0, keepdims=True))
        low = jnp.zeros((8, 128), F32)
        high = jnp.zeros((8, 128), F32)
        total = jnp.zeros((8, 128), F32)
        for big in range(8):
            here = row == big
            low = jnp.where(here, jnp.broadcast_to(source(f, cx + big, cy - 1, 1), (8, 128)), low)
            high = jnp.where(here, jnp.broadcast_to(source(f, cx + big, cy + 8, 1), (8, 128)), high)
            total = jnp.where(part == big, pick(source(f, cx + big, cy, 8), ends), total)
        v = jnp.where(low_half, pick(low, along_z), pick(high, along_z))
        put(f, 1, jnp.sum(jnp.where(rows_x, v, 0.0), axis=0, keepdims=True))
        put(f, 2, jnp.sum(jnp.where(rows_z, total, 0.0), axis=0, keepdims=True))


def plan_settle(corners, new, x_face, y_low, y_high, z_low, z_high, weight, index):
    lane = iota((16, 128), 1)
    row = iota((16, 128), 0)

    def one(x, _):
        kind = jnp.zeros((16, 128), I32)
        for c in range(REGIONS):
            cx, cy, cz = corners[c]
            step = x - cx
            inside = jnp.logical_and(step >= 0, step < 8)
            dy = row - cy
            dz = lane - cz
            in_y = jnp.logical_and(dy >= 0, dy < 8)
            in_z = jnp.logical_and(dz >= 0, dz < 8)
            near = jnp.where(dy == -1, 4, jnp.where(dy == 8, 5, 0))
            side = jnp.where(dz == -1, 6, jnp.where(dz == 8, 7, 0))
            plain = jnp.where(inside, 1, jnp.where(step == -1, 2, jnp.where(step == 8, 3, 0)))
            mine = jnp.where(
                jnp.logical_and(in_y, in_z),
                plain,
                jnp.where(inside, jnp.where(in_z, near, jnp.where(in_y, side, 0)), 0),
            )
            ys = jnp.clip(dy, 0, 7)
            zs = jnp.clip(dz, 0, 7)
            lanes = jnp.where(mine < 4, ys * 8 + zs, 32 + 8 * mine + jnp.where(mine < 6, zs, ys))
            used = mine > 0
            kind = jnp.where(used, mine, kind)
            index[x, c] = jnp.where(used, lanes + 128, 0)
        factor = jnp.where(kind < 2, 0.0, jnp.where(kind % 2 == 0, -COURANT, COURANT))
        weight[x] = jnp.where(kind == 1, 0.125, 0.0625 * factor)
        for f in range(FIELDS):
            flux = jnp.where(
                kind < 4,
                jnp.where(kind == 2, x_face[f, x + 1], x_face[f, x]),
                jnp.where(
                    kind < 6,
                    jnp.where(kind == 4, y_high[f, x], y_low[f, x]),
                    jnp.where(kind == 6, z_high[f, x], z_low[f, x]),
                ),
            )
            plain = new[f, x]
            ring = jnp.where(kind >= 2, plain - 0.5 * factor * flux, plain)
            new[f, x] = jnp.where(kind == 1, 0.0, ring)
        return 0

    lax.fori_loop(0, 16, one, 0)


def settle_rows(answers, rows):
    lane = iota((REGIONS, 128), 1)
    spot = ((lane % 16) // 8) * 64 + lane % 8
    for f in range(FIELDS):
        ends = answers[7 * f]
        rows[f, 0] = ends
        rows[f, 9] = pltpu.roll(ends, 64, 1)
        y_face = answers[7 * f + 1]
        z_face = answers[7 * f + 2]
        for big in range(8):
            cells = answers[7 * f + 3 + big // 2]
            if big % 2:
                cells = pltpu.roll(cells, 64, 1)
            around = jnp.where(
                lane < 80, pick(y_face, spot + 8 * big), pick(z_face, spot + 8 * big)
            )
            rows[f, 1 + big] = jnp.where(lane < 64, cells, around)


def settle(corners, rows, new, weight, index, out, start):
    def one(step, _):
        x = start + step
        values = [jnp.zeros((16, 128), F32) for _ in range(FIELDS)]
        for c in range(REGIONS):
            which = jnp.clip(x - corners[c][0] + 1, 0, 9)
            lanes = index[x, c]
            used = lanes >= 128
            lanes = lanes & 127
            for f in range(FIELDS):
                line = jnp.broadcast_to(rows[f, which, c : c + 1, :], (16, 128))
                values[f] = jnp.where(used, pick(line, lanes), values[f])
        for f in range(FIELDS):
            v = new[f, x] + weight[x] * values[f]
            out[f, x] = v[:, :64]
        return 0

    lax.fori_loop(0, 8, one, 0, unroll=SETTLE_UNROLL)


def whole(
    sizes,
    parent_hbm,
    plane_hbm,
    corner_hbm,
    coarse_hbm,
    fine_hbm,
    coarse_out,
    fine_out,
    parent_ref,
    corner_ref,
    plane_ref,
    coarse_ref,
    block,
    new,
    x_face,
    y_low,
    y_high,
    z_low,
    z_high,
    weight,
    index,
    y_stage,
    z_stage,
    x_rim,
    y_rim,
    z_rim,
    cut,
    rim_out,
    rim_in_old,
    rim_in_mid,
    rim,
    fine_ref,
    prim,
    half,
    fine_new,
    coarse_new,
    reg,
    route,
    relay_in,
    relay_out,
    row_stage,
    direct_out,
    direct_in,
    answer_in,
    answers,
    answer_rows,
    table,
    load_sems,
    halo_send,
    halo_recv,
    many_send,
    many_recv,
):
    n_gx, n_gy, n_gz = sizes
    members = n_gy * n_gz
    relayed = min(members, 7 * FIELDS)
    direct = 7 * FIELDS - relayed
    rim_in = (rim_in_old, rim_in_mid)
    gx = lax.axis_index("gx")
    gy = lax.axis_index("gy")
    gz = lax.axis_index("gz")
    within = gy * n_gz + gz
    myself = gx * members + within
    start = gx * (members * BOXMAX)

    def peer(distance):
        other = lax.rem(within + distance, members)
        return other, (gx, other // n_gz, lax.rem(other, n_gz))

    barrier = pltpu.get_barrier_semaphore()

    def greet(distance, _):
        pl.semaphore_signal(barrier, inc=1, device_id=peer(distance)[1], device_id_type=MESH)
        return 0

    x_next = (lax.rem(gx + 1, n_gx), gy, gz)
    x_prev = (lax.rem(gx + n_gx - 1, n_gx), gy, gz)
    y_next = (gx, lax.rem(gy + 1, n_gy), gz)
    y_prev = (gx, lax.rem(gy + n_gy - 1, n_gy), gz)
    z_next = (gx, gy, lax.rem(gz + 1, n_gz))
    z_prev = (gx, gy, lax.rem(gz + n_gz - 1, n_gz))
    pl.semaphore_signal(barrier, inc=1, device_id=x_next, device_id_type=MESH)
    pl.semaphore_signal(barrier, inc=1, device_id=x_prev, device_id_type=MESH)
    lax.fori_loop(1, members, greet, 0)

    def fetch(src, dst, index):
        copy = pltpu.make_async_copy(src, dst, load_sems.at[index])
        copy.start()
        return copy

    coarse_load = fetch(coarse_hbm, coarse_ref, 0)
    parent_load = fetch(parent_hbm, parent_ref, 1)
    corner_load = fetch(corner_hbm, corner_ref, 2)
    plane_load = fetch(plane_hbm, plane_ref, 3)
    fine_load = fetch(fine_hbm, fine_ref, 4)

    lane16 = iota((16, 128), 1)
    row16 = iota((16, 128), 0)
    coarse_load.wait()
    for f in range(FIELDS):
        block[f, 1:17, :, 0:64] = coarse_ref[f]
    for f in range(FIELDS):
        y_stage[0, f] = block[f, 1:17, 0, :]
        y_stage[1, f] = block[f, 1:17, 15, :]
        for h in range(2):
            low = jnp.zeros((16, 128), F32)
            high = jnp.zeros((16, 128), F32)
            for x in range(8):
                plane = block[f, 1 + 8 * h + x]
                here = lane16 // 16 == x
                low = jnp.where(here, jnp.broadcast_to(plane[:, 0:1], (16, 128)), low)
                high = jnp.where(here, jnp.broadcast_to(plane[:, 63:64], (16, 128)), high)
            match = row16 == lane16 % 16
            z_stage[0, h, f : f + 1, :] = jnp.sum(
                jnp.where(match, low, 0.0), axis=0, keepdims=True
            )
            z_stage[1, h, f : f + 1, :] = jnp.sum(
                jnp.where(match, high, 0.0), axis=0, keepdims=True
            )

    pl.semaphore_wait(barrier, members + 1)

    def halo(src, dst, index, device):
        copy = pltpu.make_async_remote_copy(
            src_ref=src,
            dst_ref=dst,
            send_sem=halo_send.at[index],
            recv_sem=halo_recv.at[index],
            device_id=device,
            device_id_type=MESH,
        )
        copy.start()
        return copy

    halos = [
        halo(block.at[:, 16], x_rim.at[0], 0, x_next),
        halo(block.at[:, 1], x_rim.at[1], 1, x_prev),
        halo(y_stage.at[1], y_rim.at[0], 2, y_next),
        halo(y_stage.at[0], y_rim.at[1], 3, y_prev),
        halo(z_stage.at[1], z_rim.at[0], 4, z_next),
        halo(z_stage.at[0], z_rim.at[1], 5, z_prev),
    ]

    parent_load.wait()
    corner_load.wait()

    def scan(entry, found):
        c0, c1, c2, c3 = found
        hit = parent_ref[start + entry] == myself
        return (
            jnp.where(hit, c1, c0),
            jnp.where(hit, c2, c1),
            jnp.where(hit, c3, c2),
            jnp.where(hit, entry, c3),
        )

    zero = jnp.int32(0)
    children = lax.fori_loop(0, members * BOXMAX, scan, (zero, zero, zero, zero), unroll=8)
    for c in range(REGIONS):
        for k in range(3):
            table[4 * c + k] = jnp.clip(corner_ref[k, start + children[c]], 1, 55 if k == 2 else 7)
    child_peer = [child // BOXMAX for child in children]
    own = [parent_ref[start + within * BOXMAX + s] for s in range(BOXMAX)]
    own_peer = [lax.rem(jnp.maximum(own[s], 0), members) for s in range(BOXMAX)]

    def look_up(distance, _):
        other = lax.rem(within + distance, members)
        rank = zero
        for c in range(1, REGIONS):
            rank = jnp.where(child_peer[c] == other, c, rank)
        found = zero
        for s in range(BOXMAX):
            found = jnp.where(jnp.logical_and(own[s] >= 0, own_peer[s] == other), s, found)
        table[32 + distance] = rank
        table[32 + members + distance] = found
        return 0

    lax.fori_loop(0, members, look_up, 0)

    def cut_all(when, source):
        def one(c, _):
            corner = (table[4 * c], table[4 * c + 1], table[4 * c + 2])

            def put(f, v, line):
                cut[when, c, 3 * f + v : 3 * f + v + 1, :] = line

            cut_rims(source, corner, put)
            return 0

        lax.fori_loop(0, REGIONS, one, 0, unroll=CUT_UNROLL)

    def ship(src, dst, index, device):
        pltpu.make_async_remote_copy(
            src_ref=src,
            dst_ref=dst,
            send_sem=many_send.at[index],
            recv_sem=many_recv.at[index],
            device_id=device,
            device_id_type=MESH,
        ).start()

    def slot_of(other):
        return lax.rem(within - other + 2 * members - 1, members)

    def wait_many(every, index, semaphores):
        pltpu.make_async_copy(every, every, semaphores.at[index]).wait()

    others = pl.ds(0, members - 1)

    def send_rims(when):
        def one(distance, _):
            rim_out[when, distance - 1] = cut[when, table[32 + distance]]
            ship(
                rim_out.at[when, distance - 1],
                rim_in[when].at[distance - 1],
                when,
                peer(distance)[1],
            )
            return 0

        lax.fori_loop(1, members, one, 0)
        rim_in[when][members - 1] = cut[when, table[32]]

    cut_all(0, lambda f, x, y, n: block[f, x + 1, pl.ds(y, n), :])
    send_rims(0)

    for v in range(7 * FIELDS):
        reg[v] = jnp.zeros((BOXMAX, 128), F32)

    for copy in halos:
        copy.wait()
    for f in range(FIELDS):
        block[f, 0] = x_rim[0, f]
        block[f, 17] = x_rim[1, f]
    coarse_step(block, y_rim, z_rim, new, x_face, y_low, y_high, z_low, z_high)
    cut_all(
        1,
        lambda f, x, y, n: 0.5 * (block[f, x + 1, pl.ds(y, n), :] + new[f, x, pl.ds(y, n), :]),
    )
    send_rims(1)

    plane_load.wait()
    n_rows = REGIONS * members
    columns = members * BOXMAX
    row = iota((n_rows, columns), 0)
    column = iota((n_rows, columns), 1)
    slots = plane_ref[pl.ds(gx * (columns // 128), columns // 128), :] if columns >= 128 else None
    if columns >= 128:
        slots = jnp.concatenate(
            [
                jnp.broadcast_to(slots[h : h + 1, :], (n_rows, 128))
                for h in range(columns // 128)
            ],
            axis=1,
        )
    else:
        slots = jnp.broadcast_to(plane_ref[0:1, 0:columns], (n_rows, columns))
    number = column.astype(F32)
    far = 65536.0
    candidate = jnp.where(slots == row // REGIONS + gx * members, number, far)
    chosen = jnp.full((n_rows, 1), far)
    for r in range(REGIONS):
        least = jnp.min(candidate, axis=1, keepdims=True)
        chosen = jnp.where(row[:, 0:1] % REGIONS == r, least, chosen)
        candidate = jnp.where(candidate == least, far, candidate)
    arrival = lax.rem(within - column // BOXMAX - 1 + members, members) * BOXMAX + column % BOXMAX
    route[...] = jnp.where(arrival.astype(F32) == chosen, 1.0, 0.0)

    fine_load.wait()
    fine_prims(fine_ref, prim)
    fine_inner(fine_ref, prim, half)

    sub = iota((BOXMAX, 128), 0)
    owner = jnp.zeros((BOXMAX, 128), I32)
    for s in range(BOXMAX):
        owner = jnp.where(sub == s, own[s], owner)
    filled = owner >= 0

    def take_rims(when):
        wait_many(rim_in[when].at[others], when, many_recv)
        for s in range(BOXMAX):
            rows = rim_in[when][slot_of(own_peer[s])]
            for v in range(3 * FIELDS):
                rim[v, s : s + 1, :] = rows[v : v + 1, :]

    take_rims(0)
    fine_outer(fine_ref, prim, rim, reg, filled, half, None)
    fine_prims(half, prim)
    fine_inner(half, prim, fine_new)
    take_rims(1)
    fine_outer(half, prim, rim, reg, filled, fine_new, fine_ref)

    def relay(tile):
        @pl.when(jnp.logical_and(tile != within, tile < relayed))
        def _():
            distance = lax.rem(tile - within + members, members)
            device = (gx, tile // n_gz, lax.rem(tile, n_gz))
            ship(reg.at[tile], relay_in.at[distance - 1], 2, device)

    for tile in range(relayed):
        relay(tile)
    relay_in[members - 1] = reg[within]

    fine_store = fetch(fine_new, fine_out, 5)
    if direct:
        for s in range(BOXMAX):
            row_stage[s] = reg[relayed:, s, :]

        def direct_one(distance, _):
            direct_out[distance - 1] = row_stage[table[32 + members + distance]]
            ship(direct_out.at[distance - 1], direct_in.at[distance - 1], 3, peer(distance)[1])
            return 0

        lax.fori_loop(1, members, direct_one, 0)
        direct_in[members - 1] = row_stage[table[32 + members]]

    wait_many(relay_in.at[others], 2, many_recv)
    sorted_rows = jnp.dot(
        route[...],
        relay_in[...].reshape(columns, 128),
        precision=lax.Precision.HIGHEST,
        preferred_element_type=F32,
    )
    for p in range(members):
        relay_out[p] = sorted_rows[REGIONS * p : REGIONS * p + REGIONS]

    def answer_one(distance, _):
        other, device = peer(distance)
        ship(relay_out.at[other], answer_in.at[distance - 1], 4, device)
        return 0

    lax.fori_loop(1, members, answer_one, 0)
    answer_in[members - 1] = relay_out[within]

    corners = [(table[4 * c], table[4 * c + 1], table[4 * c + 2]) for c in range(REGIONS)]
    plan_settle(corners, new, x_face, y_low, y_high, z_low, z_high, weight, index)

    if direct:
        wait_many(direct_in.at[others], 3, many_recv)
        for c in range(REGIONS):
            rows = direct_in[slot_of(child_peer[c])]
            for v in range(direct):
                answers[relayed + v, c : c + 1, :] = rows[v : v + 1, :]
    wait_many(answer_in.at[others], 4, many_recv)
    for v in range(relayed):
        answers[v] = answer_in[lax.rem(within - v + 2 * members - 1, members)]
    settle_rows(answers, answer_rows)
    coarse_stores = []
    for part in range(2):
        settle(corners, answer_rows, new, weight, index, coarse_new, 8 * part)
        planes = pl.ds(8 * part, 8)
        coarse_stores.append(fetch(coarse_new.at[:, planes], coarse_out.at[:, planes], 6 + part))
    wait_many(rim_out.at[0, others], 0, many_send)
    wait_many(rim_out.at[1, others], 1, many_send)
    wait_many(relay_in.at[others], 2, many_send)
    if direct:
        wait_many(direct_out.at[others], 3, many_send)
    wait_many(relay_out.at[others], 4, many_send)
    fine_store.wait()
    for copy in coarse_stores:
        copy.wait()


def hand_over(coarse_in, fine_in, coarse_out, fine_out, sems):
    copies = [
        pltpu.make_async_copy(coarse_in, coarse_out, sems.at[0]),
        pltpu.make_async_copy(fine_in, fine_out, sems.at[1]),
    ]
    for copy in copies:
        copy.start()
    for copy in copies:
        copy.wait()


def on_device(sizes, coarse_state, fine_state, slot_parent, slot_corner):
    members = sizes[1] * sizes[2]
    relayed = min(members, 7 * FIELDS)
    hbm = pl.BlockSpec(memory_space=pltpu.HBM)
    fine = jnp.transpose(fine_state, (1, 0, 2))
    corner = jnp.transpose(slot_corner, (1, 0))
    plane = slot_parent.reshape(-1, min(128, slot_parent.shape[0]))
    field_block = (FIELDS, 16, 16, 128)
    rows = 7 * FIELDS
    direct = max(rows - relayed, 1)
    coarse_next, fine_next = pl.pallas_call(
        functools.partial(whole, sizes),
        out_shape=(
            jax.ShapeDtypeStruct(coarse_state.shape, F32),
            jax.ShapeDtypeStruct(fine.shape, F32),
        ),
        in_specs=[hbm] * 5,
        out_specs=(hbm, hbm),
        scratch_shapes=[
            pltpu.SMEM(slot_parent.shape, I32),
            pltpu.SMEM(corner.shape, I32),
            pltpu.VMEM(plane.shape, I32),
            pltpu.VMEM(coarse_state.shape, F32),
            pltpu.VMEM((FIELDS, 18, 16, 128), F32),
            pltpu.VMEM(field_block, F32),
            pltpu.VMEM((FIELDS, 17, 16, 128), F32),
            pltpu.VMEM(field_block, F32),
            pltpu.VMEM(field_block, F32),
            pltpu.VMEM(field_block, F32),
            pltpu.VMEM(field_block, F32),
            pltpu.VMEM((16, 16, 128), F32),
            pltpu.VMEM((16, REGIONS, 16, 128), I32),
            pltpu.VMEM((2, FIELDS, 16, 128), F32),
            pltpu.VMEM((2, 2, FIELDS, 128), F32),
            pltpu.VMEM((2, FIELDS, 16, 128), F32),
            pltpu.VMEM((2, FIELDS, 16, 128), F32),
            pltpu.VMEM((2, 2, FIELDS, 128), F32),
            pltpu.VMEM((2, REGIONS, 3 * FIELDS, 128), F32),
            pltpu.VMEM((2, members, 3 * FIELDS, 128), F32),
            pltpu.VMEM((members, 3 * FIELDS, 128), F32),
            pltpu.VMEM((members, 3 * FIELDS, 128), F32),
            pltpu.VMEM((3 * FIELDS, BOXMAX, 128), F32),
            pltpu.VMEM(fine.shape, F32),
            pltpu.VMEM((3,) + fine.shape[1:], F32),
            pltpu.VMEM(fine.shape, F32),
            pltpu.VMEM(fine.shape, F32),
            pltpu.VMEM(coarse_state.shape, F32),
            pltpu.VMEM((rows, BOXMAX, 128), F32),
            pltpu.VMEM((REGIONS * members, BOXMAX * members), F32),
            pltpu.VMEM((members, BOXMAX, 128), F32),
            pltpu.VMEM((members, REGIONS, 128), F32),
            pltpu.VMEM((BOXMAX, direct, 128), F32),
            pltpu.VMEM((members, direct, 128), F32),
            pltpu.VMEM((members, direct, 128), F32),
            pltpu.VMEM((members, REGIONS, 128), F32),
            pltpu.VMEM((rows, REGIONS, 128), F32),
            pltpu.VMEM((FIELDS, 10, REGIONS, 128), F32),
            pltpu.SMEM((32 + 2 * members,), I32),
            pltpu.SemaphoreType.DMA((8,)),
            pltpu.SemaphoreType.DMA((6,)),
            pltpu.SemaphoreType.DMA((6,)),
            pltpu.SemaphoreType.DMA((5,)),
            pltpu.SemaphoreType.DMA((5,)),
        ],
        compiler_params=pltpu.CompilerParams(
            collective_id=0, has_side_effects=True, vmem_limit_bytes=62 * 1024 * 1024
        ),
    )(slot_parent, plane, corner, coarse_state, fine)
    coarse_next, fine_next = pl.pallas_call(
        hand_over,
        out_shape=(
            jax.ShapeDtypeStruct(coarse_state.shape, F32),
            jax.ShapeDtypeStruct(fine.shape, F32),
        ),
        in_specs=[hbm] * 2,
        out_specs=(hbm, hbm),
        scratch_shapes=[pltpu.SemaphoreType.DMA((2,))],
    )(coarse_next, fine_next)
    return coarse_next, jnp.transpose(fine_next, (1, 0, 2))


def solution(mesh):
    sizes = tuple(mesh.shape[name] for name in ("gx", "gy", "gz"))
    return jax.shard_map(
        functools.partial(on_device, sizes),
        mesh=mesh,
        in_specs=(P(None, "gx", "gy", "gz"), P(("gx", "gy", "gz"), None, None), P(), P()),
        out_specs=(P(None, "gx", "gy", "gz"), P(("gx", "gy", "gz"), None, None)),
        check_vma=False,
    )
```

```python
import functools

import jax
import jax.numpy as jnp
from jax import lax
from jax.experimental import pallas as pl
from jax.experimental.pallas import tpu as pltpu
from jax.sharding import PartitionSpec as P

GAMMA = 1.4
COURANT = 0.04
PRIM_UNROLL = 2
X_UNROLL = 5
YZ_UNROLL = 4
OUTER_UNROLL = 4
COARSE_UNROLL = 4
CUT_UNROLL = 4
SETTLE_UNROLL = 4
FIELDS = 5
REGIONS = 4
BOXMAX = 8
MESH = pl.DeviceIdType.MESH
F32 = jnp.float32
I32 = jnp.int32


def iota(shape, dim):
    return lax.broadcasted_iota(I32, shape, dim)


def pick(values, lanes):
    numbers = lax.GatherDimensionNumbers(
        offset_dims=(),
        collapsed_slice_dims=(1,),
        start_index_map=(1,),
        operand_batching_dims=(0,),
        start_indices_batching_dims=(0,),
    )
    return lax.gather(
        values,
        lanes[..., None],
        numbers,
        (1, 1),
        mode=lax.GatherScatterMode.PROMISE_IN_BOUNDS,
    )


def prims(q):
    inverse = pl.reciprocal(q[0], approx=True)
    inverse = inverse * (2.0 - q[0] * inverse)
    kinetic = 0.5 * (q[1] * q[1] + q[2] * q[2] + q[3] * q[3]) * inverse
    pressure = (GAMMA - 1.0) * (q[4] - kinetic)
    square = GAMMA * pressure * inverse
    sound = square * lax.rsqrt(jnp.maximum(square, 1e-30))
    return inverse, pressure, sound, q[4] + pressure


def along(q, prim, axis):
    inverse, pressure, sound, total = prim
    velocity = q[1 + axis] * inverse
    flux = [q[1 + axis], q[1] * velocity, q[2] * velocity, q[3] * velocity, total * velocity]
    flux[1 + axis] = flux[1 + axis] + pressure
    return flux, jnp.abs(velocity) + sound


def face(low, low_terms, high, high_terms):
    signal = jnp.maximum(low_terms[1], high_terms[1])
    return [
        (low_terms[0][f] + high_terms[0][f]) - signal * (high[f] - low[f]) for f in range(FIELDS)
    ]


def moved(q, terms, move):
    return [move(v) for v in q], [move(v) for v in terms[0]], move(terms[1])


def span(plane, h):
    return pl.ds(pl.multiple_of(plane * 256 + h * 128, 128), 128)


def roll(v, by):
    return pltpu.roll(v, by % 128, 1)


def fine_prims(cells, prim):
    def one(plane, _):
        for h in range(2):
            where = span(plane, h)
            inverse, pressure, sound, _ = prims([cells[f, :, where] for f in range(FIELDS)])
            prim[0, :, where] = inverse
            prim[1, :, where] = pressure
            prim[2, :, where] = sound
        return 0

    lax.fori_loop(0, 16, one, 0, unroll=PRIM_UNROLL)


def fine_inner(cells, prim, out):
    lane = iota((BOXMAX, 128), 1)
    first_row = lane < 16
    last_row = lane >= 112
    k_first = lane % 16 == 0

    def load(plane, h):
        where = span(plane, h)
        q = [cells[f, :, where] for f in range(FIELDS)]
        pressure = prim[1, :, where]
        return q, (prim[0, :, where], pressure, prim[2, :, where], q[4] + pressure)

    def x_one(plane, low):
        high = []
        for h in range(2):
            q, q_prim = load(plane, h)
            up, up_prim = load(plane + 1, h)
            flux = face(q, along(q, q_prim, 0), up, along(up, up_prim, 0))
            for f in range(FIELDS):
                out[f, :, span(plane, h)] = q[f] - (0.5 * COURANT) * (flux[f] - low[h][f])
            high.append(flux)
        return high

    none = [[jnp.zeros((BOXMAX, 128), F32)] * FIELDS] * 2
    high = lax.fori_loop(0, 15, x_one, none, unroll=X_UNROLL)
    for h in range(2):
        for f in range(FIELDS):
            out[f, :, span(15, h)] = cells[f, :, span(15, h)] + (0.5 * COURANT) * high[h][f]

    def yz_one(plane, _):
        for h in range(2):
            q, q_prim = load(plane, h)
            terms = along(q, q_prim, 2)
            shifted = moved(q, terms, lambda v: roll(v, 1))
            z = face(shifted[0], (shifted[1], shifted[2]), q, terms)
            for f in range(FIELDS):
                low = jnp.where(k_first, 0.0, z[f])
                where = span(plane, h)
                out[f, :, where] = out[f, :, where] - (0.5 * COURANT) * (roll(low, -1) - low)
        q0, prim0 = load(plane, 0)
        q1, prim1 = load(plane, 1)
        terms0 = along(q0, prim0, 1)
        terms1 = along(q1, prim1, 1)
        shifted0 = moved(q0, terms0, lambda v: roll(v, 16))
        shifted1 = moved(q1, terms1, lambda v: roll(v, 16))

        def seam(low, high):
            return jnp.where(first_row, low, high)

        low1 = (
            [seam(shifted0[0][f], shifted1[0][f]) for f in range(FIELDS)],
            ([seam(shifted0[1][f], shifted1[1][f]) for f in range(FIELDS)], seam(shifted0[2], shifted1[2])),
        )
        y0 = face(shifted0[0], (shifted0[1], shifted0[2]), q0, terms0)
        y1 = face(low1[0], low1[1], q1, terms1)
        for f in range(FIELDS):
            low = jnp.where(first_row, 0.0, y0[f])
            up0 = roll(low, -16)
            up1 = roll(y1[f], -16)
            for h, up, down in ((0, jnp.where(last_row, up1, up0), low), (1, jnp.where(last_row, up0, up1), y1[f])):
                where = span(plane, h)
                out[f, :, where] = out[f, :, where] - (0.5 * COURANT) * (up - down)
        return 0

    lax.fori_loop(0, 16, yz_one, 0, unroll=YZ_UNROLL)


def fine_outer(cells, prim, rim, reg, filled, out, old):
    second = old is not None
    lane = iota((BOXMAX, 128), 1)
    k = lane % 16
    half_k = k // 2
    quarter = lane // 32
    squeeze = ((lane % 32) // 8) * 32 + (lane % 8) * 2
    part = (lane % 64) // 8
    low_half = lane < 64
    step = 0.5 * COURANT
    y_sign = jnp.where(low_half, 1.0, -1.0)
    z_sign = jnp.where(k < 8, 1.0, -1.0)
    y_weight = (jnp.where(lane < 16, step, 0.0), jnp.where(lane >= 112, -step, 0.0))
    z_weight = jnp.where(k == 0, step, jnp.where(k == 15, -step, 0.0))

    def load(plane, h):
        where = span(plane, h)
        q = [cells[f, :, where] for f in range(FIELDS)]
        pressure = prim[1, :, where]
        return q, (prim[0, :, where], pressure, prim[2, :, where], q[4] + pressure)

    def edge(ghost, ghost_terms, q, terms, sign):
        signal = jnp.maximum(ghost_terms[1], terms[1]) * sign
        return [
            (ghost_terms[0][f] + terms[0][f]) - signal * (q[f] - ghost[f]) for f in range(FIELDS)
        ]

    for plane, side, sign in ((0, 0, 1.0), (15, 64, -1.0)):
        flux = []
        for h in range(2):
            spread = (h * 4 + quarter) * 8 + half_k + side
            ghost = [pick(rim[3 * f], spread) for f in range(FIELDS)]
            q, q_prim = load(plane, h)
            flux.append(edge(ghost, along(ghost, prims(ghost), 0), q, along(q, q_prim, 0), sign))
            for f in range(FIELDS):
                where = span(plane, h)
                out[f, :, where] = out[f, :, where] + (sign * step) * flux[h][f]
        mine = jnp.logical_and(filled, low_half if side == 0 else lane >= 64)
        for f in range(FIELDS):
            found = []
            for h in range(2):
                v = flux[h][f]
                v = v + roll(v, -1)
                v = v + roll(v, -16)
                found.append(pick(v, squeeze))
            both = jnp.where((lane % 64) < 32, found[0], found[1])
            reg[7 * f] = reg[7 * f] + jnp.where(mine, both, 0.0)

    def pair(big, _):
        y_lanes = big * 8 + half_k + jnp.where(low_half, 0, 64)
        y_ghost = [pick(rim[3 * f + 1], y_lanes) for f in range(FIELDS)]
        y_ghost_terms = along(y_ghost, prims(y_ghost), 1)
        z_ghost = []
        z_ghost_terms = []
        for h in range(2):
            z_lanes = big * 8 + h * 4 + quarter + jnp.where(k >= 8, 64, 0)
            ghost = [pick(rim[3 * f + 2], z_lanes) for f in range(FIELDS)]
            z_ghost.append(ghost)
            z_ghost_terms.append(along(ghost, prims(ghost), 2))
        y_sum = [None] * FIELDS
        z_sum = [[None] * FIELDS for _ in range(2)]
        new_sum = [[None] * FIELDS for _ in range(2)]

        def accumulate(total, v):
            return v if total is None else total + v

        for sub in range(2):
            plane = 2 * big + sub
            q, q_prim = zip(*[load(plane, h) for h in range(2)])
            near = [jnp.where(low_half, q[0][f], q[1][f]) for f in range(FIELDS)]
            near_prim = [jnp.where(low_half, q_prim[0][i], q_prim[1][i]) for i in range(4)]
            y = edge(y_ghost, y_ghost_terms, near, along(near, near_prim, 1), y_sign)
            for f in range(FIELDS):
                y_sum[f] = accumulate(y_sum[f], y[f])
            for h in range(2):
                z = edge(z_ghost[h], z_ghost_terms[h], q[h], along(q[h], q_prim[h], 2), z_sign)
                for f in range(FIELDS):
                    z_sum[h][f] = accumulate(z_sum[h][f], z[f])
                    where = span(plane, h)
                    new = out[f, :, where] + y_weight[h] * y[f] + z_weight * z[f]
                    if second:
                        new_sum[h][f] = accumulate(new_sum[h][f], new)
                        new = jnp.where(filled, new, old[f, :, where])
                    out[f, :, where] = new

        mine = jnp.logical_and(filled, part == big)
        y_from = (lane % 8) * 2 + jnp.where(low_half, 0, 112)
        z_from = (lane % 4) * 32 + jnp.where(low_half, 0, 15)
        for f in range(FIELDS):
            v = y_sum[f] + roll(y_sum[f], -1)
            reg[7 * f + 1] = reg[7 * f + 1] + jnp.where(mine, pick(v, y_from), 0.0)
            found = []
            for h in range(2):
                v = z_sum[h][f] + roll(z_sum[h][f], -16)
                found.append(pick(v, z_from))
            v = jnp.where(lane % 8 < 4, found[0], found[1])
            reg[7 * f + 2] = reg[7 * f + 2] + jnp.where(mine, v, 0.0)
            if second:
                found = []
                for h in range(2):
                    v = new_sum[h][f]
                    v = v + roll(v, -1)
                    v = v + roll(v, -16)
                    found.append(pick(v, squeeze))
                v = jnp.where((lane % 64) < 32, found[0], found[1])
                v = jnp.where(filled, v, 0.0)
                where = 7 * f + 3 + big // 2
                reg[where] = jnp.where(lane // 64 == big % 2, v, reg[where])
        return 0

    lax.fori_loop(0, 8, pair, 0, unroll=OUTER_UNROLL)


def coarse_step(block, y_rim, z_rim, new, x_face, y_low, y_high, z_low, z_high):
    lane = iota((16, 128), 1)
    row = iota((16, 128), 0)
    tip = iota((8, 128), 0)

    def load(plane):
        return [block[f, plane] for f in range(FIELDS)]

    def widen(x, _):
        column = (x % 8) * 16 + row
        for f in range(FIELDS):
            below = jnp.broadcast_to(z_rim[0, x // 8, f : f + 1, :], (16, 128))
            above = jnp.broadcast_to(z_rim[1, x // 8, f : f + 1, :], (16, 128))
            side = jnp.where(lane == 64, pick(above, column), pick(below, column))
            block[f, x + 1] = jnp.where(lane < 64, block[f, x + 1], side)
        return 0

    lax.fori_loop(0, 16, widen, 0, unroll=4)

    ghost = load(0)
    here = load(1)
    here_prim = prims(here)
    low = face(ghost, along(ghost, prims(ghost), 0), here, along(here, here_prim, 0))
    for f in range(FIELDS):
        x_face[f, 0] = low[f]

    def one(x, carried):
        here, here_prim, x_low = carried
        after = load(x + 2)
        after_prim = prims(after)
        x_high = face(here, along(here, here_prim, 0), after, along(after, after_prim, 0))

        tips = []
        for f in range(FIELDS):
            above = y_rim[1, f, pl.ds(x, 1), :]
            below = y_rim[0, f, pl.ds(x, 1), :]
            tips.append(
                jnp.where(
                    tip == 0,
                    jnp.broadcast_to(above, (8, 128)),
                    jnp.broadcast_to(below, (8, 128)),
                )
            )
        tip_terms = along(tips, prims(tips), 1)
        terms = along(here, here_prim, 1)

        def tall(low, high):
            return jnp.concatenate([low, high], axis=0)

        cells = [tall(here[f], tips[f]) for f in range(FIELDS)]
        terms = ([tall(terms[0][f], tip_terms[0][f]) for f in range(FIELDS)], tall(terms[1], tip_terms[1]))
        shifted = moved(cells, terms, lambda v: pltpu.roll(v, 1, 0))
        y = face(shifted[0], (shifted[1], shifted[2]), cells, terms)

        terms = along(here, here_prim, 2)
        shifted = moved(here, terms, lambda v: pltpu.roll(v, 1, 1))
        z = face(shifted[0], (shifted[1], shifted[2]), here, terms)
        for f in range(FIELDS):
            up = pltpu.roll(y[f], 23, 0)[:16]
            down = y[f][:16]
            right = pltpu.roll(z[f], 127, 1)
            x_face[f, x + 1] = x_high[f]
            y_low[f, x] = down
            y_high[f, x] = up
            z_low[f, x] = z[f]
            z_high[f, x] = right
            change = (x_high[f] - x_low[f]) + (up - down) + (right - z[f])
            new[f, x] = here[f] - (0.5 * COURANT) * change
        return after, after_prim, x_high

    lax.fori_loop(0, 16, one, (here, here_prim, low), unroll=COARSE_UNROLL)


def cut_rims(source, corner, put):
    cx, cy, cz = corner
    lane = iota((8, 128), 1)
    row = iota((8, 128), 0)
    low_half = lane < 64
    part = (lane % 64) // 8
    along_z = cz + lane % 8
    ends = jnp.where(low_half, cz - 1, cz + 8)
    rows_x = row == part
    rows_z = row == lane % 8
    for f in range(FIELDS):
        low = pick(source(f, cx - 1, cy, 8), along_z)
        high = pick(source(f, cx + 8, cy, 8), along_z)
        v = jnp.where(rows_x, jnp.where(low_half, low, high), 0.0)
        put(f, 0, jnp.sum(v, axis=0, keepdims=True))
        low = jnp.zeros((8, 128), F32)
        high = jnp.zeros((8, 128), F32)
        total = jnp.zeros((8, 128), F32)
        for big in range(8):
            here = row == big
            low = jnp.where(here, jnp.broadcast_to(source(f, cx + big, cy - 1, 1), (8, 128)), low)
            high = jnp.where(here, jnp.broadcast_to(source(f, cx + big, cy + 8, 1), (8, 128)), high)
            total = jnp.where(part == big, pick(source(f, cx + big, cy, 8), ends), total)
        v = jnp.where(low_half, pick(low, along_z), pick(high, along_z))
        put(f, 1, jnp.sum(jnp.where(rows_x, v, 0.0), axis=0, keepdims=True))
        put(f, 2, jnp.sum(jnp.where(rows_z, total, 0.0), axis=0, keepdims=True))


def plan_settle(corners, new, x_face, y_low, y_high, z_low, z_high, weight, index):
    lane = iota((16, 128), 1)
    row = iota((16, 128), 0)

    def one(x, _):
        kind = jnp.zeros((16, 128), I32)
        for c in range(REGIONS):
            cx, cy, cz = corners[c]
            step = x - cx
            inside = jnp.logical_and(step >= 0, step < 8)
            dy = row - cy
            dz = lane - cz
            in_y = jnp.logical_and(dy >= 0, dy < 8)
            in_z = jnp.logical_and(dz >= 0, dz < 8)
            near = jnp.where(dy == -1, 4, jnp.where(dy == 8, 5, 0))
            side = jnp.where(dz == -1, 6, jnp.where(dz == 8, 7, 0))
            plain = jnp.where(inside, 1, jnp.where(step == -1, 2, jnp.where(step == 8, 3, 0)))
            mine = jnp.where(
                jnp.logical_and(in_y, in_z),
                plain,
                jnp.where(inside, jnp.where(in_z, near, jnp.where(in_y, side, 0)), 0),
            )
            ys = jnp.clip(dy, 0, 7)
            zs = jnp.clip(dz, 0, 7)
            lanes = jnp.where(mine < 4, ys * 8 + zs, 32 + 8 * mine + jnp.where(mine < 6, zs, ys))
            used = mine > 0
            kind = jnp.where(used, mine, kind)
            index[x, c] = jnp.where(used, lanes + 128, 0)
        factor = jnp.where(kind < 2, 0.0, jnp.where(kind % 2 == 0, -COURANT, COURANT))
        weight[x] = jnp.where(kind == 1, 0.125, 0.0625 * factor)
        for f in range(FIELDS):
            flux = jnp.where(
                kind < 4,
                jnp.where(kind == 2, x_face[f, x + 1], x_face[f, x]),
                jnp.where(
                    kind < 6,
                    jnp.where(kind == 4, y_high[f, x], y_low[f, x]),
                    jnp.where(kind == 6, z_high[f, x], z_low[f, x]),
                ),
            )
            plain = new[f, x]
            ring = jnp.where(kind >= 2, plain - 0.5 * factor * flux, plain)
            new[f, x] = jnp.where(kind == 1, 0.0, ring)
        return 0

    lax.fori_loop(0, 16, one, 0)


def settle_rows(answers, rows):
    lane = iota((REGIONS, 128), 1)
    spot = ((lane % 16) // 8) * 64 + lane % 8
    for f in range(FIELDS):
        ends = answers[7 * f]
        rows[f, 0] = ends
        rows[f, 9] = pltpu.roll(ends, 64, 1)
        y_face = answers[7 * f + 1]
        z_face = answers[7 * f + 2]
        for big in range(8):
            cells = answers[7 * f + 3 + big // 2]
            if big % 2:
                cells = pltpu.roll(cells, 64, 1)
            around = jnp.where(
                lane < 80, pick(y_face, spot + 8 * big), pick(z_face, spot + 8 * big)
            )
            rows[f, 1 + big] = jnp.where(lane < 64, cells, around)


def settle(corners, rows, new, weight, index, out, start):
    def one(step, _):
        x = start + step
        values = [jnp.zeros((16, 128), F32) for _ in range(FIELDS)]
        for c in range(REGIONS):
            which = jnp.clip(x - corners[c][0] + 1, 0, 9)
            lanes = index[x, c]
            used = lanes >= 128
            lanes = lanes & 127
            for f in range(FIELDS):
                line = jnp.broadcast_to(rows[f, which, c : c + 1, :], (16, 128))
                values[f] = jnp.where(used, pick(line, lanes), values[f])
        for f in range(FIELDS):
            v = new[f, x] + weight[x] * values[f]
            out[f, x] = v[:, :64]
        return 0

    lax.fori_loop(0, 8, one, 0, unroll=SETTLE_UNROLL)


def whole(
    sizes,
    parent_hbm,
    plane_hbm,
    corner_hbm,
    coarse_hbm,
    fine_hbm,
    coarse_out,
    fine_out,
    parent_ref,
    corner_ref,
    plane_ref,
    coarse_ref,
    block,
    new,
    x_face,
    y_low,
    y_high,
    z_low,
    z_high,
    weight,
    index,
    y_stage,
    z_stage,
    x_rim,
    y_rim,
    z_rim,
    cut,
    rim_out,
    rim_in_old,
    rim_in_mid,
    rim,
    fine_ref,
    prim,
    half,
    fine_new,
    coarse_new,
    reg,
    route,
    relay_in,
    relay_out,
    row_stage,
    direct_out,
    direct_in,
    answer_in,
    answers,
    answer_rows,
    table,
    load_sems,
    halo_send,
    halo_recv,
    many_send,
    many_recv,
):
    n_gx, n_gy, n_gz = sizes
    members = n_gy * n_gz
    relayed = members
    direct = 7 * FIELDS - relayed
    rim_in = (rim_in_old, rim_in_mid)
    gx = lax.axis_index("gx")
    gy = lax.axis_index("gy")
    gz = lax.axis_index("gz")
    within = gy * n_gz + gz
    myself = gx * members + within
    start = gx * (members * BOXMAX)

    def hops(move):
        return min(move[0], n_gy - move[0]) + min(move[1], n_gz - move[1])

    moves = [(dy, dz) for dy in range(n_gy) for dz in range(n_gz) if dy or dz]
    peers = []
    for dy, dz in sorted(moves, key=hops, reverse=True):
        other_y = lax.rem(gy + dy, n_gy)
        other_z = lax.rem(gz + dz, n_gz)
        peers.append((other_y * n_gz + other_z, (gx, other_y, other_z)))

    barrier = pltpu.get_barrier_semaphore()
    for _, device in peers:
        pl.semaphore_signal(barrier, inc=1, device_id=device, device_id_type=MESH)

    x_next = (lax.rem(gx + 1, n_gx), gy, gz)
    x_prev = (lax.rem(gx + n_gx - 1, n_gx), gy, gz)
    y_next = (gx, lax.rem(gy + 1, n_gy), gz)
    y_prev = (gx, lax.rem(gy + n_gy - 1, n_gy), gz)
    z_next = (gx, gy, lax.rem(gz + 1, n_gz))
    z_prev = (gx, gy, lax.rem(gz + n_gz - 1, n_gz))
    pl.semaphore_signal(barrier, inc=1, device_id=x_next, device_id_type=MESH)
    pl.semaphore_signal(barrier, inc=1, device_id=x_prev, device_id_type=MESH)

    def fetch(src, dst, index):
        copy = pltpu.make_async_copy(src, dst, load_sems.at[index])
        copy.start()
        return copy

    coarse_load = fetch(coarse_hbm, coarse_ref, 0)
    parent_load = fetch(parent_hbm, parent_ref, 1)
    corner_load = fetch(corner_hbm, corner_ref, 2)
    plane_load = fetch(plane_hbm, plane_ref, 3)
    fine_load = fetch(fine_hbm, fine_ref, 4)

    parent_load.wait()
    corner_load.wait()

    def scan(entry, found):
        c0, c1, c2, c3 = found
        hit = parent_ref[start + entry] == myself
        return (
            jnp.where(hit, c1, c0),
            jnp.where(hit, c2, c1),
            jnp.where(hit, c3, c2),
            jnp.where(hit, entry, c3),
        )

    zero = jnp.int32(0)
    children = lax.fori_loop(0, members * BOXMAX, scan, (zero, zero, zero, zero), unroll=8)
    for c in range(REGIONS):
        for k in range(3):
            table[4 * c + k] = jnp.clip(corner_ref[k, start + children[c]], 1, 55 if k == 2 else 7)
    child_peer = [child // BOXMAX for child in children]
    own = [parent_ref[start + within * BOXMAX + s] for s in range(BOXMAX)]
    own_peer = [lax.rem(jnp.maximum(own[s], 0), members) for s in range(BOXMAX)]

    def look_up(other, _):
        rank = zero
        for c in range(1, REGIONS):
            rank = jnp.where(child_peer[c] == other, c, rank)
        found = zero
        for s in range(BOXMAX):
            found = jnp.where(jnp.logical_and(own[s] >= 0, own_peer[s] == other), s, found)
        table[32 + other] = rank
        table[32 + members + other] = found
        return 0

    lax.fori_loop(0, members, look_up, 0, unroll=4)

    def cut_all(when, source):
        def one(c, _):
            corner = (table[4 * c], table[4 * c + 1], table[4 * c + 2])

            def put(f, v, line):
                cut[when, c, 3 * f + v : 3 * f + v + 1, :] = line

            cut_rims(source, corner, put)
            return 0

        lax.fori_loop(0, REGIONS, one, 0, unroll=CUT_UNROLL)

    def ship(src, dst, index, device):
        pltpu.make_async_remote_copy(
            src_ref=src,
            dst_ref=dst,
            send_sem=many_send.at[index],
            recv_sem=many_recv.at[index],
            device_id=device,
            device_id_type=MESH,
        ).start()

    def wait_many(every, index, semaphores):
        pltpu.make_async_copy(every, every, semaphores.at[index]).wait()

    others = pl.ds(0, members - 1)

    def fill_rims(when):
        def one(other, _):
            rim_out[when, other] = cut[when, table[32 + other]]
            return 0

        lax.fori_loop(0, members, one, 0, unroll=4)
        rim_in[when][within] = rim_out[when, within]

    def send_rims(when):
        for other, device in peers:
            ship(rim_out.at[when, other], rim_in[when].at[within], when, device)

    lane16 = iota((16, 128), 1)
    row16 = iota((16, 128), 0)
    coarse_load.wait()
    for f in range(FIELDS):
        block[f, 1:17, :, 0:64] = coarse_ref[f]
    for f in range(FIELDS):
        y_stage[0, f] = block[f, 1:17, 0, :]
        y_stage[1, f] = block[f, 1:17, 15, :]
        for h in range(2):
            low = jnp.zeros((16, 128), F32)
            high = jnp.zeros((16, 128), F32)
            for x in range(8):
                plane = block[f, 1 + 8 * h + x]
                here = lane16 // 16 == x
                low = jnp.where(here, jnp.broadcast_to(plane[:, 0:1], (16, 128)), low)
                high = jnp.where(here, jnp.broadcast_to(plane[:, 63:64], (16, 128)), high)
            match = row16 == lane16 % 16
            z_stage[0, h, f : f + 1, :] = jnp.sum(
                jnp.where(match, low, 0.0), axis=0, keepdims=True
            )
            z_stage[1, h, f : f + 1, :] = jnp.sum(
                jnp.where(match, high, 0.0), axis=0, keepdims=True
            )

    cut_all(0, lambda f, x, y, n: block[f, x + 1, pl.ds(y, n), :])
    fill_rims(0)

    pl.semaphore_wait(barrier, members + 1)

    def halo(src, dst, index, device):
        copy = pltpu.make_async_remote_copy(
            src_ref=src,
            dst_ref=dst,
            send_sem=halo_send.at[index],
            recv_sem=halo_recv.at[index],
            device_id=device,
            device_id_type=MESH,
        )
        copy.start()
        return copy

    halos = [
        halo(block.at[:, 16], x_rim.at[0], 0, x_next),
        halo(block.at[:, 1], x_rim.at[1], 1, x_prev),
        halo(y_stage.at[1], y_rim.at[0], 2, y_next),
        halo(y_stage.at[0], y_rim.at[1], 3, y_prev),
        halo(z_stage.at[1], z_rim.at[0], 4, z_next),
        halo(z_stage.at[0], z_rim.at[1], 5, z_prev),
    ]

    send_rims(0)

    for v in range(7 * FIELDS):
        reg[v] = jnp.zeros((BOXMAX, 128), F32)

    for copy in halos:
        copy.wait()
    for f in range(FIELDS):
        block[f, 0] = x_rim[0, f]
        block[f, 17] = x_rim[1, f]
    coarse_step(block, y_rim, z_rim, new, x_face, y_low, y_high, z_low, z_high)
    cut_all(
        1,
        lambda f, x, y, n: 0.5 * (block[f, x + 1, pl.ds(y, n), :] + new[f, x, pl.ds(y, n), :]),
    )
    fill_rims(1)
    send_rims(1)

    plane_load.wait()
    n_rows = REGIONS * members
    columns = members * BOXMAX
    row = iota((n_rows, columns), 0)
    column = iota((n_rows, columns), 1)
    slots = plane_ref[pl.ds(gx * (columns // 128), columns // 128), :] if columns >= 128 else None
    if columns >= 128:
        slots = jnp.concatenate(
            [
                jnp.broadcast_to(slots[h : h + 1, :], (n_rows, 128))
                for h in range(columns // 128)
            ],
            axis=1,
        )
    else:
        slots = jnp.broadcast_to(plane_ref[0:1, 0:columns], (n_rows, columns))
    number = column.astype(F32)
    far = 65536.0
    candidate = jnp.where(slots == row // REGIONS + gx * members, number, far)
    chosen = jnp.full((n_rows, 1), far)
    for r in range(REGIONS):
        least = jnp.min(candidate, axis=1, keepdims=True)
        chosen = jnp.where(row[:, 0:1] % REGIONS == r, least, chosen)
        candidate = jnp.where(candidate == least, far, candidate)
    route[...] = jnp.where(number == chosen, 1.0, 0.0)

    fine_load.wait()
    fine_prims(fine_ref, prim)
    fine_inner(fine_ref, prim, half)

    sub = iota((BOXMAX, 128), 0)
    owner = jnp.zeros((BOXMAX, 128), I32)
    for s in range(BOXMAX):
        owner = jnp.where(sub == s, own[s], owner)
    filled = owner >= 0

    def take_rims(when):
        wait_many(rim_in[when].at[others], when, many_recv)
        for s in range(BOXMAX):
            rows = rim_in[when][own_peer[s]]
            for v in range(3 * FIELDS):
                rim[v, s : s + 1, :] = rows[v : v + 1, :]

    take_rims(0)
    fine_outer(fine_ref, prim, rim, reg, filled, half, None)
    fine_prims(half, prim)
    fine_inner(half, prim, fine_new)
    take_rims(1)
    fine_outer(half, prim, rim, reg, filled, fine_new, fine_ref)

    for other, device in peers:
        ship(reg.at[other], relay_in.at[within], 2, device)
    relay_in[within] = reg[within]

    fine_store = fetch(fine_new, fine_out, 5)
    if direct:
        for s in range(BOXMAX):
            row_stage[s] = reg[relayed:, s, :]

        for other, device in peers:
            direct_out[other] = row_stage[table[32 + members + other]]
            ship(direct_out.at[other], direct_in.at[within], 3, device)
        direct_in[within] = row_stage[table[32 + members + within]]

    wait_many(relay_in.at[others], 2, many_recv)
    sorted_rows = jnp.dot(
        route[...],
        relay_in[...].reshape(columns, 128),
        precision=lax.Precision.HIGHEST,
        preferred_element_type=F32,
    )
    for p in range(members):
        relay_out[p] = sorted_rows[REGIONS * p : REGIONS * p + REGIONS]

    for other, device in peers:
        ship(relay_out.at[other], answer_in.at[within], 4, device)
    answer_in[within] = relay_out[within]

    corners = [(table[4 * c], table[4 * c + 1], table[4 * c + 2]) for c in range(REGIONS)]
    plan_settle(corners, new, x_face, y_low, y_high, z_low, z_high, weight, index)

    if direct:
        wait_many(direct_in.at[others], 3, many_recv)
        for c in range(REGIONS):
            rows = direct_in[child_peer[c]]
            for v in range(direct):
                answers[relayed + v, c : c + 1, :] = rows[v : v + 1, :]
    wait_many(answer_in.at[others], 4, many_recv)
    for v in range(relayed):
        answers[v] = answer_in[v]
    settle_rows(answers, answer_rows)
    coarse_stores = []
    for part in range(2):
        settle(corners, answer_rows, new, weight, index, coarse_new, 8 * part)
        planes = pl.ds(8 * part, 8)
        coarse_stores.append(fetch(coarse_new.at[:, planes], coarse_out.at[:, planes], 6 + part))
    wait_many(rim_out.at[0, others], 0, many_send)
    wait_many(rim_out.at[1, others], 1, many_send)
    wait_many(relay_in.at[others], 2, many_send)
    if direct:
        wait_many(direct_out.at[others], 3, many_send)
    wait_many(relay_out.at[others], 4, many_send)
    fine_store.wait()
    for copy in coarse_stores:
        copy.wait()


def hand_over(coarse_in, fine_in, coarse_out, fine_out, coarse_held, fine_held, arrive, leave):
    moves = []
    for f in range(FIELDS):
        for n, (src, held, dst) in enumerate(
            ((coarse_in, coarse_held, coarse_out), (fine_in, fine_held, fine_out))
        ):
            first = pltpu.make_async_copy(src.at[f], held.at[f], arrive.at[2 * f + n])
            first.start()
            moves.append((first, pltpu.make_async_copy(held.at[f], dst.at[f], leave.at[2 * f + n])))
    for first, second in moves:
        first.wait()
        second.start()
    for _, second in moves:
        second.wait()


def on_device(sizes, coarse_state, fine_state, slot_parent, slot_corner):
    members = sizes[1] * sizes[2]
    relayed = members
    hbm = pl.BlockSpec(memory_space=pltpu.HBM)
    fine = jnp.transpose(fine_state, (1, 0, 2))
    corner = jnp.transpose(slot_corner, (1, 0))
    plane = slot_parent.reshape(-1, min(128, slot_parent.shape[0]))
    field_block = (FIELDS, 16, 16, 128)
    rows = 7 * FIELDS
    direct = max(rows - relayed, 1)
    coarse_next, fine_next = pl.pallas_call(
        functools.partial(whole, sizes),
        out_shape=(
            jax.ShapeDtypeStruct(coarse_state.shape, F32),
            jax.ShapeDtypeStruct(fine.shape, F32),
        ),
        in_specs=[hbm] * 5,
        out_specs=(hbm, hbm),
        scratch_shapes=[
            pltpu.SMEM(slot_parent.shape, I32),
            pltpu.SMEM(corner.shape, I32),
            pltpu.VMEM(plane.shape, I32),
            pltpu.VMEM(coarse_state.shape, F32),
            pltpu.VMEM((FIELDS, 18, 16, 128), F32),
            pltpu.VMEM(field_block, F32),
            pltpu.VMEM((FIELDS, 17, 16, 128), F32),
            pltpu.VMEM(field_block, F32),
            pltpu.VMEM(field_block, F32),
            pltpu.VMEM(field_block, F32),
            pltpu.VMEM(field_block, F32),
            pltpu.VMEM((16, 16, 128), F32),
            pltpu.VMEM((16, REGIONS, 16, 128), I32),
            pltpu.VMEM((2, FIELDS, 16, 128), F32),
            pltpu.VMEM((2, 2, FIELDS, 128), F32),
            pltpu.VMEM((2, FIELDS, 16, 128), F32),
            pltpu.VMEM((2, FIELDS, 16, 128), F32),
            pltpu.VMEM((2, 2, FIELDS, 128), F32),
            pltpu.VMEM((2, REGIONS, 3 * FIELDS, 128), F32),
            pltpu.VMEM((2, members, 3 * FIELDS, 128), F32),
            pltpu.VMEM((members, 3 * FIELDS, 128), F32),
            pltpu.VMEM((members, 3 * FIELDS, 128), F32),
            pltpu.VMEM((3 * FIELDS, BOXMAX, 128), F32),
            pltpu.VMEM(fine.shape, F32),
            pltpu.VMEM((3,) + fine.shape[1:], F32),
            pltpu.VMEM(fine.shape, F32),
            pltpu.VMEM(fine.shape, F32),
            pltpu.VMEM(coarse_state.shape, F32),
            pltpu.VMEM((rows, BOXMAX, 128), F32),
            pltpu.VMEM((REGIONS * members, BOXMAX * members), F32),
            pltpu.VMEM((members, BOXMAX, 128), F32),
            pltpu.VMEM((members, REGIONS, 128), F32),
            pltpu.VMEM((BOXMAX, direct, 128), F32),
            pltpu.VMEM((members, direct, 128), F32),
            pltpu.VMEM((members, direct, 128), F32),
            pltpu.VMEM((members, REGIONS, 128), F32),
            pltpu.VMEM((rows, REGIONS, 128), F32),
            pltpu.VMEM((FIELDS, 10, REGIONS, 128), F32),
            pltpu.SMEM((32 + 2 * members,), I32),
            pltpu.SemaphoreType.DMA((8,)),
            pltpu.SemaphoreType.DMA((6,)),
            pltpu.SemaphoreType.DMA((6,)),
            pltpu.SemaphoreType.DMA((5,)),
            pltpu.SemaphoreType.DMA((5,)),
        ],
        compiler_params=pltpu.CompilerParams(
            collective_id=0, has_side_effects=True, vmem_limit_bytes=62 * 1024 * 1024
        ),
    )(slot_parent, plane, corner, coarse_state, fine)
    coarse_next, fine_next = pl.pallas_call(
        hand_over,
        out_shape=(
            jax.ShapeDtypeStruct(coarse_state.shape, F32),
            jax.ShapeDtypeStruct(fine.shape, F32),
        ),
        in_specs=[hbm] * 2,
        out_specs=(hbm, hbm),
        scratch_shapes=[
            pltpu.VMEM(coarse_state.shape, F32),
            pltpu.VMEM(fine.shape, F32),
            pltpu.SemaphoreType.DMA((2 * FIELDS,)),
            pltpu.SemaphoreType.DMA((2 * FIELDS,)),
        ],
        compiler_params=pltpu.CompilerParams(vmem_limit_bytes=62 * 1024 * 1024),
    )(coarse_next, fine_next)
    return coarse_next, jnp.transpose(fine_next, (1, 0, 2))


def solution(mesh):
    sizes = tuple(mesh.shape[name] for name in ("gx", "gy", "gz"))
    return jax.shard_map(
        functools.partial(on_device, sizes),
        mesh=mesh,
        in_specs=(P(None, "gx", "gy", "gz"), P(("gx", "gy", "gz"), None, None), P(), P()),
        out_specs=(P(None, "gx", "gy", "gz"), P(("gx", "gy", "gz"), None, None)),
        check_vma=False,
    )
```

```python
import functools

import jax
import jax.numpy as jnp
from jax import lax
from jax.experimental import pallas as pl
from jax.experimental.pallas import tpu as pltpu
from jax.sharding import PartitionSpec as P

GAMMA = 1.4
COURANT = 0.04
PRIM_UNROLL = 2
X_UNROLL = 15
YZ_UNROLL = 2
OUTER_UNROLL = 4
COARSE_UNROLL = 4
CUT_UNROLL = 4
SETTLE_UNROLL = 8
FIELDS = 5
REGIONS = 4
BOXMAX = 8
MESH = pl.DeviceIdType.MESH
F32 = jnp.float32
I32 = jnp.int32


def iota(shape, dim):
    return lax.broadcasted_iota(I32, shape, dim)


def pick(values, lanes):
    numbers = lax.GatherDimensionNumbers(
        offset_dims=(),
        collapsed_slice_dims=(1,),
        start_index_map=(1,),
        operand_batching_dims=(0,),
        start_indices_batching_dims=(0,),
    )
    return lax.gather(
        values,
        lanes[..., None],
        numbers,
        (1, 1),
        mode=lax.GatherScatterMode.PROMISE_IN_BOUNDS,
    )


def prims(q):
    inverse = pl.reciprocal(q[0], approx=True)
    inverse = inverse * (2.0 - q[0] * inverse)
    kinetic = 0.5 * (q[1] * q[1] + q[2] * q[2] + q[3] * q[3]) * inverse
    pressure = (GAMMA - 1.0) * (q[4] - kinetic)
    square = GAMMA * pressure * inverse
    sound = square * lax.rsqrt(jnp.maximum(square, 1e-30))
    return inverse, pressure, sound, q[4] + pressure


def along(q, prim, axis):
    inverse, pressure, sound, total = prim
    velocity = q[1 + axis] * inverse
    flux = [q[1 + axis], q[1] * velocity, q[2] * velocity, q[3] * velocity, total * velocity]
    flux[1 + axis] = flux[1 + axis] + pressure
    return flux, jnp.abs(velocity) + sound


def face(low, low_terms, high, high_terms):
    signal = jnp.maximum(low_terms[1], high_terms[1])
    return [
        (low_terms[0][f] + high_terms[0][f]) - signal * (high[f] - low[f]) for f in range(FIELDS)
    ]


def moved(q, terms, move):
    return [move(v) for v in q], [move(v) for v in terms[0]], move(terms[1])


def span(plane, h):
    return pl.ds(pl.multiple_of(plane * 256 + h * 128, 128), 128)


def roll(v, by):
    return pltpu.roll(v, by % 128, 1)


def fine_prims(cells, prim):
    def one(plane, _):
        for h in range(2):
            where = span(plane, h)
            inverse, pressure, sound, _ = prims([cells[f, :, where] for f in range(FIELDS)])
            prim[0, :, where] = inverse
            prim[1, :, where] = pressure
            prim[2, :, where] = sound
        return 0

    lax.fori_loop(0, 16, one, 0, unroll=PRIM_UNROLL)


def fine_inner(cells, prim, out):
    lane = iota((BOXMAX, 128), 1)
    first_row = lane < 16
    last_row = lane >= 112
    k_first = lane % 16 == 0

    def load(plane, h):
        where = span(plane, h)
        q = [cells[f, :, where] for f in range(FIELDS)]
        pressure = prim[1, :, where]
        return q, (prim[0, :, where], pressure, prim[2, :, where], q[4] + pressure)

    def x_one(plane, low):
        here = [load(plane, h) for h in range(2)]
        after = [load(plane + 1, h) for h in range(2)]
        high = [
            face(
                here[h][0],
                along(here[h][0], here[h][1], 0),
                after[h][0],
                along(after[h][0], after[h][1], 0),
            )
            for h in range(2)
        ]
        for h in range(2):
            for f in range(FIELDS):
                new = here[h][0][f] - (0.5 * COURANT) * (high[h][f] - low[h][f])
                out[f, :, span(plane, h)] = new
        return high

    none = [[jnp.zeros((BOXMAX, 128), F32)] * FIELDS] * 2
    high = lax.fori_loop(0, 15, x_one, none, unroll=X_UNROLL)
    for h in range(2):
        for f in range(FIELDS):
            out[f, :, span(15, h)] = cells[f, :, span(15, h)] + (0.5 * COURANT) * high[h][f]

    def yz_one(plane, _):
        cell = [load(plane, h) for h in range(2)]
        partial = [[out[f, :, span(plane, h)] for f in range(FIELDS)] for h in range(2)]
        for h in range(2):
            q, q_prim = cell[h]
            terms = along(q, q_prim, 2)
            shifted = moved(q, terms, lambda v: roll(v, 1))
            z = face(shifted[0], (shifted[1], shifted[2]), q, terms)
            for f in range(FIELDS):
                low = jnp.where(k_first, 0.0, z[f])
                partial[h][f] = partial[h][f] - (0.5 * COURANT) * (roll(low, -1) - low)
        q0, prim0 = cell[0]
        q1, prim1 = cell[1]
        terms0 = along(q0, prim0, 1)
        terms1 = along(q1, prim1, 1)
        shifted0 = moved(q0, terms0, lambda v: roll(v, 16))
        shifted1 = moved(q1, terms1, lambda v: roll(v, 16))

        def seam(low, high):
            return jnp.where(first_row, low, high)

        low1 = (
            [seam(shifted0[0][f], shifted1[0][f]) for f in range(FIELDS)],
            (
                [seam(shifted0[1][f], shifted1[1][f]) for f in range(FIELDS)],
                seam(shifted0[2], shifted1[2]),
            ),
        )
        y0 = face(shifted0[0], (shifted0[1], shifted0[2]), q0, terms0)
        y1 = face(low1[0], low1[1], q1, terms1)
        for f in range(FIELDS):
            low = jnp.where(first_row, 0.0, y0[f])
            up0 = roll(low, -16)
            up1 = roll(y1[f], -16)
            change0 = jnp.where(last_row, up1, up0) - low
            change1 = jnp.where(last_row, up0, up1) - y1[f]
            partial[0][f] = partial[0][f] - (0.5 * COURANT) * change0
            partial[1][f] = partial[1][f] - (0.5 * COURANT) * change1
        for h in range(2):
            for f in range(FIELDS):
                out[f, :, span(plane, h)] = partial[h][f]
        return 0

    lax.fori_loop(0, 16, yz_one, 0, unroll=YZ_UNROLL)


def fine_outer(cells, prim, rim, reg, filled, out, old):
    second = old is not None
    lane = iota((BOXMAX, 128), 1)
    k = lane % 16
    half_k = k // 2
    quarter = lane // 32
    squeeze = ((lane % 32) // 8) * 32 + (lane % 8) * 2
    part = (lane % 64) // 8
    low_half = lane < 64
    step = 0.5 * COURANT
    y_sign = jnp.where(low_half, 1.0, -1.0)
    z_sign = jnp.where(k < 8, 1.0, -1.0)
    y_weight = (jnp.where(lane < 16, step, 0.0), jnp.where(lane >= 112, -step, 0.0))
    z_weight = jnp.where(k == 0, step, jnp.where(k == 15, -step, 0.0))

    def load(plane, h):
        where = span(plane, h)
        q = [cells[f, :, where] for f in range(FIELDS)]
        pressure = prim[1, :, where]
        return q, (prim[0, :, where], pressure, prim[2, :, where], q[4] + pressure)

    def edge(ghost, ghost_terms, q, terms, sign):
        signal = jnp.maximum(ghost_terms[1], terms[1]) * sign
        return [
            (ghost_terms[0][f] + terms[0][f]) - signal * (q[f] - ghost[f]) for f in range(FIELDS)
        ]

    results = []
    for plane, side, sign in ((0, 0, 1.0), (15, 64, -1.0)):
        flux = []
        for h in range(2):
            spread = (h * 4 + quarter) * 8 + half_k + side
            ghost = [pick(rim[3 * f], spread) for f in range(FIELDS)]
            q, q_prim = load(plane, h)
            flux.append(edge(ghost, along(ghost, prims(ghost), 0), q, along(q, q_prim, 0), sign))
            results.append(
                [out[f, :, span(plane, h)] + (sign * step) * flux[h][f] for f in range(FIELDS)]
            )
        for f in range(FIELDS):
            found = []
            for h in range(2):
                v = flux[h][f]
                v = v + roll(v, -1)
                v = v + roll(v, -16)
                found.append(pick(v, squeeze))
            results.append(jnp.where((lane % 64) < 32, found[0], found[1]))
    for plane, first in ((0, 0), (15, 2 + FIELDS)):
        for h in range(2):
            for f in range(FIELDS):
                out[f, :, span(plane, h)] = results[first + h][f]
    for f in range(FIELDS):
        v = jnp.where(low_half, results[2 + f], results[4 + FIELDS + f])
        reg[3 * f] = reg[3 * f] + jnp.where(filled, v, 0.0)

    def pair(big, _):
        y_lanes = big * 8 + half_k + jnp.where(low_half, 0, 64)
        y_ghost = [pick(rim[3 * f + 1], y_lanes) for f in range(FIELDS)]
        y_ghost_terms = along(y_ghost, prims(y_ghost), 1)
        z_ghost = []
        z_ghost_terms = []
        for h in range(2):
            z_lanes = big * 8 + h * 4 + quarter + jnp.where(k >= 8, 64, 0)
            ghost = [pick(rim[3 * f + 2], z_lanes) for f in range(FIELDS)]
            z_ghost.append(ghost)
            z_ghost_terms.append(along(ghost, prims(ghost), 2))
        y_sum = [None] * FIELDS
        z_sum = [[None] * FIELDS for _ in range(2)]

        def accumulate(total, v):
            return v if total is None else total + v

        for sub in range(2):
            plane = 2 * big + sub
            q, q_prim = zip(*[load(plane, h) for h in range(2)])
            near = [jnp.where(low_half, q[0][f], q[1][f]) for f in range(FIELDS)]
            near_prim = [jnp.where(low_half, q_prim[0][i], q_prim[1][i]) for i in range(4)]
            before = [[out[f, :, span(plane, h)] for f in range(FIELDS)] for h in range(2)]
            if second:
                kept = [[old[f, :, span(plane, h)] for f in range(FIELDS)] for h in range(2)]
            y = edge(y_ghost, y_ghost_terms, near, along(near, near_prim, 1), y_sign)
            for f in range(FIELDS):
                y_sum[f] = accumulate(y_sum[f], y[f])
            news = []
            for h in range(2):
                z = edge(z_ghost[h], z_ghost_terms[h], q[h], along(q[h], q_prim[h], 2), z_sign)
                for f in range(FIELDS):
                    z_sum[h][f] = accumulate(z_sum[h][f], z[f])
                    new = before[h][f] + y_weight[h] * y[f] + z_weight * z[f]
                    if second:
                        new = jnp.where(filled, new, kept[h][f])
                    news.append((f, h, new))
            for f, h, new in news:
                out[f, :, span(plane, h)] = new

        mine = jnp.logical_and(filled, part == big)
        y_from = (lane % 8) * 2 + jnp.where(low_half, 0, 112)
        z_from = (lane % 4) * 32 + jnp.where(low_half, 0, 15)
        old_regs = [[reg[3 * f + t] for t in (1, 2)] for f in range(FIELDS)]
        for f in range(FIELDS):
            v = y_sum[f] + roll(y_sum[f], -1)
            old_regs[f][0] = old_regs[f][0] + jnp.where(mine, pick(v, y_from), 0.0)
            found = []
            for h in range(2):
                v = z_sum[h][f] + roll(z_sum[h][f], -16)
                found.append(pick(v, z_from))
            v = jnp.where(lane % 8 < 4, found[0], found[1])
            old_regs[f][1] = old_regs[f][1] + jnp.where(mine, v, 0.0)
        for f in range(FIELDS):
            for t in (1, 2):
                reg[3 * f + t] = old_regs[f][t - 1]
        return 0

    lax.fori_loop(0, 8, pair, 0, unroll=OUTER_UNROLL)


def through(tx, ty, tz, group):
    lane = iota(tx.shape, 1)
    x = 2 * group + lane // 64
    y = (lane % 64) // 8
    z = lane % 8

    def sign(place):
        return jnp.where(place == 0, 1.0, jnp.where(place == 7, -1.0, 0.0))

    total = sign(y) * pick(ty, x * 8 + z + jnp.where(y == 7, 64, 0))
    total = total + sign(z) * pick(tz, x * 8 + y + jnp.where(z == 7, 64, 0))
    if group == 0:
        total = total + jnp.where(lane < 64, tx, 0.0)
    if group == 3:
        total = total - jnp.where(lane < 64, 0.0, tx)
    return total


def fine_average(cells, reg, filled, sums):
    lane = iota((BOXMAX, 128), 1)
    squeeze = ((lane % 32) // 8) * 32 + (lane % 8) * 2
    faces = [reg[v] for v in range(3 * FIELDS)]
    for group in range(4):
        tiles = []
        for f in range(FIELDS):
            for sub in range(2):
                for h in range(2):
                    plane = 4 * group + 2 * sub
                    tiles.append(cells[f, :, span(plane, h)] + cells[f, :, span(plane + 1, h)])
        tiles = [v + roll(v, -1) for v in tiles]
        tiles = [v + roll(v, -16) for v in tiles]
        tiles = [pick(v, squeeze) for v in tiles]
        crossed = [through(*faces[3 * f : 3 * f + 3], group) for f in range(FIELDS)]
        results = []
        for f in range(FIELDS):
            low = jnp.where(lane < 32, tiles[4 * f], tiles[4 * f + 1])
            high = jnp.where(lane < 96, tiles[4 * f + 2], tiles[4 * f + 3])
            v = jnp.where(lane < 64, low, high) - (0.5 * COURANT) * crossed[f]
            results.append(jnp.where(filled, v, 0.0))
        for f in range(FIELDS):
            sums[4 * f + group] = results[f]


def coarse_step(block, y_rim, z_rim, new, x_face, y_low, y_high, z_low, z_high):
    lane = iota((16, 128), 1)
    row = iota((16, 128), 0)
    tip = iota((8, 128), 0)

    def load(plane):
        return [block[f, plane] for f in range(FIELDS)]

    def widen(x, _):
        column = (x % 8) * 16 + row
        for f in range(FIELDS):
            below = jnp.broadcast_to(z_rim[0, x // 8, f : f + 1, :], (16, 128))
            above = jnp.broadcast_to(z_rim[1, x // 8, f : f + 1, :], (16, 128))
            side = jnp.where(lane == 64, pick(above, column), pick(below, column))
            block[f, x + 1] = jnp.where(lane < 64, block[f, x + 1], side)
        return 0

    lax.fori_loop(0, 16, widen, 0, unroll=4)

    ghost = load(0)
    here = load(1)
    here_prim = prims(here)
    low = face(ghost, along(ghost, prims(ghost), 0), here, along(here, here_prim, 0))
    for f in range(FIELDS):
        x_face[f, 0] = low[f]

    def one(x, carried):
        here, here_prim, x_low = carried
        after = load(x + 2)
        after_prim = prims(after)
        x_high = face(here, along(here, here_prim, 0), after, along(after, after_prim, 0))

        tips = []
        for f in range(FIELDS):
            above = y_rim[1, f, pl.ds(x, 1), :]
            below = y_rim[0, f, pl.ds(x, 1), :]
            tips.append(
                jnp.where(
                    tip == 0,
                    jnp.broadcast_to(above, (8, 128)),
                    jnp.broadcast_to(below, (8, 128)),
                )
            )
        tip_terms = along(tips, prims(tips), 1)
        terms = along(here, here_prim, 1)

        def tall(low, high):
            return jnp.concatenate([low, high], axis=0)

        cells = [tall(here[f], tips[f]) for f in range(FIELDS)]
        terms = ([tall(terms[0][f], tip_terms[0][f]) for f in range(FIELDS)], tall(terms[1], tip_terms[1]))
        shifted = moved(cells, terms, lambda v: pltpu.roll(v, 1, 0))
        y = face(shifted[0], (shifted[1], shifted[2]), cells, terms)

        terms = along(here, here_prim, 2)
        shifted = moved(here, terms, lambda v: pltpu.roll(v, 1, 1))
        z = face(shifted[0], (shifted[1], shifted[2]), here, terms)
        for f in range(FIELDS):
            up = pltpu.roll(y[f], 23, 0)[:16]
            down = y[f][:16]
            right = pltpu.roll(z[f], 127, 1)
            x_face[f, x + 1] = x_high[f]
            y_low[f, x] = down
            y_high[f, x] = up
            z_low[f, x] = z[f]
            z_high[f, x] = right
            change = (x_high[f] - x_low[f]) + (up - down) + (right - z[f])
            new[f, x] = here[f] - (0.5 * COURANT) * change
        return after, after_prim, x_high

    lax.fori_loop(0, 16, one, (here, here_prim, low), unroll=COARSE_UNROLL)


def cut_rims(source, corner, put):
    cx, cy, cz = corner
    lane = iota((8, 128), 1)
    row = iota((8, 128), 0)
    low_half = lane < 64
    part = (lane % 64) // 8
    along_z = cz + lane % 8
    ends = jnp.where(low_half, cz - 1, cz + 8)
    rows_x = row == part
    rows_z = row == lane % 8
    for f in range(FIELDS):
        low = pick(source(f, cx - 1, cy, 8), along_z)
        high = pick(source(f, cx + 8, cy, 8), along_z)
        v = jnp.where(rows_x, jnp.where(low_half, low, high), 0.0)
        put(f, 0, jnp.sum(v, axis=0, keepdims=True))
        low = jnp.zeros((8, 128), F32)
        high = jnp.zeros((8, 128), F32)
        total = jnp.zeros((8, 128), F32)
        for big in range(8):
            here = row == big
            low = jnp.where(here, jnp.broadcast_to(source(f, cx + big, cy - 1, 1), (8, 128)), low)
            high = jnp.where(here, jnp.broadcast_to(source(f, cx + big, cy + 8, 1), (8, 128)), high)
            total = jnp.where(part == big, pick(source(f, cx + big, cy, 8), ends), total)
        v = jnp.where(low_half, pick(low, along_z), pick(high, along_z))
        put(f, 1, jnp.sum(jnp.where(rows_x, v, 0.0), axis=0, keepdims=True))
        put(f, 2, jnp.sum(jnp.where(rows_z, total, 0.0), axis=0, keepdims=True))


def plan_settle(corners, new, x_face, y_low, y_high, z_low, z_high, weight, index):
    lane = iota((16, 128), 1)
    row = iota((16, 128), 0)

    def one(x, _):
        kind = jnp.zeros((16, 128), I32)
        for c in range(REGIONS):
            cx, cy, cz = corners[c]
            step = x - cx
            inside = jnp.logical_and(step >= 0, step < 8)
            dy = row - cy
            dz = lane - cz
            in_y = jnp.logical_and(dy >= 0, dy < 8)
            in_z = jnp.logical_and(dz >= 0, dz < 8)
            near = jnp.where(dy == -1, 4, jnp.where(dy == 8, 5, 0))
            side = jnp.where(dz == -1, 6, jnp.where(dz == 8, 7, 0))
            plain = jnp.where(inside, 1, jnp.where(step == -1, 2, jnp.where(step == 8, 3, 0)))
            mine = jnp.where(
                jnp.logical_and(in_y, in_z),
                plain,
                jnp.where(inside, jnp.where(in_z, near, jnp.where(in_y, side, 0)), 0),
            )
            ys = jnp.clip(dy, 0, 7)
            zs = jnp.clip(dz, 0, 7)
            lanes = jnp.where(mine < 4, ys * 8 + zs, 32 + 8 * mine + jnp.where(mine < 6, zs, ys))
            used = mine > 0
            kind = jnp.where(used, mine, kind)
            index[x, c] = jnp.where(used, lanes + 128, 0)
        factor = jnp.where(kind < 2, 0.0, jnp.where(kind % 2 == 0, -COURANT, COURANT))
        weight[x] = jnp.where(kind == 1, 0.125, 0.0625 * factor)
        for f in range(FIELDS):
            flux = jnp.where(
                kind < 4,
                jnp.where(kind == 2, x_face[f, x + 1], x_face[f, x]),
                jnp.where(
                    kind < 6,
                    jnp.where(kind == 4, y_high[f, x], y_low[f, x]),
                    jnp.where(kind == 6, z_high[f, x], z_low[f, x]),
                ),
            )
            plain = new[f, x]
            ring = jnp.where(kind >= 2, plain - 0.5 * factor * flux, plain)
            new[f, x] = jnp.where(kind == 1, 0.0, ring)
        return 0

    lax.fori_loop(0, 16, one, 0)


def settle_rows(sums, faces, rows):
    lane = iota((REGIONS, 128), 1)
    spot = ((lane % 16) // 8) * 64 + lane % 8
    results = []
    for f in range(FIELDS):
        tx, ty, tz = faces[3 * f], faces[3 * f + 1], faces[3 * f + 2]
        results.append((f, 0, tx))
        results.append((f, 9, pltpu.roll(tx, 64, 1)))
        for group in range(4):
            cells = sums[4 * f + group] + (0.5 * COURANT) * through(tx, ty, tz, group)
            for sub in range(2):
                big = 2 * group + sub
                around = jnp.where(lane < 80, pick(ty, spot + 8 * big), pick(tz, spot + 8 * big))
                mine = pltpu.roll(cells, 64, 1) if sub else cells
                results.append((f, 1 + big, jnp.where(lane < 64, mine, around)))
    for f, where, v in results:
        rows[f, where] = v


def settle(corners, rows, new, weight, index, out, start):
    def one(step, _):
        x = start + step
        values = [jnp.zeros((16, 128), F32) for _ in range(FIELDS)]
        for c in range(REGIONS):
            which = jnp.clip(x - corners[c][0] + 1, 0, 9)
            lanes = index[x, c]
            used = lanes >= 128
            lanes = lanes & 127
            for f in range(FIELDS):
                line = jnp.broadcast_to(rows[f, which, c : c + 1, :], (16, 128))
                values[f] = jnp.where(used, pick(line, lanes), values[f])
        factor = weight[x]
        results = [new[f, x] + factor * values[f] for f in range(FIELDS)]
        for f in range(FIELDS):
            out[f, x] = results[f][:, :64]
        return 0

    lax.fori_loop(0, 8, one, 0, unroll=SETTLE_UNROLL)


def whole(
    sizes,
    parent_hbm,
    plane_hbm,
    corner_hbm,
    coarse_hbm,
    fine_hbm,
    coarse_out,
    fine_out,
    parent_ref,
    corner_ref,
    plane_ref,
    coarse_ref,
    block,
    new,
    x_face,
    y_low,
    y_high,
    z_low,
    z_high,
    weight,
    index,
    y_stage,
    z_stage,
    x_rim,
    y_rim,
    z_rim,
    cut,
    rim_out,
    rim_in_old,
    rim_in_mid,
    rim,
    fine_ref,
    prim,
    half,
    fine_new,
    coarse_new,
    reg,
    route,
    relay_in,
    relay_out,
    sums,
    sums_in,
    row_stage,
    face_out,
    face_in,
    faces,
    answer_rows,
    table,
    load_sems,
    halo_send,
    halo_recv,
    many_send,
    many_recv,
):
    n_gx, n_gy, n_gz = sizes
    members = n_gy * n_gz
    share = -(-4 * FIELDS // members)
    relays = -(-4 * FIELDS // share)
    rim_in = (rim_in_old, rim_in_mid)
    gx = lax.axis_index("gx")
    gy = lax.axis_index("gy")
    gz = lax.axis_index("gz")
    within = gy * n_gz + gz
    myself = gx * members + within
    start = gx * (members * BOXMAX)

    def hops(move):
        return min(move[0], n_gy - move[0]) + min(move[1], n_gz - move[1])

    moves = [(dy, dz) for dy in range(n_gy) for dz in range(n_gz) if dy or dz]
    peers = []
    for dy, dz in sorted(moves, key=hops, reverse=True):
        other_y = lax.rem(gy + dy, n_gy)
        other_z = lax.rem(gz + dz, n_gz)
        peers.append((other_y * n_gz + other_z, (gx, other_y, other_z)))

    barrier = pltpu.get_barrier_semaphore()
    for _, device in peers:
        pl.semaphore_signal(barrier, inc=1, device_id=device, device_id_type=MESH)

    x_next = (lax.rem(gx + 1, n_gx), gy, gz)
    x_prev = (lax.rem(gx + n_gx - 1, n_gx), gy, gz)
    y_next = (gx, lax.rem(gy + 1, n_gy), gz)
    y_prev = (gx, lax.rem(gy + n_gy - 1, n_gy), gz)
    z_next = (gx, gy, lax.rem(gz + 1, n_gz))
    z_prev = (gx, gy, lax.rem(gz + n_gz - 1, n_gz))
    pl.semaphore_signal(barrier, inc=1, device_id=x_next, device_id_type=MESH)
    pl.semaphore_signal(barrier, inc=1, device_id=x_prev, device_id_type=MESH)

    def fetch(src, dst, index):
        copy = pltpu.make_async_copy(src, dst, load_sems.at[index])
        copy.start()
        return copy

    coarse_load = fetch(coarse_hbm, coarse_ref, 0)
    parent_load = fetch(parent_hbm, parent_ref, 1)
    corner_load = fetch(corner_hbm, corner_ref, 2)
    plane_load = fetch(plane_hbm, plane_ref, 3)
    fine_load = fetch(fine_hbm, fine_ref, 4)

    parent_load.wait()
    corner_load.wait()

    def scan(entry, found):
        c0, c1, c2, c3 = found
        hit = parent_ref[start + entry] == myself
        return (
            jnp.where(hit, c1, c0),
            jnp.where(hit, c2, c1),
            jnp.where(hit, c3, c2),
            jnp.where(hit, entry, c3),
        )

    zero = jnp.int32(0)
    children = lax.fori_loop(0, members * BOXMAX, scan, (zero, zero, zero, zero), unroll=8)
    for c in range(REGIONS):
        for k in range(3):
            table[4 * c + k] = jnp.clip(corner_ref[k, start + children[c]], 1, 55 if k == 2 else 7)
    child_peer = [child // BOXMAX for child in children]
    own = [parent_ref[start + within * BOXMAX + s] for s in range(BOXMAX)]
    own_peer = [lax.rem(jnp.maximum(own[s], 0), members) for s in range(BOXMAX)]

    def look_up(other, _):
        rank = zero
        for c in range(1, REGIONS):
            rank = jnp.where(child_peer[c] == other, c, rank)
        found = zero
        for s in range(BOXMAX):
            found = jnp.where(jnp.logical_and(own[s] >= 0, own_peer[s] == other), s, found)
        table[32 + other] = rank
        table[32 + members + other] = found
        return 0

    lax.fori_loop(0, members, look_up, 0, unroll=4)

    def cut_all(when, source):
        def one(c, _):
            corner = (table[4 * c], table[4 * c + 1], table[4 * c + 2])

            def put(f, v, line):
                cut[when, c, 3 * f + v : 3 * f + v + 1, :] = line

            cut_rims(source, corner, put)
            return 0

        lax.fori_loop(0, REGIONS, one, 0, unroll=CUT_UNROLL)

    def ship(src, dst, index, device):
        pltpu.make_async_remote_copy(
            src_ref=src,
            dst_ref=dst,
            send_sem=many_send.at[index],
            recv_sem=many_recv.at[index],
            device_id=device,
            device_id_type=MESH,
        ).start()

    def wait_many(every, index, semaphores):
        pltpu.make_async_copy(every, every, semaphores.at[index]).wait()

    others = pl.ds(0, members - 1)

    def fill_rims(when):
        def one(other, _):
            rim_out[when, other] = cut[when, table[32 + other]]
            return 0

        lax.fori_loop(0, members, one, 0, unroll=4)
        rim_in[when][within] = rim_out[when, within]

    def send_rims(when):
        for other, device in peers:
            ship(rim_out.at[when, other], rim_in[when].at[within], when, device)

    lane16 = iota((16, 128), 1)
    row16 = iota((16, 128), 0)
    coarse_load.wait()
    for f in range(FIELDS):
        block[f, 1:17, :, 0:64] = coarse_ref[f]
    for f in range(FIELDS):
        y_stage[0, f] = block[f, 1:17, 0, :]
        y_stage[1, f] = block[f, 1:17, 15, :]
        for h in range(2):
            low = jnp.zeros((16, 128), F32)
            high = jnp.zeros((16, 128), F32)
            for x in range(8):
                plane = block[f, 1 + 8 * h + x]
                here = lane16 // 16 == x
                low = jnp.where(here, jnp.broadcast_to(plane[:, 0:1], (16, 128)), low)
                high = jnp.where(here, jnp.broadcast_to(plane[:, 63:64], (16, 128)), high)
            match = row16 == lane16 % 16
            z_stage[0, h, f : f + 1, :] = jnp.sum(
                jnp.where(match, low, 0.0), axis=0, keepdims=True
            )
            z_stage[1, h, f : f + 1, :] = jnp.sum(
                jnp.where(match, high, 0.0), axis=0, keepdims=True
            )

    cut_all(0, lambda f, x, y, n: block[f, x + 1, pl.ds(y, n), :])
    fill_rims(0)

    pl.semaphore_wait(barrier, members + 1)

    def halo(src, dst, index, device):
        copy = pltpu.make_async_remote_copy(
            src_ref=src,
            dst_ref=dst,
            send_sem=halo_send.at[index],
            recv_sem=halo_recv.at[index],
            device_id=device,
            device_id_type=MESH,
        )
        copy.start()
        return copy

    halos = [
        halo(block.at[:, 16], x_rim.at[0], 0, x_next),
        halo(block.at[:, 1], x_rim.at[1], 1, x_prev),
        halo(y_stage.at[1], y_rim.at[0], 2, y_next),
        halo(y_stage.at[0], y_rim.at[1], 3, y_prev),
        halo(z_stage.at[1], z_rim.at[0], 4, z_next),
        halo(z_stage.at[0], z_rim.at[1], 5, z_prev),
    ]

    send_rims(0)

    for v in range(3 * FIELDS):
        reg[v] = jnp.zeros((BOXMAX, 128), F32)

    for copy in halos:
        copy.wait()
    for f in range(FIELDS):
        block[f, 0] = x_rim[0, f]
        block[f, 17] = x_rim[1, f]
    coarse_step(block, y_rim, z_rim, new, x_face, y_low, y_high, z_low, z_high)
    cut_all(
        1,
        lambda f, x, y, n: 0.5 * (block[f, x + 1, pl.ds(y, n), :] + new[f, x, pl.ds(y, n), :]),
    )
    fill_rims(1)
    send_rims(1)

    plane_load.wait()
    n_rows = REGIONS * members
    columns = members * BOXMAX
    row = iota((n_rows, columns), 0)
    column = iota((n_rows, columns), 1)
    slots = plane_ref[pl.ds(gx * (columns // 128), columns // 128), :] if columns >= 128 else None
    if columns >= 128:
        slots = jnp.concatenate(
            [
                jnp.broadcast_to(slots[h : h + 1, :], (n_rows, 128))
                for h in range(columns // 128)
            ],
            axis=1,
        )
    else:
        slots = jnp.broadcast_to(plane_ref[0:1, 0:columns], (n_rows, columns))
    number = column.astype(F32)
    far = 65536.0
    candidate = jnp.where(slots == row // REGIONS + gx * members, number, far)
    chosen = jnp.full((n_rows, 1), far)
    for r in range(REGIONS):
        least = jnp.min(candidate, axis=1, keepdims=True)
        chosen = jnp.where(row[:, 0:1] % REGIONS == r, least, chosen)
        candidate = jnp.where(candidate == least, far, candidate)
    route[...] = jnp.where(number == chosen, 1.0, 0.0)

    fine_load.wait()
    fine_prims(fine_ref, prim)
    fine_inner(fine_ref, prim, half)

    sub = iota((BOXMAX, 128), 0)
    owner = jnp.zeros((BOXMAX, 128), I32)
    for s in range(BOXMAX):
        owner = jnp.where(sub == s, own[s], owner)
    filled = owner >= 0

    def take_rims(when):
        wait_many(rim_in[when].at[others], when, many_recv)
        for s in range(BOXMAX):
            rows = rim_in[when][own_peer[s]]
            for v in range(3 * FIELDS):
                rim[v, s : s + 1, :] = rows[v : v + 1, :]

    take_rims(0)
    fine_outer(fine_ref, prim, rim, reg, filled, half, None)
    fine_prims(half, prim)
    fine_inner(half, prim, fine_new)
    fine_average(fine_new, reg, filled, sums)

    is_relay = within < relays
    for other, device in peers:

        @pl.when(other < relays)
        def _(other=other, device=device):
            ship(sums.at[pl.ds(other * share, share)], relay_in.at[within], 2, device)

    @pl.when(is_relay)
    def _():
        relay_in[within] = sums[pl.ds(within * share, share)]

    take_rims(1)
    fine_outer(half, prim, rim, reg, filled, fine_new, fine_ref)
    fine_store = fetch(fine_new, fine_out, 5)

    for s in range(BOXMAX):
        row_stage[s] = reg[:, s, :]
    for other, device in peers:
        face_out[other] = row_stage[table[32 + members + other]]
        ship(face_out.at[other], face_in.at[within], 3, device)
    face_in[within] = row_stage[table[32 + members + within]]

    @pl.when(is_relay)
    def _():
        wait_many(relay_in.at[others], 2, many_recv)
        for j in range(share):
            sorted_rows = jnp.dot(
                route[...],
                relay_in[:, j].reshape(columns, 128),
                precision=lax.Precision.HIGHEST,
                preferred_element_type=F32,
            )
            for p in range(members):
                relay_out[p, j] = sorted_rows[REGIONS * p : REGIONS * p + REGIONS]
        for other, device in peers:
            ship(relay_out.at[other], sums_in.at[pl.ds(within * share, share)], 4, device)
        sums_in[pl.ds(within * share, share)] = relay_out[within]

    corners = [(table[4 * c], table[4 * c + 1], table[4 * c + 2]) for c in range(REGIONS)]
    plan_settle(corners, new, x_face, y_low, y_high, z_low, z_high, weight, index)

    wait_many(face_in.at[others], 3, many_recv)
    for c in range(REGIONS):
        rows = face_in[child_peer[c]]
        for v in range(3 * FIELDS):
            faces[v, c : c + 1, :] = rows[v : v + 1, :]

    def wait_relays(every, index, semaphores):
        @pl.when(is_relay)
        def _():
            wait_many(every.at[pl.ds(0, (relays - 1) * share)], index, semaphores)

        @pl.when(jnp.logical_not(is_relay))
        def _():
            wait_many(every.at[pl.ds(0, relays * share)], index, semaphores)

    wait_relays(sums_in, 4, many_recv)
    settle_rows(sums_in, faces, answer_rows)
    coarse_stores = []
    for part in range(2):
        settle(corners, answer_rows, new, weight, index, coarse_new, 8 * part)
        planes = pl.ds(8 * part, 8)
        coarse_stores.append(fetch(coarse_new.at[:, planes], coarse_out.at[:, planes], 6 + part))
    wait_many(rim_out.at[0, others], 0, many_send)
    wait_many(rim_out.at[1, others], 1, many_send)
    wait_relays(sums, 2, many_send)
    wait_many(face_out.at[others], 3, many_send)

    @pl.when(is_relay)
    def _():
        wait_many(relay_out.at[others], 4, many_send)

    fine_store.wait()
    for copy in coarse_stores:
        copy.wait()


def hand_over(coarse_in, fine_in, coarse_out, fine_out, coarse_held, fine_held, arrive, leave):
    moves = []
    for f in range(FIELDS):
        for n, (src, held, dst) in enumerate(
            ((coarse_in, coarse_held, coarse_out), (fine_in, fine_held, fine_out))
        ):
            first = pltpu.make_async_copy(src.at[f], held.at[f], arrive.at[2 * f + n])
            first.start()
            moves.append((first, pltpu.make_async_copy(held.at[f], dst.at[f], leave.at[2 * f + n])))
    for first, second in moves:
        first.wait()
        second.start()
    for _, second in moves:
        second.wait()


def on_device(sizes, coarse_state, fine_state, slot_parent, slot_corner):
    members = sizes[1] * sizes[2]
    share = -(-4 * FIELDS // members)
    relays = -(-4 * FIELDS // share)
    hbm = pl.BlockSpec(memory_space=pltpu.HBM)
    fine = jnp.transpose(fine_state, (1, 0, 2))
    corner = jnp.transpose(slot_corner, (1, 0))
    plane = slot_parent.reshape(-1, min(128, slot_parent.shape[0]))
    field_block = (FIELDS, 16, 16, 128)
    rows = 3 * FIELDS
    coarse_next, fine_next = pl.pallas_call(
        functools.partial(whole, sizes),
        out_shape=(
            jax.ShapeDtypeStruct(coarse_state.shape, F32),
            jax.ShapeDtypeStruct(fine.shape, F32),
        ),
        in_specs=[hbm] * 5,
        out_specs=(hbm, hbm),
        scratch_shapes=[
            pltpu.SMEM(slot_parent.shape, I32),
            pltpu.SMEM(corner.shape, I32),
            pltpu.VMEM(plane.shape, I32),
            pltpu.VMEM(coarse_state.shape, F32),
            pltpu.VMEM((FIELDS, 18, 16, 128), F32),
            pltpu.VMEM(field_block, F32),
            pltpu.VMEM((FIELDS, 17, 16, 128), F32),
            pltpu.VMEM(field_block, F32),
            pltpu.VMEM(field_block, F32),
            pltpu.VMEM(field_block, F32),
            pltpu.VMEM(field_block, F32),
            pltpu.VMEM((16, 16, 128), F32),
            pltpu.VMEM((16, REGIONS, 16, 128), I32),
            pltpu.VMEM((2, FIELDS, 16, 128), F32),
            pltpu.VMEM((2, 2, FIELDS, 128), F32),
            pltpu.VMEM((2, FIELDS, 16, 128), F32),
            pltpu.VMEM((2, FIELDS, 16, 128), F32),
            pltpu.VMEM((2, 2, FIELDS, 128), F32),
            pltpu.VMEM((2, REGIONS, 3 * FIELDS, 128), F32),
            pltpu.VMEM((2, members, 3 * FIELDS, 128), F32),
            pltpu.VMEM((members, 3 * FIELDS, 128), F32),
            pltpu.VMEM((members, 3 * FIELDS, 128), F32),
            pltpu.VMEM((3 * FIELDS, BOXMAX, 128), F32),
            pltpu.VMEM(fine.shape, F32),
            pltpu.VMEM((3,) + fine.shape[1:], F32),
            pltpu.VMEM(fine.shape, F32),
            pltpu.VMEM(fine.shape, F32),
            pltpu.VMEM(coarse_state.shape, F32),
            pltpu.VMEM((rows, BOXMAX, 128), F32),
            pltpu.VMEM((REGIONS * members, BOXMAX * members), F32),
            pltpu.VMEM((members, share, BOXMAX, 128), F32),
            pltpu.VMEM((members, share, REGIONS, 128), F32),
            pltpu.VMEM((relays * share, BOXMAX, 128), F32),
            pltpu.VMEM((relays * share, REGIONS, 128), F32),
            pltpu.VMEM((BOXMAX, rows, 128), F32),
            pltpu.VMEM((members, rows, 128), F32),
            pltpu.VMEM((members, rows, 128), F32),
            pltpu.VMEM((rows, REGIONS, 128), F32),
            pltpu.VMEM((FIELDS, 10, REGIONS, 128), F32),
            pltpu.SMEM((32 + 2 * members,), I32),
            pltpu.SemaphoreType.DMA((8,)),
            pltpu.SemaphoreType.DMA((6,)),
            pltpu.SemaphoreType.DMA((6,)),
            pltpu.SemaphoreType.DMA((5,)),
            pltpu.SemaphoreType.DMA((5,)),
        ],
        compiler_params=pltpu.CompilerParams(
            collective_id=0, has_side_effects=True, vmem_limit_bytes=62 * 1024 * 1024
        ),
    )(slot_parent, plane, corner, coarse_state, fine)
    coarse_next, fine_next = pl.pallas_call(
        hand_over,
        out_shape=(
            jax.ShapeDtypeStruct(coarse_state.shape, F32),
            jax.ShapeDtypeStruct(fine.shape, F32),
        ),
        in_specs=[hbm] * 2,
        out_specs=(hbm, hbm),
        scratch_shapes=[
            pltpu.VMEM(coarse_state.shape, F32),
            pltpu.VMEM(fine.shape, F32),
            pltpu.SemaphoreType.DMA((2 * FIELDS,)),
            pltpu.SemaphoreType.DMA((2 * FIELDS,)),
        ],
        compiler_params=pltpu.CompilerParams(vmem_limit_bytes=62 * 1024 * 1024),
    )(coarse_next, fine_next)
    return coarse_next, jnp.transpose(fine_next, (1, 0, 2))


def solution(mesh):
    sizes = tuple(mesh.shape[name] for name in ("gx", "gy", "gz"))
    return jax.shard_map(
        functools.partial(on_device, sizes),
        mesh=mesh,
        in_specs=(P(None, "gx", "gy", "gz"), P(("gx", "gy", "gz"), None, None), P(), P()),
        out_specs=(P(None, "gx", "gy", "gz"), P(("gx", "gy", "gz"), None, None)),
        check_vma=False,
    )
```

```python
import functools

import jax
import jax.numpy as jnp
from jax import lax
from jax.experimental import pallas as pl
from jax.experimental.pallas import tpu as pltpu
from jax.sharding import PartitionSpec as P

GAMMA = 1.4
COURANT = 0.04
PRIM_UNROLL = 2
X_UNROLL = 15
YZ_UNROLL = 2
OUTER_UNROLL = 4
COARSE_UNROLL = 4
CUT_UNROLL = 4
SETTLE_UNROLL = 8
FIELDS = 5
REGIONS = 4
BOXMAX = 8
MESH = pl.DeviceIdType.MESH
F32 = jnp.float32
I32 = jnp.int32


def iota(shape, dim):
    return lax.broadcasted_iota(I32, shape, dim)


def pick(values, lanes):
    numbers = lax.GatherDimensionNumbers(
        offset_dims=(),
        collapsed_slice_dims=(1,),
        start_index_map=(1,),
        operand_batching_dims=(0,),
        start_indices_batching_dims=(0,),
    )
    return lax.gather(
        values,
        lanes[..., None],
        numbers,
        (1, 1),
        mode=lax.GatherScatterMode.PROMISE_IN_BOUNDS,
    )


def prims(q):
    inverse = pl.reciprocal(q[0], approx=True)
    inverse = inverse * (2.0 - q[0] * inverse)
    kinetic = 0.5 * (q[1] * q[1] + q[2] * q[2] + q[3] * q[3]) * inverse
    pressure = (GAMMA - 1.0) * (q[4] - kinetic)
    square = GAMMA * pressure * inverse
    sound = square * lax.rsqrt(jnp.maximum(square, 1e-30))
    return inverse, pressure, sound, q[4] + pressure


def along(q, prim, axis):
    inverse, pressure, sound, total = prim
    velocity = q[1 + axis] * inverse
    flux = [q[1 + axis], q[1] * velocity, q[2] * velocity, q[3] * velocity, total * velocity]
    flux[1 + axis] = flux[1 + axis] + pressure
    return flux, jnp.abs(velocity) + sound


def face(low, low_terms, high, high_terms):
    signal = jnp.maximum(low_terms[1], high_terms[1])
    return [
        (low_terms[0][f] + high_terms[0][f]) - signal * (high[f] - low[f]) for f in range(FIELDS)
    ]


def moved(q, terms, move):
    return [move(v) for v in q], [move(v) for v in terms[0]], move(terms[1])


def span(plane, h):
    return pl.ds(pl.multiple_of(plane * 256 + h * 128, 128), 128)


def roll(v, by):
    return pltpu.roll(v, by % 128, 1)


def fine_prims(cells, prim):
    def one(plane, _):
        for h in range(2):
            where = span(plane, h)
            inverse, pressure, sound, _ = prims([cells[f, :, where] for f in range(FIELDS)])
            prim[0, :, where] = inverse
            prim[1, :, where] = pressure
            prim[2, :, where] = sound
        return 0

    lax.fori_loop(0, 16, one, 0, unroll=PRIM_UNROLL)


def fine_inner(cells, prim, out):
    lane = iota((BOXMAX, 128), 1)
    first_row = lane < 16
    last_row = lane >= 112
    k_first = lane % 16 == 0

    def load(plane, h):
        where = span(plane, h)
        q = [cells[f, :, where] for f in range(FIELDS)]
        pressure = prim[1, :, where]
        return q, (prim[0, :, where], pressure, prim[2, :, where], q[4] + pressure)

    def x_one(plane, low):
        here = [load(plane, h) for h in range(2)]
        after = [load(plane + 1, h) for h in range(2)]
        high = [
            face(
                here[h][0],
                along(here[h][0], here[h][1], 0),
                after[h][0],
                along(after[h][0], after[h][1], 0),
            )
            for h in range(2)
        ]
        for h in range(2):
            for f in range(FIELDS):
                new = here[h][0][f] - (0.5 * COURANT) * (high[h][f] - low[h][f])
                out[f, :, span(plane, h)] = new
        return high

    none = [[jnp.zeros((BOXMAX, 128), F32)] * FIELDS] * 2
    high = lax.fori_loop(0, 15, x_one, none, unroll=X_UNROLL)
    for h in range(2):
        for f in range(FIELDS):
            out[f, :, span(15, h)] = cells[f, :, span(15, h)] + (0.5 * COURANT) * high[h][f]

    def yz_one(plane, _):
        cell = [load(plane, h) for h in range(2)]
        partial = [[out[f, :, span(plane, h)] for f in range(FIELDS)] for h in range(2)]
        for h in range(2):
            q, q_prim = cell[h]
            terms = along(q, q_prim, 2)
            shifted = moved(q, terms, lambda v: roll(v, 1))
            z = face(shifted[0], (shifted[1], shifted[2]), q, terms)
            for f in range(FIELDS):
                low = jnp.where(k_first, 0.0, z[f])
                partial[h][f] = partial[h][f] - (0.5 * COURANT) * (roll(low, -1) - low)
        q0, prim0 = cell[0]
        q1, prim1 = cell[1]
        terms0 = along(q0, prim0, 1)
        terms1 = along(q1, prim1, 1)
        shifted0 = moved(q0, terms0, lambda v: roll(v, 16))
        shifted1 = moved(q1, terms1, lambda v: roll(v, 16))

        def seam(low, high):
            return jnp.where(first_row, low, high)

        low1 = (
            [seam(shifted0[0][f], shifted1[0][f]) for f in range(FIELDS)],
            (
                [seam(shifted0[1][f], shifted1[1][f]) for f in range(FIELDS)],
                seam(shifted0[2], shifted1[2]),
            ),
        )
        y0 = face(shifted0[0], (shifted0[1], shifted0[2]), q0, terms0)
        y1 = face(low1[0], low1[1], q1, terms1)
        for f in range(FIELDS):
            low = jnp.where(first_row, 0.0, y0[f])
            up0 = roll(low, -16)
            up1 = roll(y1[f], -16)
            change0 = jnp.where(last_row, up1, up0) - low
            change1 = jnp.where(last_row, up0, up1) - y1[f]
            partial[0][f] = partial[0][f] - (0.5 * COURANT) * change0
            partial[1][f] = partial[1][f] - (0.5 * COURANT) * change1
        for h in range(2):
            for f in range(FIELDS):
                out[f, :, span(plane, h)] = partial[h][f]
        return 0

    lax.fori_loop(0, 16, yz_one, 0, unroll=YZ_UNROLL)


def fine_outer(cells, prim, rim, reg, filled, out, old):
    second = old is not None
    lane = iota((BOXMAX, 128), 1)
    k = lane % 16
    half_k = k // 2
    quarter = lane // 32
    squeeze = ((lane % 32) // 8) * 32 + (lane % 8) * 2
    part = (lane % 64) // 8
    low_half = lane < 64
    step = 0.5 * COURANT
    y_sign = jnp.where(low_half, 1.0, -1.0)
    z_sign = jnp.where(k < 8, 1.0, -1.0)
    y_weight = (jnp.where(lane < 16, step, 0.0), jnp.where(lane >= 112, -step, 0.0))
    z_weight = jnp.where(k == 0, step, jnp.where(k == 15, -step, 0.0))

    def load(plane, h):
        where = span(plane, h)
        q = [cells[f, :, where] for f in range(FIELDS)]
        pressure = prim[1, :, where]
        return q, (prim[0, :, where], pressure, prim[2, :, where], q[4] + pressure)

    def edge(ghost, ghost_terms, q, terms, sign):
        signal = jnp.maximum(ghost_terms[1], terms[1]) * sign
        return [
            (ghost_terms[0][f] + terms[0][f]) - signal * (q[f] - ghost[f]) for f in range(FIELDS)
        ]

    results = []
    for plane, side, sign in ((0, 0, 1.0), (15, 64, -1.0)):
        flux = []
        for h in range(2):
            spread = (h * 4 + quarter) * 8 + half_k + side
            ghost = [pick(rim[3 * f], spread) for f in range(FIELDS)]
            q, q_prim = load(plane, h)
            flux.append(edge(ghost, along(ghost, prims(ghost), 0), q, along(q, q_prim, 0), sign))
            results.append(
                [out[f, :, span(plane, h)] + (sign * step) * flux[h][f] for f in range(FIELDS)]
            )
        for f in range(FIELDS):
            found = []
            for h in range(2):
                v = flux[h][f]
                v = v + roll(v, -1)
                v = v + roll(v, -16)
                found.append(pick(v, squeeze))
            results.append(jnp.where((lane % 64) < 32, found[0], found[1]))
    for plane, first in ((0, 0), (15, 2 + FIELDS)):
        for h in range(2):
            for f in range(FIELDS):
                out[f, :, span(plane, h)] = results[first + h][f]
    for f in range(FIELDS):
        v = jnp.where(low_half, results[2 + f], results[4 + FIELDS + f])
        reg[3 * f] = reg[3 * f] + jnp.where(filled, v, 0.0)

    def pair(big, _):
        y_lanes = big * 8 + half_k + jnp.where(low_half, 0, 64)
        y_ghost = [pick(rim[3 * f + 1], y_lanes) for f in range(FIELDS)]
        y_ghost_terms = along(y_ghost, prims(y_ghost), 1)
        z_ghost = []
        z_ghost_terms = []
        for h in range(2):
            z_lanes = big * 8 + h * 4 + quarter + jnp.where(k >= 8, 64, 0)
            ghost = [pick(rim[3 * f + 2], z_lanes) for f in range(FIELDS)]
            z_ghost.append(ghost)
            z_ghost_terms.append(along(ghost, prims(ghost), 2))
        y_sum = [None] * FIELDS
        z_sum = [[None] * FIELDS for _ in range(2)]

        def accumulate(total, v):
            return v if total is None else total + v

        for sub in range(2):
            plane = 2 * big + sub
            q, q_prim = zip(*[load(plane, h) for h in range(2)])
            near = [jnp.where(low_half, q[0][f], q[1][f]) for f in range(FIELDS)]
            near_prim = [jnp.where(low_half, q_prim[0][i], q_prim[1][i]) for i in range(4)]
            before = [[out[f, :, span(plane, h)] for f in range(FIELDS)] for h in range(2)]
            if second:
                kept = [[old[f, :, span(plane, h)] for f in range(FIELDS)] for h in range(2)]
            y = edge(y_ghost, y_ghost_terms, near, along(near, near_prim, 1), y_sign)
            for f in range(FIELDS):
                y_sum[f] = accumulate(y_sum[f], y[f])
            news = []
            for h in range(2):
                z = edge(z_ghost[h], z_ghost_terms[h], q[h], along(q[h], q_prim[h], 2), z_sign)
                for f in range(FIELDS):
                    z_sum[h][f] = accumulate(z_sum[h][f], z[f])
                    new = before[h][f] + y_weight[h] * y[f] + z_weight * z[f]
                    if second:
                        new = jnp.where(filled, new, kept[h][f])
                    news.append((f, h, new))
            for f, h, new in news:
                out[f, :, span(plane, h)] = new

        mine = jnp.logical_and(filled, part == big)
        y_from = (lane % 8) * 2 + jnp.where(low_half, 0, 112)
        z_from = (lane % 4) * 32 + jnp.where(low_half, 0, 15)
        old_regs = [[reg[3 * f + t] for t in (1, 2)] for f in range(FIELDS)]
        for f in range(FIELDS):
            v = y_sum[f] + roll(y_sum[f], -1)
            old_regs[f][0] = old_regs[f][0] + jnp.where(mine, pick(v, y_from), 0.0)
            found = []
            for h in range(2):
                v = z_sum[h][f] + roll(z_sum[h][f], -16)
                found.append(pick(v, z_from))
            v = jnp.where(lane % 8 < 4, found[0], found[1])
            old_regs[f][1] = old_regs[f][1] + jnp.where(mine, v, 0.0)
        for f in range(FIELDS):
            for t in (1, 2):
                reg[3 * f + t] = old_regs[f][t - 1]
        return 0

    lax.fori_loop(0, 8, pair, 0, unroll=OUTER_UNROLL)


def through(tx, ty, tz, group):
    lane = iota(tx.shape, 1)
    x = 2 * group + lane // 64
    y = (lane % 64) // 8
    z = lane % 8

    def sign(place):
        return jnp.where(place == 0, 1.0, jnp.where(place == 7, -1.0, 0.0))

    total = sign(y) * pick(ty, x * 8 + z + jnp.where(y == 7, 64, 0))
    total = total + sign(z) * pick(tz, x * 8 + y + jnp.where(z == 7, 64, 0))
    if group == 0:
        total = total + jnp.where(lane < 64, tx, 0.0)
    if group == 3:
        total = total - jnp.where(lane < 64, 0.0, tx)
    return total


def fine_average(cells, reg, filled, sums):
    lane = iota((BOXMAX, 128), 1)
    squeeze = ((lane % 32) // 8) * 32 + (lane % 8) * 2
    faces = [reg[v] for v in range(3 * FIELDS)]
    for group in range(4):
        tiles = []
        for f in range(FIELDS):
            for sub in range(2):
                for h in range(2):
                    plane = 4 * group + 2 * sub
                    tiles.append(cells[f, :, span(plane, h)] + cells[f, :, span(plane + 1, h)])
        tiles = [v + roll(v, -1) for v in tiles]
        tiles = [v + roll(v, -16) for v in tiles]
        tiles = [pick(v, squeeze) for v in tiles]
        crossed = [through(*faces[3 * f : 3 * f + 3], group) for f in range(FIELDS)]
        results = []
        for f in range(FIELDS):
            low = jnp.where(lane < 32, tiles[4 * f], tiles[4 * f + 1])
            high = jnp.where(lane < 96, tiles[4 * f + 2], tiles[4 * f + 3])
            v = jnp.where(lane < 64, low, high) - (0.5 * COURANT) * crossed[f]
            results.append(jnp.where(filled, v, 0.0))
        for f in range(FIELDS):
            sums[4 * f + group] = results[f]


def coarse_step(block, y_rim, z_rim, new, x_face, y_low, y_high, z_low, z_high):
    lane = iota((16, 128), 1)
    row = iota((16, 128), 0)
    tip = iota((8, 128), 0)

    def load(plane):
        return [block[f, plane] for f in range(FIELDS)]

    def widen(x, _):
        column = (x % 8) * 16 + row
        for f in range(FIELDS):
            below = jnp.broadcast_to(z_rim[0, x // 8, f : f + 1, :], (16, 128))
            above = jnp.broadcast_to(z_rim[1, x // 8, f : f + 1, :], (16, 128))
            side = jnp.where(lane == 64, pick(above, column), pick(below, column))
            block[f, x + 1] = jnp.where(lane < 64, block[f, x + 1], side)
        return 0

    lax.fori_loop(0, 16, widen, 0, unroll=4)

    ghost = load(0)
    here = load(1)
    here_prim = prims(here)
    low = face(ghost, along(ghost, prims(ghost), 0), here, along(here, here_prim, 0))
    for f in range(FIELDS):
        x_face[f, 0] = low[f]

    def one(x, carried):
        here, here_prim, x_low = carried
        after = load(x + 2)
        after_prim = prims(after)
        x_high = face(here, along(here, here_prim, 0), after, along(after, after_prim, 0))

        tips = []
        for f in range(FIELDS):
            above = y_rim[1, f, pl.ds(x, 1), :]
            below = y_rim[0, f, pl.ds(x, 1), :]
            tips.append(
                jnp.where(
                    tip == 0,
                    jnp.broadcast_to(above, (8, 128)),
                    jnp.broadcast_to(below, (8, 128)),
                )
            )
        tip_terms = along(tips, prims(tips), 1)
        terms = along(here, here_prim, 1)

        def tall(low, high):
            return jnp.concatenate([low, high], axis=0)

        cells = [tall(here[f], tips[f]) for f in range(FIELDS)]
        terms = ([tall(terms[0][f], tip_terms[0][f]) for f in range(FIELDS)], tall(terms[1], tip_terms[1]))
        shifted = moved(cells, terms, lambda v: pltpu.roll(v, 1, 0))
        y = face(shifted[0], (shifted[1], shifted[2]), cells, terms)

        terms = along(here, here_prim, 2)
        shifted = moved(here, terms, lambda v: pltpu.roll(v, 1, 1))
        z = face(shifted[0], (shifted[1], shifted[2]), here, terms)
        for f in range(FIELDS):
            up = pltpu.roll(y[f], 23, 0)[:16]
            down = y[f][:16]
            right = pltpu.roll(z[f], 127, 1)
            x_face[f, x + 1] = x_high[f]
            y_low[f, x] = down
            y_high[f, x] = up
            z_low[f, x] = z[f]
            z_high[f, x] = right
            change = (x_high[f] - x_low[f]) + (up - down) + (right - z[f])
            new[f, x] = here[f] - (0.5 * COURANT) * change
        return after, after_prim, x_high

    lax.fori_loop(0, 16, one, (here, here_prim, low), unroll=COARSE_UNROLL)


def cut_rims(source, corner, put):
    cx, cy, cz = corner
    lane = iota((8, 128), 1)
    row = iota((8, 128), 0)
    low_half = lane < 64
    part = (lane % 64) // 8
    along_z = cz + lane % 8
    ends = jnp.where(low_half, cz - 1, cz + 8)
    rows_x = row == part
    rows_z = row == lane % 8
    for f in range(FIELDS):
        low = pick(source(f, cx - 1, cy, 8), along_z)
        high = pick(source(f, cx + 8, cy, 8), along_z)
        v = jnp.where(rows_x, jnp.where(low_half, low, high), 0.0)
        put(f, 0, jnp.sum(v, axis=0, keepdims=True))
        low = jnp.zeros((8, 128), F32)
        high = jnp.zeros((8, 128), F32)
        total = jnp.zeros((8, 128), F32)
        for big in range(8):
            here = row == big
            low = jnp.where(here, jnp.broadcast_to(source(f, cx + big, cy - 1, 1), (8, 128)), low)
            high = jnp.where(here, jnp.broadcast_to(source(f, cx + big, cy + 8, 1), (8, 128)), high)
            total = jnp.where(part == big, pick(source(f, cx + big, cy, 8), ends), total)
        v = jnp.where(low_half, pick(low, along_z), pick(high, along_z))
        put(f, 1, jnp.sum(jnp.where(rows_x, v, 0.0), axis=0, keepdims=True))
        put(f, 2, jnp.sum(jnp.where(rows_z, total, 0.0), axis=0, keepdims=True))


def plan_settle(corners, new, x_face, y_low, y_high, z_low, z_high, weight, index):
    lane = iota((16, 128), 1)
    row = iota((16, 128), 0)

    def one(x, _):
        kind = jnp.zeros((16, 128), I32)
        for c in range(REGIONS):
            cx, cy, cz = corners[c]
            step = x - cx
            inside = jnp.logical_and(step >= 0, step < 8)
            dy = row - cy
            dz = lane - cz
            in_y = jnp.logical_and(dy >= 0, dy < 8)
            in_z = jnp.logical_and(dz >= 0, dz < 8)
            near = jnp.where(dy == -1, 4, jnp.where(dy == 8, 5, 0))
            side = jnp.where(dz == -1, 6, jnp.where(dz == 8, 7, 0))
            plain = jnp.where(inside, 1, jnp.where(step == -1, 2, jnp.where(step == 8, 3, 0)))
            mine = jnp.where(
                jnp.logical_and(in_y, in_z),
                plain,
                jnp.where(inside, jnp.where(in_z, near, jnp.where(in_y, side, 0)), 0),
            )
            ys = jnp.clip(dy, 0, 7)
            zs = jnp.clip(dz, 0, 7)
            lanes = jnp.where(mine < 4, ys * 8 + zs, 32 + 8 * mine + jnp.where(mine < 6, zs, ys))
            used = mine > 0
            kind = jnp.where(used, mine, kind)
            index[x, c] = jnp.where(used, lanes + 128, 0)
        factor = jnp.where(kind < 2, 0.0, jnp.where(kind % 2 == 0, -COURANT, COURANT))
        weight[x] = jnp.where(kind == 1, 0.125, 0.0625 * factor)
        for f in range(FIELDS):
            flux = jnp.where(
                kind < 4,
                jnp.where(kind == 2, x_face[f, x + 1], x_face[f, x]),
                jnp.where(
                    kind < 6,
                    jnp.where(kind == 4, y_high[f, x], y_low[f, x]),
                    jnp.where(kind == 6, z_high[f, x], z_low[f, x]),
                ),
            )
            plain = new[f, x]
            ring = jnp.where(kind >= 2, plain - 0.5 * factor * flux, plain)
            new[f, x] = jnp.where(kind == 1, 0.0, ring)
        return 0

    lax.fori_loop(0, 16, one, 0)


def settle_rows(faces, rows, crossed):
    lane = iota((REGIONS, 128), 1)
    spot = ((lane % 16) // 8) * 64 + lane % 8
    results = []
    added = []
    for f in range(FIELDS):
        tx, ty, tz = faces[3 * f], faces[3 * f + 1], faces[3 * f + 2]
        results.append((f, 0, tx))
        results.append((f, 9, pltpu.roll(tx, 64, 1)))
        for big in range(8):
            around = jnp.where(lane < 80, pick(ty, spot + 8 * big), pick(tz, spot + 8 * big))
            results.append((f, 1 + big, jnp.where(lane < 64, 0.0, around)))
        for group in range(4):
            added.append((0.5 * COURANT) * through(tx, ty, tz, group))
    for f, where, v in results:
        rows[f, where] = v
    for tile, v in enumerate(added):
        crossed[tile] = v


def settle(corners, rows, new, weight, index, out, start):
    def one(step, _):
        x = start + step
        values = [jnp.zeros((16, 128), F32) for _ in range(FIELDS)]
        for c in range(REGIONS):
            which = jnp.clip(x - corners[c][0] + 1, 0, 9)
            lanes = index[x, c]
            used = lanes >= 128
            lanes = lanes & 127
            for f in range(FIELDS):
                line = jnp.broadcast_to(rows[f, which, c : c + 1, :], (16, 128))
                values[f] = jnp.where(used, pick(line, lanes), values[f])
        factor = weight[x]
        results = [new[f, x] + factor * values[f] for f in range(FIELDS)]
        for f in range(FIELDS):
            out[f, x] = results[f][:, :64]
        return 0

    lax.fori_loop(0, 8, one, 0, unroll=SETTLE_UNROLL)


def whole(
    sizes,
    parent_hbm,
    plane_hbm,
    corner_hbm,
    coarse_hbm,
    fine_hbm,
    coarse_out,
    fine_out,
    sums_out,
    spots_out,
    parent_ref,
    corner_ref,
    plane_ref,
    coarse_ref,
    block,
    new,
    x_face,
    y_low,
    y_high,
    z_low,
    z_high,
    weight,
    index,
    y_stage,
    z_stage,
    x_rim,
    y_rim,
    z_rim,
    cut,
    rim_out,
    rim_in_old,
    rim_in_mid,
    rim,
    fine_ref,
    prim,
    half,
    fine_new,
    coarse_new,
    reg,
    route,
    relay_in,
    relay_out,
    sums,
    sums_in,
    row_stage,
    face_out,
    face_in,
    faces,
    answer_rows,
    crossed,
    table,
    spots,
    load_sems,
    halo_send,
    halo_recv,
    many_send,
    many_recv,
):
    n_gx, n_gy, n_gz = sizes
    members = n_gy * n_gz
    share = -(-4 * FIELDS // members)
    relays = -(-4 * FIELDS // share)
    rim_in = (rim_in_old, rim_in_mid)
    gx = lax.axis_index("gx")
    gy = lax.axis_index("gy")
    gz = lax.axis_index("gz")
    within = gy * n_gz + gz
    myself = gx * members + within
    start = gx * (members * BOXMAX)

    def hops(move):
        return min(move[0], n_gy - move[0]) + min(move[1], n_gz - move[1])

    moves = [(dy, dz) for dy in range(n_gy) for dz in range(n_gz) if dy or dz]
    peers = []
    for dy, dz in sorted(moves, key=hops, reverse=True):
        other_y = lax.rem(gy + dy, n_gy)
        other_z = lax.rem(gz + dz, n_gz)
        peers.append((other_y * n_gz + other_z, (gx, other_y, other_z)))

    barrier = pltpu.get_barrier_semaphore()
    for _, device in peers:
        pl.semaphore_signal(barrier, inc=1, device_id=device, device_id_type=MESH)

    x_next = (lax.rem(gx + 1, n_gx), gy, gz)
    x_prev = (lax.rem(gx + n_gx - 1, n_gx), gy, gz)
    y_next = (gx, lax.rem(gy + 1, n_gy), gz)
    y_prev = (gx, lax.rem(gy + n_gy - 1, n_gy), gz)
    z_next = (gx, gy, lax.rem(gz + 1, n_gz))
    z_prev = (gx, gy, lax.rem(gz + n_gz - 1, n_gz))
    pl.semaphore_signal(barrier, inc=1, device_id=x_next, device_id_type=MESH)
    pl.semaphore_signal(barrier, inc=1, device_id=x_prev, device_id_type=MESH)

    def fetch(src, dst, index):
        copy = pltpu.make_async_copy(src, dst, load_sems.at[index])
        copy.start()
        return copy

    coarse_load = fetch(coarse_hbm, coarse_ref, 0)
    parent_load = fetch(parent_hbm, parent_ref, 1)
    corner_load = fetch(corner_hbm, corner_ref, 2)
    plane_load = fetch(plane_hbm, plane_ref, 3)
    fine_load = fetch(fine_hbm, fine_ref, 4)

    parent_load.wait()
    corner_load.wait()

    def scan(entry, found):
        c0, c1, c2, c3 = found
        hit = parent_ref[start + entry] == myself
        return (
            jnp.where(hit, c1, c0),
            jnp.where(hit, c2, c1),
            jnp.where(hit, c3, c2),
            jnp.where(hit, entry, c3),
        )

    zero = jnp.int32(0)
    children = lax.fori_loop(0, members * BOXMAX, scan, (zero, zero, zero, zero), unroll=8)
    for c in range(REGIONS):
        for k in range(3):
            spot = jnp.clip(corner_ref[k, start + children[c]], 1, 55 if k == 2 else 7)
            table[4 * c + k] = spot
            spots[4 * c + k] = spot
        spots[4 * c + 3] = zero
    corner_store = fetch(spots, spots_out, 9)
    child_peer = [child // BOXMAX for child in children]
    own = [parent_ref[start + within * BOXMAX + s] for s in range(BOXMAX)]
    own_peer = [lax.rem(jnp.maximum(own[s], 0), members) for s in range(BOXMAX)]

    def look_up(other, _):
        rank = zero
        for c in range(1, REGIONS):
            rank = jnp.where(child_peer[c] == other, c, rank)
        found = zero
        for s in range(BOXMAX):
            found = jnp.where(jnp.logical_and(own[s] >= 0, own_peer[s] == other), s, found)
        table[32 + other] = rank
        table[32 + members + other] = found
        return 0

    lax.fori_loop(0, members, look_up, 0, unroll=4)

    def cut_all(when, source):
        def one(c, _):
            corner = (table[4 * c], table[4 * c + 1], table[4 * c + 2])

            def put(f, v, line):
                cut[when, c, 3 * f + v : 3 * f + v + 1, :] = line

            cut_rims(source, corner, put)
            return 0

        lax.fori_loop(0, REGIONS, one, 0, unroll=CUT_UNROLL)

    def ship(src, dst, index, device):
        pltpu.make_async_remote_copy(
            src_ref=src,
            dst_ref=dst,
            send_sem=many_send.at[index],
            recv_sem=many_recv.at[index],
            device_id=device,
            device_id_type=MESH,
        ).start()

    def wait_many(every, index, semaphores):
        pltpu.make_async_copy(every, every, semaphores.at[index]).wait()

    others = pl.ds(0, members - 1)

    def fill_rims(when):
        def one(other, _):
            rim_out[when, other] = cut[when, table[32 + other]]
            return 0

        lax.fori_loop(0, members, one, 0, unroll=4)
        rim_in[when][within] = rim_out[when, within]

    def send_rims(when):
        for other, device in peers:
            ship(rim_out.at[when, other], rim_in[when].at[within], when, device)

    lane16 = iota((16, 128), 1)
    row16 = iota((16, 128), 0)
    coarse_load.wait()
    for f in range(FIELDS):
        block[f, 1:17, :, 0:64] = coarse_ref[f]
    for f in range(FIELDS):
        y_stage[0, f] = block[f, 1:17, 0, :]
        y_stage[1, f] = block[f, 1:17, 15, :]
        for h in range(2):
            low = jnp.zeros((16, 128), F32)
            high = jnp.zeros((16, 128), F32)
            for x in range(8):
                plane = block[f, 1 + 8 * h + x]
                here = lane16 // 16 == x
                low = jnp.where(here, jnp.broadcast_to(plane[:, 0:1], (16, 128)), low)
                high = jnp.where(here, jnp.broadcast_to(plane[:, 63:64], (16, 128)), high)
            match = row16 == lane16 % 16
            z_stage[0, h, f : f + 1, :] = jnp.sum(
                jnp.where(match, low, 0.0), axis=0, keepdims=True
            )
            z_stage[1, h, f : f + 1, :] = jnp.sum(
                jnp.where(match, high, 0.0), axis=0, keepdims=True
            )

    cut_all(0, lambda f, x, y, n: block[f, x + 1, pl.ds(y, n), :])
    fill_rims(0)

    pl.semaphore_wait(barrier, members + 1)

    def halo(src, dst, index, device):
        copy = pltpu.make_async_remote_copy(
            src_ref=src,
            dst_ref=dst,
            send_sem=halo_send.at[index],
            recv_sem=halo_recv.at[index],
            device_id=device,
            device_id_type=MESH,
        )
        copy.start()
        return copy

    halos = [
        halo(block.at[:, 16], x_rim.at[0], 0, x_next),
        halo(block.at[:, 1], x_rim.at[1], 1, x_prev),
        halo(y_stage.at[1], y_rim.at[0], 2, y_next),
        halo(y_stage.at[0], y_rim.at[1], 3, y_prev),
        halo(z_stage.at[1], z_rim.at[0], 4, z_next),
        halo(z_stage.at[0], z_rim.at[1], 5, z_prev),
    ]

    send_rims(0)

    for v in range(3 * FIELDS):
        reg[v] = jnp.zeros((BOXMAX, 128), F32)

    for copy in halos:
        copy.wait()
    for f in range(FIELDS):
        block[f, 0] = x_rim[0, f]
        block[f, 17] = x_rim[1, f]
    coarse_step(block, y_rim, z_rim, new, x_face, y_low, y_high, z_low, z_high)
    cut_all(
        1,
        lambda f, x, y, n: 0.5 * (block[f, x + 1, pl.ds(y, n), :] + new[f, x, pl.ds(y, n), :]),
    )
    fill_rims(1)
    send_rims(1)

    plane_load.wait()
    n_rows = REGIONS * members
    columns = members * BOXMAX
    row = iota((n_rows, columns), 0)
    column = iota((n_rows, columns), 1)
    slots = plane_ref[pl.ds(gx * (columns // 128), columns // 128), :] if columns >= 128 else None
    if columns >= 128:
        slots = jnp.concatenate(
            [
                jnp.broadcast_to(slots[h : h + 1, :], (n_rows, 128))
                for h in range(columns // 128)
            ],
            axis=1,
        )
    else:
        slots = jnp.broadcast_to(plane_ref[0:1, 0:columns], (n_rows, columns))
    number = column.astype(F32)
    far = 65536.0
    candidate = jnp.where(slots == row // REGIONS + gx * members, number, far)
    chosen = jnp.full((n_rows, 1), far)
    for r in range(REGIONS):
        least = jnp.min(candidate, axis=1, keepdims=True)
        chosen = jnp.where(row[:, 0:1] % REGIONS == r, least, chosen)
        candidate = jnp.where(candidate == least, far, candidate)
    route[...] = jnp.where(number == chosen, 1.0, 0.0)

    fine_load.wait()
    fine_prims(fine_ref, prim)
    fine_inner(fine_ref, prim, half)

    sub = iota((BOXMAX, 128), 0)
    owner = jnp.zeros((BOXMAX, 128), I32)
    for s in range(BOXMAX):
        owner = jnp.where(sub == s, own[s], owner)
    filled = owner >= 0

    def take_rims(when):
        wait_many(rim_in[when].at[others], when, many_recv)
        for s in range(BOXMAX):
            rows = rim_in[when][own_peer[s]]
            for v in range(3 * FIELDS):
                rim[v, s : s + 1, :] = rows[v : v + 1, :]

    take_rims(0)
    fine_outer(fine_ref, prim, rim, reg, filled, half, None)
    fine_prims(half, prim)
    fine_inner(half, prim, fine_new)
    fine_average(fine_new, reg, filled, sums)

    is_relay = within < relays
    for other, device in peers:

        @pl.when(other < relays)
        def _(other=other, device=device):
            ship(sums.at[pl.ds(other * share, share)], relay_in.at[within], 2, device)

    @pl.when(is_relay)
    def _():
        relay_in[within] = sums[pl.ds(within * share, share)]

    take_rims(1)
    fine_outer(half, prim, rim, reg, filled, fine_new, fine_ref)
    fine_store = fetch(fine_new, fine_out, 5)

    for s in range(BOXMAX):
        row_stage[s] = reg[:, s, :]
    for other, device in peers:
        face_out[other] = row_stage[table[32 + members + other]]
        ship(face_out.at[other], face_in.at[within], 3, device)
    face_in[within] = row_stage[table[32 + members + within]]

    @pl.when(is_relay)
    def _():
        wait_many(relay_in.at[others], 2, many_recv)
        for j in range(share):
            sorted_rows = jnp.dot(
                route[...],
                relay_in[:, j].reshape(columns, 128),
                precision=lax.Precision.HIGHEST,
                preferred_element_type=F32,
            )
            for p in range(members):
                relay_out[p, j] = sorted_rows[REGIONS * p : REGIONS * p + REGIONS]
        for other, device in peers:
            ship(relay_out.at[other], sums_in.at[pl.ds(within * share, share)], 4, device)
        sums_in[pl.ds(within * share, share)] = relay_out[within]

    corners = [(table[4 * c], table[4 * c + 1], table[4 * c + 2]) for c in range(REGIONS)]
    plan_settle(corners, new, x_face, y_low, y_high, z_low, z_high, weight, index)

    wait_many(face_in.at[others], 3, many_recv)
    for c in range(REGIONS):
        rows = face_in[child_peer[c]]
        for v in range(3 * FIELDS):
            faces[v, c : c + 1, :] = rows[v : v + 1, :]

    def wait_relays(every, index, semaphores):
        @pl.when(is_relay)
        def _():
            wait_many(every.at[pl.ds(0, (relays - 1) * share)], index, semaphores)

        @pl.when(jnp.logical_not(is_relay))
        def _():
            wait_many(every.at[pl.ds(0, relays * share)], index, semaphores)

    settle_rows(faces, answer_rows, crossed)
    coarse_stores = []
    for part in range(2):
        settle(corners, answer_rows, new, weight, index, coarse_new, 8 * part)
        planes = pl.ds(8 * part, 8)
        coarse_stores.append(fetch(coarse_new.at[:, planes], coarse_out.at[:, planes], 6 + part))
    wait_relays(sums_in, 4, many_recv)
    for tile in range(4 * FIELDS):
        crossed[tile] = sums_in[tile] + crossed[tile]
    sums_store = fetch(crossed, sums_out, 8)
    wait_many(rim_out.at[0, others], 0, many_send)
    wait_many(rim_out.at[1, others], 1, many_send)
    wait_relays(sums, 2, many_send)
    wait_many(face_out.at[others], 3, many_send)

    @pl.when(is_relay)
    def _():
        wait_many(relay_out.at[others], 4, many_send)

    fine_store.wait()
    sums_store.wait()
    corner_store.wait()
    for copy in coarse_stores:
        copy.wait()


def average_down(
    coarse_in, fine_in, sums_in, spots_in, coarse_out, fine_out, coarse, fine, sums, spots, arrive, leave
):
    def move(src, dst, sems, index):
        copy = pltpu.make_async_copy(src, dst, sems.at[index])
        copy.start()
        return copy

    spots_load = move(spots_in, spots, arrive, 2 * FIELDS)
    sums_load = move(sums_in, sums, arrive, 2 * FIELDS + 1)
    coarse_loads = [move(coarse_in.at[f], coarse.at[f], arrive, f) for f in range(FIELDS)]
    fine_loads = [move(fine_in.at[f], fine.at[f], arrive, FIELDS + f) for f in range(FIELDS)]
    spots_load.wait()
    sums_load.wait()
    lane = iota((8, 128), 1)
    row = iota((8, 128), 0)
    stores = []
    for f in range(FIELDS):
        coarse_loads[f].wait()
        for c in range(REGIONS):
            cx, cy, cz = spots[4 * c], spots[4 * c + 1], spots[4 * c + 2]
            z = lane - cz
            inside = jnp.logical_and(z >= 0, z < 8)[:, :64]
            place = row * 8 + jnp.clip(z, 0, 7)
            rows = pl.ds(cy, 8)
            old = [coarse[f, cx + x, rows, :] for x in range(8)]
            news = []
            for x in range(8):
                line = jnp.broadcast_to(sums[4 * f + x // 2, c : c + 1, :], (8, 128))
                value = 0.125 * pick(line, place + 64 * (x % 2))
                news.append(jnp.where(inside, value[:, :64], old[x]))
            for x in range(8):
                coarse[f, cx + x, rows, :] = news[x]
        stores.append(move(coarse.at[f], coarse_out.at[f], leave, f))
        fine_loads[f].wait()
        stores.append(move(fine.at[f], fine_out.at[f], leave, FIELDS + f))
    for copy in stores:
        copy.wait()


def on_device(sizes, coarse_state, fine_state, slot_parent, slot_corner):
    members = sizes[1] * sizes[2]
    share = -(-4 * FIELDS // members)
    relays = -(-4 * FIELDS // share)
    hbm = pl.BlockSpec(memory_space=pltpu.HBM)
    fine = jnp.transpose(fine_state, (1, 0, 2))
    corner = jnp.transpose(slot_corner, (1, 0))
    plane = slot_parent.reshape(-1, min(128, slot_parent.shape[0]))
    field_block = (FIELDS, 16, 16, 128)
    rows = 3 * FIELDS
    ringed, fine_next, sums, spots = pl.pallas_call(
        functools.partial(whole, sizes),
        out_shape=(
            jax.ShapeDtypeStruct(coarse_state.shape, F32),
            jax.ShapeDtypeStruct(fine.shape, F32),
            jax.ShapeDtypeStruct((4 * FIELDS, REGIONS, 128), F32),
            jax.ShapeDtypeStruct((4 * REGIONS,), I32),
        ),
        in_specs=[hbm] * 5,
        out_specs=(hbm, hbm, hbm, hbm),
        scratch_shapes=[
            pltpu.SMEM(slot_parent.shape, I32),
            pltpu.SMEM(corner.shape, I32),
            pltpu.VMEM(plane.shape, I32),
            pltpu.VMEM(coarse_state.shape, F32),
            pltpu.VMEM((FIELDS, 18, 16, 128), F32),
            pltpu.VMEM(field_block, F32),
            pltpu.VMEM((FIELDS, 17, 16, 128), F32),
            pltpu.VMEM(field_block, F32),
            pltpu.VMEM(field_block, F32),
            pltpu.VMEM(field_block, F32),
            pltpu.VMEM(field_block, F32),
            pltpu.VMEM((16, 16, 128), F32),
            pltpu.VMEM((16, REGIONS, 16, 128), I32),
            pltpu.VMEM((2, FIELDS, 16, 128), F32),
            pltpu.VMEM((2, 2, FIELDS, 128), F32),
            pltpu.VMEM((2, FIELDS, 16, 128), F32),
            pltpu.VMEM((2, FIELDS, 16, 128), F32),
            pltpu.VMEM((2, 2, FIELDS, 128), F32),
            pltpu.VMEM((2, REGIONS, 3 * FIELDS, 128), F32),
            pltpu.VMEM((2, members, 3 * FIELDS, 128), F32),
            pltpu.VMEM((members, 3 * FIELDS, 128), F32),
            pltpu.VMEM((members, 3 * FIELDS, 128), F32),
            pltpu.VMEM((3 * FIELDS, BOXMAX, 128), F32),
            pltpu.VMEM(fine.shape, F32),
            pltpu.VMEM((3,) + fine.shape[1:], F32),
            pltpu.VMEM(fine.shape, F32),
            pltpu.VMEM(fine.shape, F32),
            pltpu.VMEM(coarse_state.shape, F32),
            pltpu.VMEM((rows, BOXMAX, 128), F32),
            pltpu.VMEM((REGIONS * members, BOXMAX * members), F32),
            pltpu.VMEM((members, share, BOXMAX, 128), F32),
            pltpu.VMEM((members, share, REGIONS, 128), F32),
            pltpu.VMEM((relays * share, BOXMAX, 128), F32),
            pltpu.VMEM((relays * share, REGIONS, 128), F32),
            pltpu.VMEM((BOXMAX, rows, 128), F32),
            pltpu.VMEM((members, rows, 128), F32),
            pltpu.VMEM((members, rows, 128), F32),
            pltpu.VMEM((rows, REGIONS, 128), F32),
            pltpu.VMEM((FIELDS, 10, REGIONS, 128), F32),
            pltpu.VMEM((4 * FIELDS, REGIONS, 128), F32),
            pltpu.SMEM((32 + 2 * members,), I32),
            pltpu.SMEM((4 * REGIONS,), I32),
            pltpu.SemaphoreType.DMA((10,)),
            pltpu.SemaphoreType.DMA((6,)),
            pltpu.SemaphoreType.DMA((6,)),
            pltpu.SemaphoreType.DMA((5,)),
            pltpu.SemaphoreType.DMA((5,)),
        ],
        compiler_params=pltpu.CompilerParams(
            collective_id=0, has_side_effects=True, vmem_limit_bytes=62 * 1024 * 1024
        ),
    )(slot_parent, plane, corner, coarse_state, fine)
    coarse_next, fine_next = pl.pallas_call(
        average_down,
        out_shape=(
            jax.ShapeDtypeStruct(coarse_state.shape, F32),
            jax.ShapeDtypeStruct(fine.shape, F32),
        ),
        in_specs=[hbm] * 4,
        out_specs=(hbm, hbm),
        scratch_shapes=[
            pltpu.VMEM(coarse_state.shape, F32),
            pltpu.VMEM(fine.shape, F32),
            pltpu.VMEM((4 * FIELDS, REGIONS, 128), F32),
            pltpu.SMEM((4 * REGIONS,), I32),
            pltpu.SemaphoreType.DMA((2 * FIELDS + 2,)),
            pltpu.SemaphoreType.DMA((2 * FIELDS,)),
        ],
        compiler_params=pltpu.CompilerParams(vmem_limit_bytes=62 * 1024 * 1024),
    )(ringed, fine_next, sums, spots)
    return coarse_next, jnp.transpose(fine_next, (1, 0, 2))


def solution(mesh):
    sizes = tuple(mesh.shape[name] for name in ("gx", "gy", "gz"))
    return jax.shard_map(
        functools.partial(on_device, sizes),
        mesh=mesh,
        in_specs=(P(None, "gx", "gy", "gz"), P(("gx", "gy", "gz"), None, None), P(), P()),
        out_specs=(P(None, "gx", "gy", "gz"), P(("gx", "gy", "gz"), None, None)),
        check_vma=False,
    )
```

```python
import functools

import jax
import jax.numpy as jnp
from jax import lax
from jax.experimental import pallas as pl
from jax.experimental.pallas import tpu as pltpu
from jax.sharding import PartitionSpec as P

GAMMA = 1.4
COURANT = 0.04
PRIM_UNROLL = 2
YZ_UNROLL = 2
OUTER_UNROLL = 8
GATHER_UNROLL = 8
COARSE_UNROLL = 4
CUT_UNROLL = 4
SETTLE_UNROLL = 4
FIELDS = 5
REGIONS = 4
BOXMAX = 8
MESH = pl.DeviceIdType.MESH
F32 = jnp.float32
I32 = jnp.int32


def iota(shape, dim):
    return lax.broadcasted_iota(I32, shape, dim)


def pick(values, lanes):
    numbers = lax.GatherDimensionNumbers(
        offset_dims=(),
        collapsed_slice_dims=(1,),
        start_index_map=(1,),
        operand_batching_dims=(0,),
        start_indices_batching_dims=(0,),
    )
    return lax.gather(
        values,
        lanes[..., None],
        numbers,
        (1, 1),
        mode=lax.GatherScatterMode.PROMISE_IN_BOUNDS,
    )


def prims(q):
    inverse = pl.reciprocal(q[0], approx=True)
    inverse = inverse * (2.0 - q[0] * inverse)
    kinetic = 0.5 * (q[1] * q[1] + q[2] * q[2] + q[3] * q[3]) * inverse
    pressure = (GAMMA - 1.0) * (q[4] - kinetic)
    square = GAMMA * pressure * inverse
    sound = square * lax.rsqrt(jnp.maximum(square, 1e-30))
    return inverse, pressure, sound, q[4] + pressure


def along(q, prim, axis):
    inverse, pressure, sound, total = prim
    velocity = q[1 + axis] * inverse
    flux = [q[1 + axis], q[1] * velocity, q[2] * velocity, q[3] * velocity, total * velocity]
    flux[1 + axis] = flux[1 + axis] + pressure
    return flux, jnp.abs(velocity) + sound


def face(low, low_terms, high, high_terms):
    signal = jnp.maximum(low_terms[1], high_terms[1])
    return [
        (low_terms[0][f] + high_terms[0][f]) - signal * (high[f] - low[f]) for f in range(FIELDS)
    ]


def moved(q, terms, move):
    return [move(v) for v in q], [move(v) for v in terms[0]], move(terms[1])


def span(plane, h):
    return pl.ds(pl.multiple_of(plane * 256 + h * 128, 128), 128)


def roll(v, by):
    return pltpu.roll(v, by % 128, 1)


def fine_prims(cells, prim):
    def one(plane, _):
        for h in range(2):
            where = span(plane, h)
            inverse, pressure, sound, _ = prims([cells[f, :, where] for f in range(FIELDS)])
            prim[0, :, where] = inverse
            prim[1, :, where] = pressure
            prim[2, :, where] = sound
        return 0

    lax.fori_loop(0, 16, one, 0, unroll=PRIM_UNROLL)


def fine_inner(cells, prim, out):
    lane = iota((BOXMAX, 128), 1)
    first_row = lane < 16
    last_row = lane >= 112
    k_first = lane % 16 == 0

    def load(plane, h):
        where = span(plane, h)
        q = [cells[f, :, where] for f in range(FIELDS)]
        pressure = prim[1, :, where]
        return q, (prim[0, :, where], pressure, prim[2, :, where], q[4] + pressure)

    none = [[jnp.zeros((BOXMAX, 128), F32)] * FIELDS] * 2

    def one(plane, x_low):
        cell = [load(plane, h) for h in range(2)]
        after = [load(jnp.minimum(plane + 1, 15), h) for h in range(2)]
        partial = [cell[h][0] for h in range(2)]
        for h in range(2):
            q, q_prim = cell[h]
            terms = along(q, q_prim, 2)
            shifted = moved(q, terms, lambda v: roll(v, 1))
            z = face(shifted[0], (shifted[1], shifted[2]), q, terms)
            partial[h] = list(partial[h])
            for f in range(FIELDS):
                low = jnp.where(k_first, 0.0, z[f])
                partial[h][f] = partial[h][f] - (0.5 * COURANT) * (roll(low, -1) - low)
        q0, prim0 = cell[0]
        q1, prim1 = cell[1]
        terms0 = along(q0, prim0, 1)
        terms1 = along(q1, prim1, 1)
        shifted0 = moved(q0, terms0, lambda v: roll(v, 16))
        shifted1 = moved(q1, terms1, lambda v: roll(v, 16))

        def seam(low, high):
            return jnp.where(first_row, low, high)

        low1 = (
            [seam(shifted0[0][f], shifted1[0][f]) for f in range(FIELDS)],
            (
                [seam(shifted0[1][f], shifted1[1][f]) for f in range(FIELDS)],
                seam(shifted0[2], shifted1[2]),
            ),
        )
        y0 = face(shifted0[0], (shifted0[1], shifted0[2]), q0, terms0)
        y1 = face(low1[0], low1[1], q1, terms1)
        for f in range(FIELDS):
            low = jnp.where(first_row, 0.0, y0[f])
            up0 = roll(low, -16)
            up1 = roll(y1[f], -16)
            change0 = jnp.where(last_row, up1, up0) - low
            change1 = jnp.where(last_row, up0, up1) - y1[f]
            partial[0][f] = partial[0][f] - (0.5 * COURANT) * change0
            partial[1][f] = partial[1][f] - (0.5 * COURANT) * change1
        x_high = [
            face(
                cell[h][0],
                along(cell[h][0], cell[h][1], 0),
                after[h][0],
                along(after[h][0], after[h][1], 0),
            )
            for h in range(2)
        ]
        x_high = [[jnp.where(plane < 15, v, 0.0) for v in x_high[h]] for h in range(2)]
        for h in range(2):
            for f in range(FIELDS):
                out[f, :, span(plane, h)] = partial[h][f] - (0.5 * COURANT) * (
                    x_high[h][f] - x_low[h][f]
                )
        return x_high

    lax.fori_loop(0, 16, one, none, unroll=YZ_UNROLL)


def fine_outer(cells, prim, rim, reg, filled, out, old, edges):
    second = old is not None
    lane = iota((BOXMAX, 128), 1)
    k = lane % 16
    half_k = k // 2
    quarter = lane // 32
    squeeze = ((lane % 32) // 8) * 32 + (lane % 8) * 2
    part = (lane % 64) // 8
    low_half = lane < 64
    step = 0.5 * COURANT
    y_sign = jnp.where(low_half, 1.0, -1.0)
    z_sign = jnp.where(k < 8, 1.0, -1.0)
    y_weight = (jnp.where(lane < 16, step, 0.0), jnp.where(lane >= 112, -step, 0.0))
    z_weight = jnp.where(k == 0, step, jnp.where(k == 15, -step, 0.0))

    def load(plane, h):
        where = span(plane, h)
        q = [cells[f, :, where] for f in range(FIELDS)]
        pressure = prim[1, :, where]
        return q, (prim[0, :, where], pressure, prim[2, :, where], q[4] + pressure)

    def edge(ghost, ghost_terms, q, terms, sign):
        signal = jnp.maximum(ghost_terms[1], terms[1]) * sign
        return [
            (ghost_terms[0][f] + terms[0][f]) - signal * (q[f] - ghost[f]) for f in range(FIELDS)
        ]

    results = []
    for plane, side, sign in ((0, 0, 1.0), (15, 64, -1.0)):
        flux = []
        for h in range(2):
            spread = (h * 4 + quarter) * 8 + half_k + side
            ghost = [pick(rim[3 * f], spread) for f in range(FIELDS)]
            q, q_prim = load(plane, h)
            flux.append(edge(ghost, along(ghost, prims(ghost), 0), q, along(q, q_prim, 0), sign))
            results.append(
                [out[f, :, span(plane, h)] + (sign * step) * flux[h][f] for f in range(FIELDS)]
            )
        for f in range(FIELDS):
            found = []
            for h in range(2):
                v = flux[h][f]
                v = v + roll(v, -1)
                v = v + roll(v, -16)
                found.append(pick(v, squeeze))
            results.append(jnp.where((lane % 64) < 32, found[0], found[1]))
    for plane, first in ((0, 0), (15, 2 + FIELDS)):
        for h in range(2):
            for f in range(FIELDS):
                out[f, :, span(plane, h)] = results[first + h][f]
    for f in range(FIELDS):
        v = jnp.where(low_half, results[2 + f], results[4 + FIELDS + f])
        reg[3 * f] = reg[3 * f] + jnp.where(filled, v, 0.0)

    def pair(big, _):
        y_lanes = big * 8 + half_k + jnp.where(low_half, 0, 64)
        y_ghost = [pick(rim[3 * f + 1], y_lanes) for f in range(FIELDS)]
        y_ghost_terms = along(y_ghost, prims(y_ghost), 1)
        z_ghost = []
        z_ghost_terms = []
        for h in range(2):
            z_lanes = big * 8 + h * 4 + quarter + jnp.where(k >= 8, 64, 0)
            ghost = [pick(rim[3 * f + 2], z_lanes) for f in range(FIELDS)]
            z_ghost.append(ghost)
            z_ghost_terms.append(along(ghost, prims(ghost), 2))
        y_sum = [None] * FIELDS
        z_sum = [[None] * FIELDS for _ in range(2)]

        def accumulate(total, v):
            return v if total is None else total + v

        for sub in range(2):
            plane = 2 * big + sub
            q, q_prim = zip(*[load(plane, h) for h in range(2)])
            near = [jnp.where(low_half, q[0][f], q[1][f]) for f in range(FIELDS)]
            near_prim = [jnp.where(low_half, q_prim[0][i], q_prim[1][i]) for i in range(4)]
            before = [[out[f, :, span(plane, h)] for f in range(FIELDS)] for h in range(2)]
            if second:
                kept = [[old[f, :, span(plane, h)] for f in range(FIELDS)] for h in range(2)]
            y = edge(y_ghost, y_ghost_terms, near, along(near, near_prim, 1), y_sign)
            for f in range(FIELDS):
                y_sum[f] = accumulate(y_sum[f], y[f])
            news = []
            for h in range(2):
                z = edge(z_ghost[h], z_ghost_terms[h], q[h], along(q[h], q_prim[h], 2), z_sign)
                for f in range(FIELDS):
                    z_sum[h][f] = accumulate(z_sum[h][f], z[f])
                    new = before[h][f] + y_weight[h] * y[f] + z_weight * z[f]
                    if second:
                        new = jnp.where(filled, new, kept[h][f])
                    news.append((f, h, new))
            for f, h, new in news:
                out[f, :, span(plane, h)] = new

        for f in range(FIELDS):
            edges[big, f] = y_sum[f]
            edges[big, FIELDS + f] = z_sum[0][f]
            edges[big, 2 * FIELDS + f] = z_sum[1][f]
        return 0

    lax.fori_loop(0, 8, pair, 0, unroll=OUTER_UNROLL)

    def gather(big, totals):
        y_sum = [edges[big, f] for f in range(FIELDS)]
        z_sum = [[edges[big, (1 + h) * FIELDS + f] for f in range(FIELDS)] for h in range(2)]
        mine = jnp.logical_and(filled, part == big)
        y_from = (lane % 8) * 2 + jnp.where(low_half, 0, 112)
        z_from = (lane % 4) * 32 + jnp.where(low_half, 0, 15)
        new_totals = []
        for f in range(FIELDS):
            v = y_sum[f] + roll(y_sum[f], -1)
            new_totals.append(totals[2 * f] + jnp.where(mine, pick(v, y_from), 0.0))
            found = []
            for h in range(2):
                v = z_sum[h][f] + roll(z_sum[h][f], -16)
                found.append(pick(v, z_from))
            v = jnp.where(lane % 8 < 4, found[0], found[1])
            new_totals.append(totals[2 * f + 1] + jnp.where(mine, v, 0.0))
        return new_totals

    totals = [reg[3 * f + t] for f in range(FIELDS) for t in (1, 2)]
    totals = lax.fori_loop(0, 8, gather, totals, unroll=GATHER_UNROLL)
    for f in range(FIELDS):
        reg[3 * f + 1] = totals[2 * f]
        reg[3 * f + 2] = totals[2 * f + 1]


def through(tx, ty, tz, group):
    lane = iota(tx.shape, 1)
    x = 2 * group + lane // 64
    y = (lane % 64) // 8
    z = lane % 8

    def sign(place):
        return jnp.where(place == 0, 1.0, jnp.where(place == 7, -1.0, 0.0))

    total = sign(y) * pick(ty, x * 8 + z + jnp.where(y == 7, 64, 0))
    total = total + sign(z) * pick(tz, x * 8 + y + jnp.where(z == 7, 64, 0))
    if group == 0:
        total = total + jnp.where(lane < 64, tx, 0.0)
    if group == 3:
        total = total - jnp.where(lane < 64, 0.0, tx)
    return total


def fine_average(cells, reg, filled, sums):
    lane = iota((BOXMAX, 128), 1)
    squeeze = ((lane % 32) // 8) * 32 + (lane % 8) * 2
    faces = [reg[v] for v in range(3 * FIELDS)]
    for group in range(4):
        tiles = []
        for f in range(FIELDS):
            for sub in range(2):
                for h in range(2):
                    plane = 4 * group + 2 * sub
                    tiles.append(cells[f, :, span(plane, h)] + cells[f, :, span(plane + 1, h)])
        tiles = [v + roll(v, -1) for v in tiles]
        tiles = [v + roll(v, -16) for v in tiles]
        tiles = [pick(v, squeeze) for v in tiles]
        crossed = [through(*faces[3 * f : 3 * f + 3], group) for f in range(FIELDS)]
        results = []
        for f in range(FIELDS):
            low = jnp.where(lane < 32, tiles[4 * f], tiles[4 * f + 1])
            high = jnp.where(lane < 96, tiles[4 * f + 2], tiles[4 * f + 3])
            v = jnp.where(lane < 64, low, high) - (0.5 * COURANT) * crossed[f]
            results.append(jnp.where(filled, v, 0.0))
        for f in range(FIELDS):
            sums[4 * f + group] = results[f]


def coarse_step(block, y_rim, z_rim, new, x_face, y_low, y_high, z_low, z_high):
    lane = iota((16, 128), 1)
    row = iota((16, 128), 0)
    tip = iota((8, 128), 0)

    def load(plane):
        return [block[f, plane] for f in range(FIELDS)]

    def widen(x, _):
        column = (x % 8) * 16 + row
        for f in range(FIELDS):
            below = jnp.broadcast_to(z_rim[0, x // 8, f : f + 1, :], (16, 128))
            above = jnp.broadcast_to(z_rim[1, x // 8, f : f + 1, :], (16, 128))
            side = jnp.where(lane == 64, pick(above, column), pick(below, column))
            block[f, x + 1] = jnp.where(lane < 64, block[f, x + 1], side)
        return 0

    lax.fori_loop(0, 16, widen, 0, unroll=4)

    ghost = load(0)
    here = load(1)
    here_prim = prims(here)
    low = face(ghost, along(ghost, prims(ghost), 0), here, along(here, here_prim, 0))
    for f in range(FIELDS):
        x_face[f, 0] = low[f]

    def one(x, carried):
        here, here_prim, x_low = carried
        after = load(x + 2)
        after_prim = prims(after)
        x_high = face(here, along(here, here_prim, 0), after, along(after, after_prim, 0))

        tips = []
        for f in range(FIELDS):
            above = y_rim[1, f, pl.ds(x, 1), :]
            below = y_rim[0, f, pl.ds(x, 1), :]
            tips.append(
                jnp.where(
                    tip == 0,
                    jnp.broadcast_to(above, (8, 128)),
                    jnp.broadcast_to(below, (8, 128)),
                )
            )
        tip_terms = along(tips, prims(tips), 1)
        terms = along(here, here_prim, 1)

        def tall(low, high):
            return jnp.concatenate([low, high], axis=0)

        cells = [tall(here[f], tips[f]) for f in range(FIELDS)]
        terms = ([tall(terms[0][f], tip_terms[0][f]) for f in range(FIELDS)], tall(terms[1], tip_terms[1]))
        shifted = moved(cells, terms, lambda v: pltpu.roll(v, 1, 0))
        y = face(shifted[0], (shifted[1], shifted[2]), cells, terms)

        terms = along(here, here_prim, 2)
        shifted = moved(here, terms, lambda v: pltpu.roll(v, 1, 1))
        z = face(shifted[0], (shifted[1], shifted[2]), here, terms)
        for f in range(FIELDS):
            up = pltpu.roll(y[f], 23, 0)[:16]
            down = y[f][:16]
            right = pltpu.roll(z[f], 127, 1)
            x_face[f, x + 1] = x_high[f]
            y_low[f, x] = down
            y_high[f, x] = up
            z_low[f, x] = z[f]
            z_high[f, x] = right
            change = (x_high[f] - x_low[f]) + (up - down) + (right - z[f])
            new[f, x] = here[f] - (0.5 * COURANT) * change
        return after, after_prim, x_high

    lax.fori_loop(0, 16, one, (here, here_prim, low), unroll=COARSE_UNROLL)


def cut_rims(source, corner):
    cx, cy, cz = corner
    lane = iota((8, 128), 1)
    row = iota((8, 128), 0)
    low_half = lane < 64
    part = (lane % 64) // 8
    along_z = cz + lane % 8
    ends = jnp.where(low_half, cz - 1, cz + 8)
    rows_x = row == part
    rows_z = row == lane % 8
    lines = []
    for f in range(FIELDS):
        low = pick(source(f, cx - 1, cy, 8), along_z)
        high = pick(source(f, cx + 8, cy, 8), along_z)
        v = jnp.where(rows_x, jnp.where(low_half, low, high), 0.0)
        lines.append(jnp.sum(v, axis=0, keepdims=True))
        low = jnp.zeros((8, 128), F32)
        high = jnp.zeros((8, 128), F32)
        total = jnp.zeros((8, 128), F32)
        for big in range(8):
            here = row == big
            low = jnp.where(here, jnp.broadcast_to(source(f, cx + big, cy - 1, 1), (8, 128)), low)
            high = jnp.where(here, jnp.broadcast_to(source(f, cx + big, cy + 8, 1), (8, 128)), high)
            total = jnp.where(part == big, pick(source(f, cx + big, cy, 8), ends), total)
        v = jnp.where(low_half, pick(low, along_z), pick(high, along_z))
        lines.append(jnp.sum(jnp.where(rows_x, v, 0.0), axis=0, keepdims=True))
        lines.append(jnp.sum(jnp.where(rows_z, total, 0.0), axis=0, keepdims=True))
    return lines


def plan_settle(corners, new, x_face, y_low, y_high, z_low, z_high, weight, index):
    lane = iota((16, 128), 1)
    row = iota((16, 128), 0)

    def one(x, _):
        kind = jnp.zeros((16, 128), I32)
        for c in range(REGIONS):
            cx, cy, cz = corners[c]
            step = x - cx
            inside = jnp.logical_and(step >= 0, step < 8)
            dy = row - cy
            dz = lane - cz
            in_y = jnp.logical_and(dy >= 0, dy < 8)
            in_z = jnp.logical_and(dz >= 0, dz < 8)
            near = jnp.where(dy == -1, 4, jnp.where(dy == 8, 5, 0))
            side = jnp.where(dz == -1, 6, jnp.where(dz == 8, 7, 0))
            plain = jnp.where(inside, 1, jnp.where(step == -1, 2, jnp.where(step == 8, 3, 0)))
            mine = jnp.where(
                jnp.logical_and(in_y, in_z),
                plain,
                jnp.where(inside, jnp.where(in_z, near, jnp.where(in_y, side, 0)), 0),
            )
            ys = jnp.clip(dy, 0, 7)
            zs = jnp.clip(dz, 0, 7)
            lanes = jnp.where(mine < 4, ys * 8 + zs, 32 + 8 * mine + jnp.where(mine < 6, zs, ys))
            used = mine > 0
            kind = jnp.where(used, mine, kind)
            index[x, c] = jnp.where(used, lanes + 128, 0)
        factor = jnp.where(kind < 2, 0.0, jnp.where(kind % 2 == 0, -COURANT, COURANT))
        weight[x] = jnp.where(kind == 1, 0.125, 0.0625 * factor)
        for f in range(FIELDS):
            flux = jnp.where(
                kind < 4,
                jnp.where(kind == 2, x_face[f, x + 1], x_face[f, x]),
                jnp.where(
                    kind < 6,
                    jnp.where(kind == 4, y_high[f, x], y_low[f, x]),
                    jnp.where(kind == 6, z_high[f, x], z_low[f, x]),
                ),
            )
            plain = new[f, x]
            ring = jnp.where(kind >= 2, plain - 0.5 * factor * flux, plain)
            new[f, x] = jnp.where(kind == 1, 0.0, ring)
        return 0

    lax.fori_loop(0, 16, one, 0)


def settle_rows(faces, rows, crossed):
    lane = iota((REGIONS, 128), 1)
    spot = ((lane % 16) // 8) * 64 + lane % 8
    results = []
    added = []
    for f in range(FIELDS):
        tx, ty, tz = faces[3 * f], faces[3 * f + 1], faces[3 * f + 2]
        results.append((f, 0, tx))
        results.append((f, 9, pltpu.roll(tx, 64, 1)))
        for big in range(8):
            around = jnp.where(lane < 80, pick(ty, spot + 8 * big), pick(tz, spot + 8 * big))
            results.append((f, 1 + big, jnp.where(lane < 64, 0.0, around)))
        for group in range(4):
            added.append((0.5 * COURANT) * through(tx, ty, tz, group))
    for f, where, v in results:
        rows[f, where] = v
    for tile, v in enumerate(added):
        crossed[tile] = v


def settle(corners, rows, new, weight, index, out, start):
    def one(step, _):
        x = start + step
        values = [jnp.zeros((16, 128), F32) for _ in range(FIELDS)]
        for c in range(REGIONS):
            which = jnp.clip(x - corners[c][0] + 1, 0, 9)
            lanes = index[x, c]
            used = lanes >= 128
            lanes = lanes & 127
            for f in range(FIELDS):
                line = jnp.broadcast_to(rows[f, which, c : c + 1, :], (16, 128))
                values[f] = jnp.where(used, pick(line, lanes), values[f])
        factor = weight[x]
        results = [new[f, x] + factor * values[f] for f in range(FIELDS)]
        for f in range(FIELDS):
            out[f, x] = results[f][:, :64]
        return 0

    lax.fori_loop(0, 4, one, 0, unroll=SETTLE_UNROLL)


def whole(
    sizes,
    parent_hbm,
    plane_hbm,
    corner_hbm,
    coarse_hbm,
    fine_hbm,
    coarse_out,
    fine_out,
    sums_out,
    spots_out,
    parent_ref,
    corner_ref,
    plane_ref,
    coarse_ref,
    block,
    new,
    x_face,
    y_low,
    y_high,
    z_low,
    z_high,
    weight,
    index,
    y_stage,
    z_stage,
    x_rim,
    y_rim,
    z_rim,
    cut,
    rim_out,
    rim_in_old,
    rim_in_mid,
    rim,
    fine_ref,
    prim,
    half,
    fine_new,
    coarse_new,
    reg,
    edges,
    route,
    relay_in,
    relay_out,
    sums,
    sums_in,
    row_stage,
    face_out,
    face_in,
    faces,
    answer_rows,
    crossed,
    table,
    spots,
    load_sems,
    halo_send,
    halo_recv,
    many_send,
    many_recv,
):
    n_gx, n_gy, n_gz = sizes
    members = n_gy * n_gz
    share = -(-4 * FIELDS // members)
    relays = -(-4 * FIELDS // share)
    rim_in = (rim_in_old, rim_in_mid)
    gx = lax.axis_index("gx")
    gy = lax.axis_index("gy")
    gz = lax.axis_index("gz")
    within = gy * n_gz + gz
    myself = gx * members + within
    start = gx * (members * BOXMAX)

    def hops(move):
        return min(move[0], n_gy - move[0]) + min(move[1], n_gz - move[1])

    moves = [(dy, dz) for dy in range(n_gy) for dz in range(n_gz) if dy or dz]
    peers = []
    for dy, dz in sorted(moves, key=hops, reverse=True):
        other_y = lax.rem(gy + dy, n_gy)
        other_z = lax.rem(gz + dz, n_gz)
        peers.append((other_y * n_gz + other_z, (gx, other_y, other_z)))

    barrier = pltpu.get_barrier_semaphore()
    for _, device in peers:
        pl.semaphore_signal(barrier, inc=1, device_id=device, device_id_type=MESH)

    x_next = (lax.rem(gx + 1, n_gx), gy, gz)
    x_prev = (lax.rem(gx + n_gx - 1, n_gx), gy, gz)
    y_next = (gx, lax.rem(gy + 1, n_gy), gz)
    y_prev = (gx, lax.rem(gy + n_gy - 1, n_gy), gz)
    z_next = (gx, gy, lax.rem(gz + 1, n_gz))
    z_prev = (gx, gy, lax.rem(gz + n_gz - 1, n_gz))
    pl.semaphore_signal(barrier, inc=1, device_id=x_next, device_id_type=MESH)
    pl.semaphore_signal(barrier, inc=1, device_id=x_prev, device_id_type=MESH)

    def fetch(src, dst, index):
        copy = pltpu.make_async_copy(src, dst, load_sems.at[index])
        copy.start()
        return copy

    coarse_load = fetch(coarse_hbm, coarse_ref, 0)
    parent_load = fetch(parent_hbm, parent_ref, 1)
    corner_load = fetch(corner_hbm, corner_ref, 2)
    plane_load = fetch(plane_hbm, plane_ref, 3)
    fine_load = fetch(fine_hbm, fine_ref, 4)

    parent_load.wait()
    corner_load.wait()

    def scan(entry, found):
        c0, c1, c2, c3 = found
        hit = parent_ref[start + entry] == myself
        return (
            jnp.where(hit, c1, c0),
            jnp.where(hit, c2, c1),
            jnp.where(hit, c3, c2),
            jnp.where(hit, entry, c3),
        )

    zero = jnp.int32(0)
    children = lax.fori_loop(0, members * BOXMAX, scan, (zero, zero, zero, zero), unroll=8)
    for c in range(REGIONS):
        for k in range(3):
            spot = jnp.clip(corner_ref[k, start + children[c]], 1, 55 if k == 2 else 7)
            table[4 * c + k] = spot
            spots[4 * c + k] = spot
        spots[4 * c + 3] = zero
    corner_store = fetch(spots, spots_out, 11)
    child_peer = [child // BOXMAX for child in children]
    own = [parent_ref[start + within * BOXMAX + s] for s in range(BOXMAX)]
    own_peer = [lax.rem(jnp.maximum(own[s], 0), members) for s in range(BOXMAX)]

    def look_up(other, _):
        rank = zero
        for c in range(1, REGIONS):
            rank = jnp.where(child_peer[c] == other, c, rank)
        found = zero
        for s in range(BOXMAX):
            found = jnp.where(jnp.logical_and(own[s] >= 0, own_peer[s] == other), s, found)
        table[32 + other] = rank
        table[32 + members + other] = found
        return 0

    lax.fori_loop(0, members, look_up, 0, unroll=4)

    def cut_all(when, source):
        def one(c, _):
            corner = (table[4 * c], table[4 * c + 1], table[4 * c + 2])

            for v, line in enumerate(cut_rims(source, corner)):
                cut[when, c, v : v + 1, :] = line
            return 0

        lax.fori_loop(0, REGIONS, one, 0, unroll=CUT_UNROLL)

    def ship(src, dst, index, device):
        pltpu.make_async_remote_copy(
            src_ref=src,
            dst_ref=dst,
            send_sem=many_send.at[index],
            recv_sem=many_recv.at[index],
            device_id=device,
            device_id_type=MESH,
        ).start()

    def wait_many(every, index, semaphores):
        pltpu.make_async_copy(every, every, semaphores.at[index]).wait()

    others = pl.ds(0, members - 1)

    def fill_rims(when):
        def one(other, _):
            rim_out[when, other] = cut[when, table[32 + other]]
            return 0

        lax.fori_loop(0, members, one, 0, unroll=4)
        rim_in[when][within] = rim_out[when, within]

    def send_rims(when):
        for other, device in peers:
            ship(rim_out.at[when, other], rim_in[when].at[within], when, device)

    lane16 = iota((16, 128), 1)
    row16 = iota((16, 128), 0)
    coarse_load.wait()
    for f in range(FIELDS):
        block[f, 1:17, :, 0:64] = coarse_ref[f]
    match = row16 == lane16 % 16
    edge_rows = [(block[f, 1:17, 0, :], block[f, 1:17, 15, :]) for f in range(FIELDS)]
    columns_found = []
    for f in range(FIELDS):
        for h in range(2):
            low = jnp.zeros((16, 128), F32)
            high = jnp.zeros((16, 128), F32)
            for x in range(8):
                plane = block[f, 1 + 8 * h + x]
                here = lane16 // 16 == x
                low = jnp.where(here, jnp.broadcast_to(plane[:, 0:1], (16, 128)), low)
                high = jnp.where(here, jnp.broadcast_to(plane[:, 63:64], (16, 128)), high)
            low = jnp.sum(jnp.where(match, low, 0.0), axis=0, keepdims=True)
            high = jnp.sum(jnp.where(match, high, 0.0), axis=0, keepdims=True)
            columns_found.append((f, h, low, high))
    for f in range(FIELDS):
        y_stage[0, f] = edge_rows[f][0]
        y_stage[1, f] = edge_rows[f][1]
    for f, h, low, high in columns_found:
        z_stage[0, h, f : f + 1, :] = low
        z_stage[1, h, f : f + 1, :] = high

    cut_all(0, lambda f, x, y, n: block[f, x + 1, pl.ds(y, n), :])
    fill_rims(0)

    pl.semaphore_wait(barrier, members + 1)

    def halo(src, dst, index, device):
        copy = pltpu.make_async_remote_copy(
            src_ref=src,
            dst_ref=dst,
            send_sem=halo_send.at[index],
            recv_sem=halo_recv.at[index],
            device_id=device,
            device_id_type=MESH,
        )
        copy.start()
        return copy

    halos = [
        halo(block.at[:, 16], x_rim.at[0], 0, x_next),
        halo(block.at[:, 1], x_rim.at[1], 1, x_prev),
        halo(y_stage.at[1], y_rim.at[0], 2, y_next),
        halo(y_stage.at[0], y_rim.at[1], 3, y_prev),
        halo(z_stage.at[1], z_rim.at[0], 4, z_next),
        halo(z_stage.at[0], z_rim.at[1], 5, z_prev),
    ]

    send_rims(0)

    for v in range(3 * FIELDS):
        reg[v] = jnp.zeros((BOXMAX, 128), F32)

    for copy in halos:
        copy.wait()
    for f in range(FIELDS):
        block[f, 0] = x_rim[0, f]
        block[f, 17] = x_rim[1, f]
    coarse_step(block, y_rim, z_rim, new, x_face, y_low, y_high, z_low, z_high)
    cut_all(
        1,
        lambda f, x, y, n: 0.5 * (block[f, x + 1, pl.ds(y, n), :] + new[f, x, pl.ds(y, n), :]),
    )
    fill_rims(1)
    send_rims(1)

    plane_load.wait()
    n_rows = REGIONS * members
    columns = members * BOXMAX
    row = iota((n_rows, columns), 0)
    column = iota((n_rows, columns), 1)
    slots = plane_ref[pl.ds(gx * (columns // 128), columns // 128), :] if columns >= 128 else None
    if columns >= 128:
        slots = jnp.concatenate(
            [
                jnp.broadcast_to(slots[h : h + 1, :], (n_rows, 128))
                for h in range(columns // 128)
            ],
            axis=1,
        )
    else:
        slots = jnp.broadcast_to(plane_ref[0:1, 0:columns], (n_rows, columns))
    number = column.astype(F32)
    far = 65536.0
    candidate = jnp.where(slots == row // REGIONS + gx * members, number, far)
    chosen = jnp.full((n_rows, 1), far)
    for r in range(REGIONS):
        least = jnp.min(candidate, axis=1, keepdims=True)
        chosen = jnp.where(row[:, 0:1] % REGIONS == r, least, chosen)
        candidate = jnp.where(candidate == least, far, candidate)
    route[...] = jnp.where(number == chosen, 1.0, 0.0)

    fine_load.wait()
    fine_prims(fine_ref, prim)
    fine_inner(fine_ref, prim, half)

    sub = iota((BOXMAX, 128), 0)
    owner = jnp.zeros((BOXMAX, 128), I32)
    for s in range(BOXMAX):
        owner = jnp.where(sub == s, own[s], owner)
    filled = owner >= 0

    def take_rims(when):
        wait_many(rim_in[when].at[others], when, many_recv)
        for s in range(BOXMAX):
            rows = rim_in[when][own_peer[s]]
            for v in range(3 * FIELDS):
                rim[v, s : s + 1, :] = rows[v : v + 1, :]

    take_rims(0)
    fine_outer(fine_ref, prim, rim, reg, filled, half, None, edges)
    fine_prims(half, prim)
    fine_inner(half, prim, fine_new)
    fine_average(fine_new, reg, filled, sums)

    is_relay = within < relays
    for other, device in peers:

        @pl.when(other < relays)
        def _(other=other, device=device):
            ship(sums.at[pl.ds(other * share, share)], relay_in.at[within], 2, device)

    @pl.when(is_relay)
    def _():
        relay_in[within] = sums[pl.ds(within * share, share)]

    take_rims(1)
    fine_outer(half, prim, rim, reg, filled, fine_new, fine_ref, edges)
    fine_store = fetch(fine_new, fine_out, 5)

    for s in range(BOXMAX):
        row_stage[s] = reg[:, s, :]
    for other, device in peers:
        face_out[other] = row_stage[table[32 + members + other]]
        ship(face_out.at[other], face_in.at[within], 3, device)
    face_in[within] = row_stage[table[32 + members + within]]

    @pl.when(is_relay)
    def _():
        wait_many(relay_in.at[others], 2, many_recv)
        for j in range(share):
            sorted_rows = jnp.dot(
                route[...],
                relay_in[:, j].reshape(columns, 128),
                precision=lax.Precision.HIGHEST,
                preferred_element_type=F32,
            )
            for p in range(members):
                relay_out[p, j] = sorted_rows[REGIONS * p : REGIONS * p + REGIONS]
        for other, device in peers:
            ship(relay_out.at[other], sums_in.at[pl.ds(within * share, share)], 4, device)
        sums_in[pl.ds(within * share, share)] = relay_out[within]

    corners = [(table[4 * c], table[4 * c + 1], table[4 * c + 2]) for c in range(REGIONS)]
    plan_settle(corners, new, x_face, y_low, y_high, z_low, z_high, weight, index)

    wait_many(face_in.at[others], 3, many_recv)
    for c in range(REGIONS):
        rows = face_in[child_peer[c]]
        for v in range(3 * FIELDS):
            faces[v, c : c + 1, :] = rows[v : v + 1, :]

    def wait_relays(every, index, semaphores):
        @pl.when(is_relay)
        def _():
            wait_many(every.at[pl.ds(0, (relays - 1) * share)], index, semaphores)

        @pl.when(jnp.logical_not(is_relay))
        def _():
            wait_many(every.at[pl.ds(0, relays * share)], index, semaphores)

    settle_rows(faces, answer_rows, crossed)
    coarse_stores = []
    for part in range(4):
        settle(corners, answer_rows, new, weight, index, coarse_new, 4 * part)
        planes = pl.ds(4 * part, 4)
        coarse_stores.append(fetch(coarse_new.at[:, planes], coarse_out.at[:, planes], 6 + part))
    wait_relays(sums_in, 4, many_recv)
    for tile in range(4 * FIELDS):
        crossed[tile] = sums_in[tile] + crossed[tile]
    sums_store = fetch(crossed, sums_out, 10)
    wait_many(rim_out.at[0, others], 0, many_send)
    wait_many(rim_out.at[1, others], 1, many_send)
    wait_relays(sums, 2, many_send)
    wait_many(face_out.at[others], 3, many_send)

    @pl.when(is_relay)
    def _():
        wait_many(relay_out.at[others], 4, many_send)

    fine_store.wait()
    sums_store.wait()
    corner_store.wait()
    for copy in coarse_stores:
        copy.wait()


def average_down(
    coarse_in, fine_in, sums_in, spots_in, coarse_out, fine_out, coarse, fine, sums, spots, arrive, leave
):
    def move(src, dst, sems, index):
        copy = pltpu.make_async_copy(src, dst, sems.at[index])
        copy.start()
        return copy

    spots_load = move(spots_in, spots, arrive, 2 * FIELDS)
    sums_load = move(sums_in, sums, arrive, 2 * FIELDS + 1)
    coarse_loads = [move(coarse_in.at[f], coarse.at[f], arrive, f) for f in range(FIELDS)]
    fine_loads = [move(fine_in.at[f], fine.at[f], arrive, FIELDS + f) for f in range(FIELDS)]
    spots_load.wait()
    sums_load.wait()
    lane = iota((8, 128), 1)
    row = iota((8, 128), 0)
    stores = []
    for f in range(FIELDS):
        coarse_loads[f].wait()
        for c in range(REGIONS):
            cx, cy, cz = spots[4 * c], spots[4 * c + 1], spots[4 * c + 2]
            z = lane - cz
            inside = jnp.logical_and(z >= 0, z < 8)[:, :64]
            place = row * 8 + jnp.clip(z, 0, 7)
            rows = pl.ds(cy, 8)
            old = [coarse[f, cx + x, rows, :] for x in range(8)]
            news = []
            for x in range(8):
                line = jnp.broadcast_to(sums[4 * f + x // 2, c : c + 1, :], (8, 128))
                value = 0.125 * pick(line, place + 64 * (x % 2))
                news.append(jnp.where(inside, value[:, :64], old[x]))
            for x in range(8):
                coarse[f, cx + x, rows, :] = news[x]
        stores.append(move(coarse.at[f], coarse_out.at[f], leave, f))
        fine_loads[f].wait()
        stores.append(move(fine.at[f], fine_out.at[f], leave, FIELDS + f))
    for copy in stores:
        copy.wait()


def on_device(sizes, coarse_state, fine_state, slot_parent, slot_corner):
    members = sizes[1] * sizes[2]
    share = -(-4 * FIELDS // members)
    relays = -(-4 * FIELDS // share)
    hbm = pl.BlockSpec(memory_space=pltpu.HBM)
    fine = jnp.transpose(fine_state, (1, 0, 2))
    corner = jnp.transpose(slot_corner, (1, 0))
    plane = slot_parent.reshape(-1, min(128, slot_parent.shape[0]))
    field_block = (FIELDS, 16, 16, 128)
    rows = 3 * FIELDS
    ringed, fine_next, sums, spots = pl.pallas_call(
        functools.partial(whole, sizes),
        out_shape=(
            jax.ShapeDtypeStruct(coarse_state.shape, F32),
            jax.ShapeDtypeStruct(fine.shape, F32),
            jax.ShapeDtypeStruct((4 * FIELDS, REGIONS, 128), F32),
            jax.ShapeDtypeStruct((4 * REGIONS,), I32),
        ),
        in_specs=[hbm] * 5,
        out_specs=(hbm, hbm, hbm, hbm),
        scratch_shapes=[
            pltpu.SMEM(slot_parent.shape, I32),
            pltpu.SMEM(corner.shape, I32),
            pltpu.VMEM(plane.shape, I32),
            pltpu.VMEM(coarse_state.shape, F32),
            pltpu.VMEM((FIELDS, 18, 16, 128), F32),
            pltpu.VMEM(field_block, F32),
            pltpu.VMEM((FIELDS, 17, 16, 128), F32),
            pltpu.VMEM(field_block, F32),
            pltpu.VMEM(field_block, F32),
            pltpu.VMEM(field_block, F32),
            pltpu.VMEM(field_block, F32),
            pltpu.VMEM((16, 16, 128), F32),
            pltpu.VMEM((16, REGIONS, 16, 128), I32),
            pltpu.VMEM((2, FIELDS, 16, 128), F32),
            pltpu.VMEM((2, 2, FIELDS, 128), F32),
            pltpu.VMEM((2, FIELDS, 16, 128), F32),
            pltpu.VMEM((2, FIELDS, 16, 128), F32),
            pltpu.VMEM((2, 2, FIELDS, 128), F32),
            pltpu.VMEM((2, REGIONS, 3 * FIELDS, 128), F32),
            pltpu.VMEM((2, members, 3 * FIELDS, 128), F32),
            pltpu.VMEM((members, 3 * FIELDS, 128), F32),
            pltpu.VMEM((members, 3 * FIELDS, 128), F32),
            pltpu.VMEM((3 * FIELDS, BOXMAX, 128), F32),
            pltpu.VMEM(fine.shape, F32),
            pltpu.VMEM((3,) + fine.shape[1:], F32),
            pltpu.VMEM(fine.shape, F32),
            pltpu.VMEM(fine.shape, F32),
            pltpu.VMEM(coarse_state.shape, F32),
            pltpu.VMEM((rows, BOXMAX, 128), F32),
            pltpu.VMEM((8, rows, BOXMAX, 128), F32),
            pltpu.VMEM((REGIONS * members, BOXMAX * members), F32),
            pltpu.VMEM((members, share, BOXMAX, 128), F32),
            pltpu.VMEM((members, share, REGIONS, 128), F32),
            pltpu.VMEM((relays * share, BOXMAX, 128), F32),
            pltpu.VMEM((relays * share, REGIONS, 128), F32),
            pltpu.VMEM((BOXMAX, rows, 128), F32),
            pltpu.VMEM((members, rows, 128), F32),
            pltpu.VMEM((members, rows, 128), F32),
            pltpu.VMEM((rows, REGIONS, 128), F32),
            pltpu.VMEM((FIELDS, 10, REGIONS, 128), F32),
            pltpu.VMEM((4 * FIELDS, REGIONS, 128), F32),
            pltpu.SMEM((32 + 2 * members,), I32),
            pltpu.SMEM((4 * REGIONS,), I32),
            pltpu.SemaphoreType.DMA((12,)),
            pltpu.SemaphoreType.DMA((6,)),
            pltpu.SemaphoreType.DMA((6,)),
            pltpu.SemaphoreType.DMA((5,)),
            pltpu.SemaphoreType.DMA((5,)),
        ],
        compiler_params=pltpu.CompilerParams(
            collective_id=0, has_side_effects=True, vmem_limit_bytes=62 * 1024 * 1024
        ),
    )(slot_parent, plane, corner, coarse_state, fine)
    coarse_next, fine_next = pl.pallas_call(
        average_down,
        out_shape=(
            jax.ShapeDtypeStruct(coarse_state.shape, F32),
            jax.ShapeDtypeStruct(fine.shape, F32),
        ),
        in_specs=[hbm] * 4,
        out_specs=(hbm, hbm),
        scratch_shapes=[
            pltpu.VMEM(coarse_state.shape, F32),
            pltpu.VMEM(fine.shape, F32),
            pltpu.VMEM((4 * FIELDS, REGIONS, 128), F32),
            pltpu.SMEM((4 * REGIONS,), I32),
            pltpu.SemaphoreType.DMA((2 * FIELDS + 2,)),
            pltpu.SemaphoreType.DMA((2 * FIELDS,)),
        ],
        compiler_params=pltpu.CompilerParams(vmem_limit_bytes=62 * 1024 * 1024),
    )(ringed, fine_next, sums, spots)
    return coarse_next, jnp.transpose(fine_next, (1, 0, 2))


def solution(mesh):
    sizes = tuple(mesh.shape[name] for name in ("gx", "gy", "gz"))
    return jax.shard_map(
        functools.partial(on_device, sizes),
        mesh=mesh,
        in_specs=(P(None, "gx", "gy", "gz"), P(("gx", "gy", "gz"), None, None), P(), P()),
        out_specs=(P(None, "gx", "gy", "gz"), P(("gx", "gy", "gz"), None, None)),
        check_vma=False,
    )
```

```python
import functools

import jax
import jax.numpy as jnp
from jax import lax
from jax.experimental import pallas as pl
from jax.experimental.pallas import tpu as pltpu
from jax.sharding import PartitionSpec as P

GAMMA = 1.4
COURANT = 0.04
PRIM_UNROLL = 2
YZ_UNROLL = 2
OUTER_UNROLL = 8
GATHER_UNROLL = 8
COARSE_UNROLL = 4
CUT_UNROLL = 4
SETTLE_UNROLL = 4
FIELDS = 5
REGIONS = 4
BOXMAX = 8
MESH = pl.DeviceIdType.MESH
F32 = jnp.float32
I32 = jnp.int32


def iota(shape, dim):
    return lax.broadcasted_iota(I32, shape, dim)


def pick(values, lanes):
    numbers = lax.GatherDimensionNumbers(
        offset_dims=(),
        collapsed_slice_dims=(1,),
        start_index_map=(1,),
        operand_batching_dims=(0,),
        start_indices_batching_dims=(0,),
    )
    return lax.gather(
        values,
        lanes[..., None],
        numbers,
        (1, 1),
        mode=lax.GatherScatterMode.PROMISE_IN_BOUNDS,
    )


def prims(q):
    inverse = pl.reciprocal(q[0], approx=True)
    inverse = inverse * (2.0 - q[0] * inverse)
    kinetic = 0.5 * (q[1] * q[1] + q[2] * q[2] + q[3] * q[3]) * inverse
    pressure = (GAMMA - 1.0) * (q[4] - kinetic)
    square = GAMMA * pressure * inverse
    sound = square * lax.rsqrt(jnp.maximum(square, 1e-30))
    return inverse, pressure, sound, q[4] + pressure


def along(q, prim, axis):
    inverse, pressure, sound, total = prim
    velocity = q[1 + axis] * inverse
    flux = [q[1 + axis], q[1] * velocity, q[2] * velocity, q[3] * velocity, total * velocity]
    flux[1 + axis] = flux[1 + axis] + pressure
    return flux, jnp.abs(velocity) + sound


def face(low, low_terms, high, high_terms):
    signal = jnp.maximum(low_terms[1], high_terms[1])
    return [
        (low_terms[0][f] + high_terms[0][f]) - signal * (high[f] - low[f]) for f in range(FIELDS)
    ]


def moved(q, terms, move):
    return [move(v) for v in q], [move(v) for v in terms[0]], move(terms[1])


def span(plane, h):
    return pl.ds(pl.multiple_of(plane * 256 + h * 128, 128), 128)


def roll(v, by):
    return pltpu.roll(v, by % 128, 1)


def fine_prims(cells, prim):
    def one(plane, _):
        for h in range(2):
            where = span(plane, h)
            inverse, pressure, sound, _ = prims([cells[f, :, where] for f in range(FIELDS)])
            prim[0, :, where] = inverse
            prim[1, :, where] = pressure
            prim[2, :, where] = sound
        return 0

    lax.fori_loop(0, 16, one, 0, unroll=PRIM_UNROLL)


def fine_inner(cells, prim, out):
    lane = iota((BOXMAX, 128), 1)
    first_row = lane < 16
    last_row = lane >= 112
    k_first = lane % 16 == 0

    def load(plane, h):
        where = span(plane, h)
        q = [cells[f, :, where] for f in range(FIELDS)]
        pressure = prim[1, :, where]
        return q, (prim[0, :, where], pressure, prim[2, :, where], q[4] + pressure)

    none = [[jnp.zeros((BOXMAX, 128), F32)] * FIELDS] * 2

    def one(plane, x_low):
        cell = [load(plane, h) for h in range(2)]
        after = [load(jnp.minimum(plane + 1, 15), h) for h in range(2)]
        partial = [cell[h][0] for h in range(2)]
        for h in range(2):
            q, q_prim = cell[h]
            terms = along(q, q_prim, 2)
            shifted = moved(q, terms, lambda v: roll(v, 1))
            z = face(shifted[0], (shifted[1], shifted[2]), q, terms)
            partial[h] = list(partial[h])
            for f in range(FIELDS):
                low = jnp.where(k_first, 0.0, z[f])
                partial[h][f] = partial[h][f] - (0.5 * COURANT) * (roll(low, -1) - low)
        q0, prim0 = cell[0]
        q1, prim1 = cell[1]
        terms0 = along(q0, prim0, 1)
        terms1 = along(q1, prim1, 1)
        shifted0 = moved(q0, terms0, lambda v: roll(v, 16))
        shifted1 = moved(q1, terms1, lambda v: roll(v, 16))

        def seam(low, high):
            return jnp.where(first_row, low, high)

        low1 = (
            [seam(shifted0[0][f], shifted1[0][f]) for f in range(FIELDS)],
            (
                [seam(shifted0[1][f], shifted1[1][f]) for f in range(FIELDS)],
                seam(shifted0[2], shifted1[2]),
            ),
        )
        y0 = face(shifted0[0], (shifted0[1], shifted0[2]), q0, terms0)
        y1 = face(low1[0], low1[1], q1, terms1)
        for f in range(FIELDS):
            low = jnp.where(first_row, 0.0, y0[f])
            up0 = roll(low, -16)
            up1 = roll(y1[f], -16)
            change0 = jnp.where(last_row, up1, up0) - low
            change1 = jnp.where(last_row, up0, up1) - y1[f]
            partial[0][f] = partial[0][f] - (0.5 * COURANT) * change0
            partial[1][f] = partial[1][f] - (0.5 * COURANT) * change1
        x_high = [
            face(
                cell[h][0],
                along(cell[h][0], cell[h][1], 0),
                after[h][0],
                along(after[h][0], after[h][1], 0),
            )
            for h in range(2)
        ]
        x_high = [[jnp.where(plane < 15, v, 0.0) for v in x_high[h]] for h in range(2)]
        for h in range(2):
            for f in range(FIELDS):
                out[f, :, span(plane, h)] = partial[h][f] - (0.5 * COURANT) * (
                    x_high[h][f] - x_low[h][f]
                )
        return x_high

    lax.fori_loop(0, 16, one, none, unroll=YZ_UNROLL)


def fine_outer(cells, prim, rim, reg, filled, out, old, edges):
    second = old is not None
    lane = iota((BOXMAX, 128), 1)
    k = lane % 16
    half_k = k // 2
    quarter = lane // 32
    squeeze = ((lane % 32) // 8) * 32 + (lane % 8) * 2
    part = (lane % 64) // 8
    low_half = lane < 64
    step = 0.5 * COURANT
    y_sign = jnp.where(low_half, 1.0, -1.0)
    z_sign = jnp.where(k < 8, 1.0, -1.0)
    y_weight = (jnp.where(lane < 16, step, 0.0), jnp.where(lane >= 112, -step, 0.0))
    z_weight = jnp.where(k == 0, step, jnp.where(k == 15, -step, 0.0))

    def load(plane, h):
        where = span(plane, h)
        q = [cells[f, :, where] for f in range(FIELDS)]
        pressure = prim[1, :, where]
        return q, (prim[0, :, where], pressure, prim[2, :, where], q[4] + pressure)

    def edge(ghost, ghost_terms, q, terms, sign):
        signal = jnp.maximum(ghost_terms[1], terms[1]) * sign
        return [
            (ghost_terms[0][f] + terms[0][f]) - signal * (q[f] - ghost[f]) for f in range(FIELDS)
        ]

    results = []
    for plane, side, sign in ((0, 0, 1.0), (15, 64, -1.0)):
        flux = []
        for h in range(2):
            spread = (h * 4 + quarter) * 8 + half_k + side
            ghost = [pick(rim[3 * f], spread) for f in range(FIELDS)]
            q, q_prim = load(plane, h)
            flux.append(edge(ghost, along(ghost, prims(ghost), 0), q, along(q, q_prim, 0), sign))
            results.append(
                [out[f, :, span(plane, h)] + (sign * step) * flux[h][f] for f in range(FIELDS)]
            )
        for f in range(FIELDS):
            found = []
            for h in range(2):
                v = flux[h][f]
                v = v + roll(v, -1)
                v = v + roll(v, -16)
                found.append(pick(v, squeeze))
            results.append(jnp.where((lane % 64) < 32, found[0], found[1]))
    for plane, first in ((0, 0), (15, 2 + FIELDS)):
        for h in range(2):
            for f in range(FIELDS):
                out[f, :, span(plane, h)] = results[first + h][f]
    for f in range(FIELDS):
        v = jnp.where(low_half, results[2 + f], results[4 + FIELDS + f])
        reg[3 * f] = reg[3 * f] + jnp.where(filled, v, 0.0)

    def pair(big, _):
        y_lanes = big * 8 + half_k + jnp.where(low_half, 0, 64)
        y_ghost = [pick(rim[3 * f + 1], y_lanes) for f in range(FIELDS)]
        y_ghost_terms = along(y_ghost, prims(y_ghost), 1)
        z_ghost = []
        z_ghost_terms = []
        for h in range(2):
            z_lanes = big * 8 + h * 4 + quarter + jnp.where(k >= 8, 64, 0)
            ghost = [pick(rim[3 * f + 2], z_lanes) for f in range(FIELDS)]
            z_ghost.append(ghost)
            z_ghost_terms.append(along(ghost, prims(ghost), 2))
        y_sum = [None] * FIELDS
        z_sum = [[None] * FIELDS for _ in range(2)]

        def accumulate(total, v):
            return v if total is None else total + v

        for sub in range(2):
            plane = 2 * big + sub
            q, q_prim = zip(*[load(plane, h) for h in range(2)])
            near = [jnp.where(low_half, q[0][f], q[1][f]) for f in range(FIELDS)]
            near_prim = [jnp.where(low_half, q_prim[0][i], q_prim[1][i]) for i in range(4)]
            before = [[out[f, :, span(plane, h)] for f in range(FIELDS)] for h in range(2)]
            if second:
                kept = [[old[f, :, span(plane, h)] for f in range(FIELDS)] for h in range(2)]
            y = edge(y_ghost, y_ghost_terms, near, along(near, near_prim, 1), y_sign)
            for f in range(FIELDS):
                y_sum[f] = accumulate(y_sum[f], y[f])
            news = []
            for h in range(2):
                z = edge(z_ghost[h], z_ghost_terms[h], q[h], along(q[h], q_prim[h], 2), z_sign)
                for f in range(FIELDS):
                    z_sum[h][f] = accumulate(z_sum[h][f], z[f])
                    new = before[h][f] + y_weight[h] * y[f] + z_weight * z[f]
                    if second:
                        new = jnp.where(filled, new, kept[h][f])
                    news.append((f, h, new))
            for f, h, new in news:
                out[f, :, span(plane, h)] = new

        for f in range(FIELDS):
            edges[big, f] = y_sum[f]
            edges[big, FIELDS + f] = z_sum[0][f]
            edges[big, 2 * FIELDS + f] = z_sum[1][f]
        return 0

    lax.fori_loop(0, 8, pair, 0, unroll=OUTER_UNROLL)

    def gather(big, totals):
        y_sum = [edges[big, f] for f in range(FIELDS)]
        z_sum = [[edges[big, (1 + h) * FIELDS + f] for f in range(FIELDS)] for h in range(2)]
        mine = jnp.logical_and(filled, part == big)
        y_from = (lane % 8) * 2 + jnp.where(low_half, 0, 112)
        z_from = (lane % 4) * 32 + jnp.where(low_half, 0, 15)
        new_totals = []
        for f in range(FIELDS):
            v = y_sum[f] + roll(y_sum[f], -1)
            new_totals.append(totals[2 * f] + jnp.where(mine, pick(v, y_from), 0.0))
            found = []
            for h in range(2):
                v = z_sum[h][f] + roll(z_sum[h][f], -16)
                found.append(pick(v, z_from))
            v = jnp.where(lane % 8 < 4, found[0], found[1])
            new_totals.append(totals[2 * f + 1] + jnp.where(mine, v, 0.0))
        return new_totals

    totals = [reg[3 * f + t] for f in range(FIELDS) for t in (1, 2)]
    totals = lax.fori_loop(0, 8, gather, totals, unroll=GATHER_UNROLL)
    for f in range(FIELDS):
        reg[3 * f + 1] = totals[2 * f]
        reg[3 * f + 2] = totals[2 * f + 1]


def through(tx, ty, tz, group):
    lane = iota(tx.shape, 1)
    x = 2 * group + lane // 64
    y = (lane % 64) // 8
    z = lane % 8

    def sign(place):
        return jnp.where(place == 0, 1.0, jnp.where(place == 7, -1.0, 0.0))

    total = sign(y) * pick(ty, x * 8 + z + jnp.where(y == 7, 64, 0))
    total = total + sign(z) * pick(tz, x * 8 + y + jnp.where(z == 7, 64, 0))
    if group == 0:
        total = total + jnp.where(lane < 64, tx, 0.0)
    if group == 3:
        total = total - jnp.where(lane < 64, 0.0, tx)
    return total


def fine_average(cells, reg, filled, sums):
    lane = iota((BOXMAX, 128), 1)
    even_k = lane % 2 == 0
    even_j = (lane // 16) % 2 == 0
    squeeze = (2 * ((lane % 32) // 8) + lane // 64) * 16 + (lane % 8) * 2 + (lane % 64) // 32
    faces = [reg[v] for v in range(3 * FIELDS)]
    for group in range(4):
        tiles = []
        for f in range(FIELDS):
            for sub in range(2):
                for h in range(2):
                    plane = 4 * group + 2 * sub
                    tiles.append(cells[f, :, span(plane, h)] + cells[f, :, span(plane + 1, h)])
        tiles = [v + roll(v, 1 if n % 2 else -1) for n, v in enumerate(tiles)]
        tiles = [jnp.where(even_k, tiles[n], tiles[n + 1]) for n in range(0, 4 * FIELDS, 2)]
        tiles = [v + roll(v, 16 if n % 2 else -16) for n, v in enumerate(tiles)]
        tiles = [jnp.where(even_j, tiles[n], tiles[n + 1]) for n in range(0, 2 * FIELDS, 2)]
        tiles = [pick(v, squeeze) for v in tiles]
        crossed = [through(*faces[3 * f : 3 * f + 3], group) for f in range(FIELDS)]
        results = [
            jnp.where(filled, tiles[f] - (0.5 * COURANT) * crossed[f], 0.0) for f in range(FIELDS)
        ]
        for f in range(FIELDS):
            sums[4 * f + group] = results[f]


def coarse_step(block, y_rim, z_rim, new, x_face, y_low, y_high, z_low, z_high):
    lane = iota((16, 128), 1)
    row = iota((16, 128), 0)
    tip = iota((8, 128), 0)

    def load(plane):
        return [block[f, plane] for f in range(FIELDS)]

    def widen(x, _):
        column = (x % 8) * 16 + row
        for f in range(FIELDS):
            below = jnp.broadcast_to(z_rim[0, x // 8, f : f + 1, :], (16, 128))
            above = jnp.broadcast_to(z_rim[1, x // 8, f : f + 1, :], (16, 128))
            side = jnp.where(lane == 64, pick(above, column), pick(below, column))
            block[f, x + 1] = jnp.where(lane < 64, block[f, x + 1], side)
        return 0

    lax.fori_loop(0, 16, widen, 0, unroll=4)

    ghost = load(0)
    here = load(1)
    here_prim = prims(here)
    low = face(ghost, along(ghost, prims(ghost), 0), here, along(here, here_prim, 0))
    for f in range(FIELDS):
        x_face[f, 0] = low[f]

    def one(x, carried):
        here, here_prim, x_low = carried
        after = load(x + 2)
        after_prim = prims(after)
        x_high = face(here, along(here, here_prim, 0), after, along(after, after_prim, 0))

        tips = []
        for f in range(FIELDS):
            above = y_rim[1, f, pl.ds(x, 1), :]
            below = y_rim[0, f, pl.ds(x, 1), :]
            tips.append(
                jnp.where(
                    tip == 0,
                    jnp.broadcast_to(above, (8, 128)),
                    jnp.broadcast_to(below, (8, 128)),
                )
            )
        tip_terms = along(tips, prims(tips), 1)
        terms = along(here, here_prim, 1)

        def tall(low, high):
            return jnp.concatenate([low, high], axis=0)

        cells = [tall(here[f], tips[f]) for f in range(FIELDS)]
        terms = ([tall(terms[0][f], tip_terms[0][f]) for f in range(FIELDS)], tall(terms[1], tip_terms[1]))
        shifted = moved(cells, terms, lambda v: pltpu.roll(v, 1, 0))
        y = face(shifted[0], (shifted[1], shifted[2]), cells, terms)

        terms = along(here, here_prim, 2)
        shifted = moved(here, terms, lambda v: pltpu.roll(v, 1, 1))
        z = face(shifted[0], (shifted[1], shifted[2]), here, terms)
        for f in range(FIELDS):
            up = pltpu.roll(y[f], 23, 0)[:16]
            down = y[f][:16]
            right = pltpu.roll(z[f], 127, 1)
            x_face[f, x + 1] = x_high[f]
            y_low[f, x] = down
            y_high[f, x] = up
            z_low[f, x] = z[f]
            z_high[f, x] = right
            change = (x_high[f] - x_low[f]) + (up - down) + (right - z[f])
            new[f, x] = here[f] - (0.5 * COURANT) * change
        return after, after_prim, x_high

    lax.fori_loop(0, 16, one, (here, here_prim, low), unroll=COARSE_UNROLL)


def cut_rims(source, corner):
    cx, cy, cz = corner
    lane = iota((8, 128), 1)
    row = iota((8, 128), 0)
    low_half = lane < 64
    part = (lane % 64) // 8
    along_z = cz + lane % 8
    ends = jnp.where(low_half, cz - 1, cz + 8)
    rows_x = row == part
    rows_z = row == lane % 8
    lines = []
    for f in range(FIELDS):
        low = pick(source(f, cx - 1, cy, 8), along_z)
        high = pick(source(f, cx + 8, cy, 8), along_z)
        v = jnp.where(rows_x, jnp.where(low_half, low, high), 0.0)
        lines.append(jnp.sum(v, axis=0, keepdims=True))
        low = jnp.zeros((8, 128), F32)
        high = jnp.zeros((8, 128), F32)
        total = jnp.zeros((8, 128), F32)
        for big in range(8):
            here = row == big
            low = jnp.where(here, jnp.broadcast_to(source(f, cx + big, cy - 1, 1), (8, 128)), low)
            high = jnp.where(here, jnp.broadcast_to(source(f, cx + big, cy + 8, 1), (8, 128)), high)
            total = jnp.where(part == big, pick(source(f, cx + big, cy, 8), ends), total)
        v = jnp.where(low_half, pick(low, along_z), pick(high, along_z))
        lines.append(jnp.sum(jnp.where(rows_x, v, 0.0), axis=0, keepdims=True))
        lines.append(jnp.sum(jnp.where(rows_z, total, 0.0), axis=0, keepdims=True))
    return lines


def plan_settle(corners, new, x_face, y_low, y_high, z_low, z_high, weight, index):
    lane = iota((16, 128), 1)
    row = iota((16, 128), 0)

    def one(x, _):
        kind = jnp.zeros((16, 128), I32)
        for c in range(REGIONS):
            cx, cy, cz = corners[c]
            step = x - cx
            inside = jnp.logical_and(step >= 0, step < 8)
            dy = row - cy
            dz = lane - cz
            in_y = jnp.logical_and(dy >= 0, dy < 8)
            in_z = jnp.logical_and(dz >= 0, dz < 8)
            near = jnp.where(dy == -1, 4, jnp.where(dy == 8, 5, 0))
            side = jnp.where(dz == -1, 6, jnp.where(dz == 8, 7, 0))
            plain = jnp.where(inside, 1, jnp.where(step == -1, 2, jnp.where(step == 8, 3, 0)))
            mine = jnp.where(
                jnp.logical_and(in_y, in_z),
                plain,
                jnp.where(inside, jnp.where(in_z, near, jnp.where(in_y, side, 0)), 0),
            )
            ys = jnp.clip(dy, 0, 7)
            zs = jnp.clip(dz, 0, 7)
            lanes = jnp.where(mine < 4, ys * 8 + zs, 32 + 8 * mine + jnp.where(mine < 6, zs, ys))
            used = mine > 0
            kind = jnp.where(used, mine, kind)
            index[x, c] = jnp.where(used, lanes + 128, 0)
        factor = jnp.where(kind < 2, 0.0, jnp.where(kind % 2 == 0, -COURANT, COURANT))
        weight[x] = jnp.where(kind == 1, 0.125, 0.0625 * factor)
        for f in range(FIELDS):
            flux = jnp.where(
                kind < 4,
                jnp.where(kind == 2, x_face[f, x + 1], x_face[f, x]),
                jnp.where(
                    kind < 6,
                    jnp.where(kind == 4, y_high[f, x], y_low[f, x]),
                    jnp.where(kind == 6, z_high[f, x], z_low[f, x]),
                ),
            )
            plain = new[f, x]
            ring = jnp.where(kind >= 2, plain - 0.5 * factor * flux, plain)
            new[f, x] = jnp.where(kind == 1, 0.0, ring)
        return 0

    lax.fori_loop(0, 16, one, 0)


def settle_rows(faces, rows, crossed):
    lane = iota((REGIONS, 128), 1)
    spot = ((lane % 16) // 8) * 64 + lane % 8
    results = []
    added = []
    for f in range(FIELDS):
        tx, ty, tz = faces[3 * f], faces[3 * f + 1], faces[3 * f + 2]
        results.append((f, 0, tx))
        results.append((f, 9, pltpu.roll(tx, 64, 1)))
        for big in range(8):
            around = jnp.where(lane < 80, pick(ty, spot + 8 * big), pick(tz, spot + 8 * big))
            results.append((f, 1 + big, jnp.where(lane < 64, 0.0, around)))
        for group in range(4):
            added.append((0.5 * COURANT) * through(tx, ty, tz, group))
    for f, where, v in results:
        rows[f, where] = v
    for tile, v in enumerate(added):
        crossed[tile] = v


def settle(corners, rows, new, weight, index, out, start):
    def one(step, _):
        x = start + step
        values = [jnp.zeros((16, 128), F32) for _ in range(FIELDS)]
        for c in range(REGIONS):
            which = jnp.clip(x - corners[c][0] + 1, 0, 9)
            lanes = index[x, c]
            used = lanes >= 128
            lanes = lanes & 127
            for f in range(FIELDS):
                line = jnp.broadcast_to(rows[f, which, c : c + 1, :], (16, 128))
                values[f] = jnp.where(used, pick(line, lanes), values[f])
        factor = weight[x]
        results = [new[f, x] + factor * values[f] for f in range(FIELDS)]
        for f in range(FIELDS):
            out[f, x] = results[f][:, :64]
        return 0

    lax.fori_loop(0, 4, one, 0, unroll=SETTLE_UNROLL)


def whole(
    sizes,
    parent_hbm,
    plane_hbm,
    corner_hbm,
    coarse_hbm,
    fine_hbm,
    coarse_out,
    fine_out,
    sums_out,
    spots_out,
    parent_ref,
    corner_ref,
    plane_ref,
    coarse_ref,
    block,
    new,
    x_face,
    y_low,
    y_high,
    z_low,
    z_high,
    weight,
    index,
    y_stage,
    z_stage,
    x_rim,
    y_packed,
    y_rim,
    z_rim,
    cut,
    rim_out,
    rim_in_old,
    rim_in_mid,
    rim,
    fine_ref,
    prim,
    half,
    fine_new,
    coarse_new,
    reg,
    edges,
    route,
    relay_in,
    relay_out,
    sums,
    sums_in,
    row_stage,
    face_out,
    face_in,
    faces,
    answer_rows,
    crossed,
    table,
    spots,
    load_sems,
    halo_send,
    halo_recv,
    many_send,
    many_recv,
):
    n_gx, n_gy, n_gz = sizes
    members = n_gy * n_gz
    share = -(-4 * FIELDS // members)
    relays = -(-4 * FIELDS // share)
    rim_in = (rim_in_old, rim_in_mid)
    gx = lax.axis_index("gx")
    gy = lax.axis_index("gy")
    gz = lax.axis_index("gz")
    within = gy * n_gz + gz
    myself = gx * members + within
    start = gx * (members * BOXMAX)

    def hops(move):
        return min(move[0], n_gy - move[0]) + min(move[1], n_gz - move[1])

    moves = [(dy, dz) for dy in range(n_gy) for dz in range(n_gz) if dy or dz]
    peers = []
    for dy, dz in sorted(moves, key=hops, reverse=True):
        other_y = lax.rem(gy + dy, n_gy)
        other_z = lax.rem(gz + dz, n_gz)
        peers.append((other_y * n_gz + other_z, (gx, other_y, other_z)))

    barrier = pltpu.get_barrier_semaphore()
    for _, device in peers:
        pl.semaphore_signal(barrier, inc=1, device_id=device, device_id_type=MESH)

    x_next = (lax.rem(gx + 1, n_gx), gy, gz)
    x_prev = (lax.rem(gx + n_gx - 1, n_gx), gy, gz)
    y_next = (gx, lax.rem(gy + 1, n_gy), gz)
    y_prev = (gx, lax.rem(gy + n_gy - 1, n_gy), gz)
    z_next = (gx, gy, lax.rem(gz + 1, n_gz))
    z_prev = (gx, gy, lax.rem(gz + n_gz - 1, n_gz))
    pl.semaphore_signal(barrier, inc=1, device_id=x_next, device_id_type=MESH)
    pl.semaphore_signal(barrier, inc=1, device_id=x_prev, device_id_type=MESH)

    def fetch(src, dst, index):
        copy = pltpu.make_async_copy(src, dst, load_sems.at[index])
        copy.start()
        return copy

    coarse_load = fetch(coarse_hbm, coarse_ref, 0)
    parent_load = fetch(parent_hbm, parent_ref, 1)
    corner_load = fetch(corner_hbm, corner_ref, 2)
    plane_load = fetch(plane_hbm, plane_ref, 3)
    fine_load = fetch(fine_hbm, fine_ref, 4)

    parent_load.wait()
    corner_load.wait()

    def scan(entry, found):
        c0, c1, c2, c3 = found
        hit = parent_ref[start + entry] == myself
        return (
            jnp.where(hit, c1, c0),
            jnp.where(hit, c2, c1),
            jnp.where(hit, c3, c2),
            jnp.where(hit, entry, c3),
        )

    zero = jnp.int32(0)
    children = lax.fori_loop(0, members * BOXMAX, scan, (zero, zero, zero, zero), unroll=8)
    for c in range(REGIONS):
        for k in range(3):
            spot = jnp.clip(corner_ref[k, start + children[c]], 1, 55 if k == 2 else 7)
            table[4 * c + k] = spot
            spots[4 * c + k] = spot
        spots[4 * c + 3] = zero
    corner_store = fetch(spots, spots_out, 11)
    child_peer = [child // BOXMAX for child in children]
    own = [parent_ref[start + within * BOXMAX + s] for s in range(BOXMAX)]
    own_peer = [lax.rem(jnp.maximum(own[s], 0), members) for s in range(BOXMAX)]

    def look_up(other, _):
        rank = zero
        for c in range(1, REGIONS):
            rank = jnp.where(child_peer[c] == other, c, rank)
        found = zero
        for s in range(BOXMAX):
            found = jnp.where(jnp.logical_and(own[s] >= 0, own_peer[s] == other), s, found)
        table[32 + other] = rank
        table[32 + members + other] = found
        return 0

    lax.fori_loop(0, members, look_up, 0, unroll=4)

    def cut_all(when, source):
        def one(c, _):
            corner = (table[4 * c], table[4 * c + 1], table[4 * c + 2])

            for v, line in enumerate(cut_rims(source, corner)):
                cut[when, c, v : v + 1, :] = line
            return 0

        lax.fori_loop(0, REGIONS, one, 0, unroll=CUT_UNROLL)

    def ship(src, dst, index, device):
        pltpu.make_async_remote_copy(
            src_ref=src,
            dst_ref=dst,
            send_sem=many_send.at[index],
            recv_sem=many_recv.at[index],
            device_id=device,
            device_id_type=MESH,
        ).start()

    def wait_many(every, index, semaphores):
        pltpu.make_async_copy(every, every, semaphores.at[index]).wait()

    others = pl.ds(0, members - 1)

    def fill_rims(when):
        def one(other, _):
            rim_out[when, other] = cut[when, table[32 + other]]
            return 0

        lax.fori_loop(0, members, one, 0, unroll=4)
        rim_in[when][within] = rim_out[when, within]

    def send_rims(when):
        for other, device in peers:
            ship(rim_out.at[when, other], rim_in[when].at[within], when, device)

    lane16 = iota((16, 128), 1)
    row16 = iota((16, 128), 0)
    coarse_load.wait()
    for f in range(FIELDS):
        block[f, 1:17, :, 0:64] = coarse_ref[f]
    match = row16 == lane16 % 16
    lane8 = iota((8, 128), 1)
    edge_rows = [(block[f, 1:17, 0, :], block[f, 1:17, 15, :]) for f in range(FIELDS)]
    columns_found = []
    for f in range(FIELDS):
        for h in range(2):
            low = jnp.zeros((16, 128), F32)
            high = jnp.zeros((16, 128), F32)
            for x in range(8):
                plane = block[f, 1 + 8 * h + x]
                here = lane16 // 16 == x
                low = jnp.where(here, jnp.broadcast_to(plane[:, 0:1], (16, 128)), low)
                high = jnp.where(here, jnp.broadcast_to(plane[:, 63:64], (16, 128)), high)
            low = jnp.sum(jnp.where(match, low, 0.0), axis=0, keepdims=True)
            high = jnp.sum(jnp.where(match, high, 0.0), axis=0, keepdims=True)
            columns_found.append((f, h, low, high))
    for f in range(FIELDS):
        for side in range(2):
            rows = edge_rows[f][side]
            y_stage[side, f] = jnp.where(lane8 < 64, rows[:8], pltpu.roll(rows[8:], 64, 1))
    for f, h, low, high in columns_found:
        z_stage[0, h, f : f + 1, :] = low
        z_stage[1, h, f : f + 1, :] = high

    cut_all(0, lambda f, x, y, n: block[f, x + 1, pl.ds(y, n), :])
    fill_rims(0)

    pl.semaphore_wait(barrier, members + 1)

    def halo(src, dst, index, device):
        copy = pltpu.make_async_remote_copy(
            src_ref=src,
            dst_ref=dst,
            send_sem=halo_send.at[index],
            recv_sem=halo_recv.at[index],
            device_id=device,
            device_id_type=MESH,
        )
        copy.start()
        return copy

    halos = [
        halo(block.at[:, 16], x_rim.at[0], 0, x_next),
        halo(block.at[:, 1], x_rim.at[1], 1, x_prev),
        halo(y_stage.at[1], y_packed.at[0], 2, y_next),
        halo(y_stage.at[0], y_packed.at[1], 3, y_prev),
        halo(z_stage.at[1], z_rim.at[0], 4, z_next),
        halo(z_stage.at[0], z_rim.at[1], 5, z_prev),
    ]

    send_rims(0)

    for v in range(3 * FIELDS):
        reg[v] = jnp.zeros((BOXMAX, 128), F32)

    for copy in halos:
        copy.wait()
    for f in range(FIELDS):
        block[f, 0] = x_rim[0, f]
        block[f, 17] = x_rim[1, f]
        for side in range(2):
            y_rim[side, f, 0:8] = y_packed[side, f]
            y_rim[side, f, 8:16] = pltpu.roll(y_packed[side, f], 64, 1)
    coarse_step(block, y_rim, z_rim, new, x_face, y_low, y_high, z_low, z_high)
    cut_all(
        1,
        lambda f, x, y, n: 0.5 * (block[f, x + 1, pl.ds(y, n), :] + new[f, x, pl.ds(y, n), :]),
    )
    fill_rims(1)
    send_rims(1)

    plane_load.wait()
    n_rows = REGIONS * members
    columns = members * BOXMAX
    row = iota((n_rows, columns), 0)
    column = iota((n_rows, columns), 1)
    slots = plane_ref[pl.ds(gx * (columns // 128), columns // 128), :] if columns >= 128 else None
    if columns >= 128:
        slots = jnp.concatenate(
            [
                jnp.broadcast_to(slots[h : h + 1, :], (n_rows, 128))
                for h in range(columns // 128)
            ],
            axis=1,
        )
    else:
        slots = jnp.broadcast_to(plane_ref[0:1, 0:columns], (n_rows, columns))
    number = column.astype(F32)
    far = 65536.0
    candidate = jnp.where(slots == row // REGIONS + gx * members, number, far)
    chosen = jnp.full((n_rows, 1), far)
    for r in range(REGIONS):
        least = jnp.min(candidate, axis=1, keepdims=True)
        chosen = jnp.where(row[:, 0:1] % REGIONS == r, least, chosen)
        candidate = jnp.where(candidate == least, far, candidate)
    route[...] = jnp.where(number == chosen, 1.0, 0.0)

    fine_load.wait()
    fine_prims(fine_ref, prim)
    fine_inner(fine_ref, prim, half)

    sub = iota((BOXMAX, 128), 0)
    owner = jnp.zeros((BOXMAX, 128), I32)
    for s in range(BOXMAX):
        owner = jnp.where(sub == s, own[s], owner)
    filled = owner >= 0

    def take_rims(when):
        wait_many(rim_in[when].at[others], when, many_recv)
        for s in range(BOXMAX):
            rows = rim_in[when][own_peer[s]]
            for v in range(3 * FIELDS):
                rim[v, s : s + 1, :] = rows[v : v + 1, :]

    take_rims(0)
    fine_outer(fine_ref, prim, rim, reg, filled, half, None, edges)
    fine_prims(half, prim)
    fine_inner(half, prim, fine_new)
    fine_average(fine_new, reg, filled, sums)

    is_relay = within < relays
    for other, device in peers:

        @pl.when(other < relays)
        def _(other=other, device=device):
            ship(sums.at[pl.ds(other * share, share)], relay_in.at[within], 2, device)

    @pl.when(is_relay)
    def _():
        relay_in[within] = sums[pl.ds(within * share, share)]

    take_rims(1)
    fine_outer(half, prim, rim, reg, filled, fine_new, fine_ref, edges)
    fine_store = fetch(fine_new, fine_out, 5)

    for s in range(BOXMAX):
        row_stage[s] = reg[:, s, :]
    for other, device in peers:
        face_out[other] = row_stage[table[32 + members + other]]
        ship(face_out.at[other], face_in.at[within], 3, device)
    face_in[within] = row_stage[table[32 + members + within]]

    @pl.when(is_relay)
    def _():
        wait_many(relay_in.at[others], 2, many_recv)
        for j in range(share):
            sorted_rows = jnp.dot(
                route[...],
                relay_in[:, j].reshape(columns, 128),
                precision=lax.Precision.HIGHEST,
                preferred_element_type=F32,
            )
            for p in range(members):
                relay_out[p, j] = sorted_rows[REGIONS * p : REGIONS * p + REGIONS]
        for other, device in peers:
            ship(relay_out.at[other], sums_in.at[pl.ds(within * share, share)], 4, device)
        sums_in[pl.ds(within * share, share)] = relay_out[within]

    corners = [(table[4 * c], table[4 * c + 1], table[4 * c + 2]) for c in range(REGIONS)]
    plan_settle(corners, new, x_face, y_low, y_high, z_low, z_high, weight, index)

    wait_many(face_in.at[others], 3, many_recv)
    for c in range(REGIONS):
        rows = face_in[child_peer[c]]
        for v in range(3 * FIELDS):
            faces[v, c : c + 1, :] = rows[v : v + 1, :]

    def wait_relays(every, index, semaphores):
        @pl.when(is_relay)
        def _():
            wait_many(every.at[pl.ds(0, (relays - 1) * share)], index, semaphores)

        @pl.when(jnp.logical_not(is_relay))
        def _():
            wait_many(every.at[pl.ds(0, relays * share)], index, semaphores)

    settle_rows(faces, answer_rows, crossed)
    coarse_stores = []
    for part in range(4):
        settle(corners, answer_rows, new, weight, index, coarse_new, 4 * part)
        planes = pl.ds(4 * part, 4)
        coarse_stores.append(fetch(coarse_new.at[:, planes], coarse_out.at[:, planes], 6 + part))
    wait_relays(sums_in, 4, many_recv)
    for tile in range(4 * FIELDS):
        crossed[tile] = sums_in[tile] + crossed[tile]
    sums_store = fetch(crossed, sums_out, 10)
    wait_many(rim_out.at[0, others], 0, many_send)
    wait_many(rim_out.at[1, others], 1, many_send)
    wait_relays(sums, 2, many_send)
    wait_many(face_out.at[others], 3, many_send)

    @pl.when(is_relay)
    def _():
        wait_many(relay_out.at[others], 4, many_send)

    fine_store.wait()
    sums_store.wait()
    corner_store.wait()
    for copy in coarse_stores:
        copy.wait()


def average_down(
    coarse_in, fine_in, sums_in, spots_in, coarse_out, fine_out, coarse, fine, sums, spots, arrive, leave
):
    def move(src, dst, sems, index):
        copy = pltpu.make_async_copy(src, dst, sems.at[index])
        copy.start()
        return copy

    spots_load = move(spots_in, spots, arrive, 2 * FIELDS)
    sums_load = move(sums_in, sums, arrive, 2 * FIELDS + 1)
    coarse_loads = [move(coarse_in.at[f], coarse.at[f], arrive, f) for f in range(FIELDS)]
    fine_loads = [move(fine_in.at[f], fine.at[f], arrive, FIELDS + f) for f in range(FIELDS)]
    spots_load.wait()
    sums_load.wait()
    lane = iota((8, 128), 1)
    row = iota((8, 128), 0)
    stores = []
    for f in range(FIELDS):
        coarse_loads[f].wait()
        for c in range(REGIONS):
            cx, cy, cz = spots[4 * c], spots[4 * c + 1], spots[4 * c + 2]
            z = lane - cz
            inside = jnp.logical_and(z >= 0, z < 8)[:, :64]
            place = row * 8 + jnp.clip(z, 0, 7)
            rows = pl.ds(cy, 8)
            old = [coarse[f, cx + x, rows, :] for x in range(8)]
            news = []
            for x in range(8):
                line = jnp.broadcast_to(sums[4 * f + x // 2, c : c + 1, :], (8, 128))
                value = 0.125 * pick(line, place + 64 * (x % 2))
                news.append(jnp.where(inside, value[:, :64], old[x]))
            for x in range(8):
                coarse[f, cx + x, rows, :] = news[x]
        stores.append(move(coarse.at[f], coarse_out.at[f], leave, f))
        fine_loads[f].wait()
        stores.append(move(fine.at[f], fine_out.at[f], leave, FIELDS + f))
    for copy in stores:
        copy.wait()


def on_device(sizes, coarse_state, fine_state, slot_parent, slot_corner):
    members = sizes[1] * sizes[2]
    share = -(-4 * FIELDS // members)
    relays = -(-4 * FIELDS // share)
    hbm = pl.BlockSpec(memory_space=pltpu.HBM)
    fine = jnp.transpose(fine_state, (1, 0, 2))
    corner = jnp.transpose(slot_corner, (1, 0))
    plane = slot_parent.reshape(-1, min(128, slot_parent.shape[0]))
    field_block = (FIELDS, 16, 16, 128)
    rows = 3 * FIELDS
    ringed, fine_next, sums, spots = pl.pallas_call(
        functools.partial(whole, sizes),
        out_shape=(
            jax.ShapeDtypeStruct(coarse_state.shape, F32),
            jax.ShapeDtypeStruct(fine.shape, F32),
            jax.ShapeDtypeStruct((4 * FIELDS, REGIONS, 128), F32),
            jax.ShapeDtypeStruct((4 * REGIONS,), I32),
        ),
        in_specs=[hbm] * 5,
        out_specs=(hbm, hbm, hbm, hbm),
        scratch_shapes=[
            pltpu.SMEM(slot_parent.shape, I32),
            pltpu.SMEM(corner.shape, I32),
            pltpu.VMEM(plane.shape, I32),
            pltpu.VMEM(coarse_state.shape, F32),
            pltpu.VMEM((FIELDS, 18, 16, 128), F32),
            pltpu.VMEM(field_block, F32),
            pltpu.VMEM((FIELDS, 17, 16, 128), F32),
            pltpu.VMEM(field_block, F32),
            pltpu.VMEM(field_block, F32),
            pltpu.VMEM(field_block, F32),
            pltpu.VMEM(field_block, F32),
            pltpu.VMEM((16, 16, 128), F32),
            pltpu.VMEM((16, REGIONS, 16, 128), I32),
            pltpu.VMEM((2, FIELDS, 8, 128), F32),
            pltpu.VMEM((2, 2, FIELDS, 128), F32),
            pltpu.VMEM((2, FIELDS, 16, 128), F32),
            pltpu.VMEM((2, FIELDS, 8, 128), F32),
            pltpu.VMEM((2, FIELDS, 16, 128), F32),
            pltpu.VMEM((2, 2, FIELDS, 128), F32),
            pltpu.VMEM((2, REGIONS, 3 * FIELDS, 128), F32),
            pltpu.VMEM((2, members, 3 * FIELDS, 128), F32),
            pltpu.VMEM((members, 3 * FIELDS, 128), F32),
            pltpu.VMEM((members, 3 * FIELDS, 128), F32),
            pltpu.VMEM((3 * FIELDS, BOXMAX, 128), F32),
            pltpu.VMEM(fine.shape, F32),
            pltpu.VMEM((3,) + fine.shape[1:], F32),
            pltpu.VMEM(fine.shape, F32),
            pltpu.VMEM(fine.shape, F32),
            pltpu.VMEM(coarse_state.shape, F32),
            pltpu.VMEM((rows, BOXMAX, 128), F32),
            pltpu.VMEM((8, rows, BOXMAX, 128), F32),
            pltpu.VMEM((REGIONS * members, BOXMAX * members), F32),
            pltpu.VMEM((members, share, BOXMAX, 128), F32),
            pltpu.VMEM((members, share, REGIONS, 128), F32),
            pltpu.VMEM((relays * share, BOXMAX, 128), F32),
            pltpu.VMEM((relays * share, REGIONS, 128), F32),
            pltpu.VMEM((BOXMAX, rows, 128), F32),
            pltpu.VMEM((members, rows, 128), F32),
            pltpu.VMEM((members, rows, 128), F32),
            pltpu.VMEM((rows, REGIONS, 128), F32),
            pltpu.VMEM((FIELDS, 10, REGIONS, 128), F32),
            pltpu.VMEM((4 * FIELDS, REGIONS, 128), F32),
            pltpu.SMEM((32 + 2 * members,), I32),
            pltpu.SMEM((4 * REGIONS,), I32),
            pltpu.SemaphoreType.DMA((12,)),
            pltpu.SemaphoreType.DMA((6,)),
            pltpu.SemaphoreType.DMA((6,)),
            pltpu.SemaphoreType.DMA((5,)),
            pltpu.SemaphoreType.DMA((5,)),
        ],
        compiler_params=pltpu.CompilerParams(
            collective_id=0, has_side_effects=True, vmem_limit_bytes=62 * 1024 * 1024
        ),
    )(slot_parent, plane, corner, coarse_state, fine)
    coarse_next, fine_next = pl.pallas_call(
        average_down,
        out_shape=(
            jax.ShapeDtypeStruct(coarse_state.shape, F32),
            jax.ShapeDtypeStruct(fine.shape, F32),
        ),
        in_specs=[hbm] * 4,
        out_specs=(hbm, hbm),
        scratch_shapes=[
            pltpu.VMEM(coarse_state.shape, F32),
            pltpu.VMEM(fine.shape, F32),
            pltpu.VMEM((4 * FIELDS, REGIONS, 128), F32),
            pltpu.SMEM((4 * REGIONS,), I32),
            pltpu.SemaphoreType.DMA((2 * FIELDS + 2,)),
            pltpu.SemaphoreType.DMA((2 * FIELDS,)),
        ],
        compiler_params=pltpu.CompilerParams(vmem_limit_bytes=62 * 1024 * 1024),
    )(ringed, fine_next, sums, spots)
    return coarse_next, jnp.transpose(fine_next, (1, 0, 2))


def solution(mesh):
    sizes = tuple(mesh.shape[name] for name in ("gx", "gy", "gz"))
    return jax.shard_map(
        functools.partial(on_device, sizes),
        mesh=mesh,
        in_specs=(P(None, "gx", "gy", "gz"), P(("gx", "gy", "gz"), None, None), P(), P()),
        out_specs=(P(None, "gx", "gy", "gz"), P(("gx", "gy", "gz"), None, None)),
        check_vma=False,
    )
```

```python
import functools

import jax
import jax.numpy as jnp
from jax import lax
from jax.experimental import pallas as pl
from jax.experimental.pallas import tpu as pltpu
from jax.sharding import PartitionSpec as P

GAMMA = 1.4
COURANT = 0.04
PRIM_UNROLL = 2
YZ_UNROLL = 2
OUTER_UNROLL = 8
GATHER_UNROLL = 8
COARSE_UNROLL = 4
CUT_UNROLL = 4
SETTLE_UNROLL = 4
FIELDS = 5
REGIONS = 4
BOXMAX = 8
MESH = pl.DeviceIdType.MESH
F32 = jnp.float32
I32 = jnp.int32


def iota(shape, dim):
    return lax.broadcasted_iota(I32, shape, dim)


def pick(values, lanes):
    numbers = lax.GatherDimensionNumbers(
        offset_dims=(),
        collapsed_slice_dims=(1,),
        start_index_map=(1,),
        operand_batching_dims=(0,),
        start_indices_batching_dims=(0,),
    )
    return lax.gather(
        values,
        lanes[..., None],
        numbers,
        (1, 1),
        mode=lax.GatherScatterMode.PROMISE_IN_BOUNDS,
    )


def prims(q):
    inverse = pl.reciprocal(q[0], approx=True)
    inverse = inverse * (2.0 - q[0] * inverse)
    kinetic = 0.5 * (q[1] * q[1] + q[2] * q[2] + q[3] * q[3]) * inverse
    pressure = (GAMMA - 1.0) * (q[4] - kinetic)
    square = GAMMA * pressure * inverse
    sound = square * lax.rsqrt(jnp.maximum(square, 1e-30))
    return inverse, pressure, sound, q[4] + pressure


def along(q, prim, axis):
    inverse, pressure, sound, total = prim
    velocity = q[1 + axis] * inverse
    flux = [q[1 + axis], q[1] * velocity, q[2] * velocity, q[3] * velocity, total * velocity]
    flux[1 + axis] = flux[1 + axis] + pressure
    return flux, jnp.abs(velocity) + sound


def face(low, low_terms, high, high_terms):
    signal = jnp.maximum(low_terms[1], high_terms[1])
    return [
        (low_terms[0][f] + high_terms[0][f]) - signal * (high[f] - low[f]) for f in range(FIELDS)
    ]


def moved(q, terms, move):
    return [move(v) for v in q], [move(v) for v in terms[0]], move(terms[1])


def span(plane, h):
    return pl.ds(pl.multiple_of(plane * 256 + h * 128, 128), 128)


def roll(v, by):
    return pltpu.roll(v, by % 128, 1)


def fine_prims(cells, prim):
    def one(plane, _):
        for h in range(2):
            where = span(plane, h)
            inverse, pressure, sound, _ = prims([cells[f, :, where] for f in range(FIELDS)])
            prim[0, :, where] = inverse
            prim[1, :, where] = pressure
            prim[2, :, where] = sound
        return 0

    lax.fori_loop(0, 16, one, 0, unroll=PRIM_UNROLL)


def pulled(q, prim, axis, by):
    cells = [roll(v, by) for v in q]
    inverse, pressure, sound = [roll(v, by) for v in prim[:3]]
    flux, signal = along(cells, (inverse, pressure, sound, cells[4] + pressure), axis)
    return cells, flux, signal


def fine_inner(cells, prim, out):
    lane = iota((BOXMAX, 128), 1)
    first_row = lane < 16
    last_row = lane >= 112
    k_first = lane % 16 == 0

    def load(plane, h):
        where = span(plane, h)
        q = [cells[f, :, where] for f in range(FIELDS)]
        pressure = prim[1, :, where]
        return q, (prim[0, :, where], pressure, prim[2, :, where], q[4] + pressure)

    none = [[jnp.zeros((BOXMAX, 128), F32)] * FIELDS] * 2

    def one(plane, x_low):
        cell = [load(plane, h) for h in range(2)]
        after = [load(jnp.minimum(plane + 1, 15), h) for h in range(2)]
        partial = [cell[h][0] for h in range(2)]
        for h in range(2):
            q, q_prim = cell[h]
            terms = along(q, q_prim, 2)
            shifted = pulled(q, q_prim, 2, 1)
            z = face(shifted[0], (shifted[1], shifted[2]), q, terms)
            partial[h] = list(partial[h])
            for f in range(FIELDS):
                low = jnp.where(k_first, 0.0, z[f])
                partial[h][f] = partial[h][f] - (0.5 * COURANT) * (roll(low, -1) - low)
        q0, prim0 = cell[0]
        q1, prim1 = cell[1]
        terms0 = along(q0, prim0, 1)
        terms1 = along(q1, prim1, 1)
        shifted0 = pulled(q0, prim0, 1, 16)
        shifted1 = pulled(q1, prim1, 1, 16)

        def seam(low, high):
            return jnp.where(first_row, low, high)

        low1 = (
            [seam(shifted0[0][f], shifted1[0][f]) for f in range(FIELDS)],
            (
                [seam(shifted0[1][f], shifted1[1][f]) for f in range(FIELDS)],
                seam(shifted0[2], shifted1[2]),
            ),
        )
        y0 = face(shifted0[0], (shifted0[1], shifted0[2]), q0, terms0)
        y1 = face(low1[0], low1[1], q1, terms1)
        for f in range(FIELDS):
            low = jnp.where(first_row, 0.0, y0[f])
            up0 = roll(low, -16)
            up1 = roll(y1[f], -16)
            change0 = jnp.where(last_row, up1, up0) - low
            change1 = jnp.where(last_row, up0, up1) - y1[f]
            partial[0][f] = partial[0][f] - (0.5 * COURANT) * change0
            partial[1][f] = partial[1][f] - (0.5 * COURANT) * change1
        x_high = [
            face(
                cell[h][0],
                along(cell[h][0], cell[h][1], 0),
                after[h][0],
                along(after[h][0], after[h][1], 0),
            )
            for h in range(2)
        ]
        x_high = [[jnp.where(plane < 15, v, 0.0) for v in x_high[h]] for h in range(2)]
        for h in range(2):
            for f in range(FIELDS):
                out[f, :, span(plane, h)] = partial[h][f] - (0.5 * COURANT) * (
                    x_high[h][f] - x_low[h][f]
                )
        return x_high

    lax.fori_loop(0, 16, one, none, unroll=YZ_UNROLL)


def fine_outer(cells, prim, rim, reg, filled, out, old, edges):
    second = old is not None
    lane = iota((BOXMAX, 128), 1)
    k = lane % 16
    half_k = k // 2
    quarter = lane // 32
    squeeze = ((lane % 32) // 8) * 32 + (lane % 8) * 2
    part = (lane % 64) // 8
    low_half = lane < 64
    step = 0.5 * COURANT
    y_sign = jnp.where(low_half, 1.0, -1.0)
    z_sign = jnp.where(k < 8, 1.0, -1.0)
    y_weight = (jnp.where(lane < 16, step, 0.0), jnp.where(lane >= 112, -step, 0.0))
    z_weight = jnp.where(k == 0, step, jnp.where(k == 15, -step, 0.0))

    def load(plane, h):
        where = span(plane, h)
        q = [cells[f, :, where] for f in range(FIELDS)]
        pressure = prim[1, :, where]
        return q, (prim[0, :, where], pressure, prim[2, :, where], q[4] + pressure)

    def edge(ghost, ghost_terms, q, terms, sign):
        signal = jnp.maximum(ghost_terms[1], terms[1]) * sign
        return [
            (ghost_terms[0][f] + terms[0][f]) - signal * (q[f] - ghost[f]) for f in range(FIELDS)
        ]

    results = []
    for plane, side, sign in ((0, 0, 1.0), (15, 64, -1.0)):
        flux = []
        for h in range(2):
            spread = (h * 4 + quarter) * 8 + half_k + side
            ghost = [pick(rim[3 * f], spread) for f in range(FIELDS)]
            q, q_prim = load(plane, h)
            flux.append(edge(ghost, along(ghost, prims(ghost), 0), q, along(q, q_prim, 0), sign))
            results.append(
                [out[f, :, span(plane, h)] + (sign * step) * flux[h][f] for f in range(FIELDS)]
            )
        for f in range(FIELDS):
            found = []
            for h in range(2):
                v = flux[h][f]
                v = v + roll(v, -1)
                v = v + roll(v, -16)
                found.append(pick(v, squeeze))
            results.append(jnp.where((lane % 64) < 32, found[0], found[1]))
    for plane, first in ((0, 0), (15, 2 + FIELDS)):
        for h in range(2):
            for f in range(FIELDS):
                out[f, :, span(plane, h)] = results[first + h][f]
    for f in range(FIELDS):
        v = jnp.where(low_half, results[2 + f], results[4 + FIELDS + f])
        reg[3 * f] = reg[3 * f] + jnp.where(filled, v, 0.0)

    def pair(big, _):
        y_lanes = big * 8 + half_k + jnp.where(low_half, 0, 64)
        y_ghost = [pick(rim[3 * f + 1], y_lanes) for f in range(FIELDS)]
        y_ghost_terms = along(y_ghost, prims(y_ghost), 1)
        z_ghost = []
        z_ghost_terms = []
        for h in range(2):
            z_lanes = big * 8 + h * 4 + quarter + jnp.where(k >= 8, 64, 0)
            ghost = [pick(rim[3 * f + 2], z_lanes) for f in range(FIELDS)]
            z_ghost.append(ghost)
            z_ghost_terms.append(along(ghost, prims(ghost), 2))
        y_sum = [None] * FIELDS
        z_sum = [[None] * FIELDS for _ in range(2)]

        def accumulate(total, v):
            return v if total is None else total + v

        for sub in range(2):
            plane = 2 * big + sub
            q, q_prim = zip(*[load(plane, h) for h in range(2)])
            near = [jnp.where(low_half, q[0][f], q[1][f]) for f in range(FIELDS)]
            near_prim = [jnp.where(low_half, q_prim[0][i], q_prim[1][i]) for i in range(4)]
            before = [[out[f, :, span(plane, h)] for f in range(FIELDS)] for h in range(2)]
            if second:
                kept = [[old[f, :, span(plane, h)] for f in range(FIELDS)] for h in range(2)]
            y = edge(y_ghost, y_ghost_terms, near, along(near, near_prim, 1), y_sign)
            for f in range(FIELDS):
                y_sum[f] = accumulate(y_sum[f], y[f])
            news = []
            for h in range(2):
                z = edge(z_ghost[h], z_ghost_terms[h], q[h], along(q[h], q_prim[h], 2), z_sign)
                for f in range(FIELDS):
                    z_sum[h][f] = accumulate(z_sum[h][f], z[f])
                    new = before[h][f] + y_weight[h] * y[f] + z_weight * z[f]
                    if second:
                        new = jnp.where(filled, new, kept[h][f])
                    news.append((f, h, new))
            for f, h, new in news:
                out[f, :, span(plane, h)] = new

        for f in range(FIELDS):
            edges[big, f] = y_sum[f]
            edges[big, FIELDS + f] = z_sum[0][f]
            edges[big, 2 * FIELDS + f] = z_sum[1][f]
        return 0

    lax.fori_loop(0, 8, pair, 0, unroll=OUTER_UNROLL)

    def gather(big, totals):
        y_sum = [edges[big, f] for f in range(FIELDS)]
        z_sum = [[edges[big, (1 + h) * FIELDS + f] for f in range(FIELDS)] for h in range(2)]
        mine = jnp.logical_and(filled, part == big)
        y_from = (lane % 8) * 2 + jnp.where(low_half, 0, 112)
        z_from = (lane % 4) * 32 + jnp.where(low_half, 0, 15)
        new_totals = []
        for f in range(FIELDS):
            v = y_sum[f] + roll(y_sum[f], -1)
            new_totals.append(totals[2 * f] + jnp.where(mine, pick(v, y_from), 0.0))
            found = []
            for h in range(2):
                v = z_sum[h][f] + roll(z_sum[h][f], -16)
                found.append(pick(v, z_from))
            v = jnp.where(lane % 8 < 4, found[0], found[1])
            new_totals.append(totals[2 * f + 1] + jnp.where(mine, v, 0.0))
        return new_totals

    totals = [reg[3 * f + t] for f in range(FIELDS) for t in (1, 2)]
    totals = lax.fori_loop(0, 8, gather, totals, unroll=GATHER_UNROLL)
    for f in range(FIELDS):
        reg[3 * f + 1] = totals[2 * f]
        reg[3 * f + 2] = totals[2 * f + 1]


def through(tx, ty, tz, group):
    lane = iota(tx.shape, 1)
    x = 2 * group + lane // 64
    y = (lane % 64) // 8
    z = lane % 8

    def sign(place):
        return jnp.where(place == 0, 1.0, jnp.where(place == 7, -1.0, 0.0))

    total = sign(y) * pick(ty, x * 8 + z + jnp.where(y == 7, 64, 0))
    total = total + sign(z) * pick(tz, x * 8 + y + jnp.where(z == 7, 64, 0))
    if group == 0:
        total = total + jnp.where(lane < 64, tx, 0.0)
    if group == 3:
        total = total - jnp.where(lane < 64, 0.0, tx)
    return total


def fine_average(cells, reg, filled, sums):
    lane = iota((BOXMAX, 128), 1)
    even_k = lane % 2 == 0
    even_j = (lane // 16) % 2 == 0
    squeeze = (2 * ((lane % 32) // 8) + lane // 64) * 16 + (lane % 8) * 2 + (lane % 64) // 32
    faces = [reg[v] for v in range(3 * FIELDS)]
    for group in range(4):
        tiles = []
        for f in range(FIELDS):
            for sub in range(2):
                for h in range(2):
                    plane = 4 * group + 2 * sub
                    tiles.append(cells[f, :, span(plane, h)] + cells[f, :, span(plane + 1, h)])
        tiles = [v + roll(v, 1 if n % 2 else -1) for n, v in enumerate(tiles)]
        tiles = [jnp.where(even_k, tiles[n], tiles[n + 1]) for n in range(0, 4 * FIELDS, 2)]
        tiles = [v + roll(v, 16 if n % 2 else -16) for n, v in enumerate(tiles)]
        tiles = [jnp.where(even_j, tiles[n], tiles[n + 1]) for n in range(0, 2 * FIELDS, 2)]
        tiles = [pick(v, squeeze) for v in tiles]
        crossed = [through(*faces[3 * f : 3 * f + 3], group) for f in range(FIELDS)]
        results = [
            jnp.where(filled, tiles[f] - (0.5 * COURANT) * crossed[f], 0.0) for f in range(FIELDS)
        ]
        for f in range(FIELDS):
            sums[4 * f + group] = results[f]


def coarse_step(block, y_rim, z_rim, new, x_face, y_low, y_high, z_low, z_high):
    lane = iota((16, 128), 1)
    row = iota((16, 128), 0)
    tip = iota((8, 128), 0)

    def load(plane):
        return [block[f, plane] for f in range(FIELDS)]

    def widen(x, _):
        column = (x % 8) * 16 + row
        for f in range(FIELDS):
            below = jnp.broadcast_to(z_rim[0, x // 8, f : f + 1, :], (16, 128))
            above = jnp.broadcast_to(z_rim[1, x // 8, f : f + 1, :], (16, 128))
            side = jnp.where(lane == 64, pick(above, column), pick(below, column))
            block[f, x + 1] = jnp.where(lane < 64, block[f, x + 1], side)
        return 0

    lax.fori_loop(0, 16, widen, 0, unroll=4)

    ghost = load(0)
    here = load(1)
    here_prim = prims(here)
    low = face(ghost, along(ghost, prims(ghost), 0), here, along(here, here_prim, 0))
    for f in range(FIELDS):
        x_face[f, 0] = low[f]

    def one(x, carried):
        here, here_prim, x_low = carried
        after = load(x + 2)
        after_prim = prims(after)
        x_high = face(here, along(here, here_prim, 0), after, along(after, after_prim, 0))

        tips = []
        for f in range(FIELDS):
            above = y_rim[1, f, pl.ds(x, 1), :]
            below = y_rim[0, f, pl.ds(x, 1), :]
            tips.append(
                jnp.where(
                    tip == 0,
                    jnp.broadcast_to(above, (8, 128)),
                    jnp.broadcast_to(below, (8, 128)),
                )
            )
        tip_terms = along(tips, prims(tips), 1)
        terms = along(here, here_prim, 1)

        def tall(low, high):
            return jnp.concatenate([low, high], axis=0)

        cells = [tall(here[f], tips[f]) for f in range(FIELDS)]
        terms = ([tall(terms[0][f], tip_terms[0][f]) for f in range(FIELDS)], tall(terms[1], tip_terms[1]))
        shifted = moved(cells, terms, lambda v: pltpu.roll(v, 1, 0))
        y = face(shifted[0], (shifted[1], shifted[2]), cells, terms)

        terms = along(here, here_prim, 2)
        shifted = moved(here, terms, lambda v: pltpu.roll(v, 1, 1))
        z = face(shifted[0], (shifted[1], shifted[2]), here, terms)
        for f in range(FIELDS):
            up = pltpu.roll(y[f], 23, 0)[:16]
            down = y[f][:16]
            right = pltpu.roll(z[f], 127, 1)
            x_face[f, x + 1] = x_high[f]
            y_low[f, x] = down
            y_high[f, x] = up
            z_low[f, x] = z[f]
            z_high[f, x] = right
            change = (x_high[f] - x_low[f]) + (up - down) + (right - z[f])
            new[f, x] = here[f] - (0.5 * COURANT) * change
        return after, after_prim, x_high

    lax.fori_loop(0, 16, one, (here, here_prim, low), unroll=COARSE_UNROLL)


def cut_rims(source, corner):
    cx, cy, cz = corner
    lane = iota((8, 128), 1)
    row = iota((8, 128), 0)
    low_half = lane < 64
    part = (lane % 64) // 8
    along_z = cz + lane % 8
    ends = jnp.where(low_half, cz - 1, cz + 8)
    rows_x = row == part
    rows_z = row == lane % 8
    lines = []
    for f in range(FIELDS):
        low = pick(source(f, cx - 1, cy, 8), along_z)
        high = pick(source(f, cx + 8, cy, 8), along_z)
        v = jnp.where(rows_x, jnp.where(low_half, low, high), 0.0)
        lines.append(jnp.sum(v, axis=0, keepdims=True))
        low = jnp.zeros((8, 128), F32)
        high = jnp.zeros((8, 128), F32)
        total = jnp.zeros((8, 128), F32)
        for big in range(8):
            here = row == big
            low = jnp.where(here, jnp.broadcast_to(source(f, cx + big, cy - 1, 1), (8, 128)), low)
            high = jnp.where(here, jnp.broadcast_to(source(f, cx + big, cy + 8, 1), (8, 128)), high)
            total = jnp.where(part == big, pick(source(f, cx + big, cy, 8), ends), total)
        v = jnp.where(low_half, pick(low, along_z), pick(high, along_z))
        lines.append(jnp.sum(jnp.where(rows_x, v, 0.0), axis=0, keepdims=True))
        lines.append(jnp.sum(jnp.where(rows_z, total, 0.0), axis=0, keepdims=True))
    return lines


def plan_settle(corners, new, x_face, y_low, y_high, z_low, z_high, weight, index):
    lane = iota((16, 128), 1)
    row = iota((16, 128), 0)

    def one(x, _):
        kind = jnp.zeros((16, 128), I32)
        for c in range(REGIONS):
            cx, cy, cz = corners[c]
            step = x - cx
            inside = jnp.logical_and(step >= 0, step < 8)
            dy = row - cy
            dz = lane - cz
            in_y = jnp.logical_and(dy >= 0, dy < 8)
            in_z = jnp.logical_and(dz >= 0, dz < 8)
            near = jnp.where(dy == -1, 4, jnp.where(dy == 8, 5, 0))
            side = jnp.where(dz == -1, 6, jnp.where(dz == 8, 7, 0))
            plain = jnp.where(inside, 1, jnp.where(step == -1, 2, jnp.where(step == 8, 3, 0)))
            mine = jnp.where(
                jnp.logical_and(in_y, in_z),
                plain,
                jnp.where(inside, jnp.where(in_z, near, jnp.where(in_y, side, 0)), 0),
            )
            ys = jnp.clip(dy, 0, 7)
            zs = jnp.clip(dz, 0, 7)
            lanes = jnp.where(mine < 4, ys * 8 + zs, 32 + 8 * mine + jnp.where(mine < 6, zs, ys))
            used = mine > 0
            kind = jnp.where(used, mine, kind)
            index[x, c] = jnp.where(used, lanes + 128, 0)
        factor = jnp.where(kind < 2, 0.0, jnp.where(kind % 2 == 0, -COURANT, COURANT))
        weight[x] = jnp.where(kind == 1, 0.125, 0.0625 * factor)
        for f in range(FIELDS):
            flux = jnp.where(
                kind < 4,
                jnp.where(kind == 2, x_face[f, x + 1], x_face[f, x]),
                jnp.where(
                    kind < 6,
                    jnp.where(kind == 4, y_high[f, x], y_low[f, x]),
                    jnp.where(kind == 6, z_high[f, x], z_low[f, x]),
                ),
            )
            plain = new[f, x]
            ring = jnp.where(kind >= 2, plain - 0.5 * factor * flux, plain)
            new[f, x] = jnp.where(kind == 1, 0.0, ring)
        return 0

    lax.fori_loop(0, 16, one, 0)


def settle_rows(faces, rows, crossed):
    lane = iota((REGIONS, 128), 1)
    spot = ((lane % 16) // 8) * 64 + lane % 8
    results = []
    added = []
    for f in range(FIELDS):
        tx, ty, tz = faces[3 * f], faces[3 * f + 1], faces[3 * f + 2]
        results.append((f, 0, tx))
        results.append((f, 9, pltpu.roll(tx, 64, 1)))
        for big in range(8):
            around = jnp.where(lane < 80, pick(ty, spot + 8 * big), pick(tz, spot + 8 * big))
            results.append((f, 1 + big, jnp.where(lane < 64, 0.0, around)))
        for group in range(4):
            added.append((0.5 * COURANT) * through(tx, ty, tz, group))
    for f, where, v in results:
        rows[f, where] = v
    for tile, v in enumerate(added):
        crossed[tile] = v


def settle(corners, rows, new, weight, index, out, start):
    def one(step, _):
        x = start + step
        values = [jnp.zeros((16, 128), F32) for _ in range(FIELDS)]
        for c in range(REGIONS):
            which = jnp.clip(x - corners[c][0] + 1, 0, 9)
            lanes = index[x, c]
            used = lanes >= 128
            lanes = lanes & 127
            for f in range(FIELDS):
                line = jnp.broadcast_to(rows[f, which, c : c + 1, :], (16, 128))
                values[f] = jnp.where(used, pick(line, lanes), values[f])
        factor = weight[x]
        results = [new[f, x] + factor * values[f] for f in range(FIELDS)]
        for f in range(FIELDS):
            out[f, x] = results[f][:, :64]
        return 0

    lax.fori_loop(0, 4, one, 0, unroll=SETTLE_UNROLL)


def whole(
    sizes,
    parent_hbm,
    plane_hbm,
    corner_hbm,
    coarse_hbm,
    fine_hbm,
    coarse_out,
    fine_out,
    sums_out,
    spots_out,
    parent_ref,
    corner_ref,
    plane_ref,
    coarse_ref,
    block,
    new,
    x_face,
    y_low,
    y_high,
    z_low,
    z_high,
    weight,
    index,
    y_stage,
    z_stage,
    x_rim,
    y_packed,
    y_rim,
    z_rim,
    cut,
    rim_out,
    rim_in_old,
    rim_in_mid,
    rim,
    fine_ref,
    prim,
    half,
    fine_new,
    coarse_new,
    reg,
    edges,
    route,
    relay_in,
    relay_out,
    sums,
    sums_in,
    row_stage,
    face_out,
    face_in,
    faces,
    answer_rows,
    crossed,
    table,
    spots,
    load_sems,
    halo_send,
    halo_recv,
    many_send,
    many_recv,
):
    n_gx, n_gy, n_gz = sizes
    members = n_gy * n_gz
    share = -(-4 * FIELDS // members)
    relays = -(-4 * FIELDS // share)
    rim_in = (rim_in_old, rim_in_mid)
    gx = lax.axis_index("gx")
    gy = lax.axis_index("gy")
    gz = lax.axis_index("gz")
    within = gy * n_gz + gz
    myself = gx * members + within
    start = gx * (members * BOXMAX)

    def hops(move):
        return min(move[0], n_gy - move[0]) + min(move[1], n_gz - move[1])

    moves = [(dy, dz) for dy in range(n_gy) for dz in range(n_gz) if dy or dz]
    peers = []
    for dy, dz in sorted(moves, key=hops, reverse=True):
        other_y = lax.rem(gy + dy, n_gy)
        other_z = lax.rem(gz + dz, n_gz)
        peers.append((other_y * n_gz + other_z, (gx, other_y, other_z)))

    barrier = pltpu.get_barrier_semaphore()
    for _, device in peers:
        pl.semaphore_signal(barrier, inc=1, device_id=device, device_id_type=MESH)

    x_next = (lax.rem(gx + 1, n_gx), gy, gz)
    x_prev = (lax.rem(gx + n_gx - 1, n_gx), gy, gz)
    y_next = (gx, lax.rem(gy + 1, n_gy), gz)
    y_prev = (gx, lax.rem(gy + n_gy - 1, n_gy), gz)
    z_next = (gx, gy, lax.rem(gz + 1, n_gz))
    z_prev = (gx, gy, lax.rem(gz + n_gz - 1, n_gz))
    pl.semaphore_signal(barrier, inc=1, device_id=x_next, device_id_type=MESH)
    pl.semaphore_signal(barrier, inc=1, device_id=x_prev, device_id_type=MESH)

    def fetch(src, dst, index):
        copy = pltpu.make_async_copy(src, dst, load_sems.at[index])
        copy.start()
        return copy

    coarse_load = fetch(coarse_hbm, coarse_ref, 0)
    parent_load = fetch(parent_hbm, parent_ref, 1)
    corner_load = fetch(corner_hbm, corner_ref, 2)
    plane_load = fetch(plane_hbm, plane_ref, 3)
    fine_load = fetch(fine_hbm, fine_ref, 4)

    parent_load.wait()
    corner_load.wait()

    def scan(entry, found):
        c0, c1, c2, c3 = found
        hit = parent_ref[start + entry] == myself
        return (
            jnp.where(hit, c1, c0),
            jnp.where(hit, c2, c1),
            jnp.where(hit, c3, c2),
            jnp.where(hit, entry, c3),
        )

    zero = jnp.int32(0)
    children = lax.fori_loop(0, members * BOXMAX, scan, (zero, zero, zero, zero), unroll=8)
    for c in range(REGIONS):
        for k in range(3):
            spot = jnp.clip(corner_ref[k, start + children[c]], 1, 55 if k == 2 else 7)
            table[4 * c + k] = spot
            spots[4 * c + k] = spot
        spots[4 * c + 3] = zero
    corner_store = fetch(spots, spots_out, 11)
    child_peer = [child // BOXMAX for child in children]
    own = [parent_ref[start + within * BOXMAX + s] for s in range(BOXMAX)]
    own_peer = [lax.rem(jnp.maximum(own[s], 0), members) for s in range(BOXMAX)]

    def look_up(other, _):
        rank = zero
        for c in range(1, REGIONS):
            rank = jnp.where(child_peer[c] == other, c, rank)
        found = zero
        for s in range(BOXMAX):
            found = jnp.where(jnp.logical_and(own[s] >= 0, own_peer[s] == other), s, found)
        table[32 + other] = rank
        table[32 + members + other] = found
        return 0

    lax.fori_loop(0, members, look_up, 0, unroll=4)

    def cut_all(when, source):
        def one(c, _):
            corner = (table[4 * c], table[4 * c + 1], table[4 * c + 2])

            for v, line in enumerate(cut_rims(source, corner)):
                cut[when, c, v : v + 1, :] = line
            return 0

        lax.fori_loop(0, REGIONS, one, 0, unroll=CUT_UNROLL)

    def ship(src, dst, index, device):
        pltpu.make_async_remote_copy(
            src_ref=src,
            dst_ref=dst,
            send_sem=many_send.at[index],
            recv_sem=many_recv.at[index],
            device_id=device,
            device_id_type=MESH,
        ).start()

    def wait_many(every, index, semaphores):
        pltpu.make_async_copy(every, every, semaphores.at[index]).wait()

    others = pl.ds(0, members - 1)

    def fill_rims(when):
        def one(other, _):
            rim_out[when, other] = cut[when, table[32 + other]]
            return 0

        lax.fori_loop(0, members, one, 0, unroll=4)
        rim_in[when][within] = rim_out[when, within]

    def send_rims(when):
        for other, device in peers:
            ship(rim_out.at[when, other], rim_in[when].at[within], when, device)

    lane16 = iota((16, 128), 1)
    row16 = iota((16, 128), 0)
    coarse_load.wait()
    for f in range(FIELDS):
        block[f, 1:17, :, 0:64] = coarse_ref[f]
    match = row16 == lane16 % 16
    lane8 = iota((8, 128), 1)
    edge_rows = [(block[f, 1:17, 0, :], block[f, 1:17, 15, :]) for f in range(FIELDS)]
    columns_found = []
    for f in range(FIELDS):
        for h in range(2):
            low = jnp.zeros((16, 128), F32)
            high = jnp.zeros((16, 128), F32)
            for x in range(8):
                plane = block[f, 1 + 8 * h + x]
                here = lane16 // 16 == x
                low = jnp.where(here, jnp.broadcast_to(plane[:, 0:1], (16, 128)), low)
                high = jnp.where(here, jnp.broadcast_to(plane[:, 63:64], (16, 128)), high)
            low = jnp.sum(jnp.where(match, low, 0.0), axis=0, keepdims=True)
            high = jnp.sum(jnp.where(match, high, 0.0), axis=0, keepdims=True)
            columns_found.append((f, h, low, high))
    for f in range(FIELDS):
        for side in range(2):
            rows = edge_rows[f][side]
            y_stage[side, f] = jnp.where(lane8 < 64, rows[:8], pltpu.roll(rows[8:], 64, 1))
    for f, h, low, high in columns_found:
        z_stage[0, h, f : f + 1, :] = low
        z_stage[1, h, f : f + 1, :] = high

    cut_all(0, lambda f, x, y, n: block[f, x + 1, pl.ds(y, n), :])
    fill_rims(0)

    pl.semaphore_wait(barrier, members + 1)

    def halo(src, dst, index, device):
        copy = pltpu.make_async_remote_copy(
            src_ref=src,
            dst_ref=dst,
            send_sem=halo_send.at[index],
            recv_sem=halo_recv.at[index],
            device_id=device,
            device_id_type=MESH,
        )
        copy.start()
        return copy

    halos = [
        halo(block.at[:, 16], x_rim.at[0], 0, x_next),
        halo(block.at[:, 1], x_rim.at[1], 1, x_prev),
        halo(y_stage.at[1], y_packed.at[0], 2, y_next),
        halo(y_stage.at[0], y_packed.at[1], 3, y_prev),
        halo(z_stage.at[1], z_rim.at[0], 4, z_next),
        halo(z_stage.at[0], z_rim.at[1], 5, z_prev),
    ]

    send_rims(0)

    for v in range(3 * FIELDS):
        reg[v] = jnp.zeros((BOXMAX, 128), F32)

    for copy in halos:
        copy.wait()
    for f in range(FIELDS):
        block[f, 0] = x_rim[0, f]
        block[f, 17] = x_rim[1, f]
        for side in range(2):
            y_rim[side, f, 0:8] = y_packed[side, f]
            y_rim[side, f, 8:16] = pltpu.roll(y_packed[side, f], 64, 1)
    coarse_step(block, y_rim, z_rim, new, x_face, y_low, y_high, z_low, z_high)
    cut_all(
        1,
        lambda f, x, y, n: 0.5 * (block[f, x + 1, pl.ds(y, n), :] + new[f, x, pl.ds(y, n), :]),
    )
    fill_rims(1)
    send_rims(1)

    plane_load.wait()
    n_rows = REGIONS * members
    columns = members * BOXMAX
    row = iota((n_rows, columns), 0)
    column = iota((n_rows, columns), 1)
    slots = plane_ref[pl.ds(gx * (columns // 128), columns // 128), :] if columns >= 128 else None
    if columns >= 128:
        slots = jnp.concatenate(
            [
                jnp.broadcast_to(slots[h : h + 1, :], (n_rows, 128))
                for h in range(columns // 128)
            ],
            axis=1,
        )
    else:
        slots = jnp.broadcast_to(plane_ref[0:1, 0:columns], (n_rows, columns))
    number = column.astype(F32)
    far = 65536.0
    candidate = jnp.where(slots == row // REGIONS + gx * members, number, far)
    chosen = jnp.full((n_rows, 1), far)
    for r in range(REGIONS):
        least = jnp.min(candidate, axis=1, keepdims=True)
        chosen = jnp.where(row[:, 0:1] % REGIONS == r, least, chosen)
        candidate = jnp.where(candidate == least, far, candidate)
    route[...] = jnp.where(number == chosen, 1.0, 0.0)

    fine_load.wait()
    fine_prims(fine_ref, prim)
    fine_inner(fine_ref, prim, half)

    sub = iota((BOXMAX, 128), 0)
    owner = jnp.zeros((BOXMAX, 128), I32)
    for s in range(BOXMAX):
        owner = jnp.where(sub == s, own[s], owner)
    filled = owner >= 0

    def take_rims(when):
        wait_many(rim_in[when].at[others], when, many_recv)
        for s in range(BOXMAX):
            rows = rim_in[when][own_peer[s]]
            for v in range(3 * FIELDS):
                rim[v, s : s + 1, :] = rows[v : v + 1, :]

    take_rims(0)
    fine_outer(fine_ref, prim, rim, reg, filled, half, None, edges)
    fine_prims(half, prim)
    fine_inner(half, prim, fine_new)
    fine_average(fine_new, reg, filled, sums)

    is_relay = within < relays
    for other, device in peers:

        @pl.when(other < relays)
        def _(other=other, device=device):
            ship(sums.at[pl.ds(other * share, share)], relay_in.at[within], 2, device)

    @pl.when(is_relay)
    def _():
        relay_in[within] = sums[pl.ds(within * share, share)]

    take_rims(1)
    fine_outer(half, prim, rim, reg, filled, fine_new, fine_ref, edges)
    fine_store = fetch(fine_new, fine_out, 5)

    for s in range(BOXMAX):
        row_stage[s] = reg[:, s, :]
    for other, device in peers:
        face_out[other] = row_stage[table[32 + members + other]]
        ship(face_out.at[other], face_in.at[within], 3, device)
    face_in[within] = row_stage[table[32 + members + within]]

    @pl.when(is_relay)
    def _():
        wait_many(relay_in.at[others], 2, many_recv)
        for j in range(share):
            sorted_rows = jnp.dot(
                route[...],
                relay_in[:, j].reshape(columns, 128),
                precision=lax.Precision.HIGHEST,
                preferred_element_type=F32,
            )
            for p in range(members):
                relay_out[p, j] = sorted_rows[REGIONS * p : REGIONS * p + REGIONS]
        for other, device in peers:
            ship(relay_out.at[other], sums_in.at[pl.ds(within * share, share)], 4, device)
        sums_in[pl.ds(within * share, share)] = relay_out[within]

    corners = [(table[4 * c], table[4 * c + 1], table[4 * c + 2]) for c in range(REGIONS)]
    plan_settle(corners, new, x_face, y_low, y_high, z_low, z_high, weight, index)

    wait_many(face_in.at[others], 3, many_recv)
    for c in range(REGIONS):
        rows = face_in[child_peer[c]]
        for v in range(3 * FIELDS):
            faces[v, c : c + 1, :] = rows[v : v + 1, :]

    def wait_relays(every, index, semaphores):
        @pl.when(is_relay)
        def _():
            wait_many(every.at[pl.ds(0, (relays - 1) * share)], index, semaphores)

        @pl.when(jnp.logical_not(is_relay))
        def _():
            wait_many(every.at[pl.ds(0, relays * share)], index, semaphores)

    settle_rows(faces, answer_rows, crossed)
    coarse_stores = []
    for part in range(4):
        settle(corners, answer_rows, new, weight, index, coarse_new, 4 * part)
        planes = pl.ds(4 * part, 4)
        coarse_stores.append(fetch(coarse_new.at[:, planes], coarse_out.at[:, planes], 6 + part))
    wait_relays(sums_in, 4, many_recv)
    for tile in range(4 * FIELDS):
        crossed[tile] = sums_in[tile] + crossed[tile]
    sums_store = fetch(crossed, sums_out, 10)
    wait_many(rim_out.at[0, others], 0, many_send)
    wait_many(rim_out.at[1, others], 1, many_send)
    wait_relays(sums, 2, many_send)
    wait_many(face_out.at[others], 3, many_send)

    @pl.when(is_relay)
    def _():
        wait_many(relay_out.at[others], 4, many_send)

    fine_store.wait()
    sums_store.wait()
    corner_store.wait()
    for copy in coarse_stores:
        copy.wait()


def average_down(
    coarse_in, fine_in, sums_in, spots_in, coarse_out, fine_out, coarse, fine, sums, spots, arrive, leave
):
    def move(src, dst, sems, index):
        copy = pltpu.make_async_copy(src, dst, sems.at[index])
        copy.start()
        return copy

    spots_load = move(spots_in, spots, arrive, 2 * FIELDS)
    sums_load = move(sums_in, sums, arrive, 2 * FIELDS + 1)
    coarse_loads = [move(coarse_in.at[f], coarse.at[f], arrive, f) for f in range(FIELDS)]
    fine_loads = [move(fine_in.at[f], fine.at[f], arrive, FIELDS + f) for f in range(FIELDS)]
    spots_load.wait()
    sums_load.wait()
    lane = iota((8, 128), 1)
    row = iota((8, 128), 0)
    stores = []
    for f in range(FIELDS):
        coarse_loads[f].wait()
        for c in range(REGIONS):
            cx, cy, cz = spots[4 * c], spots[4 * c + 1], spots[4 * c + 2]
            z = lane - cz
            inside = jnp.logical_and(z >= 0, z < 8)[:, :64]
            place = row * 8 + jnp.clip(z, 0, 7)
            rows = pl.ds(cy, 8)
            old = [coarse[f, cx + x, rows, :] for x in range(8)]
            news = []
            for x in range(8):
                line = jnp.broadcast_to(sums[4 * f + x // 2, c : c + 1, :], (8, 128))
                value = 0.125 * pick(line, place + 64 * (x % 2))
                news.append(jnp.where(inside, value[:, :64], old[x]))
            for x in range(8):
                coarse[f, cx + x, rows, :] = news[x]
        stores.append(move(coarse.at[f], coarse_out.at[f], leave, f))
        fine_loads[f].wait()
        stores.append(move(fine.at[f], fine_out.at[f], leave, FIELDS + f))
    for copy in stores:
        copy.wait()


def on_device(sizes, coarse_state, fine_state, slot_parent, slot_corner):
    members = sizes[1] * sizes[2]
    share = -(-4 * FIELDS // members)
    relays = -(-4 * FIELDS // share)
    hbm = pl.BlockSpec(memory_space=pltpu.HBM)
    fine = jnp.transpose(fine_state, (1, 0, 2))
    corner = jnp.transpose(slot_corner, (1, 0))
    plane = slot_parent.reshape(-1, min(128, slot_parent.shape[0]))
    field_block = (FIELDS, 16, 16, 128)
    rows = 3 * FIELDS
    ringed, fine_next, sums, spots = pl.pallas_call(
        functools.partial(whole, sizes),
        out_shape=(
            jax.ShapeDtypeStruct(coarse_state.shape, F32),
            jax.ShapeDtypeStruct(fine.shape, F32),
            jax.ShapeDtypeStruct((4 * FIELDS, REGIONS, 128), F32),
            jax.ShapeDtypeStruct((4 * REGIONS,), I32),
        ),
        in_specs=[hbm] * 5,
        out_specs=(hbm, hbm, hbm, hbm),
        scratch_shapes=[
            pltpu.SMEM(slot_parent.shape, I32),
            pltpu.SMEM(corner.shape, I32),
            pltpu.VMEM(plane.shape, I32),
            pltpu.VMEM(coarse_state.shape, F32),
            pltpu.VMEM((FIELDS, 18, 16, 128), F32),
            pltpu.VMEM(field_block, F32),
            pltpu.VMEM((FIELDS, 17, 16, 128), F32),
            pltpu.VMEM(field_block, F32),
            pltpu.VMEM(field_block, F32),
            pltpu.VMEM(field_block, F32),
            pltpu.VMEM(field_block, F32),
            pltpu.VMEM((16, 16, 128), F32),
            pltpu.VMEM((16, REGIONS, 16, 128), I32),
            pltpu.VMEM((2, FIELDS, 8, 128), F32),
            pltpu.VMEM((2, 2, FIELDS, 128), F32),
            pltpu.VMEM((2, FIELDS, 16, 128), F32),
            pltpu.VMEM((2, FIELDS, 8, 128), F32),
            pltpu.VMEM((2, FIELDS, 16, 128), F32),
            pltpu.VMEM((2, 2, FIELDS, 128), F32),
            pltpu.VMEM((2, REGIONS, 3 * FIELDS, 128), F32),
            pltpu.VMEM((2, members, 3 * FIELDS, 128), F32),
            pltpu.VMEM((members, 3 * FIELDS, 128), F32),
            pltpu.VMEM((members, 3 * FIELDS, 128), F32),
            pltpu.VMEM((3 * FIELDS, BOXMAX, 128), F32),
            pltpu.VMEM(fine.shape, F32),
            pltpu.VMEM((3,) + fine.shape[1:], F32),
            pltpu.VMEM(fine.shape, F32),
            pltpu.VMEM(fine.shape, F32),
            pltpu.VMEM(coarse_state.shape, F32),
            pltpu.VMEM((rows, BOXMAX, 128), F32),
            pltpu.VMEM((8, rows, BOXMAX, 128), F32),
            pltpu.VMEM((REGIONS * members, BOXMAX * members), F32),
            pltpu.VMEM((members, share, BOXMAX, 128), F32),
            pltpu.VMEM((members, share, REGIONS, 128), F32),
            pltpu.VMEM((relays * share, BOXMAX, 128), F32),
            pltpu.VMEM((relays * share, REGIONS, 128), F32),
            pltpu.VMEM((BOXMAX, rows, 128), F32),
            pltpu.VMEM((members, rows, 128), F32),
            pltpu.VMEM((members, rows, 128), F32),
            pltpu.VMEM((rows, REGIONS, 128), F32),
            pltpu.VMEM((FIELDS, 10, REGIONS, 128), F32),
            pltpu.VMEM((4 * FIELDS, REGIONS, 128), F32),
            pltpu.SMEM((32 + 2 * members,), I32),
            pltpu.SMEM((4 * REGIONS,), I32),
            pltpu.SemaphoreType.DMA((12,)),
            pltpu.SemaphoreType.DMA((6,)),
            pltpu.SemaphoreType.DMA((6,)),
            pltpu.SemaphoreType.DMA((5,)),
            pltpu.SemaphoreType.DMA((5,)),
        ],
        compiler_params=pltpu.CompilerParams(
            collective_id=0, has_side_effects=True, vmem_limit_bytes=62 * 1024 * 1024
        ),
    )(slot_parent, plane, corner, coarse_state, fine)
    coarse_next, fine_next = pl.pallas_call(
        average_down,
        out_shape=(
            jax.ShapeDtypeStruct(coarse_state.shape, F32),
            jax.ShapeDtypeStruct(fine.shape, F32),
        ),
        in_specs=[hbm] * 4,
        out_specs=(hbm, hbm),
        scratch_shapes=[
            pltpu.VMEM(coarse_state.shape, F32),
            pltpu.VMEM(fine.shape, F32),
            pltpu.VMEM((4 * FIELDS, REGIONS, 128), F32),
            pltpu.SMEM((4 * REGIONS,), I32),
            pltpu.SemaphoreType.DMA((2 * FIELDS + 2,)),
            pltpu.SemaphoreType.DMA((2 * FIELDS,)),
        ],
        compiler_params=pltpu.CompilerParams(vmem_limit_bytes=62 * 1024 * 1024),
    )(ringed, fine_next, sums, spots)
    return coarse_next, jnp.transpose(fine_next, (1, 0, 2))


def solution(mesh):
    sizes = tuple(mesh.shape[name] for name in ("gx", "gy", "gz"))
    return jax.shard_map(
        functools.partial(on_device, sizes),
        mesh=mesh,
        in_specs=(P(None, "gx", "gy", "gz"), P(("gx", "gy", "gz"), None, None), P(), P()),
        out_specs=(P(None, "gx", "gy", "gz"), P(("gx", "gy", "gz"), None, None)),
        check_vma=False,
    )
```
